32 devices in a mesh: dp: 2 (over y), seq: 4 (over x, core), fsdp: 4 (over z).
Axes of the slice: x: 2, y: 2, z: 4, core: 2. Of those that a mesh axis runs over, the one named last changes fastest.
Arguments:
- tokens: bfloat16 [8, 1024, 2048], P(('dp', 'fsdp'), 'seq'), may hold values from -6 to 6
- lengths: int32 [8, 4], P(('dp', 'fsdp')), may hold values from 1 to 769, 1024 in all within a row
- norm_gain: float32 [2048], replicated, may hold values from 0.5 to 1.5
- w_in: bfloat16 [2048, 8448], P(('dp', 'seq', 'fsdp')), may hold values from -0.125 to 0.125
- w_dt: bfloat16 [2048, 64], P(('dp', 'seq', 'fsdp')), may hold values from -0.25 to 0.25
- conv_w: float32 [4, 4352], replicated, may hold values from -3 to 3
- conv_b: float32 [4352], replicated, may hold values from -0.5 to 0.5
- dt_bias: float32 [64], replicated, may hold values from -5 to -3
- a_log: float32 [64], replicated, may hold values from -6 to 0
- skip: float32 [64], replicated, may hold values from 0.5 to 1.5
- gate_gain: float32 [4096], replicated, may hold values from 0.5 to 1.5
- w_out: bfloat16 [4096, 2048], P(('dp', 'seq', 'fsdp')), may hold values from -0.125 to 0.125
- cotangent: bfloat16 [4, 8, 1024, 2048], P(None, ('dp', 'fsdp'), 'seq'), may hold values from -6 to 6
Outputs:
- mixed: bfloat16 [4, 8, 1024, 2048], P(None, ('dp', 'fsdp'), 'seq')
- grad_tokens: bfloat16 [8, 1024, 2048], P(('dp', 'fsdp'), 'seq')
- grad_norm_gain: float32 [2048], replicated
- grad_w_in: float32 [2048, 8448], P(('dp', 'seq', 'fsdp'))
- grad_w_dt: float32 [2048, 64], P(('dp', 'seq', 'fsdp'))
- grad_conv_w: float32 [4, 4352], replicated
- grad_conv_b: float32 [4352], replicated
- grad_dt_bias: float32 [64], replicated
- grad_a_log: float32 [64], replicated
- grad_skip: float32 [64], replicated
- grad_gate_gain: float32 [4096], replicated
- grad_w_out: float32 [4096, 2048], P(('dp', 'seq', 'fsdp'))
The draws below stay inside these ranges and needn't reach their ends.
Inputs may be any that keep to these rules, and one draw needn't show every extreme that they name: `lengths`: each row sums to 1024; each sequence holds one document of exactly 769 tokens.
All inputs are finite; a program needn't handle non-finite values.
Results may differ from the reference program's by a relative error of at most 0.014.
Values may be sent and summed in bfloat16 or wider, within the bound.
No kernel may reach another device: no remote copies, remote signals or barrier semaphores. Data moves between devices by JAX's collectives and lax.ppermute only.
A program may use at most 512 MiB of HBM per device.

```python
import math
import jax
import jax.numpy as jnp
import numpy as np
from jax import lax

D = 2048
HEADS = 64
HEADDIM = 64
STATE = 128
CONV = 4
SPAN = 256
DOCS = 4
TOK_DEV = 256
INNER = 4096
LENGTH = 1024
SEQS = 8


def draw_a_log(key, part):
    key = jax.random.fold_in(key, 11)
    return jax.random.uniform(key, (HEADS,), jnp.float32, -5.5, 0.0)


def block_scale(stream_key, shape, shards, smallest, largest):
    def one(position, shards_of):
        heights = jax.random.uniform(jax.random.fold_in(jax.random.fold_in(stream_key, 6), position), (shards_of,), jnp.float32, smallest / len(shards), largest / len(shards))
        return jnp.repeat(jnp.exp(heights), shape[position] // shards_of).reshape((-1,) + (1,) * (len(shape) - position - 1))

    factor_of = one(*shards[0])
    for cut in shards[1:]:
        factor_of = factor_of * one(*cut)
    return factor_of


def length_profile(number_of, total, limit, slope):
    loads = [(1 << 20) // math.isqrt(standing ** slope) + 1 for standing in range(2, number_of + 1)]
    surplus, counts = total - limit - (number_of - 1), [1] * (number_of - 1)
    while surplus > 0:
        candidates = [i for i in range(number_of - 1) if counts[i] < limit]
        mass, left = sum([loads[i] for i in candidates]), surplus
        for i in candidates:
            extra = min(limit - counts[i], max(1, left * loads[i] // mass), surplus)
            counts[i] = counts[i] + extra
            surplus = surplus - extra
    return np.array([limit] + counts)


def ragged(stream_key, count, total, bound, slope):
    if count == 2:
        one = jax.random.randint(stream_key, (), max(1, total - bound), min(bound, total - 1) + 1)
        return jnp.stack([one, total - one])
    sizes = jnp.asarray(length_profile(count, total, bound, slope), jnp.int32)
    twos = (count - 1) // 2
    donor, sink = sizes[1:1 + 2 * twos:2], sizes[2:2 + 2 * twos:2]
    slack = jnp.minimum(donor - 1, bound - sink)
    moved = jax.random.randint(jax.random.fold_in(stream_key, 1), (twos,), 0, 1 << 20) % (slack + 1)
    sizes = sizes.at[1:1 + 2 * twos:2].set(donor - moved).at[2:2 + 2 * twos:2].set(sink + moved)
    return sizes[jax.random.permutation(jax.random.fold_in(stream_key, 2), count)]


def scatter_about(rng, dims, scale, bound, cuts=(), kind=jnp.bfloat16):
    drawn = scale * jax.random.normal(rng, dims, jnp.float32)
    if cuts:
        drawn = drawn * block_scale(rng, dims, cuts, -0.22, 0.18)
    return jnp.clip(drawn, -bound, bound).astype(kind)


def setup_inputs(seed: int = 0) -> dict:
    seeds = jax.random.split(jax.random.key(seed), 14)
    tokens = scatter_about(seeds[0], (SEQS, LENGTH, D), 1.0, 6.0, ((0, 8), (1, 4)))
    lengths = jax.vmap(lambda own: ragged(own, DOCS, LENGTH, LENGTH - TOK_DEV + 1, 2))(jax.random.split(seeds[1], SEQS)).reshape((SEQS, DOCS)).astype(jnp.int32)
    norm_gain = jnp.clip(1.0 + 0.1 * jax.random.normal(seeds[2], (D,), jnp.float32), 0.5, 1.5)
    w_in = scatter_about(seeds[3], (D, 2 * INNER + 2 * STATE), D ** -0.5, 0.125, ((0, 32),))
    w_dt = scatter_about(seeds[4], (D, HEADS), (D // 4) ** -0.5, 0.25, ((0, 32),))
    conv_w = scatter_about(seeds[5], (CONV, INNER + 2 * STATE), CONV ** -0.5, 3.0, (), jnp.float32)
    conv_b = jnp.clip(jax.random.uniform(seeds[6], (INNER + 2 * STATE,), jnp.float32, -0.5, 0.5), -0.5, 0.5)
    dt_bias = jnp.clip(jax.random.uniform(seeds[7], (HEADS,), jnp.float32, -5.0, -3.0), -5.0, -3.0)
    a_log = draw_a_log(jax.random.fold_in(seeds[13], 71), 0)
    skip = jnp.clip(jax.random.uniform(seeds[9], (HEADS,), jnp.float32, 0.5, 1.5), 0.5, 1.5)
    gate_gain = jnp.clip(1.0 + 0.1 * jax.random.normal(seeds[10], (INNER,), jnp.float32), 0.5, 1.5)
    w_out = scatter_about(seeds[11], (INNER, D), (INNER // 2) ** -0.5, 0.125, ((0, 32),))
    cotangent = scatter_about(seeds[12], (4, SEQS, LENGTH, D), 1.0, 6.0, ((1, 8), (2, 4)))
    return dict(tokens=tokens, lengths=lengths, norm_gain=norm_gain, w_in=w_in, w_dt=w_dt, conv_w=conv_w, conv_b=conv_b, dt_bias=dt_bias, a_log=a_log, skip=skip, gate_gain=gate_gain, w_out=w_out, cotangent=cotangent)


@jax.custom_vjp
def low(v):
    return lax.optimization_barrier(v.astype(jnp.bfloat16)).astype(jnp.float32)

@jax.custom_vjp
def low_back(v):
    return v

def low_keep(v):
    return (low(v), None)

def low_pass(kept, grad):
    return (grad,)

def back_keep(v):
    return (v, None)

def back_low(kept, grad):
    return (low(grad),)
low.defvjp(low_keep, low_pass)
low_back.defvjp(back_keep, back_low)
EPS = 1e-05
HIGH = lax.Precision.HIGHEST

def doc_ids(sizes, positions):
    ends = jnp.cumsum(sizes)[:-1]
    count = lax.optimization_barrier(jnp.sum((positions[..., None] >= ends).astype(jnp.int32), axis=-1))
    return jnp.where(positions < 0, -1, count).astype(jnp.int32)

def span_parts(xs, bm, cm, dt, rate, seg, seg_prev):
    size = xs.shape[0]
    cum = jnp.cumsum(dt * rate[None, :], axis=0)
    order = jnp.arange(size)
    allowed = (order[:, None] >= order[None, :]) & (seg[:, None] == seg[None, :])
    spread = jnp.where(allowed[:, :, None], cum[:, None, :] - cum[None, :, :], -1e+30)
    mixing = jnp.dot(cm, bm.T, precision=HIGH)
    weights = jnp.exp(spread) * mixing[:, :, None] * dt[None, :, :]
    inner_y = jnp.einsum('ijh,jhp->ihp', weights, xs, precision=HIGH)
    to_end = jnp.where((seg == seg[-1])[:, None], jnp.exp(cum[-1][None, :] - cum), 0.0)
    state = jnp.einsum('jh,jhp,jn->hpn', to_end * dt, xs, bm, precision=HIGH)
    keep = jnp.where((seg == seg_prev)[:, None], jnp.exp(cum), 0.0)
    return (inner_y, state, keep, keep[-1])

def span_step(xs, bm, cm, dt, rate, skip, prior, seg, seg_prev):
    inner_y, state, keep, factor = span_parts(xs, bm, cm, dt, rate, seg, seg_prev)
    carried = jnp.einsum('in,hpn->ihp', cm, prior, precision=HIGH) * keep[:, :, None]
    out_y = inner_y + carried + skip[None, :, None] * xs
    after = factor[:, None, None] * prior + state
    return (out_y, after)

def layer(x, norm_gain, w_in, w_dt, conv_w, conv_b, dt_bias, a_log, skip, gate_gain, w_out, seg):
    length = x.shape[0]
    scale = lax.rsqrt(lax.optimization_barrier(jnp.mean(x * x, axis=-1, keepdims=True)) + EPS)
    normed_in = low(x * scale * norm_gain)
    proj = low(low_back(jnp.dot(normed_in, w_in, precision=HIGH)))
    raw = low(low_back(jnp.dot(normed_in, w_dt, precision=HIGH)))
    gate_z = proj[:, :INNER]
    mixer_in = proj[:, INNER:]
    padded = jnp.concatenate([jnp.zeros((CONV - 1, mixer_in.shape[1]), jnp.float32), mixer_in], axis=0)
    seg_pad = jnp.concatenate([jnp.full((CONV - 1,), -1, jnp.int32), seg]).astype(jnp.int32)
    conv_sum = conv_b[None, :] + jnp.zeros_like(mixer_in)
    for tap in range(CONV):
        same = (seg_pad[tap:tap + length] == seg)[:, None]
        conv_sum = conv_sum + jnp.where(same, padded[tap:tap + length] * conv_w[tap][None, :], 0.0)
    acted = jax.nn.silu(conv_sum)
    blocks = length // SPAN
    values = acted[:, :INNER].reshape(blocks, SPAN, HEADS, HEADDIM)
    b_in = acted[:, INNER:INNER + STATE].reshape(blocks, SPAN, STATE)
    c_out = acted[:, INNER + STATE:].reshape(blocks, SPAN, STATE)
    steps_dt = jax.nn.softplus(raw + dt_bias[None, :]).reshape(blocks, SPAN, HEADS)
    rate = -jnp.exp(a_log)
    seg_blocks = seg.reshape(blocks, SPAN)
    seg_prev = jnp.concatenate([jnp.full((1,), -1, jnp.int32), seg[SPAN - 1:length - 1:SPAN]]).astype(jnp.int32)

    def one_block(prior, pieces):
        vals, bins, couts, dts, segs, segp = pieces
        out_y, after = span_step(vals, bins, couts, dts, rate, skip, prior, segs, segp)
        return (after, out_y)
    start = jnp.zeros((HEADS, HEADDIM, STATE), jnp.float32)
    _, ys = lax.scan(jax.checkpoint(one_block), start, (values, b_in, c_out, steps_dt, seg_blocks, seg_prev))
    mixed_y = ys.reshape(length, INNER)
    results = []
    for level in range(4):
        width = (HEADS >> 3 - level) * HEADDIM
        gated = mixed_y[:, :width] * jax.nn.silu(gate_z[:, :width])
        ratio = lax.rsqrt(lax.optimization_barrier(jnp.mean(gated * gated, axis=-1, keepdims=True)) + EPS)
        normed = low(gated * ratio * gate_gain[:width])
        results.append(x + jnp.dot(normed, w_out[:width], precision=HIGH))
    return jnp.stack(results)

def reference(tokens, lengths, norm_gain, w_in, w_dt, conv_w, conv_b, dt_bias, a_log, skip, gate_gain, w_out, cotangent):
    params = tuple((p.astype(jnp.float32) for p in (norm_gain, w_in, w_dt, conv_w, conv_b, dt_bias, a_log, skip, gate_gain, w_out)))
    length = tokens.shape[1]
    positions = jnp.arange(length, dtype=jnp.int32)

    def one_sequence(totals, pieces):
        row, sizes, cot = pieces
        seg = doc_ids(sizes, positions)

        def forward(x, p0, p1, p2, p3, p4, p5, p6, p7, p8, p9):
            return layer(x, p0, p1, p2, p3, p4, p5, p6, p7, p8, p9, seg)
        outs, pull = jax.vjp(forward, row.astype(jnp.float32), *params)
        grads = pull(cot.astype(jnp.float32))
        totals = tuple((a + b for a, b in zip(totals, grads[1:])))
        return (totals, (outs.astype(jnp.bfloat16), grads[0].astype(jnp.bfloat16)))
    zeros = tuple((jnp.zeros_like(p) for p in params))
    totals, (mixed, grad_tokens) = lax.scan(one_sequence, zeros, (tokens, lengths, jnp.moveaxis(cotangent, 1, 0)))
    mixed = jnp.moveaxis(mixed, 0, 1)
    return (mixed, grad_tokens, totals[0], totals[1], totals[2], totals[3], totals[4], totals[5], totals[6], totals[7], totals[8], totals[9])
```

```python
import functools

import jax
import jax.numpy as jnp
import numpy as np
from jax import lax
from jax.experimental import pallas as pl
from jax.experimental.pallas import tpu as pltpu
from jax.sharding import PartitionSpec as P

D = 2048
HEADS = 64
HEADDIM = 64
STATE = 128
CONV = 4
SPAN = 256
INNER = 4096
EPS = 1e-05
LEVELS = 4
BF = jnp.bfloat16
F32 = jnp.float32
HIGH = lax.Precision.HIGHEST
LANES = 128
VMEM_LIMIT = 48 * 1024 * 1024


def dot(a, b, dims=((1,), (0,)), precision=None):
    return lax.dot_general(a, b, (dims, ((), ())), preferred_element_type=F32, precision=precision)


def silu_slope(v):
    sig = jax.nn.sigmoid(v)
    return sig * (1.0 + v * (1.0 - sig))


def level_of(head):
    return 0 if head < 8 else 1 if head < 16 else 2 if head < 32 else 3


def swapped(value, axis, k, keep=None):
    pairs = [(i, i ^ k) for i in range(lax.axis_size(axis))]
    if keep is not None:
        pairs = [p for p in pairs if keep(*p)]
    return lax.ppermute(value, axis, pairs)


def butterfly(value, axis):
    k = 1
    while k < lax.axis_size(axis):
        value = value + swapped(value, axis, k)
        k *= 2
    return value


def picked(array, index):
    return lax.dynamic_index_in_dim(array, index, 0, keepdims=False)


def placed_by_xor(pieces, here):
    out = jnp.zeros((len(pieces),) + pieces[0].shape, pieces[0].dtype)
    for k, piece in enumerate(pieces):
        out = lax.dynamic_update_index_in_dim(out, piece, here ^ k, 0)
    return out


def seq_gather(block, here):
    across = swapped(block, "seq", 2)
    beside = swapped(block, "seq", 1)
    far = swapped(across, "seq", 1)
    return placed_by_xor([block, beside, across, far], here)


def seq_exchange(pieces, here):
    got = [picked(pieces, here)]
    for k in range(1, pieces.shape[0]):
        got.append(swapped(picked(pieces, here ^ k), "seq", k))
    return placed_by_xor(got, here)


def tri(rows_first):
    a = lax.broadcasted_iota(jnp.int32, (SPAN, SPAN), 0)
    b = lax.broadcasted_iota(jnp.int32, (SPAN, SPAN), 1)
    return (a >= b) if rows_first else (a <= b)


def pair_of(lo, cols, p):
    return jnp.where(lo, cols[:, 2 * p : 2 * p + 1], cols[:, 2 * p + 1 : 2 * p + 2])


def decays(segc, segr, segp, dt, dtr, rate, rater):
    lower = tri(True).astype(F32)
    upper = tri(False).astype(F32)
    cum = dot(lower, dt * rate, precision=HIGH)
    cumr = dot(dtr * rater, upper, precision=HIGH)
    last = cum[SPAN - 1 : SPAN, :]
    keep = jnp.where(segc == segp, jnp.exp(cum), 0.0)
    to_end = jnp.where(segc == segr[:, SPAN - 1 : SPAN], jnp.exp(last - cum), 0.0)
    return cum, cumr, keep, to_end


def forward_kernel(
    heads,
    segp_ref,
    segc_ref,
    segr_ref,
    x_ref,
    b_ref,
    c_ref,
    dt_ref,
    dtr_ref,
    rate_ref,
    rater_ref,
    skip_ref,
    y_ref,
    prior_ref,
    carry,
    to_end_u,
):
    block = pl.program_id(0)

    @pl.when(block == 0)
    def _():
        carry[...] = jnp.zeros_like(carry)

    prior_ref[0] = carry[...]
    segc, segr = segc_ref[...], segr_ref[...]
    dt = dt_ref[...]
    cum, cumr, keep, to_end = decays(
        segc, segr, segp_ref[block], dt, dtr_ref[...], rate_ref[...], rater_ref[...]
    )
    bm, cm = b_ref[...], c_ref[...]
    mixing = dot(cm, bm, ((1,), (1,)))
    mixing = jnp.where(tri(True) & (segc == segr), mixing, 0.0)
    lo = lax.broadcasted_iota(jnp.int32, (SPAN, LANES), 1) < HEADDIM
    for p in range(heads // 2):
        at = slice(p * LANES, (p + 1) * LANES)
        x2 = x_ref[:, at].astype(F32)
        u2 = x2 * pair_of(lo, dt, p)
        sides = (jnp.where(lo, u2, 0.0).astype(BF), jnp.where(lo, 0.0, u2).astype(BF))
        total = dot(cm, carry[:, at].astype(BF)) * pair_of(lo, keep, p) + skip_ref[:, at] * x2
        for k in range(2):
            h = 2 * p + k
            decay = jnp.exp(jnp.minimum(cum[:, h : h + 1] - cumr[h : h + 1, :], 0.0))
            total = total + dot((decay * mixing).astype(BF), sides[k])
        y_ref[:, at] = total
        to_end_u[:, at] = (u2 * pair_of(lo, to_end, p)).astype(BF)
    fresh = dot(bm, to_end_u[...], ((0,), (0,)))
    lo_row = lax.broadcasted_iota(jnp.int32, (1, LANES), 1) < HEADDIM
    for p in range(heads // 2):
        at = slice(p * LANES, (p + 1) * LANES)
        factor = pair_of(lo_row, keep[SPAN - 1 : SPAN, :], p)
        carry[:, at] = factor * carry[:, at] + fresh[:, at]


def split_dot(value, ones):
    high = value.astype(BF)
    low = (value - high.astype(F32)).astype(BF)
    return dot(high, ones) + dot(low, ones)


def backward_kernel(
    heads,
    segp_ref,
    segc_ref,
    segr_ref,
    x_ref,
    b_ref,
    c_ref,
    dt_ref,
    dtr_ref,
    rate_ref,
    rater_ref,
    skip_ref,
    y_ref,
    prior_ref,
    dy_ref,
    dx_ref,
    dbc_ref,
    ddt_ref,
    drate_ref,
    dskip_ref,
    dcarry,
    after,
    keep_dy,
    to_end_u,
    slopes,
    along,
):
    step = pl.program_id(0)
    block = pl.num_programs(0) - 1 - step

    @pl.when(step == 0)
    def _():
        dcarry[...] = jnp.zeros_like(dcarry)
        after[...] = jnp.zeros_like(after)
        drate_ref[...] = jnp.zeros_like(drate_ref)
        dskip_ref[...] = jnp.zeros_like(dskip_ref)

    segc, segr = segc_ref[...], segr_ref[...]
    dt = dt_ref[...]
    cum, cumr, keep, to_end = decays(
        segc, segr, segp_ref[block], dt, dtr_ref[...], rate_ref[...], rater_ref[...]
    )
    bm, cm = b_ref[...], c_ref[...]
    allowed = tri(False) & (segc == segr)
    mixing = jnp.where(allowed, dot(bm, cm, ((1,), (1,))), 0.0)
    lo = lax.broadcasted_iota(jnp.int32, (SPAN, LANES), 1) < HEADDIM
    dmixing = jnp.zeros((SPAN, SPAN), F32)
    for p in range(heads // 2):
        at = slice(p * LANES, (p + 1) * LANES)
        x2 = x_ref[:, at].astype(F32)
        dt2 = pair_of(lo, dt, p)
        u2 = x2 * dt2
        dyb = dy_ref[:, at]
        dy2 = dyb.astype(F32)
        skip = skip_ref[:, at]
        te2 = pair_of(lo, to_end, p)
        u_sides = (jnp.where(lo, u2, 0.0).astype(BF), jnp.where(lo, 0.0, u2).astype(BF))
        dy_sides = (jnp.where(lo, dy2, 0.0).astype(BF), jnp.where(lo, 0.0, dy2).astype(BF))
        du = te2 * dot(bm, dcarry[:, at].astype(BF))
        for k in range(2):
            h = 2 * p + k
            decay = jnp.exp(jnp.minimum(cumr[h : h + 1, :] - cum[:, h : h + 1], 0.0))
            du = du + dot((decay * mixing).astype(BF), dy_sides[k])
            dmixing = dmixing + decay * dot(u_sides[k], dyb, ((1,), (1,)))
        dx_ref[:, at] = (dt2 * du + skip * dy2).astype(dx_ref.dtype)
        keep_dy[:, at] = (pair_of(lo, keep, p) * dy2).astype(BF)
        to_end_u[:, at] = (te2 * u2).astype(BF)
        slopes[:, at] = dy2 * (y_ref[:, at] - skip * x2) - u2.astype(BF).astype(F32) * du
        along[:, at] = x2 * du
        dskip_ref[:, at] += jnp.sum(dy2 * x2, axis=0, keepdims=True)
    dmixing = jnp.where(allowed, dmixing, 0.0).astype(BF)
    dstate = dcarry[...].astype(BF)
    prior = prior_ref[0]
    dbc_ref[:, :STATE] = dot(dmixing, cm) + dot(to_end_u[...], dstate, ((1,), (1,)))
    dbc_ref[:, STATE:] = dot(dmixing, bm, ((0,), (0,))) + dot(
        keep_dy[...], prior.astype(BF), ((1,), (1,))
    )
    width = heads * HEADDIM
    ones = (
        lax.broadcasted_iota(jnp.int32, (width, LANES), 0) // HEADDIM
        == lax.broadcasted_iota(jnp.int32, (width, LANES), 1)
    ).astype(BF)
    at_end = jnp.sum(dcarry[...] * after[...], axis=0, keepdims=True)
    at_end = split_dot(jnp.broadcast_to(at_end, (16, width)), ones)[:1]
    dcum = split_dot(slopes[...], ones)
    da = dot(tri(False).astype(F32), dcum, precision=HIGH) + at_end
    ddt_ref[...] = rate_ref[...] * da + split_dot(along[...], ones)
    drate_ref[...] += jnp.sum(dt * da, axis=0, keepdims=True)
    fresh = dot(cm, keep_dy[...], ((0,), (0,)))
    lo_row = lax.broadcasted_iota(jnp.int32, (1, LANES), 1) < HEADDIM
    for p in range(heads // 2):
        at = slice(p * LANES, (p + 1) * LANES)
        factor = pair_of(lo_row, keep[SPAN - 1 : SPAN, :], p)
        dcarry[:, at] = factor * dcarry[:, at] + fresh[:, at]
    after[...] = prior


def scan_specs(heads, at):
    width = heads * HEADDIM

    def rows(n):
        return pl.BlockSpec((SPAN, n), lambda i: (at(i), 0))

    def whole(*shape):
        return pl.BlockSpec(shape, lambda i: (0,) * len(shape))

    ins = [
        pl.BlockSpec(memory_space=pltpu.SMEM),
        rows(1),
        pl.BlockSpec((1, SPAN), lambda i: (0, at(i))),
        rows(width),
        rows(STATE),
        rows(STATE),
        rows(LANES),
        pl.BlockSpec((heads, SPAN), lambda i: (0, at(i))),
        whole(1, LANES),
        whole(heads, 1),
        whole(1, width),
    ]
    prior = pl.BlockSpec((1, STATE, width), lambda i: (at(i), 0, 0))
    return rows, whole, ins, prior


def scan_forward(heads, blocks, operands):
    rows, whole, ins, prior = scan_specs(heads, lambda i: i)
    width = heads * HEADDIM
    return pl.pallas_call(
        functools.partial(forward_kernel, heads),
        grid=(blocks,),
        in_specs=ins,
        out_specs=[rows(width), prior],
        out_shape=[
            jax.ShapeDtypeStruct((blocks * SPAN, width), F32),
            jax.ShapeDtypeStruct((blocks, STATE, width), F32),
        ],
        scratch_shapes=[pltpu.VMEM((STATE, width), F32), pltpu.VMEM((SPAN, width), BF)],
        compiler_params=pltpu.CompilerParams(vmem_limit_bytes=VMEM_LIMIT),
        cost_estimate=pl.CostEstimate(
            flops=blocks * heads * 4 * SPAN * SPAN * LANES,
            bytes_accessed=16 * 1024 * 1024,
            transcendentals=blocks * heads * SPAN * SPAN,
        ),
        name="scan_forward",
    )(*operands)


def scan_backward(heads, blocks, operands, y, priors, dy):
    rows, whole, ins, prior = scan_specs(heads, lambda i: blocks - 1 - i)
    width = heads * HEADDIM
    return pl.pallas_call(
        functools.partial(backward_kernel, heads),
        grid=(blocks,),
        in_specs=ins + [rows(width), prior, rows(width)],
        out_specs=[rows(width), rows(2 * STATE), rows(LANES), whole(1, LANES), whole(1, width)],
        out_shape=[
            jax.ShapeDtypeStruct((blocks * SPAN, width), BF),
            jax.ShapeDtypeStruct((blocks * SPAN, 2 * STATE), F32),
            jax.ShapeDtypeStruct((blocks * SPAN, LANES), F32),
            jax.ShapeDtypeStruct((1, LANES), F32),
            jax.ShapeDtypeStruct((1, width), F32),
        ],
        scratch_shapes=[
            pltpu.VMEM((STATE, width), F32),
            pltpu.VMEM((STATE, width), F32),
            pltpu.VMEM((SPAN, width), BF),
            pltpu.VMEM((SPAN, width), BF),
            pltpu.VMEM((SPAN, width), F32),
            pltpu.VMEM((SPAN, width), F32),
        ],
        compiler_params=pltpu.CompilerParams(vmem_limit_bytes=VMEM_LIMIT),
        cost_estimate=pl.CostEstimate(
            flops=blocks * heads * 8 * SPAN * SPAN * LANES,
            bytes_accessed=24 * 1024 * 1024,
            transcendentals=blocks * heads * SPAN * SPAN,
        ),
        name="scan_backward",
    )(*operands, y, priors, dy)


def row_sums(halves, other_halves):
    nf = lax.axis_size("fsdp")
    f = lax.axis_index("fsdp")
    got = [swapped(other, "dp", k + 1) for k, other in enumerate(other_halves)]

    def part(index):
        total = picked(halves, index)
        for other in got:
            total = total + picked(other, index).astype(F32)
        return total

    sent = [swapped(part(f ^ k).astype(BF), "fsdp", k) for k in range(1, nf)]
    total = part(f)
    for piece in sent:
        total = total + piece.astype(F32)
    return total


def shards(
    tokens,
    lengths,
    norm_gain,
    w_in,
    w_dt,
    conv_w,
    conv_b,
    dt_bias,
    a_log,
    skip,
    gate_gain,
    w_out,
    cotangent,
):
    nd, ns, nf = lax.axis_size("dp"), lax.axis_size("seq"), lax.axis_size("fsdp")
    d, s = lax.axis_index("dp"), lax.axis_index("seq")
    tok = tokens.shape[1]
    length = ns * tok
    blocks = length // SPAN
    heads = HEADS // ns
    run = heads // nd
    width = heads * HEADDIM
    own_bc = 2 * STATE // ns
    used = width + own_bc
    cols = -(-(used + heads) // LANES) * LANES
    rows_in = w_in.shape[0]
    reach = CONV - 1

    levels = np.array(
        [[level_of(dd * (HEADS // nd) + ss * run + i) for dd in range(nd) for i in range(run)] for ss in range(ns)]
    )
    cuts = [0] + [h for h in range(1, heads) if (levels[:, h] != levels[:, h - 1]).any()] + [heads]
    ranges = [(a, b) for a, b in zip(cuts, cuts[1:])]
    range_level = np.array([[levels[ss, a] for a, _ in ranges] for ss in range(ns)])
    counts = (range_level[:, :, None] <= np.arange(LEVELS)[None, None, :]).astype(np.float32)
    counted = picked(jnp.asarray(counts), s)
    lowest = [int(range_level[ss].min()) for ss in range(ns)]

    def by_head(vector):
        lead = vector.shape[:-1]
        per = vector.shape[-1] // HEADS
        cut = vector.reshape(lead + (nd, ns, run * per))
        mine = lax.dynamic_index_in_dim(cut, s, len(lead) + 1, keepdims=False)
        return mine.reshape(lead + (heads * per,))

    def for_groups(matrix):
        per = matrix.shape[1] // HEADS
        cut = matrix.reshape(matrix.shape[0], nd, ns, run * per)
        return jnp.transpose(cut, (2, 0, 1, 3)).reshape(ns, matrix.shape[0], heads * per)

    def from_groups(stack):
        per = stack.shape[2] // heads
        cut = stack.reshape(ns, stack.shape[1], nd, run * per)
        return jnp.transpose(cut, (1, 2, 0, 3)).reshape(stack.shape[1], HEADS * per)

    def gathered_rows(stack):
        mine = seq_exchange(stack, s)
        full = lax.all_gather(mine, ("dp", "fsdp"), axis=0, tiled=False)
        full = full.reshape(nd, nf, ns, rows_in, stack.shape[2])
        return jnp.transpose(full, (0, 2, 1, 3, 4)).reshape(D, stack.shape[2])

    pad_cols = cols - used - heads
    bc_cols = w_in[:, 2 * INNER :].reshape(rows_in, ns, own_bc).transpose(1, 0, 2)
    stack_x = jnp.concatenate(
        [
            for_groups(w_in[:, INNER : 2 * INNER]),
            bc_cols,
            for_groups(w_dt),
            jnp.zeros((ns, rows_in, pad_cols), BF),
        ],
        axis=2,
    )
    full_x = gathered_rows(stack_x)
    full_z = gathered_rows(for_groups(w_in[:, :INNER]))
    full_out = lax.all_gather(w_out, ("dp", "fsdp"), axis=0, tiled=True)

    own_x = tokens[0].astype(F32)
    scale = lax.rsqrt(jnp.mean(own_x * own_x, axis=-1, keepdims=True) + EPS)
    xn = seq_gather((own_x * scale * norm_gain).astype(BF), s).reshape(length, D)

    cots = []
    for level in range(LEVELS):
        block = cotangent[level, 0]

        def wanted(at):
            return lowest[at] <= level

        across = swapped(block, "seq", 2, lambda a, b: wanted(b) or wanted(b ^ 1))
        beside = swapped(block, "seq", 1, lambda a, b: wanted(b))
        far = swapped(across, "seq", 1, lambda a, b: wanted(b))
        cots.append(placed_by_xor([block, beside, across, far], s).reshape(length, D))

    positions = jnp.arange(length, dtype=jnp.int32)
    ends = jnp.cumsum(lengths[0])[:-1]
    seg = jnp.sum((positions[:, None] >= ends[None, :]).astype(jnp.int32), axis=1)
    seg_before = jnp.concatenate([jnp.full((1,), -1, jnp.int32), seg[SPAN - 1 : length - 1 : SPAN]])

    proj_x = dot(xn, full_x).astype(BF)
    proj_z = dot(xn, full_z).astype(BF)

    w_conv = jnp.concatenate(
        [
            by_head(conv_w[:, :INNER]),
            lax.dynamic_slice_in_dim(conv_w, INNER + s * own_bc, own_bc, 1),
            jnp.zeros((CONV, cols - used), F32),
        ],
        axis=1,
    )
    b_conv = jnp.concatenate(
        [
            by_head(conv_b[:INNER]),
            lax.dynamic_slice_in_dim(conv_b, INNER + s * own_bc, own_bc, 0),
            jnp.zeros((cols - used,), F32),
        ]
    )
    mixer = jnp.concatenate([jnp.zeros((reach, cols), BF), proj_x], axis=0)
    seg_pad = jnp.concatenate([jnp.full((reach,), -1, jnp.int32), seg])
    masks = [(seg_pad[k : k + length] == seg)[:, None] for k in range(CONV)]

    def taken(k):
        return jnp.where(masks[k], mixer[k : k + length].astype(F32), 0.0)

    pre = b_conv
    for k in range(CONV):
        pre = pre + taken(k) * w_conv[k]
    acted = jax.nn.silu(pre).astype(BF)
    bc = seq_gather(acted[:, width:used], s)
    half = ns // 2
    b_in = jnp.concatenate([bc[j] for j in range(half)], axis=1)
    c_out = jnp.concatenate([bc[j] for j in range(half, ns)], axis=1)

    def padded(rows):
        return jnp.pad(rows, ((0, 0), (0, LANES - rows.shape[1])))

    bias = by_head(dt_bias)
    rate = -jnp.exp(by_head(a_log))
    pre_dt = proj_x[:, used : used + heads].astype(F32) + bias
    steps = jax.nn.softplus(pre_dt)
    skip_own = by_head(skip)
    operands = (
        seg_before,
        seg[:, None],
        seg[None, :],
        acted[:, :width],
        b_in,
        c_out,
        padded(steps),
        steps.T,
        padded(rate[None, :]),
        rate[:, None],
        jnp.repeat(skip_own, HEADDIM)[None, :],
    )
    y, priors = scan_forward(heads, blocks, operands)

    gain = by_head(gate_gain)
    zf = proj_z.astype(F32)
    act_z = jax.nn.silu(zf)
    q = y * act_z
    q_gain = (q * gain).astype(BF)
    lanes = [(a * HEADDIM, b * HEADDIM) for a, b in ranges]
    squares = jnp.stack([jnp.sum(q[:, a:b] * q[:, a:b], axis=1) for a, b in lanes])
    widths = np.array([[(HEADS >> 3 - w) * HEADDIM] for w in range(LEVELS)], np.float32)

    def by_level(per_range):
        return jnp.sum(counted[:, :, None] * per_range[:, None, :], axis=0)

    ratio = lax.rsqrt(butterfly(by_level(squares), "seq") / widths + EPS)

    products = [dot(q_gain[:, a:b], full_out[a:b]).astype(BF) for a, b in lanes]
    inner = []
    for w in range(LEVELS):
        total = 0.0
        for j in range(len(ranges)):
            if range_level[:, j].min() <= w:
                total = total + counted[j, w] * products[j].astype(F32)
        inner.append(jnp.sum(total * cots[w].astype(F32), axis=1))
    means = butterfly(jnp.stack(inner), "seq") / widths

    def own_tokens(array, at):
        return lax.dynamic_slice_in_dim(array, at * tok, tok, array.ndim - 1)

    ratio_own = own_tokens(ratio, s)
    sums = [0.0] * LEVELS
    for k in range(ns):
        at = s ^ k
        parts = [lax.dynamic_slice_in_dim(p, at * tok, tok, 0) for p in products]
        if k:
            parts = [swapped(p, "seq", k) for p in parts]
        theirs = picked(jnp.asarray(counts), at)
        for w in range(LEVELS):
            for j in range(len(ranges)):
                if range_level[:, j].min() <= w:
                    sums[w] = sums[w] + theirs[j, w] * parts[j].astype(F32)
    mixed = jnp.stack(
        [(own_x + ratio_own[w][:, None] * sums[w]).astype(BF) for w in range(LEVELS)]
    )[:, None]

    upper, grads_t, coefs = [], [], []
    for j, (a, b) in enumerate(lanes):
        total = 0.0
        coef = 0.0
        for w in range(LEVELS):
            if range_level[:, j].min() <= w:
                total = total + (counted[j, w] * ratio[w])[:, None] * cots[w].astype(F32)
                coef = coef + counted[j, w] * ratio[w] ** 3 * means[w]
        upper.append(total.astype(BF))
        coefs.append(coef)
        grads_t.append(dot(upper[j], full_out[a:b], ((1,), (1,))))
    grad_t = jnp.concatenate(grads_t, axis=1)
    coef = jnp.concatenate(
        [jnp.broadcast_to(c[:, None], (length, b - a)) for c, (a, b) in zip(coefs, lanes)], axis=1
    )
    dq = gain * grad_t - q * coef
    grad_gate = jnp.sum(q * grad_t, axis=0)
    dy = (dq * act_z).astype(BF)
    dz = (dq * y * silu_slope(zf)).astype(BF)

    out_rows = width // nd
    grad_out = jnp.concatenate(
        [dot(q_gain[:, a:b], upper[j], ((0,), (0,))).astype(BF) for j, (a, b) in enumerate(lanes)]
    ).reshape(nd, nf, out_rows // nf, D)
    sum_out = row_sums(
        picked(grad_out, d).astype(F32), [picked(grad_out, d ^ k) for k in range(1, nd)]
    )

    def in_grad(dproj):
        part = D // nd

        def terms(at):
            left = lax.dynamic_slice_in_dim(xn, at * part, part, 1)
            out = dot(left, dproj, ((0,), (0,)))
            out = out.reshape(ns, nf, rows_in, dproj.shape[1])
            return jnp.transpose(out, (1, 0, 2, 3)).reshape(nf, ns * rows_in, dproj.shape[1])

        others = [terms(d ^ k).astype(BF) for k in range(1, nd)]
        total = row_sums(terms(d), others).astype(BF)
        return seq_exchange(total.reshape(ns, rows_in, dproj.shape[1]), s)

    got_z = in_grad(dz)

    dxs, dbc, ddt, drate, dskip = scan_backward(heads, blocks, operands, y, priors, dy)
    dbc_parts = jnp.transpose(dbc.astype(BF).reshape(length, ns, own_bc), (1, 0, 2))
    dbc_own = picked(dbc_parts, s).astype(F32)
    for k in range(1, ns):
        dbc_own = dbc_own + swapped(picked(dbc_parts, s ^ k), "seq", k).astype(F32)
    acted_grad = jnp.concatenate(
        [dxs.astype(F32), dbc_own, jnp.zeros((length, cols - used), F32)], axis=1
    )
    dpre = acted_grad * silu_slope(pre)
    grad_conv_b = jnp.sum(dpre, axis=0)
    grad_conv_w = jnp.stack([jnp.sum(dpre * taken(k), axis=0) for k in range(CONV)])
    dmixer = 0.0
    for k in range(CONV):
        moved = jnp.where(masks[k], dpre, 0.0)
        back = reach - k
        moved = jnp.concatenate([moved[back:], jnp.zeros((back, cols), F32)], axis=0)
        dmixer = dmixer + moved * w_conv[k]
    dpre_dt = ddt[:, :heads] * jax.nn.sigmoid(pre_dt)
    grad_bias = jnp.sum(dpre_dt, axis=0)
    dproj = jnp.concatenate(
        [
            dmixer[:, :used].astype(BF),
            dpre_dt.astype(BF),
            jnp.zeros((length, pad_cols), BF),
        ],
        axis=1,
    )
    got_x = in_grad(dproj)

    dxn = dot(dz, full_z, ((1,), (1,))) + dot(dproj, full_x, ((1,), (1,)))
    dxn_parts = dxn.reshape(ns, tok, D)
    dxn_own = picked(dxn_parts, s)
    for k in range(1, ns):
        dxn_own = dxn_own + swapped(picked(dxn_parts, s ^ k).astype(BF), "seq", k).astype(F32)
    grad_norm = jnp.sum(dxn_own * own_x * scale, axis=0)
    scaled = norm_gain * dxn_own
    dx = scale * scaled - own_x * scale**3 * jnp.mean(own_x * scaled, axis=-1, keepdims=True)
    dx = dx + jnp.sum(cotangent[:, 0].astype(F32), axis=0)

    sum_in = jnp.concatenate(
        [
            from_groups(got_z),
            from_groups(got_x[:, :, :width]),
            jnp.transpose(got_x[:, :, width:used], (1, 0, 2)).reshape(rows_in, 2 * STATE),
        ],
        axis=1,
    ).astype(F32)
    sum_dt = from_groups(got_x[:, :, used : used + heads]).astype(F32)

    small = [
        grad_norm,
        grad_conv_w[:, :used].reshape(-1),
        grad_conv_b[:used],
        grad_gate,
        grad_bias,
        drate[0, :heads] * rate,
        jnp.sum(dskip[0].reshape(heads, HEADDIM), axis=1),
    ]
    sizes = [v.shape[0] for v in small]
    flat = jnp.concatenate(small)
    flat = jnp.pad(flat, (0, -flat.shape[0] % 1024)).reshape(-1, LANES)
    flat = butterfly(butterfly(flat, "dp"), "fsdp")
    every = seq_gather(flat, s).reshape(ns, -1)
    starts = np.cumsum([0] + sizes)
    pieces = [every[:, a : a + n] for a, n in zip(starts, sizes)]

    def heads_back(rows):
        lead = rows.shape[1:-1]
        cut = rows.reshape((ns,) + lead + (nd, rows.shape[-1] // nd))
        order = tuple(range(1, 1 + len(lead))) + (1 + len(lead), 0, 2 + len(lead))
        return jnp.transpose(cut, order).reshape(lead + (-1,))

    conv_rows = pieces[1].reshape(ns, CONV, used)
    conv_all = jnp.concatenate(
        [
            heads_back(conv_rows[:, :, :width]),
            jnp.transpose(conv_rows[:, :, width:], (1, 0, 2)).reshape(CONV, 2 * STATE),
        ],
        axis=1,
    )
    bias_all = jnp.concatenate([heads_back(pieces[2][:, :width]), pieces[2][:, width:].reshape(-1)])
    return (
        mixed,
        dx.astype(BF)[None],
        jnp.sum(pieces[0], axis=0),
        sum_in,
        sum_dt,
        conv_all,
        bias_all,
        heads_back(pieces[4]),
        heads_back(pieces[5]),
        heads_back(pieces[6]),
        heads_back(pieces[3]),
        sum_out,
    )


def solution(mesh):
    rows = P(("dp", "seq", "fsdp"), None)
    held = P(("dp", "fsdp"), "seq", None)
    levels = P(None, ("dp", "fsdp"), "seq", None)
    placed = (held, P(("dp", "fsdp"), None), P(), rows, rows, P(), P(), P(), P(), P(), P(), rows, levels)
    return jax.shard_map(
        shards,
        mesh=mesh,
        in_specs=placed,
        out_specs=(levels, held, P(), rows, rows, P(), P(), P(), P(), P(), P(), rows),
        check_vma=False,
    )
```

```python
import functools

import jax
import jax.numpy as jnp
import numpy as np
from jax import lax
from jax.experimental import pallas as pl
from jax.experimental.pallas import tpu as pltpu
from jax.sharding import PartitionSpec as P

D = 2048
HEADS = 64
HEADDIM = 64
STATE = 128
CONV = 4
SPAN = 256
INNER = 4096
EPS = 1e-05
LEVELS = 4
BF = jnp.bfloat16
F32 = jnp.float32
HIGH = lax.Precision.HIGHEST
LANES = 128
VMEM_LIMIT = 48 * 1024 * 1024


def dot(a, b, dims=((1,), (0,)), precision=None):
    return lax.dot_general(a, b, (dims, ((), ())), preferred_element_type=F32, precision=precision)


def silu_slope(v):
    sig = jax.nn.sigmoid(v)
    return sig * (1.0 + v * (1.0 - sig))


def level_of(head):
    return 0 if head < 8 else 1 if head < 16 else 2 if head < 32 else 3


def swapped(value, axis, k, keep=None):
    pairs = [(i, i ^ k) for i in range(lax.axis_size(axis))]
    if keep is not None:
        pairs = [p for p in pairs if keep(*p)]
    return lax.ppermute(value, axis, pairs)


def after(value, *others):
    return lax.optimization_barrier((value,) + others)[0]


def together(*values):
    return lax.optimization_barrier(values)


def flattened(vectors):
    flat = jnp.concatenate(vectors)
    return jnp.pad(flat, (0, -flat.shape[0] % 1024)).reshape(-1, LANES)


def butterfly(value, axis):
    k = 1
    while k < lax.axis_size(axis):
        value = value + swapped(value, axis, k)
        k *= 2
    return value


def picked(array, index):
    return lax.dynamic_index_in_dim(array, index, 0, keepdims=False)


def placed_by_xor(pieces, here):
    out = jnp.zeros((len(pieces),) + pieces[0].shape, pieces[0].dtype)
    for k, piece in enumerate(pieces):
        out = lax.dynamic_update_index_in_dim(out, piece, here ^ k, 0)
    return out


def seq_gather(block, here):
    across = swapped(block, "seq", 2)
    beside = swapped(block, "seq", 1)
    far = swapped(across, "seq", 1)
    return placed_by_xor([block, beside, across, far], here)


def seq_exchange(pieces, here):
    got = [picked(pieces, here)]
    for k in range(1, pieces.shape[0]):
        got.append(swapped(picked(pieces, here ^ k), "seq", k))
    return placed_by_xor(got, here)


def tri(rows_first):
    a = lax.broadcasted_iota(jnp.int32, (SPAN, SPAN), 0)
    b = lax.broadcasted_iota(jnp.int32, (SPAN, SPAN), 1)
    return (a >= b) if rows_first else (a <= b)


def pair_of(lo, cols, p):
    return jnp.where(lo, cols[:, 2 * p : 2 * p + 1], cols[:, 2 * p + 1 : 2 * p + 2])


def decays(segc, segr, segp, dt, dtr, rate, rater):
    lower = tri(True).astype(F32)
    upper = tri(False).astype(F32)
    cum = dot(lower, dt * rate, precision=HIGH)
    cumr = dot(dtr * rater, upper, precision=HIGH)
    last = cum[SPAN - 1 : SPAN, :]
    keep = jnp.where(segc == segp, jnp.exp(cum), 0.0)
    to_end = jnp.where(segc == segr[:, SPAN - 1 : SPAN], jnp.exp(last - cum), 0.0)
    return cum, cumr, keep, to_end


def forward_kernel(
    heads,
    segp_ref,
    segc_ref,
    segr_ref,
    x_ref,
    b_ref,
    c_ref,
    dt_ref,
    dtr_ref,
    rate_ref,
    rater_ref,
    skip_ref,
    y_ref,
    prior_ref,
    carry,
    to_end_u,
):
    block = pl.program_id(0)

    @pl.when(block == 0)
    def _():
        carry[...] = jnp.zeros_like(carry)

    prior_ref[0] = carry[...]
    segc, segr = segc_ref[...], segr_ref[...]
    dt = dt_ref[...]
    cum, cumr, keep, to_end = decays(
        segc, segr, segp_ref[block], dt, dtr_ref[...], rate_ref[...], rater_ref[...]
    )
    bm, cm = b_ref[...], c_ref[...]
    mixing = dot(cm, bm, ((1,), (1,)))
    mixing = jnp.where(tri(True) & (segc == segr), mixing, 0.0)
    lo = lax.broadcasted_iota(jnp.int32, (SPAN, LANES), 1) < HEADDIM
    for p in range(heads // 2):
        at = slice(p * LANES, (p + 1) * LANES)
        x2 = x_ref[:, at].astype(F32)
        u2 = x2 * pair_of(lo, dt, p)
        sides = (jnp.where(lo, u2, 0.0).astype(BF), jnp.where(lo, 0.0, u2).astype(BF))
        total = dot(cm, carry[:, at].astype(BF)) * pair_of(lo, keep, p) + skip_ref[:, at] * x2
        for k in range(2):
            h = 2 * p + k
            decay = jnp.exp(jnp.minimum(cum[:, h : h + 1] - cumr[h : h + 1, :], 0.0))
            total = total + dot((decay * mixing).astype(BF), sides[k])
        y_ref[:, at] = total
        to_end_u[:, at] = (u2 * pair_of(lo, to_end, p)).astype(BF)
    fresh = dot(bm, to_end_u[...], ((0,), (0,)))
    lo_row = lax.broadcasted_iota(jnp.int32, (1, LANES), 1) < HEADDIM
    for p in range(heads // 2):
        at = slice(p * LANES, (p + 1) * LANES)
        factor = pair_of(lo_row, keep[SPAN - 1 : SPAN, :], p)
        carry[:, at] = factor * carry[:, at] + fresh[:, at]


def split_dot(value, ones):
    high = value.astype(BF)
    low = (value - high.astype(F32)).astype(BF)
    return dot(high, ones) + dot(low, ones)


def backward_kernel(
    heads,
    segp_ref,
    segc_ref,
    segr_ref,
    x_ref,
    b_ref,
    c_ref,
    dt_ref,
    dtr_ref,
    rate_ref,
    rater_ref,
    skip_ref,
    y_ref,
    prior_ref,
    dy_ref,
    dx_ref,
    dbc_ref,
    ddt_ref,
    drate_ref,
    dskip_ref,
    dcarry,
    after,
    keep_dy,
    to_end_u,
    slopes,
    along,
):
    step = pl.program_id(0)
    block = pl.num_programs(0) - 1 - step

    @pl.when(step == 0)
    def _():
        dcarry[...] = jnp.zeros_like(dcarry)
        after[...] = jnp.zeros_like(after)
        drate_ref[...] = jnp.zeros_like(drate_ref)
        dskip_ref[...] = jnp.zeros_like(dskip_ref)

    segc, segr = segc_ref[...], segr_ref[...]
    dt = dt_ref[...]
    cum, cumr, keep, to_end = decays(
        segc, segr, segp_ref[block], dt, dtr_ref[...], rate_ref[...], rater_ref[...]
    )
    bm, cm = b_ref[...], c_ref[...]
    allowed = tri(False) & (segc == segr)
    mixing = jnp.where(allowed, dot(bm, cm, ((1,), (1,))), 0.0)
    lo = lax.broadcasted_iota(jnp.int32, (SPAN, LANES), 1) < HEADDIM
    dmixing = jnp.zeros((SPAN, SPAN), F32)
    for p in range(heads // 2):
        at = slice(p * LANES, (p + 1) * LANES)
        x2 = x_ref[:, at].astype(F32)
        dt2 = pair_of(lo, dt, p)
        u2 = x2 * dt2
        dyb = dy_ref[:, at]
        dy2 = dyb.astype(F32)
        skip = skip_ref[:, at]
        te2 = pair_of(lo, to_end, p)
        u_sides = (jnp.where(lo, u2, 0.0).astype(BF), jnp.where(lo, 0.0, u2).astype(BF))
        dy_sides = (jnp.where(lo, dy2, 0.0).astype(BF), jnp.where(lo, 0.0, dy2).astype(BF))
        du = te2 * dot(bm, dcarry[:, at].astype(BF))
        for k in range(2):
            h = 2 * p + k
            decay = jnp.exp(jnp.minimum(cumr[h : h + 1, :] - cum[:, h : h + 1], 0.0))
            du = du + dot((decay * mixing).astype(BF), dy_sides[k])
            dmixing = dmixing + decay * dot(u_sides[k], dyb, ((1,), (1,)))
        dx_ref[:, at] = (dt2 * du + skip * dy2).astype(dx_ref.dtype)
        keep_dy[:, at] = (pair_of(lo, keep, p) * dy2).astype(BF)
        to_end_u[:, at] = (te2 * u2).astype(BF)
        slopes[:, at] = dy2 * (y_ref[:, at] - skip * x2) - u2.astype(BF).astype(F32) * du
        along[:, at] = x2 * du
        dskip_ref[:, at] += jnp.sum(dy2 * x2, axis=0, keepdims=True)
    dmixing = jnp.where(allowed, dmixing, 0.0).astype(BF)
    dstate = dcarry[...].astype(BF)
    prior = prior_ref[0]
    dbc_ref[:, :STATE] = dot(dmixing, cm) + dot(to_end_u[...], dstate, ((1,), (1,)))
    dbc_ref[:, STATE:] = dot(dmixing, bm, ((0,), (0,))) + dot(
        keep_dy[...], prior.astype(BF), ((1,), (1,))
    )
    width = heads * HEADDIM
    ones = (
        lax.broadcasted_iota(jnp.int32, (width, LANES), 0) // HEADDIM
        == lax.broadcasted_iota(jnp.int32, (width, LANES), 1)
    ).astype(BF)
    at_end = jnp.sum(dcarry[...] * after[...], axis=0, keepdims=True)
    at_end = split_dot(jnp.broadcast_to(at_end, (16, width)), ones)[:1]
    dcum = split_dot(slopes[...], ones)
    da = dot(tri(False).astype(F32), dcum, precision=HIGH) + at_end
    ddt_ref[...] = rate_ref[...] * da + split_dot(along[...], ones)
    drate_ref[...] += jnp.sum(dt * da, axis=0, keepdims=True)
    fresh = dot(cm, keep_dy[...], ((0,), (0,)))
    lo_row = lax.broadcasted_iota(jnp.int32, (1, LANES), 1) < HEADDIM
    for p in range(heads // 2):
        at = slice(p * LANES, (p + 1) * LANES)
        factor = pair_of(lo_row, keep[SPAN - 1 : SPAN, :], p)
        dcarry[:, at] = factor * dcarry[:, at] + fresh[:, at]
    after[...] = prior


def scan_specs(heads, at):
    width = heads * HEADDIM

    def rows(n):
        return pl.BlockSpec((SPAN, n), lambda i: (at(i), 0))

    def whole(*shape):
        return pl.BlockSpec(shape, lambda i: (0,) * len(shape))

    ins = [
        pl.BlockSpec(memory_space=pltpu.SMEM),
        rows(1),
        pl.BlockSpec((1, SPAN), lambda i: (0, at(i))),
        rows(width),
        rows(STATE),
        rows(STATE),
        rows(LANES),
        pl.BlockSpec((heads, SPAN), lambda i: (0, at(i))),
        whole(1, LANES),
        whole(heads, 1),
        whole(1, width),
    ]
    prior = pl.BlockSpec((1, STATE, width), lambda i: (at(i), 0, 0))
    return rows, whole, ins, prior


def scan_forward(heads, blocks, operands):
    rows, whole, ins, prior = scan_specs(heads, lambda i: i)
    width = heads * HEADDIM
    return pl.pallas_call(
        functools.partial(forward_kernel, heads),
        grid=(blocks,),
        in_specs=ins,
        out_specs=[rows(width), prior],
        out_shape=[
            jax.ShapeDtypeStruct((blocks * SPAN, width), F32),
            jax.ShapeDtypeStruct((blocks, STATE, width), F32),
        ],
        scratch_shapes=[pltpu.VMEM((STATE, width), F32), pltpu.VMEM((SPAN, width), BF)],
        compiler_params=pltpu.CompilerParams(vmem_limit_bytes=VMEM_LIMIT),
        cost_estimate=pl.CostEstimate(flops=1, bytes_accessed=1, transcendentals=0),
        name="scan_forward",
    )(*operands)


def scan_backward(heads, blocks, operands, y, priors, dy):
    rows, whole, ins, prior = scan_specs(heads, lambda i: blocks - 1 - i)
    width = heads * HEADDIM
    return pl.pallas_call(
        functools.partial(backward_kernel, heads),
        grid=(blocks,),
        in_specs=ins + [rows(width), prior, rows(width)],
        out_specs=[rows(width), rows(2 * STATE), rows(LANES), whole(1, LANES), whole(1, width)],
        out_shape=[
            jax.ShapeDtypeStruct((blocks * SPAN, width), BF),
            jax.ShapeDtypeStruct((blocks * SPAN, 2 * STATE), F32),
            jax.ShapeDtypeStruct((blocks * SPAN, LANES), F32),
            jax.ShapeDtypeStruct((1, LANES), F32),
            jax.ShapeDtypeStruct((1, width), F32),
        ],
        scratch_shapes=[
            pltpu.VMEM((STATE, width), F32),
            pltpu.VMEM((STATE, width), F32),
            pltpu.VMEM((SPAN, width), BF),
            pltpu.VMEM((SPAN, width), BF),
            pltpu.VMEM((SPAN, width), F32),
            pltpu.VMEM((SPAN, width), F32),
        ],
        compiler_params=pltpu.CompilerParams(vmem_limit_bytes=VMEM_LIMIT),
        cost_estimate=pl.CostEstimate(flops=1, bytes_accessed=1, transcendentals=0),
        name="scan_backward",
    )(*operands, y, priors, dy)


def dp_terms(others):
    return [swapped(other, "dp", k + 1) for k, other in enumerate(others)]


def fsdp_half(own, got):
    nf = lax.axis_size("fsdp")
    f = lax.axis_index("fsdp")

    def part(offset):
        total = picked(own, f ^ offset).astype(F32)
        for other in got:
            total = total + picked(other, f ^ offset).astype(F32)
        return total.astype(BF)

    kept = jnp.stack([part(e) for e in range(0, nf, 2)])
    sent = jnp.stack([part(e ^ 1) for e in range(0, nf, 2)])
    return kept, sent


def fsdp_rest(kept, got):
    k = 2
    while k < lax.axis_size("fsdp"):
        total = (kept.astype(F32) + got.astype(F32)).astype(BF)
        kept, sent = total[::2], total[1::2]
        got = swapped(sent, "fsdp", k)
        k *= 2
    return kept[0], got[0]


def shards(
    tokens,
    lengths,
    norm_gain,
    w_in,
    w_dt,
    conv_w,
    conv_b,
    dt_bias,
    a_log,
    skip,
    gate_gain,
    w_out,
    cotangent,
):
    nd, ns, nf = lax.axis_size("dp"), lax.axis_size("seq"), lax.axis_size("fsdp")
    d, s, f = lax.axis_index("dp"), lax.axis_index("seq"), lax.axis_index("fsdp")
    tok = tokens.shape[1]
    length = ns * tok
    blocks = length // SPAN
    heads = HEADS // ns
    run = heads // nd
    width = heads * HEADDIM
    own_bc = 2 * STATE // ns
    used = width + own_bc
    cols = -(-(used + heads) // LANES) * LANES
    rows_in = w_in.shape[0]
    reach = CONV - 1

    levels = np.array(
        [[level_of(dd * (HEADS // nd) + ss * run + i) for dd in range(nd) for i in range(run)] for ss in range(ns)]
    )
    cuts = [0] + [h for h in range(1, heads) if (levels[:, h] != levels[:, h - 1]).any()] + [heads]
    ranges = [(a, b) for a, b in zip(cuts, cuts[1:])]
    range_level = np.array([[levels[ss, a] for a, _ in ranges] for ss in range(ns)])
    counts = (range_level[:, :, None] <= np.arange(LEVELS)[None, None, :]).astype(np.float32)
    counted = picked(jnp.asarray(counts), s)
    lowest = [int(range_level[ss].min()) for ss in range(ns)]

    def by_head(vector):
        lead = vector.shape[:-1]
        per = vector.shape[-1] // HEADS
        cut = vector.reshape(lead + (nd, ns, run * per))
        mine = lax.dynamic_index_in_dim(cut, s, len(lead) + 1, keepdims=False)
        return mine.reshape(lead + (heads * per,))

    def for_groups(matrix):
        per = matrix.shape[1] // HEADS
        cut = matrix.reshape(matrix.shape[0], nd, ns, run * per)
        return jnp.transpose(cut, (2, 0, 1, 3)).reshape(ns, matrix.shape[0], heads * per)

    def from_groups(stack):
        per = stack.shape[2] // heads
        cut = stack.reshape(ns, stack.shape[1], nd, run * per)
        return jnp.transpose(cut, (1, 2, 0, 3)).reshape(stack.shape[1], HEADS * per)

    pad_cols = cols - used - heads
    stack = jnp.concatenate(
        [
            for_groups(w_in[:, INNER : 2 * INNER]),
            w_in[:, 2 * INNER :].reshape(rows_in, ns, own_bc).transpose(1, 0, 2),
            for_groups(w_dt),
            jnp.zeros((ns, rows_in, pad_cols), BF),
            for_groups(w_in[:, :INNER]),
        ],
        axis=2,
    )
    mine = seq_exchange(stack, s)
    mine_x, mine_z = mine[:, :, :cols], mine[:, :, cols:]
    full_z = lax.all_gather(mine_z, ("dp", "fsdp"), axis=0, tiled=False)
    full_z = full_z.reshape(nd, nf, ns, rows_in, width)
    full_z = jnp.transpose(full_z, (0, 2, 1, 3, 4)).reshape(D, width)
    along = [mine_x] + [swapped(mine_x, "fsdp", k) for k in range(1, nf)]
    full_x = jnp.zeros((nd, ns, nf, rows_in, cols), BF)
    last = None
    for k, piece in enumerate(along):
        for j in range(nd):
            last = swapped(piece, "dp", j) if j else piece
            full_x = lax.dynamic_update_slice(
                full_x, last[None, :, None], (d ^ j, 0, f ^ k, 0, 0)
            )
    full_x = full_x.reshape(D, cols)
    full_out = lax.all_gather(after(w_out, along[-1]), ("dp", "fsdp"), axis=0, tiled=True)

    own_x = tokens[0].astype(F32)
    scale = lax.rsqrt(jnp.mean(own_x * own_x, axis=-1, keepdims=True) + EPS)
    xn_own = after((own_x * scale * norm_gain).astype(BF), mine)
    xn_across = swapped(xn_own, "seq", 2)
    xn = placed_by_xor(
        [xn_own, swapped(xn_own, "seq", 1), xn_across, swapped(xn_across, "seq", 1)], s
    ).reshape(length, D)

    cotangent = after(cotangent, xn_across)

    def wants(at, level):
        return lowest[at] <= level

    cots = []
    level = 0
    while level < LEVELS:
        chips = [any(wants(p, level) for p in (at, at ^ 1)) for at in range(ns)]
        end = level + 1
        while end < LEVELS and chips == [any(wants(p, end) for p in (at, at ^ 1)) for at in range(ns)]:
            end += 1
        block = cotangent[level:end, 0]
        across = swapped(block, "seq", 2, lambda i, j: chips[j])
        beside = swapped(block, "seq", 1, lambda i, j: chips[j])
        far = swapped(across, "seq", 1, lambda i, j: chips[j])
        all_blocks = placed_by_xor([block, beside, across, far], s)
        cots += [all_blocks[:, i].reshape(length, D) for i in range(end - level)]
        level = end

    positions = jnp.arange(length, dtype=jnp.int32)
    ends = jnp.cumsum(lengths[0])[:-1]
    seg = jnp.sum((positions[:, None] >= ends[None, :]).astype(jnp.int32), axis=1)
    seg_before = jnp.concatenate([jnp.full((1,), -1, jnp.int32), seg[SPAN - 1 : length - 1 : SPAN]])

    proj_x = dot(xn, full_x).astype(BF)
    proj_z = dot(xn, full_z).astype(BF)

    w_conv = jnp.concatenate(
        [
            by_head(conv_w[:, :INNER]),
            lax.dynamic_slice_in_dim(conv_w, INNER + s * own_bc, own_bc, 1),
            jnp.zeros((CONV, cols - used), F32),
        ],
        axis=1,
    )
    b_conv = jnp.concatenate(
        [
            by_head(conv_b[:INNER]),
            lax.dynamic_slice_in_dim(conv_b, INNER + s * own_bc, own_bc, 0),
            jnp.zeros((cols - used,), F32),
        ]
    )
    mixer = jnp.concatenate([jnp.zeros((reach, cols), BF), proj_x], axis=0)
    seg_pad = jnp.concatenate([jnp.full((reach,), -1, jnp.int32), seg])
    masks = [(seg_pad[k : k + length] == seg)[:, None] for k in range(CONV)]

    def taken(k, at=slice(None)):
        return jnp.where(masks[k], mixer[k : k + length, at].astype(F32), 0.0)

    pre = b_conv
    for k in range(CONV):
        pre = pre + taken(k) * w_conv[k]
    acted = jax.nn.silu(pre).astype(BF)
    bc = seq_gather(acted[:, width:used], s)
    half = ns // 2
    b_in = jnp.concatenate([bc[j] for j in range(half)], axis=1)
    c_out = jnp.concatenate([bc[j] for j in range(half, ns)], axis=1)

    def padded(rows):
        return jnp.pad(rows, ((0, 0), (0, LANES - rows.shape[1])))

    bias = by_head(dt_bias)
    rate = -jnp.exp(by_head(a_log))
    pre_dt = proj_x[:, used : used + heads].astype(F32) + bias
    steps = jax.nn.softplus(pre_dt)
    skip_own = by_head(skip)
    operands = (
        seg_before,
        seg[:, None],
        seg[None, :],
        acted[:, :width],
        b_in,
        c_out,
        padded(steps),
        steps.T,
        padded(rate[None, :]),
        rate[:, None],
        jnp.repeat(skip_own, HEADDIM)[None, :],
    )
    y, priors = scan_forward(heads, blocks, operands)

    gain = by_head(gate_gain)
    zf = proj_z.astype(F32)
    act_z = jax.nn.silu(zf)
    q = y * act_z
    q_gain = (q * gain).astype(BF)
    lanes = [(a * HEADDIM, b * HEADDIM) for a, b in ranges]
    squares = jnp.stack([jnp.sum(q[:, a:b] * q[:, a:b], axis=1) for a, b in lanes])
    widths = np.array([[(HEADS >> 3 - w) * HEADDIM] for w in range(LEVELS)], np.float32)

    def by_level(per_range):
        return jnp.sum(counted[:, :, None] * per_range[:, None, :], axis=0)

    ratio = lax.rsqrt(butterfly(by_level(squares), "seq") / widths + EPS)

    upper = []
    for j, (a, b) in enumerate(lanes):
        total = 0.0
        for w in range(LEVELS):
            if range_level[:, j].min() <= w:
                total = total + (counted[j, w] * ratio[w])[:, None] * cots[w].astype(F32)
        upper.append(total.astype(BF))
    grad_out = jnp.concatenate(
        [dot(q_gain[:, a:b], upper[j], ((0,), (0,))).astype(BF) for j, (a, b) in enumerate(lanes)]
    ).reshape(nd, nf, width // nd // nf, D)
    out_got = dp_terms([picked(grad_out, d ^ k) for k in range(1, nd)])
    out_own = picked(grad_out, d)

    q_late = after(q_gain, grad_out)
    products = [dot(q_late[:, a:b], full_out[a:b]).astype(BF) for a, b in lanes]
    shares = []
    for k in range(ns):
        parts = jnp.stack(
            [lax.dynamic_slice_in_dim(p, (s ^ k) * tok, tok, 0) for p in products]
        )
        shares.append(swapped(parts, "seq", k) if k else parts)
    inner = []
    for w in range(LEVELS):
        total = 0.0
        for j in range(len(ranges)):
            if range_level[:, j].min() <= w:
                total = total + counted[j, w] * products[j].astype(F32)
        inner.append(jnp.sum(total * cots[w].astype(F32), axis=1))
    means = butterfly(jnp.stack(inner), "seq") / widths

    grad_t = jnp.concatenate(
        [dot(upper[j], full_out[a:b], ((1,), (1,))) for j, (a, b) in enumerate(lanes)], axis=1
    )
    coefs = []
    for j in range(len(ranges)):
        coefs.append(jnp.sum(counted[j][:, None] * ratio**3 * means, axis=0))
    coef = jnp.concatenate(
        [jnp.broadcast_to(c[:, None], (length, b - a)) for c, (a, b) in zip(coefs, lanes)], axis=1
    )
    dq = gain * grad_t - q * coef
    grad_gate = jnp.sum(q * grad_t, axis=0)
    dy = (dq * act_z).astype(BF)
    dz = (dq * y * silu_slope(zf)).astype(BF)

    part = D // nd

    def in_terms(dproj, at):
        left = lax.dynamic_slice_in_dim(xn, at * part, part, 1)
        out = dot(left, dproj, ((0,), (0,))).astype(BF)
        out = out.reshape(ns, nf, rows_in, dproj.shape[1])
        return jnp.transpose(out, (1, 0, 2, 3)).reshape(nf, ns * rows_in, dproj.shape[1])

    z_other = [in_terms(dz, d ^ k) for k in range(1, nd)]
    z_got = dp_terms(z_other)
    out_kept, out_sent = fsdp_half(out_own, out_got)
    dy = after(dy, *z_other, out_sent)

    dxs, dbc, ddt, drate, dskip = scan_backward(heads, blocks, operands, y, priors, dy)
    dskip = jnp.sum(dskip[0].reshape(heads, HEADDIM), axis=1)
    out_half = swapped(out_sent, "fsdp", 1)
    dxs, out_half, shares[1] = together(dxs, out_half, shares[1])
    out_pair = fsdp_rest(out_kept, out_half)
    dbc_parts = jnp.transpose(dbc.astype(BF).reshape(length, ns, own_bc), (1, 0, 2))
    dbc_own = picked(dbc_parts, s).astype(F32)
    for k in range(1, ns):
        dbc_own = dbc_own + swapped(picked(dbc_parts, s ^ k), "seq", k).astype(F32)

    def conv_back(grad, at):
        dpre = grad * silu_slope(pre[:, at])
        grad_b = jnp.sum(dpre, axis=0)
        grad_w = jnp.stack([jnp.sum(dpre * taken(k, at), axis=0) for k in range(CONV)])
        dmixer = 0.0
        for k in range(CONV):
            moved = jnp.where(masks[k], dpre, 0.0)
            back = reach - k
            moved = jnp.concatenate(
                [moved[back:], jnp.zeros((back, moved.shape[1]), F32)], axis=0
            )
            dmixer = dmixer + moved * w_conv[k, at]
        return dmixer.astype(BF), grad_b, grad_w

    dproj_s, grad_b_s, grad_w_s = conv_back(dxs.astype(F32), slice(0, width))
    dproj_bc, grad_b_bc, grad_w_bc = conv_back(dbc_own, slice(width, used))
    grad_conv_b = jnp.concatenate([grad_b_s, grad_b_bc])
    grad_conv_w = jnp.concatenate([grad_w_s, grad_w_bc], axis=1)
    dpre_dt = ddt[:, :heads] * jax.nn.sigmoid(pre_dt)
    grad_bias = jnp.sum(dpre_dt, axis=0)
    dproj_s, z_got, shares, out_pair = together(dproj_s, z_got, shares, out_pair)
    sum_out = out_pair[0].astype(F32) + out_pair[1].astype(F32)
    dproj_r = jnp.concatenate(
        [dproj_bc, dpre_dt.astype(BF), jnp.zeros((length, pad_cols), BF)], axis=1
    )
    dproj = jnp.concatenate([dproj_s, dproj_r], axis=1)
    cut = width // 2
    flat = flattened([grad_conv_w.reshape(-1), grad_conv_b, grad_gate, grad_bias, drate[0, :heads] * rate, dskip])
    flat = butterfly(flat, "dp")
    left_other = [in_terms(after(dproj, flat)[:, :cut], d ^ k) for k in range(1, nd)]
    left_got = dp_terms(left_other)
    z_kept, z_sent = fsdp_half(after(in_terms(dz, d), dproj_s), z_got)
    z_pair = fsdp_rest(z_kept, swapped(z_sent, "fsdp", 1))
    right_other = [after(in_terms(dproj[:, cut:], d ^ k), *left_other) for k in range(1, nd)]
    right_got = dp_terms(right_other)

    dxn = dot(dz, full_z, ((1,), (1,))) + dot(after(dproj, *right_other), full_x, ((1,), (1,)))
    dxn_parts = dxn.reshape(ns, tok, D)
    near = picked(dxn_parts, s) + swapped(picked(dxn_parts, s ^ 1).astype(BF), "seq", 1).astype(F32)
    far = picked(dxn_parts, s ^ 2) + swapped(picked(dxn_parts, s ^ 3).astype(BF), "seq", 1).astype(F32)
    dxn_own = near + swapped(far.astype(BF), "seq", 2).astype(F32)
    grad_norm = jnp.sum(dxn_own * own_x * scale, axis=0)
    scaled = norm_gain * dxn_own
    dx = scale * scaled - own_x * scale**3 * jnp.mean(own_x * scaled, axis=-1, keepdims=True)
    dx = dx + jnp.sum(cotangent[:, 0].astype(F32), axis=0)

    left_kept, left_sent = fsdp_half(in_terms(dproj[:, :cut], d), left_got)
    left_pair = fsdp_rest(left_kept, swapped(left_sent, "fsdp", 1))
    right_kept, right_sent = fsdp_half(in_terms(dproj[:, cut:], d), right_got)
    right_pair = fsdp_rest(right_kept, swapped(right_sent, "fsdp", 1))

    def to_owner(pair, *others):
        total = after((pair[0].astype(F32) + pair[1].astype(F32)).astype(BF), *others)
        return seq_exchange(total.reshape(ns, rows_in, total.shape[1]), s)

    got_z = to_owner(z_pair)
    got_x = jnp.concatenate([to_owner(left_pair, right_sent), to_owner(right_pair)], axis=2)

    ratio_own = lax.dynamic_slice_in_dim(ratio, s * tok, tok, 1)
    sums = [0.0] * LEVELS
    for k in range(ns):
        theirs = picked(jnp.asarray(counts), s ^ k)
        for w in range(LEVELS):
            for j in range(len(ranges)):
                if range_level[:, j].min() <= w:
                    sums[w] = sums[w] + theirs[j, w] * shares[k][j].astype(F32)
    mixed = jnp.stack(
        [(own_x + ratio_own[w][:, None] * sums[w]).astype(BF) for w in range(LEVELS)]
    )[:, None]

    sum_in = jnp.concatenate(
        [
            from_groups(got_z),
            from_groups(got_x[:, :, :width]),
            jnp.transpose(got_x[:, :, width:used], (1, 0, 2)).reshape(rows_in, 2 * STATE),
        ],
        axis=1,
    ).astype(F32)
    sum_dt = from_groups(got_x[:, :, used : used + heads]).astype(F32)

    norm = butterfly(grad_norm.reshape(-1, LANES), "seq")
    norm = butterfly(butterfly(norm, "dp"), "fsdp").reshape(-1)
    flat = butterfly(after(flat, dxn_own), "fsdp")
    sizes = [CONV * used, used, width, heads, heads, heads]
    every = seq_gather(flat, s).reshape(ns, -1)
    starts = np.cumsum([0] + sizes)
    pieces = [every[:, a : a + n] for a, n in zip(starts, sizes)]

    def heads_back(rows):
        lead = rows.shape[1:-1]
        cut = rows.reshape((ns,) + lead + (nd, rows.shape[-1] // nd))
        order = tuple(range(1, 1 + len(lead))) + (1 + len(lead), 0, 2 + len(lead))
        return jnp.transpose(cut, order).reshape(lead + (-1,))

    conv_rows = pieces[0].reshape(ns, CONV, used)
    conv_all = jnp.concatenate(
        [
            heads_back(conv_rows[:, :, :width]),
            jnp.transpose(conv_rows[:, :, width:], (1, 0, 2)).reshape(CONV, 2 * STATE),
        ],
        axis=1,
    )
    bias_all = jnp.concatenate([heads_back(pieces[1][:, :width]), pieces[1][:, width:].reshape(-1)])
    return (
        mixed,
        dx.astype(BF)[None],
        norm,
        sum_in,
        sum_dt,
        conv_all,
        bias_all,
        heads_back(pieces[3]),
        heads_back(pieces[4]),
        heads_back(pieces[5]),
        heads_back(pieces[2]),
        sum_out,
    )


def solution(mesh):
    rows = P(("dp", "seq", "fsdp"), None)
    held = P(("dp", "fsdp"), "seq", None)
    levels = P(None, ("dp", "fsdp"), "seq", None)
    placed = (held, P(("dp", "fsdp"), None), P(), rows, rows, P(), P(), P(), P(), P(), P(), rows, levels)
    return jax.shard_map(
        shards,
        mesh=mesh,
        in_specs=placed,
        out_specs=(levels, held, P(), rows, rows, P(), P(), P(), P(), P(), P(), rows),
        check_vma=False,
    )
```

```python
import functools

import jax
import jax.numpy as jnp
import numpy as np
from jax import lax
from jax.experimental import pallas as pl
from jax.experimental.pallas import tpu as pltpu
from jax.sharding import PartitionSpec as P

D = 2048
HEADS = 64
HEADDIM = 64
STATE = 128
CONV = 4
SPAN = 256
INNER = 4096
EPS = 1e-05
LEVELS = 4
BF = jnp.bfloat16
F32 = jnp.float32
HIGH = lax.Precision.HIGHEST
LANES = 128
HALO = 16
TILE = 256
VMEM_LIMIT = 48 * 1024 * 1024


def dot(a, b, dims=((1,), (0,)), precision=None):
    return lax.dot_general(a, b, (dims, ((), ())), preferred_element_type=F32, precision=precision)


def silu_slope(v):
    sig = jax.nn.sigmoid(v)
    return sig * (1.0 + v * (1.0 - sig))


def level_of(head):
    return 0 if head < 8 else 1 if head < 16 else 2 if head < 32 else 3


def swapped(value, axis, k, keep=None):
    pairs = [(i, i ^ k) for i in range(lax.axis_size(axis))]
    if keep is not None:
        pairs = [p for p in pairs if keep(*p)]
    return lax.ppermute(value, axis, pairs)


def after(value, *others):
    return lax.optimization_barrier((value,) + others)[0]


def together(*values):
    return lax.optimization_barrier(values)


def flattened(vectors):
    flat = jnp.concatenate(vectors)
    return jnp.pad(flat, (0, -flat.shape[0] % 1024)).reshape(-1, LANES)


def butterfly(value, axis):
    k = 1
    while k < lax.axis_size(axis):
        value = value + swapped(value, axis, k)
        k *= 2
    return value


def picked(array, index):
    return lax.dynamic_index_in_dim(array, index, 0, keepdims=False)


def placed_by_xor(pieces, here):
    out = jnp.zeros((len(pieces),) + pieces[0].shape, pieces[0].dtype)
    for k, piece in enumerate(pieces):
        out = lax.dynamic_update_index_in_dim(out, piece, here ^ k, 0)
    return out


def seq_gather(block, here):
    return placed_by_xor([block] + [swapped(block, "seq", k) for k in range(1, 4)], here)


def reordered_by_xor(pieces, here):
    k = 1
    while k < len(pieces):
        flip = (here & k) > 0
        pieces = [jnp.where(flip, pieces[j ^ k], piece) for j, piece in enumerate(pieces)]
        k *= 2
    return pieces


def seq_exchange(pieces, here):
    got = [picked(pieces, here)]
    for k in range(1, pieces.shape[0]):
        got.append(swapped(picked(pieces, here ^ k), "seq", k))
    return placed_by_xor(got, here)


def call(kernel, **kwargs):
    return pl.pallas_call(
        kernel,
        compiler_params=pltpu.CompilerParams(vmem_limit_bytes=VMEM_LIMIT),
        cost_estimate=pl.CostEstimate(flops=1, bytes_accessed=1, transcendentals=0),
        **kwargs,
    )


def filled(shape, moves):
    arrays, scalars, plan = [], [], []
    for piece, lead, place in moves:
        at = next((i for i, a in enumerate(arrays) if a is piece), len(arrays))
        if at == len(arrays):
            arrays.append(piece)
        spots = []
        for size, index in zip(shape, place):
            spots.append((None, size) if index is None else (len(scalars), size))
            if index is not None:
                scalars.append(index)
        plan.append((at, lead, spots))

    def kernel(index_ref, *refs):
        pieces, out, sems = refs[: len(arrays)], refs[len(arrays)], refs[len(arrays) + 1]
        copies = []
        for m, (at, lead, spots) in enumerate(plan):
            place = tuple(pl.ds(0, size) if n is None else index_ref[n] for n, size in spots)
            source = pieces[at] if lead is None else pieces[at].at[lead]
            copies.append(pltpu.make_async_copy(source, out.at[place], sems.at[m]))
        for copy in copies:
            copy.start()
        for copy in copies:
            copy.wait()

    return call(
        kernel,
        in_specs=[pl.BlockSpec(memory_space=pltpu.SMEM)]
        + [pl.BlockSpec(memory_space=pl.ANY)] * len(arrays),
        out_specs=pl.BlockSpec(memory_space=pl.ANY),
        out_shape=jax.ShapeDtypeStruct(shape, arrays[0].dtype),
        scratch_shapes=[pltpu.SemaphoreType.DMA((len(plan),))],
        name="filled",
    )(jnp.stack(scalars).astype(jnp.int32), *arrays)


def tri(rows_first):
    a = lax.broadcasted_iota(jnp.int32, (SPAN, SPAN), 0)
    b = lax.broadcasted_iota(jnp.int32, (SPAN, SPAN), 1)
    return (a >= b) if rows_first else (a <= b)


def pair_of(lo, cols, p):
    return jnp.where(lo, cols[:, 2 * p : 2 * p + 1], cols[:, 2 * p + 1 : 2 * p + 2])


def decays(segc, segr, segp, dt, dtr, rate, rater):
    lower = tri(True).astype(F32)
    upper = tri(False).astype(F32)
    cum = dot(lower, dt * rate, precision=HIGH)
    cumr = dot(dtr * rater, upper, precision=HIGH)
    last = cum[SPAN - 1 : SPAN, :]
    keep = jnp.where(segc == segp, jnp.exp(cum), 0.0)
    to_end = jnp.where(segc == segr[:, SPAN - 1 : SPAN], jnp.exp(last - cum), 0.0)
    return cum, cumr, keep, to_end


def spread_columns(ref, first, count):
    return [jnp.broadcast_to(ref[:, first + k : first + k + 1], (SPAN, LANES)) for k in range(count)]


def taps(ext, masks, at):
    terms = [ext[pl.ds(HALO - CONV + 1 + k, SPAN), at] for k in range(CONV)]
    return [t * m for t, m in zip(terms, masks)] + terms[CONV - 1 :]


def convolved(terms, weight_ref, at):
    total = weight_ref[CONV : CONV + 1, at] + terms[0] * weight_ref[0:1, at]
    for k in range(1, CONV):
        total = total + terms[k] * weight_ref[k : k + 1, at]
    return total


def forward_kernel(
    heads,
    segp_ref,
    segc_ref,
    segr_ref,
    mask_ref,
    in_ref,
    halo_ref,
    weight_ref,
    b_ref,
    c_ref,
    dt_ref,
    dtr_ref,
    rate_ref,
    rater_ref,
    skip_ref,
    y_ref,
    prior_ref,
    carry,
    to_end_u,
    ext,
):
    block = pl.program_id(0)
    width = heads * HEADDIM

    @pl.when(block == 0)
    def _():
        carry[...] = jnp.zeros_like(carry)

    prior_ref[0] = carry[...]
    ext[0:HALO] = halo_ref[0].astype(F32)
    ext[HALO:] = in_ref[...].astype(F32)
    segc, segr = segc_ref[...], segr_ref[...]
    dt = dt_ref[...]
    cum, cumr, keep, to_end = decays(
        segc, segr, segp_ref[block], dt, dtr_ref[...], rate_ref[...], rater_ref[...]
    )
    bm, cm = b_ref[...], c_ref[...]
    mixing = dot(cm, bm, ((1,), (1,)))
    mixing = jnp.where(tri(True) & (segc == segr), mixing, 0.0)
    masks = spread_columns(mask_ref, 0, CONV - 1)
    lo = lax.broadcasted_iota(jnp.int32, (SPAN, LANES), 1) < HEADDIM
    for p in range(heads // 2):
        at = slice(p * LANES, (p + 1) * LANES)
        pre = convolved(taps(ext, masks, at), weight_ref, at)
        x2 = pre * jax.nn.sigmoid(pre)
        u2 = x2 * pair_of(lo, dt, p)
        sides = (jnp.where(lo, u2, 0.0).astype(BF), jnp.where(lo, 0.0, u2).astype(BF))
        total = dot(cm, carry[:, at].astype(BF)) * pair_of(lo, keep, p) + skip_ref[:, at] * x2
        for k in range(2):
            h = 2 * p + k
            decay = jnp.exp(jnp.minimum(cum[:, h : h + 1] - cumr[h : h + 1, :], 0.0))
            total = total + dot((decay * mixing).astype(BF), sides[k])
        y_ref[:, at] = total
        to_end_u[:, at] = (u2 * pair_of(lo, to_end, p)).astype(BF)
    fresh = dot(bm, to_end_u[...], ((0,), (0,)))
    lo_row = lax.broadcasted_iota(jnp.int32, (1, LANES), 1) < HEADDIM
    for p in range(heads // 2):
        at = slice(p * LANES, (p + 1) * LANES)
        factor = pair_of(lo_row, keep[SPAN - 1 : SPAN, :], p)
        carry[:, at] = factor * carry[:, at] + fresh[:, at]


def split_dot(value, ones):
    high = value.astype(BF)
    low = (value - high.astype(F32)).astype(BF)
    return dot(high, ones) + dot(low, ones)


def backward_kernel(
    heads,
    segp_ref,
    segc_ref,
    segr_ref,
    mask_ref,
    in_ref,
    halo_ref,
    weight_ref,
    b_ref,
    c_ref,
    dt_ref,
    dtr_ref,
    rate_ref,
    rater_ref,
    skip_ref,
    y_ref,
    prior_ref,
    dy_ref,
    din_ref,
    dbc_ref,
    ddt_ref,
    drate_ref,
    dsum_ref,
    dcarry,
    after_state,
    keep_dy,
    to_end_u,
    slopes,
    along,
    ext,
    dext,
):
    step = pl.program_id(0)
    block = pl.num_programs(0) - 1 - step

    @pl.when(step == 0)
    def _():
        dcarry[...] = jnp.zeros_like(dcarry)
        after_state[...] = jnp.zeros_like(after_state)
        drate_ref[...] = jnp.zeros_like(drate_ref)
        dsum_ref[...] = jnp.zeros_like(dsum_ref)
        dext[SPAN:] = jnp.zeros((HALO, dext.shape[1]), F32)

    ext[0:HALO] = halo_ref[0].astype(F32)
    ext[HALO:] = in_ref[...].astype(F32)
    segc, segr = segc_ref[...], segr_ref[...]
    dt = dt_ref[...]
    cum, cumr, keep, to_end = decays(
        segc, segr, segp_ref[block], dt, dtr_ref[...], rate_ref[...], rater_ref[...]
    )
    bm, cm = b_ref[...], c_ref[...]
    allowed = tri(False) & (segc == segr)
    mixing = jnp.where(allowed, dot(bm, cm, ((1,), (1,))), 0.0)
    masks = spread_columns(mask_ref, 0, CONV - 1)
    moved = spread_columns(mask_ref, CONV - 1, CONV - 1)
    lo = lax.broadcasted_iota(jnp.int32, (SPAN, LANES), 1) < HEADDIM
    dmixing = jnp.zeros((SPAN, SPAN), F32)
    for p in range(heads // 2):
        at = slice(p * LANES, (p + 1) * LANES)
        terms = taps(ext, masks, at)
        pre = convolved(terms, weight_ref, at)
        sig = jax.nn.sigmoid(pre)
        x2 = pre * sig
        dt2 = pair_of(lo, dt, p)
        u2 = x2 * dt2
        dyb = dy_ref[:, at]
        dy2 = dyb.astype(F32)
        skip = skip_ref[:, at]
        te2 = pair_of(lo, to_end, p)
        u_sides = (jnp.where(lo, u2, 0.0).astype(BF), jnp.where(lo, 0.0, u2).astype(BF))
        dy_sides = (jnp.where(lo, dy2, 0.0).astype(BF), jnp.where(lo, 0.0, dy2).astype(BF))
        du = te2 * dot(bm, dcarry[:, at].astype(BF))
        for k in range(2):
            h = 2 * p + k
            decay = jnp.exp(jnp.minimum(cumr[h : h + 1, :] - cum[:, h : h + 1], 0.0))
            du = du + dot((decay * mixing).astype(BF), dy_sides[k])
            dmixing = dmixing + decay * dot(u_sides[k], dyb, ((1,), (1,)))
        keep_dy[:, at] = (pair_of(lo, keep, p) * dy2).astype(BF)
        to_end_u[:, at] = (te2 * u2).astype(BF)
        slopes[:, at] = dy2 * (y_ref[:, at] - skip * x2) - u2.astype(BF).astype(F32) * du
        along[:, at] = x2 * du
        dpre = (dt2 * du + skip * dy2) * (sig * (1.0 + pre * (1.0 - sig)))
        dext[0:SPAN, at] = dpre
        for k in range(CONV):
            dsum_ref[k : k + 1, at] += jnp.sum(dpre * terms[k], axis=0, keepdims=True)
        dsum_ref[CONV : CONV + 1, at] += jnp.sum(dpre, axis=0, keepdims=True)
        dsum_ref[CONV + 1 : CONV + 2, at] += jnp.sum(dy2 * x2, axis=0, keepdims=True)
        din = dpre * weight_ref[CONV - 1 : CONV, at]
        for k in range(CONV - 1):
            later = dext[pl.ds(CONV - 1 - k, SPAN), at]
            din = din + later * moved[k] * weight_ref[k : k + 1, at]
        din_ref[:, at] = din.astype(BF)
    dext[SPAN:] = dext[0:HALO]
    dmixing = jnp.where(allowed, dmixing, 0.0).astype(BF)
    dstate = dcarry[...].astype(BF)
    prior = prior_ref[0]
    dbc_ref[:, :STATE] = dot(dmixing, cm) + dot(to_end_u[...], dstate, ((1,), (1,)))
    dbc_ref[:, STATE:] = dot(dmixing, bm, ((0,), (0,))) + dot(
        keep_dy[...], prior.astype(BF), ((1,), (1,))
    )
    width = heads * HEADDIM
    ones = (
        lax.broadcasted_iota(jnp.int32, (width, LANES), 0) // HEADDIM
        == lax.broadcasted_iota(jnp.int32, (width, LANES), 1)
    ).astype(BF)
    at_end = jnp.sum(dcarry[...] * after_state[...], axis=0, keepdims=True)
    at_end = split_dot(jnp.broadcast_to(at_end, (16, width)), ones)[:1]
    dcum = split_dot(slopes[...], ones)
    da = dot(tri(False).astype(F32), dcum, precision=HIGH) + at_end
    ddt_ref[...] = rate_ref[...] * da + split_dot(along[...], ones)
    drate_ref[...] += jnp.sum(dt * da, axis=0, keepdims=True)
    fresh = dot(cm, keep_dy[...], ((0,), (0,)))
    lo_row = lax.broadcasted_iota(jnp.int32, (1, LANES), 1) < HEADDIM
    for p in range(heads // 2):
        at = slice(p * LANES, (p + 1) * LANES)
        factor = pair_of(lo_row, keep[SPAN - 1 : SPAN, :], p)
        dcarry[:, at] = factor * dcarry[:, at] + fresh[:, at]
    after_state[...] = prior


def scan_specs(heads, at):
    width = heads * HEADDIM

    def rows(n):
        return pl.BlockSpec((SPAN, n), lambda i: (at(i), 0))

    def whole(*shape):
        return pl.BlockSpec(shape, lambda i: (0,) * len(shape))

    ins = [
        pl.BlockSpec(memory_space=pltpu.SMEM),
        rows(1),
        pl.BlockSpec((1, SPAN), lambda i: (0, at(i))),
        rows(LANES),
        rows(width),
        pl.BlockSpec((1, HALO, width), lambda i: (at(i), 0, 0)),
        whole(8, width),
        rows(STATE),
        rows(STATE),
        rows(LANES),
        pl.BlockSpec((heads, SPAN), lambda i: (0, at(i))),
        whole(1, LANES),
        whole(heads, 1),
        whole(1, width),
    ]
    prior = pl.BlockSpec((1, STATE, width), lambda i: (at(i), 0, 0))
    return rows, whole, ins, prior


def scan_forward(heads, blocks, operands):
    rows, whole, ins, prior = scan_specs(heads, lambda i: i)
    width = heads * HEADDIM
    return call(
        functools.partial(forward_kernel, heads),
        grid=(blocks,),
        in_specs=ins,
        out_specs=[rows(width), prior],
        out_shape=[
            jax.ShapeDtypeStruct((blocks * SPAN, width), F32),
            jax.ShapeDtypeStruct((blocks, STATE, width), F32),
        ],
        scratch_shapes=[
            pltpu.VMEM((STATE, width), F32),
            pltpu.VMEM((SPAN, width), BF),
            pltpu.VMEM((HALO + SPAN, width), F32),
        ],
        name="scan_forward",
    )(*operands)


def scan_backward(heads, blocks, operands, y, priors, dy):
    rows, whole, ins, prior = scan_specs(heads, lambda i: blocks - 1 - i)
    width = heads * HEADDIM
    return call(
        functools.partial(backward_kernel, heads),
        grid=(blocks,),
        in_specs=ins + [rows(width), prior, rows(width)],
        out_specs=[rows(width), rows(2 * STATE), rows(LANES), whole(1, LANES), whole(8, width)],
        out_shape=[
            jax.ShapeDtypeStruct((blocks * SPAN, width), BF),
            jax.ShapeDtypeStruct((blocks * SPAN, 2 * STATE), F32),
            jax.ShapeDtypeStruct((blocks * SPAN, LANES), F32),
            jax.ShapeDtypeStruct((1, LANES), F32),
            jax.ShapeDtypeStruct((8, width), F32),
        ],
        scratch_shapes=[
            pltpu.VMEM((STATE, width), F32),
            pltpu.VMEM((STATE, width), F32),
            pltpu.VMEM((SPAN, width), BF),
            pltpu.VMEM((SPAN, width), BF),
            pltpu.VMEM((SPAN, width), F32),
            pltpu.VMEM((SPAN, width), F32),
            pltpu.VMEM((HALO + SPAN, width), F32),
            pltpu.VMEM((SPAN + HALO, width), F32),
        ],
        name="scan_backward",
    )(*operands, y, priors, dy)


def level_pieces(groups):
    return [(g, i) for g, count in enumerate(groups) for i in range(count)]


def upper_kernel(plan, lanes, tok, ns, here_ref, coef_ref, q_ref, *refs):
    pieces, (upper_ref, grad_ref, q_turned) = refs[:-3], refs[-3:]

    @pl.when(pl.program_id(0) == 0)
    def _():
        q_turned[...] = q_ref[...].T

    for j, (a, b) in enumerate(lanes):
        for k in range(ns):
            at = here_ref[0] ^ k
            rows = pl.ds(pl.multiple_of(at * tok, tok), tok)
            total = None
            for w, g, i in plan[j]:
                n = j * LEVELS + w
                term = coef_ref[rows, n : n + 1] * pieces[g * ns + k][i].astype(F32)
                total = term if total is None else total + term
            total = total.astype(BF)
            upper_ref[j, rows, :] = total
        grad_ref[a:b, :] = dot(q_turned[a:b, :], upper_ref[j]).astype(BF)


def products_kernel(plan, lanes, tok, ns, here_ref, count_ref, q_ref, w_ref, *refs):
    pieces, (prod_ref, inner_ref, sums) = refs[:-3], refs[-3:]
    step = pl.program_id(0)

    @pl.when(step == 0)
    def _():
        sums[...] = jnp.zeros_like(sums)

    for k in range(ns):
        at = here_ref[0] ^ k
        rows = pl.ds(pl.multiple_of(at * tok, tok), tok)
        for j, (a, b) in enumerate(lanes):
            value = dot(q_ref[rows, a:b], w_ref[a:b, :])
            prod_ref[at, j] = value.astype(BF)
            for w, g, i in plan[j]:
                part = value * (pieces[g * ns + k][i].astype(F32) * count_ref[j, w])
                folded = part[:, :LANES]
                for c in range(LANES, part.shape[1], LANES):
                    folded = folded + part[:, c : c + LANES]
                sums[w, rows, :] += folded

    @pl.when(step == pl.num_programs(0) - 1)
    def _():
        lane = lax.broadcasted_iota(jnp.int32, inner_ref.shape, 1)
        total = jnp.zeros(inner_ref.shape, F32)
        for w in range(LEVELS):
            total = jnp.where(lane == w, jnp.sum(sums[w], axis=1, keepdims=True), total)
        inner_ref[...] = total


def gate_kernel(lanes, upper_ref, w_ref, y_ref, z_ref, gain_ref, coef_ref, dy_ref, dz_ref, grad_ref):
    @pl.when(pl.program_id(0) == 0)
    def _():
        grad_ref[...] = jnp.zeros_like(grad_ref)

    for j, (a, b) in enumerate(lanes):
        upper = upper_ref[j]
        coef = coef_ref[:, j : j + 1]
        wide = TILE if (b - a) % TILE == 0 else LANES
        for c in range(a, b, wide):
            at = slice(c, c + wide)
            grad_t = dot(upper, w_ref[at, :], ((1,), (1,)))
            z = z_ref[:, at].astype(F32)
            sig = jax.nn.sigmoid(z)
            act = z * sig
            y = y_ref[:, at]
            q = y * act
            dq = gain_ref[:, at] * grad_t - q * coef
            dy_ref[:, at] = (dq * act).astype(BF)
            dz_ref[:, at] = (dq * y * (sig * (1.0 + z * (1.0 - sig)))).astype(BF)
            grad_ref[0:1, at] += jnp.sum(q * grad_t, axis=0, keepdims=True)


def mixed_kernel(plan, ns, count_ref, ratio_ref, x_ref, *refs):
    shares, out_ref = refs[:-1], refs[-1]
    x = x_ref[...].astype(F32)
    for w in range(LEVELS):
        total = None
        for k in range(ns):
            for j in plan[w]:
                term = shares[k][j].astype(F32) * count_ref[k, j * LEVELS + w]
                total = term if total is None else total + term
        out_ref[w] = (x + ratio_ref[:, w : w + 1] * total).astype(BF)


def dp_terms(others):
    return [swapped(other, "dp", k + 1) for k, other in enumerate(others)]


def fsdp_half(own, got):
    nf = lax.axis_size("fsdp")
    f = lax.axis_index("fsdp")

    def part(offset):
        total = picked(own, f ^ offset).astype(F32)
        for other in got:
            total = total + picked(other, f ^ offset).astype(F32)
        return total.astype(BF)

    kept = jnp.stack([part(e) for e in range(0, nf, 2)])
    sent = jnp.stack([part(e ^ 1) for e in range(0, nf, 2)])
    return kept, sent


def fsdp_rest(kept, got):
    k = 2
    while k < lax.axis_size("fsdp"):
        total = (kept.astype(F32) + got.astype(F32)).astype(BF)
        kept, sent = total[::2], total[1::2]
        got = swapped(sent, "fsdp", k)
        k *= 2
    return kept[0], got[0]


def shards(
    tokens,
    lengths,
    norm_gain,
    w_in,
    w_dt,
    conv_w,
    conv_b,
    dt_bias,
    a_log,
    skip,
    gate_gain,
    w_out,
    cotangent,
):
    nd, ns, nf = lax.axis_size("dp"), lax.axis_size("seq"), lax.axis_size("fsdp")
    d, s, f = lax.axis_index("dp"), lax.axis_index("seq"), lax.axis_index("fsdp")
    tok = tokens.shape[1]
    length = ns * tok
    blocks = length // SPAN
    heads = HEADS // ns
    run = heads // nd
    width = heads * HEADDIM
    own_bc = 2 * STATE // ns
    used = width + own_bc
    cols = -(-(used + heads) // LANES) * LANES
    rows_in = w_in.shape[0]
    reach = CONV - 1

    levels = np.array(
        [[level_of(dd * (HEADS // nd) + ss * run + i) for dd in range(nd) for i in range(run)] for ss in range(ns)]
    )
    cuts = [0] + [h for h in range(1, heads) if (levels[:, h] != levels[:, h - 1]).any()] + [heads]
    ranges = [(a, b) for a, b in zip(cuts, cuts[1:])]
    range_level = np.array([[levels[ss, a] for a, _ in ranges] for ss in range(ns)])
    counts = (range_level[:, :, None] <= np.arange(LEVELS)[None, None, :]).astype(np.float32)
    counted = picked(jnp.asarray(counts), s)
    lowest = [int(range_level[ss].min()) for ss in range(ns)]

    def by_head(vector):
        lead = vector.shape[:-1]
        per = vector.shape[-1] // HEADS
        cut = vector.reshape(lead + (nd, ns, run * per))
        mine = lax.dynamic_index_in_dim(cut, s, len(lead) + 1, keepdims=False)
        return mine.reshape(lead + (heads * per,))

    def for_groups(matrix):
        per = matrix.shape[1] // HEADS
        cut = matrix.reshape(matrix.shape[0], nd, ns, run * per)
        return jnp.transpose(cut, (2, 0, 1, 3)).reshape(ns, matrix.shape[0], heads * per)

    def from_groups(stack):
        per = stack.shape[2] // heads
        cut = stack.reshape(ns, stack.shape[1], nd, run * per)
        return jnp.transpose(cut, (1, 2, 0, 3)).reshape(stack.shape[1], HEADS * per)

    pad_cols = cols - used - heads
    stack = jnp.concatenate(
        [
            for_groups(w_in[:, INNER : 2 * INNER]),
            w_in[:, 2 * INNER :].reshape(rows_in, ns, own_bc).transpose(1, 0, 2),
            for_groups(w_dt),
            jnp.zeros((ns, rows_in, pad_cols), BF),
            for_groups(w_in[:, :INNER]),
        ],
        axis=2,
    )
    arrived = [picked(stack, s)] + [swapped(picked(stack, s ^ k), "seq", k) for k in range(1, ns)]
    mine = filled((ns, rows_in, stack.shape[2]), [(p, None, (s ^ k, None, None)) for k, p in enumerate(arrived)])
    mine_x, mine_z = mine[:, :, :cols], mine[:, :, cols:]

    own_x = tokens[0].astype(F32)
    scale = lax.rsqrt(jnp.mean(own_x * own_x, axis=-1, keepdims=True) + EPS)
    xn_own = (own_x * scale * norm_gain).astype(BF)
    xn_across = swapped(xn_own, "seq", 2)
    xn_pieces = [xn_own, swapped(xn_own, "seq", 1), xn_across, swapped(xn_across, "seq", 1)]
    xn = filled((ns, tok, D), [(p, None, (s ^ k, None, None)) for k, p in enumerate(xn_pieces)])
    xn = xn.reshape(length, D)

    along = [mine_x] + [swapped(mine_x, "fsdp", k) for k in range(1, nf)]
    moves = []
    for k, piece in enumerate(along):
        for j in range(nd):
            moved = swapped(piece, "dp", j) if j else piece
            moves.append((moved, None, (d ^ j, None, f ^ k, None, None)))
    full_x = filled((nd, ns, nf, rows_in, cols), moves).reshape(D, cols)

    def doubled(chunk):
        held, offsets, bit = chunk[None], [0], nf // 2
        while bit > 1:
            held = jnp.concatenate([held, swapped(held, "fsdp", bit)])
            offsets = offsets + [o ^ bit for o in offsets]
            bit //= 2
        return held, offsets

    def spread_over_dp(held, offsets, middle):
        out = []
        for j in range(nd):
            moved = swapped(held, "dp", j) if j else held
            for i, o in enumerate(offsets):
                out.append((moved, i, (d ^ j,) + middle + (f ^ o,)))
        return out

    held_z, offsets = doubled(after(mine_z, *along[1:]))
    other_offsets = [o ^ 1 for o in offsets]

    def wants(at, level):
        return lowest[at] <= level

    def chips_of(level):
        return [any(wants(p, level) for p in (at, at ^ 1)) for at in range(ns)]

    groups = []
    for level in range(LEVELS):
        if groups and chips_of(level) == chips_of(level - 1):
            groups[-1][1] = level + 1
        else:
            groups.append([level, level + 1])

    def cotangent_pieces(group, *others):
        chips = chips_of(group[0])
        block = after(cotangent[group[0] : group[1], 0], *others)
        across = swapped(block, "seq", 2, lambda i, j: chips[j])
        beside = swapped(block, "seq", 1, lambda i, j: chips[j])
        far = swapped(across, "seq", 1, lambda i, j: chips[j])
        return [block, beside, across, far]

    cots = [None] * len(groups)
    cots[-1] = cotangent_pieces(groups[-1], xn_across)

    positions = jnp.arange(length, dtype=jnp.int32)
    ends = jnp.cumsum(lengths[0])[:-1]
    seg = jnp.sum((positions[:, None] >= ends[None, :]).astype(jnp.int32), axis=1)
    seg_before = jnp.concatenate([jnp.full((1,), -1, jnp.int32), seg[SPAN - 1 : length - 1 : SPAN]])
    seg_pad = jnp.concatenate([jnp.full((reach,), -1, jnp.int32), seg])
    masks = [(seg_pad[k : k + length] == seg) for k in range(reach)]
    mask_cols = [m.astype(F32) for m in masks]
    mask_cols += [jnp.pad(m, (0, reach - k))[reach - k :] for k, m in enumerate(mask_cols)]
    mask_cols = jnp.pad(jnp.stack(mask_cols, axis=1), ((0, 0), (0, LANES - 2 * reach)))

    weight_s = jnp.concatenate(
        [by_head(conv_w[:, :INNER]), by_head(conv_b[None, :INNER]), jnp.zeros((3, width), F32)]
    )
    weight_r = jnp.pad(
        lax.dynamic_slice_in_dim(conv_w, INNER + s * own_bc, own_bc, 1), ((0, 0), (0, cols - used))
    )
    bias_r = jnp.pad(
        lax.dynamic_slice_in_dim(conv_b, INNER + s * own_bc, own_bc, 0), (0, cols - used)
    )
    bias = by_head(dt_bias)
    rate = -jnp.exp(by_head(a_log))
    skip_own = by_head(skip)
    gain = by_head(gate_gain)

    proj = dot(xn, full_x).astype(BF)
    proj, held_z = together(proj, held_z)
    turned_z = swapped(held_z, "fsdp", 1)
    held_out, _ = doubled(after(w_out, held_z))
    moves_z = spread_over_dp(held_z, offsets, (None,))

    proj_r = proj[:, width:]
    mixer = jnp.concatenate([jnp.zeros((reach, cols - width), BF), proj_r], axis=0)

    def taken(k):
        rows = mixer[k : k + length].astype(F32)
        return jnp.where(masks[k][:, None], rows, 0.0) if k < reach else rows

    pre_r = bias_r
    for k in range(CONV):
        pre_r = pre_r + taken(k) * weight_r[k]
    bc_own = jax.nn.silu(pre_r).astype(BF)[:, :own_bc]
    bc = [bc_own] + [swapped(bc_own, "seq", k) for k in range(1, ns)]
    for g in range(len(groups) - 1):
        cots[g] = cotangent_pieces(groups[g], *bc)
    bc = reordered_by_xor(bc, s)
    b_in = jnp.concatenate(bc[: ns // 2], axis=1)
    c_out = jnp.concatenate(bc[ns // 2 :], axis=1)

    def padded(rows):
        return jnp.pad(rows, ((0, 0), (0, LANES - rows.shape[1])))

    pre_dt = proj_r[:, own_bc : own_bc + heads].astype(F32) + bias
    steps = jax.nn.softplus(pre_dt)
    tails = proj.reshape(blocks, SPAN, cols)[: blocks - 1, SPAN - HALO :, :width]
    operands = (
        seg_before,
        seg[:, None],
        seg[None, :],
        mask_cols,
        proj,
        jnp.concatenate([jnp.zeros((1, HALO, width), BF), tails]),
        weight_s,
        b_in,
        c_out,
        padded(steps),
        steps.T,
        padded(rate[None, :]),
        rate[:, None],
        jnp.repeat(skip_own, HEADDIM)[None, :],
    )
    y, priors = scan_forward(heads, blocks, operands)
    y, turned_z, held_out = together(y, turned_z, held_out)
    moves_z += spread_over_dp(turned_z, other_offsets, (None,))
    moves_z = [(p, lead, place[:2] + place[2:] + (None, None)) for p, lead, place in moves_z]
    full_z = filled((nd, ns, nf, rows_in, width), moves_z).reshape(D, width)
    turned_out = swapped(held_out, "fsdp", 1)
    moves_out = spread_over_dp(held_out, offsets, ())

    proj_z = dot(xn, full_z).astype(BF)
    proj_z, turned_out = together(proj_z, turned_out)
    moves_out += spread_over_dp(turned_out, other_offsets, ())
    moves_out = [(p, lead, place + (None, None)) for p, lead, place in moves_out]
    q = y * jax.nn.silu(proj_z.astype(F32))
    q_gain = (q * gain).astype(BF)
    lanes = [(a * HEADDIM, b * HEADDIM) for a, b in ranges]
    squares = jnp.stack([jnp.sum(q[:, a:b] * q[:, a:b], axis=1) for a, b in lanes])
    widths = np.array([[(HEADS >> 3 - w) * HEADDIM] for w in range(LEVELS)], np.float32)
    per_level = jnp.sum(counted[:, :, None] * squares[:, None, :], axis=0)
    ratio = lax.rsqrt(butterfly(per_level, "seq") / widths + EPS)

    order = level_pieces([b - a for a, b in groups])
    plan = [[(w,) + order[w] for w in range(LEVELS) if range_level[:, j].min() <= w] for j in range(len(lanes))]
    here = s.astype(jnp.int32)[None]
    tile = pl.BlockSpec((length, TILE), lambda i: (0, i))
    cot_specs = [
        pl.BlockSpec((b - a, tok, TILE), lambda i: (0, 0, i)) for a, b in groups for _ in range(ns)
    ]
    cot_pieces = [piece for group in cots for piece in group]
    smem = pl.BlockSpec(memory_space=pltpu.SMEM)
    coef = jnp.concatenate([counted[j][:, None] * ratio for j in range(len(lanes))])
    upper, grad_out = call(
        functools.partial(upper_kernel, plan, lanes, tok, ns),
        grid=(D // TILE,),
        in_specs=[
            smem,
            pl.BlockSpec((length, LANES), lambda i: (0, 0)),
            pl.BlockSpec((length, width), lambda i: (0, 0)),
        ]
        + cot_specs,
        out_specs=[
            pl.BlockSpec((len(lanes), length, TILE), lambda i: (0, 0, i)),
            pl.BlockSpec((width, TILE), lambda i: (0, i)),
        ],
        out_shape=[
            jax.ShapeDtypeStruct((len(lanes), length, D), BF),
            jax.ShapeDtypeStruct((width, D), BF),
        ],
        scratch_shapes=[pltpu.VMEM((width, length), BF)],
        name="upper",
    )(here, padded(coef.T), q_gain, *cot_pieces)
    grad_out = grad_out.reshape(nd, nf, width // nd // nf, D)
    out_other = [picked(grad_out, d ^ k) for k in range(1, nd)]
    out_got = dp_terms(out_other)
    out_own = picked(grad_out, d)

    full_out = filled((nd, nf) + w_out.shape, moves_out).reshape(width, D)
    full_out, out_other = together(full_out, out_other)
    products, inner = call(
        functools.partial(products_kernel, plan, lanes, tok, ns),
        grid=(D // TILE,),
        in_specs=[
            smem,
            smem,
            pl.BlockSpec((length, width), lambda i: (0, 0)),
            pl.BlockSpec((width, TILE), lambda i: (0, i)),
        ]
        + cot_specs,
        out_specs=[
            pl.BlockSpec((ns, len(lanes), tok, TILE), lambda i: (0, 0, 0, i)),
            pl.BlockSpec((length, LANES), lambda i: (0, 0)),
        ],
        out_shape=[
            jax.ShapeDtypeStruct((ns, len(lanes), tok, D), BF),
            jax.ShapeDtypeStruct((length, LANES), F32),
        ],
        scratch_shapes=[pltpu.VMEM((LEVELS, length, LANES), F32)],
        name="products",
    )(here, counted, q_gain, full_out, *cot_pieces)
    means = butterfly(inner[:, :LEVELS].T, "seq") / widths
    shares = [picked(products, s ^ k) for k in range(ns)]
    shares[1:3] = [swapped(after(shares[k], means), "seq", k) for k in (1, 2)]

    coef = jnp.sum(counted[:, :, None] * (ratio**3 * means)[None], axis=1)
    rows = pl.BlockSpec((SPAN, width), lambda i: (i, 0))
    dy, dz, grad_gate = call(
        functools.partial(gate_kernel, lanes),
        grid=(blocks,),
        in_specs=[
            pl.BlockSpec((len(lanes), SPAN, D), lambda i: (0, i, 0)),
            pl.BlockSpec((width, D), lambda i: (0, 0)),
            rows,
            rows,
            pl.BlockSpec((1, width), lambda i: (0, 0)),
            pl.BlockSpec((SPAN, LANES), lambda i: (i, 0)),
        ],
        out_specs=[rows, rows, pl.BlockSpec((8, width), lambda i: (0, 0))],
        out_shape=[
            jax.ShapeDtypeStruct((length, width), BF),
            jax.ShapeDtypeStruct((length, width), BF),
            jax.ShapeDtypeStruct((8, width), F32),
        ],
        name="gate_backward",
    )(upper, full_out, y, proj_z, gain[None], padded(coef.T))
    grad_gate = grad_gate[0]

    part = D // nd

    def in_terms(dproj, at):
        left = lax.dynamic_slice_in_dim(xn, at * part, part, 1)
        out = dot(left, dproj, ((0,), (0,))).astype(BF)
        out = out.reshape(ns, nf, rows_in, dproj.shape[1])
        return jnp.transpose(out, (1, 0, 2, 3)).reshape(nf, ns * rows_in, dproj.shape[1])

    z_other = [in_terms(dz, d ^ k) for k in range(1, nd)]
    z_got = dp_terms(z_other)
    out_kept, out_sent = fsdp_half(out_own, out_got)
    dy = after(dy, *z_other, out_sent)
    out_half = swapped(out_sent, "fsdp", 1)

    dproj_s, dbc, ddt, drate, dsum = scan_backward(heads, blocks, operands, y, priors, dy)
    dproj_s, dbc, out_half, shares[1] = together(dproj_s, dbc, out_half, shares[1])
    out_pair = fsdp_rest(out_kept, out_half)
    dbc = dbc.astype(BF)
    dbc_parts = reordered_by_xor([dbc[:, j * own_bc : (j + 1) * own_bc] for j in range(ns)], s)
    dbc_got = [swapped(dbc_parts[k], "seq", k) for k in range(1, ns)]
    dbc_own = dbc_parts[0].astype(F32)
    for got in dbc_got:
        dbc_own = dbc_own + got.astype(F32)
    shares[3] = swapped(after(shares[3], *dbc_got), "seq", 3)

    dpre = jnp.pad(dbc_own, ((0, 0), (0, cols - used))) * silu_slope(pre_r)
    grad_b_r = jnp.sum(dpre, axis=0)[:own_bc]
    grad_w_r = jnp.stack([jnp.sum(dpre * taken(k), axis=0) for k in range(CONV)])[:, :own_bc]
    dmixer = dpre * weight_r[reach]
    for k in range(reach):
        back = reach - k
        later = jnp.where(masks[k][:, None], dpre, 0.0)[back:]
        dmixer = dmixer + jnp.pad(later, ((0, back), (0, 0))) * weight_r[k]
    dpre_dt = ddt[:, :heads] * jax.nn.sigmoid(pre_dt)
    dproj_r = jnp.concatenate(
        [dmixer[:, :own_bc].astype(BF), dpre_dt.astype(BF), jnp.zeros((length, pad_cols), BF)], axis=1
    )
    cut = width // 2
    left_in = dproj_s[:, :cut]
    left_other = [in_terms(left_in, d ^ k) for k in range(1, nd)]
    left_got = dp_terms(left_other)
    dproj_r = after(dproj_r, *left_other)
    right_in = jnp.concatenate([dproj_s[:, cut:], dproj_r], axis=1)
    right_other = [in_terms(right_in, d ^ k) for k in range(1, nd)]
    right_got = dp_terms(right_other)
    z_kept, z_sent = fsdp_half(after(in_terms(dz, d), *left_other), z_got)
    z_pair = fsdp_rest(z_kept, swapped(z_sent, "fsdp", 1))
    flat = flattened(
        [
            jnp.concatenate([dsum[:CONV], grad_w_r], axis=1).reshape(-1),
            dsum[CONV],
            grad_b_r,
            grad_gate,
            jnp.sum(dpre_dt, axis=0),
            drate[0, :heads] * rate,
            jnp.sum(dsum[CONV + 1].reshape(heads, HEADDIM), axis=1),
        ]
    )
    flat = butterfly(butterfly(after(flat, *right_other), "dp"), "fsdp")

    dxn = dot(dz, full_z, ((1,), (1,))) + dot(
        jnp.concatenate([dproj_s, after(dproj_r, *right_other)], axis=1), full_x, ((1,), (1,))
    )
    dxn_parts = dxn.reshape(ns, tok, D)
    near = picked(dxn_parts, s) + swapped(picked(dxn_parts, s ^ 1).astype(BF), "seq", 1).astype(F32)
    far = picked(dxn_parts, s ^ 2) + swapped(picked(dxn_parts, s ^ 3).astype(BF), "seq", 1).astype(F32)
    dxn_own = near + swapped(after(far.astype(BF), shares[3]), "seq", 2).astype(F32)
    grad_norm = jnp.sum(dxn_own * own_x * scale, axis=0)
    scaled = norm_gain * dxn_own
    dx = scale * scaled - own_x * scale**3 * jnp.mean(own_x * scaled, axis=-1, keepdims=True)
    dx = dx + jnp.sum(cotangent[:, 0].astype(F32), axis=0)

    left_kept, left_sent = fsdp_half(in_terms(left_in, d), left_got)
    left_pair = fsdp_rest(left_kept, swapped(left_sent, "fsdp", 1))
    right_kept, right_sent = fsdp_half(in_terms(right_in, d), right_got)
    right_pair = fsdp_rest(right_kept, swapped(right_sent, "fsdp", 1))

    def to_owner(pair, *others):
        total = after((pair[0].astype(F32) + pair[1].astype(F32)).astype(BF), *others)
        return seq_exchange(total.reshape(ns, rows_in, total.shape[1]), s)

    sum_out = out_pair[0].astype(F32) + out_pair[1].astype(F32)
    got_z = to_owner(z_pair)
    got_x = jnp.concatenate([to_owner(left_pair, right_sent), to_owner(right_pair)], axis=2)

    ratio_own = padded(lax.dynamic_slice_in_dim(ratio, s * tok, tok, 1).T)
    theirs = jnp.stack([picked(jnp.asarray(counts), s ^ k).reshape(-1) for k in range(ns)])
    mixed = call(
        functools.partial(
            mixed_kernel,
            [[j for j in range(len(lanes)) if range_level[:, j].min() <= w] for w in range(LEVELS)],
            ns,
        ),
        grid=(D // TILE,),
        in_specs=[
            smem,
            pl.BlockSpec((tok, LANES), lambda i: (0, 0)),
            pl.BlockSpec((tok, TILE), lambda i: (0, i)),
        ]
        + [pl.BlockSpec((len(lanes), tok, TILE), lambda i: (0, 0, i))] * ns,
        out_specs=pl.BlockSpec((LEVELS, tok, TILE), lambda i: (0, 0, i)),
        out_shape=jax.ShapeDtypeStruct((LEVELS, tok, D), BF),
        name="mixed",
    )(theirs, ratio_own, tokens[0], *shares)[:, None]

    sum_in = jnp.concatenate(
        [
            from_groups(got_z),
            from_groups(got_x[:, :, :width]),
            jnp.transpose(got_x[:, :, width:used], (1, 0, 2)).reshape(rows_in, 2 * STATE),
        ],
        axis=1,
    ).astype(F32)
    sum_dt = from_groups(got_x[:, :, used : used + heads]).astype(F32)

    norm = butterfly(after(grad_norm.reshape(-1, LANES), right_sent), "seq")
    norm = butterfly(butterfly(norm, "dp"), "fsdp").reshape(-1)
    sizes = [CONV * used, used, width, heads, heads, heads]
    every = seq_gather(flat, s).reshape(ns, -1)
    starts = np.cumsum([0] + sizes)
    pieces = [every[:, a : a + n] for a, n in zip(starts, sizes)]

    def heads_back(rows):
        lead = rows.shape[1:-1]
        cut = rows.reshape((ns,) + lead + (nd, rows.shape[-1] // nd))
        order = tuple(range(1, 1 + len(lead))) + (1 + len(lead), 0, 2 + len(lead))
        return jnp.transpose(cut, order).reshape(lead + (-1,))

    conv_rows = pieces[0].reshape(ns, CONV, used)
    conv_all = jnp.concatenate(
        [
            heads_back(conv_rows[:, :, :width]),
            jnp.transpose(conv_rows[:, :, width:], (1, 0, 2)).reshape(CONV, 2 * STATE),
        ],
        axis=1,
    )
    bias_all = jnp.concatenate([heads_back(pieces[1][:, :width]), pieces[1][:, width:].reshape(-1)])
    return (
        mixed,
        dx.astype(BF)[None],
        norm,
        sum_in,
        sum_dt,
        conv_all,
        bias_all,
        heads_back(pieces[3]),
        heads_back(pieces[4]),
        heads_back(pieces[5]),
        heads_back(pieces[2]),
        sum_out,
    )


def solution(mesh):
    rows = P(("dp", "seq", "fsdp"), None)
    held = P(("dp", "fsdp"), "seq", None)
    levels = P(None, ("dp", "fsdp"), "seq", None)
    placed = (held, P(("dp", "fsdp"), None), P(), rows, rows, P(), P(), P(), P(), P(), P(), rows, levels)
    return jax.shard_map(
        shards,
        mesh=mesh,
        in_specs=placed,
        out_specs=(levels, held, P(), rows, rows, P(), P(), P(), P(), P(), P(), rows),
        check_vma=False,
    )
```

```python
import functools

import jax
import jax.numpy as jnp
import numpy as np
from jax import lax
from jax.experimental import pallas as pl
from jax.experimental.pallas import tpu as pltpu
from jax.sharding import PartitionSpec as P

D = 2048
HEADS = 64
HEADDIM = 64
STATE = 128
CONV = 4
SPAN = 256
INNER = 4096
EPS = 1e-05
LEVELS = 4
BF = jnp.bfloat16
F32 = jnp.float32
HIGH = lax.Precision.HIGHEST
LANES = 128
HALO = 16
TILE = 256
VMEM_LIMIT = 48 * 1024 * 1024


def dot(a, b, dims=((1,), (0,)), precision=None):
    return lax.dot_general(a, b, (dims, ((), ())), preferred_element_type=F32, precision=precision)


def silu_slope(v):
    sig = jax.nn.sigmoid(v)
    return sig * (1.0 + v * (1.0 - sig))


def level_of(head):
    return 0 if head < 8 else 1 if head < 16 else 2 if head < 32 else 3


def swapped(value, axis, k, keep=None):
    pairs = [(i, i ^ k) for i in range(lax.axis_size(axis))]
    if keep is not None:
        pairs = [p for p in pairs if keep(*p)]
    return lax.ppermute(value, axis, pairs)


def after(value, *others):
    return lax.optimization_barrier((value,) + others)[0]


def together(*values):
    return lax.optimization_barrier(values)


def flattened(vectors):
    flat = jnp.concatenate(vectors)
    return jnp.pad(flat, (0, -flat.shape[0] % 1024)).reshape(-1, LANES)


def butterfly(value, axis):
    k = 1
    while k < lax.axis_size(axis):
        value = value + swapped(value, axis, k)
        k *= 2
    return value


def picked(array, index):
    return lax.dynamic_index_in_dim(array, index, 0, keepdims=False)


def placed_by_xor(pieces, here):
    out = jnp.zeros((len(pieces),) + pieces[0].shape, pieces[0].dtype)
    for k, piece in enumerate(pieces):
        out = lax.dynamic_update_index_in_dim(out, piece, here ^ k, 0)
    return out


def seq_gather(block, here):
    return placed_by_xor([block] + [swapped(block, "seq", k) for k in range(1, 4)], here)


def reordered_by_xor(pieces, here):
    k = 1
    while k < len(pieces):
        flip = (here & k) > 0
        pieces = [jnp.where(flip, pieces[j ^ k], piece) for j, piece in enumerate(pieces)]
        k *= 2
    return pieces


def seq_exchange(pieces, here):
    got = [picked(pieces, here)]
    for k in range(1, pieces.shape[0]):
        got.append(swapped(picked(pieces, here ^ k), "seq", k))
    return placed_by_xor(got, here)


def call(kernel, **kwargs):
    return pl.pallas_call(
        kernel,
        compiler_params=pltpu.CompilerParams(vmem_limit_bytes=VMEM_LIMIT),
        cost_estimate=pl.CostEstimate(flops=1, bytes_accessed=1, transcendentals=0),
        **kwargs,
    )


def filled(shape, moves):
    arrays, plan, rows = [], [], []
    block = tuple(size if index is None else 1 for size, index in zip(shape, moves[0][2]))
    for piece, lead, place in moves:
        at = next((i for i, a in enumerate(arrays) if a is piece), len(arrays))
        if at == len(arrays):
            arrays.append(piece)
        plan.append((at, lead))
        rows.append(jnp.stack([jnp.asarray(0 if n is None else n, jnp.int32) for n in place]))

    def kernel(index_ref, *refs):
        pieces, out = refs[:-1], refs[-1]
        for m, (at, lead) in enumerate(plan):

            @pl.when(pl.program_id(0) == m)
            def _():
                value = pieces[at][...] if lead is None else pieces[at][lead]
                out[...] = value.reshape(block)

    return call(
        kernel,
        grid_spec=pltpu.PrefetchScalarGridSpec(
            num_scalar_prefetch=1,
            grid=(len(plan),),
            in_specs=[
                pl.BlockSpec(a.shape, lambda i, t, n=a.ndim: (0,) * n) for a in arrays
            ],
            out_specs=pl.BlockSpec(
                block, lambda i, t: tuple(t[i, n] for n in range(len(shape)))
            ),
        ),
        out_shape=jax.ShapeDtypeStruct(shape, arrays[0].dtype),
        name="filled",
    )(jnp.stack(rows), *arrays)


def terms_kernel(at_ref, left_ref, right_ref, out_ref):
    value = dot(left_ref[...], right_ref[...]).astype(BF)
    out_ref[...] = value.reshape(out_ref.shape)


def row_terms(turned, right, at, nd, ns, nf):
    depth = turned.shape[1]
    rows = turned.shape[0] // (nd * ns)
    columns = right.shape[1]
    return call(
        terms_kernel,
        grid_spec=pltpu.PrefetchScalarGridSpec(
            num_scalar_prefetch=1,
            grid=(ns,),
            in_specs=[
                pl.BlockSpec((rows, depth), lambda i, t: (t[0] * ns + i, 0)),
                pl.BlockSpec((depth, columns), lambda i, t: (0, 0)),
            ],
            out_specs=pl.BlockSpec((nf, 1, rows // nf, columns), lambda i, t: (0, i, 0, 0)),
        ),
        out_shape=jax.ShapeDtypeStruct((nf, ns, rows // nf, columns), BF),
        name="row_terms",
    )(at.astype(jnp.int32)[None], turned, right)


def input_grad_kernel(dz_ref, ds_ref, dr_ref, wz_ref, wx_ref, out_ref):
    width = ds_ref.shape[1]
    columns = ((1,), (1,))
    total = dot(dz_ref[...], wz_ref[...], columns)
    total = total + dot(ds_ref[...], wx_ref[:, :width], columns)
    total = total + dot(dr_ref[...], wx_ref[:, width:], columns)
    out_ref[0] = total.astype(BF)


def input_grad(dz, ds, dr, wz, wx, blocks, tok):
    def rows(a):
        return pl.BlockSpec((tok, a.shape[1]), lambda i: (i, 0))

    def whole(a):
        return pl.BlockSpec(a.shape, lambda i: (0, 0))

    return call(
        input_grad_kernel,
        grid=(blocks,),
        in_specs=[rows(dz), rows(ds), rows(dr), whole(wz), whole(wx)],
        out_specs=pl.BlockSpec((1, tok, wz.shape[0]), lambda i: (i, 0, 0)),
        out_shape=jax.ShapeDtypeStruct((blocks, tok, wz.shape[0]), BF),
        name="input_grad",
    )(dz, ds, dr, wz, wx)


def tri(rows_first):
    a = lax.broadcasted_iota(jnp.int32, (SPAN, SPAN), 0)
    b = lax.broadcasted_iota(jnp.int32, (SPAN, SPAN), 1)
    return (a >= b) if rows_first else (a <= b)


def pair_of(lo, cols, p):
    return jnp.where(lo, cols[:, 2 * p : 2 * p + 1], cols[:, 2 * p + 1 : 2 * p + 2])


def decays(segc, segr, segp, dt, dtr, rate, rater):
    lower = tri(True).astype(F32)
    upper = tri(False).astype(F32)
    cum = dot(lower, dt * rate, precision=HIGH)
    cumr = dot(dtr * rater, upper, precision=HIGH)
    last = cum[SPAN - 1 : SPAN, :]
    keep = jnp.where(segc == segp, jnp.exp(cum), 0.0)
    to_end = jnp.where(segc == segr[:, SPAN - 1 : SPAN], jnp.exp(last - cum), 0.0)
    return cum, cumr, keep, to_end


def spread_columns(ref, first, count):
    return [jnp.broadcast_to(ref[:, first + k : first + k + 1], (SPAN, LANES)) for k in range(count)]


def taps(ext, masks, at):
    terms = [ext[pl.ds(HALO - CONV + 1 + k, SPAN), at] for k in range(CONV)]
    return [t * m for t, m in zip(terms, masks)] + terms[CONV - 1 :]


def convolved(terms, weight_ref, at):
    total = weight_ref[CONV : CONV + 1, at] + terms[0] * weight_ref[0:1, at]
    for k in range(1, CONV):
        total = total + terms[k] * weight_ref[k : k + 1, at]
    return total


def forward_kernel(
    heads,
    segp_ref,
    segc_ref,
    segr_ref,
    mask_ref,
    in_ref,
    halo_ref,
    weight_ref,
    b_ref,
    c_ref,
    dt_ref,
    dtr_ref,
    rate_ref,
    rater_ref,
    skip_ref,
    y_ref,
    prior_ref,
    carry,
    to_end_u,
    ext,
):
    block = pl.program_id(0)
    width = heads * HEADDIM

    @pl.when(block == 0)
    def _():
        carry[...] = jnp.zeros_like(carry)

    prior_ref[0] = carry[...]
    ext[0:HALO] = halo_ref[0].astype(F32)
    ext[HALO:] = in_ref[...].astype(F32)
    segc, segr = segc_ref[...], segr_ref[...]
    dt = dt_ref[...]
    cum, cumr, keep, to_end = decays(
        segc, segr, segp_ref[block], dt, dtr_ref[...], rate_ref[...], rater_ref[...]
    )
    bm, cm = b_ref[...], c_ref[...]
    mixing = dot(cm, bm, ((1,), (1,)))
    mixing = jnp.where(tri(True) & (segc == segr), mixing, 0.0)
    masks = spread_columns(mask_ref, 0, CONV - 1)
    lo = lax.broadcasted_iota(jnp.int32, (SPAN, LANES), 1) < HEADDIM
    for p in range(heads // 2):
        at = slice(p * LANES, (p + 1) * LANES)
        pre = convolved(taps(ext, masks, at), weight_ref, at)
        x2 = pre * jax.nn.sigmoid(pre)
        u2 = x2 * pair_of(lo, dt, p)
        sides = (jnp.where(lo, u2, 0.0).astype(BF), jnp.where(lo, 0.0, u2).astype(BF))
        total = dot(cm, carry[:, at].astype(BF)) * pair_of(lo, keep, p) + skip_ref[:, at] * x2
        for k in range(2):
            h = 2 * p + k
            decay = jnp.exp(jnp.minimum(cum[:, h : h + 1] - cumr[h : h + 1, :], 0.0))
            total = total + dot((decay * mixing).astype(BF), sides[k])
        y_ref[:, at] = total
        to_end_u[:, at] = (u2 * pair_of(lo, to_end, p)).astype(BF)
    fresh = dot(bm, to_end_u[...], ((0,), (0,)))
    lo_row = lax.broadcasted_iota(jnp.int32, (1, LANES), 1) < HEADDIM
    for p in range(heads // 2):
        at = slice(p * LANES, (p + 1) * LANES)
        factor = pair_of(lo_row, keep[SPAN - 1 : SPAN, :], p)
        carry[:, at] = factor * carry[:, at] + fresh[:, at]


def split_dot(value, ones):
    high = value.astype(BF)
    low = (value - high.astype(F32)).astype(BF)
    return dot(high, ones) + dot(low, ones)


def backward_kernel(
    heads,
    segp_ref,
    segc_ref,
    segr_ref,
    mask_ref,
    in_ref,
    halo_ref,
    weight_ref,
    b_ref,
    c_ref,
    dt_ref,
    dtr_ref,
    rate_ref,
    rater_ref,
    skip_ref,
    y_ref,
    prior_ref,
    dy_ref,
    din_ref,
    dbc_ref,
    ddt_ref,
    drate_ref,
    dsum_ref,
    dcarry,
    after_state,
    keep_dy,
    to_end_u,
    slopes,
    along,
    ext,
    dext,
):
    step = pl.program_id(0)
    block = pl.num_programs(0) - 1 - step

    @pl.when(step == 0)
    def _():
        dcarry[...] = jnp.zeros_like(dcarry)
        after_state[...] = jnp.zeros_like(after_state)
        drate_ref[...] = jnp.zeros_like(drate_ref)
        dsum_ref[...] = jnp.zeros_like(dsum_ref)
        dext[SPAN:] = jnp.zeros((HALO, dext.shape[1]), F32)

    ext[0:HALO] = halo_ref[0].astype(F32)
    ext[HALO:] = in_ref[...].astype(F32)
    segc, segr = segc_ref[...], segr_ref[...]
    dt = dt_ref[...]
    cum, cumr, keep, to_end = decays(
        segc, segr, segp_ref[block], dt, dtr_ref[...], rate_ref[...], rater_ref[...]
    )
    bm, cm = b_ref[...], c_ref[...]
    allowed = tri(False) & (segc == segr)
    mixing = jnp.where(allowed, dot(bm, cm, ((1,), (1,))), 0.0)
    masks = spread_columns(mask_ref, 0, CONV - 1)
    moved = spread_columns(mask_ref, CONV - 1, CONV - 1)
    lo = lax.broadcasted_iota(jnp.int32, (SPAN, LANES), 1) < HEADDIM
    dmixing = jnp.zeros((SPAN, SPAN), F32)
    for p in range(heads // 2):
        at = slice(p * LANES, (p + 1) * LANES)
        terms = taps(ext, masks, at)
        pre = convolved(terms, weight_ref, at)
        sig = jax.nn.sigmoid(pre)
        x2 = pre * sig
        dt2 = pair_of(lo, dt, p)
        u2 = x2 * dt2
        dyb = dy_ref[:, at]
        dy2 = dyb.astype(F32)
        skip = skip_ref[:, at]
        te2 = pair_of(lo, to_end, p)
        u_sides = (jnp.where(lo, u2, 0.0).astype(BF), jnp.where(lo, 0.0, u2).astype(BF))
        dy_sides = (jnp.where(lo, dy2, 0.0).astype(BF), jnp.where(lo, 0.0, dy2).astype(BF))
        du = te2 * dot(bm, dcarry[:, at].astype(BF))
        for k in range(2):
            h = 2 * p + k
            decay = jnp.exp(jnp.minimum(cumr[h : h + 1, :] - cum[:, h : h + 1], 0.0))
            du = du + dot((decay * mixing).astype(BF), dy_sides[k])
            dmixing = dmixing + decay * dot(u_sides[k], dyb, ((1,), (1,)))
        keep_dy[:, at] = (pair_of(lo, keep, p) * dy2).astype(BF)
        to_end_u[:, at] = (te2 * u2).astype(BF)
        slopes[:, at] = dy2 * (y_ref[:, at] - skip * x2) - u2.astype(BF).astype(F32) * du
        along[:, at] = x2 * du
        dpre = (dt2 * du + skip * dy2) * (sig * (1.0 + pre * (1.0 - sig)))
        dext[0:SPAN, at] = dpre
        for k in range(CONV):
            dsum_ref[k : k + 1, at] += jnp.sum(dpre * terms[k], axis=0, keepdims=True)
        dsum_ref[CONV : CONV + 1, at] += jnp.sum(dpre, axis=0, keepdims=True)
        dsum_ref[CONV + 1 : CONV + 2, at] += jnp.sum(dy2 * x2, axis=0, keepdims=True)
        din = dpre * weight_ref[CONV - 1 : CONV, at]
        for k in range(CONV - 1):
            later = dext[pl.ds(CONV - 1 - k, SPAN), at]
            din = din + later * moved[k] * weight_ref[k : k + 1, at]
        din_ref[:, at] = din.astype(BF)
    dext[SPAN:] = dext[0:HALO]
    dmixing = jnp.where(allowed, dmixing, 0.0).astype(BF)
    dstate = dcarry[...].astype(BF)
    prior = prior_ref[0]
    dbc_ref[:, :STATE] = dot(dmixing, cm) + dot(to_end_u[...], dstate, ((1,), (1,)))
    dbc_ref[:, STATE:] = dot(dmixing, bm, ((0,), (0,))) + dot(
        keep_dy[...], prior.astype(BF), ((1,), (1,))
    )
    width = heads * HEADDIM
    ones = (
        lax.broadcasted_iota(jnp.int32, (width, LANES), 0) // HEADDIM
        == lax.broadcasted_iota(jnp.int32, (width, LANES), 1)
    ).astype(BF)
    at_end = jnp.sum(dcarry[...] * after_state[...], axis=0, keepdims=True)
    at_end = split_dot(jnp.broadcast_to(at_end, (16, width)), ones)[:1]
    dcum = split_dot(slopes[...], ones)
    da = dot(tri(False).astype(F32), dcum, precision=HIGH) + at_end
    ddt_ref[...] = rate_ref[...] * da + split_dot(along[...], ones)
    drate_ref[...] += jnp.sum(dt * da, axis=0, keepdims=True)
    fresh = dot(cm, keep_dy[...], ((0,), (0,)))
    lo_row = lax.broadcasted_iota(jnp.int32, (1, LANES), 1) < HEADDIM
    for p in range(heads // 2):
        at = slice(p * LANES, (p + 1) * LANES)
        factor = pair_of(lo_row, keep[SPAN - 1 : SPAN, :], p)
        dcarry[:, at] = factor * dcarry[:, at] + fresh[:, at]
    after_state[...] = prior


def scan_specs(heads, at):
    width = heads * HEADDIM

    def rows(n):
        return pl.BlockSpec((SPAN, n), lambda i: (at(i), 0))

    def whole(*shape):
        return pl.BlockSpec(shape, lambda i: (0,) * len(shape))

    ins = [
        pl.BlockSpec(memory_space=pltpu.SMEM),
        rows(1),
        pl.BlockSpec((1, SPAN), lambda i: (0, at(i))),
        rows(LANES),
        rows(width),
        pl.BlockSpec((1, HALO, width), lambda i: (at(i), 0, 0)),
        whole(8, width),
        rows(STATE),
        rows(STATE),
        rows(LANES),
        pl.BlockSpec((heads, SPAN), lambda i: (0, at(i))),
        whole(1, LANES),
        whole(heads, 1),
        whole(1, width),
    ]
    prior = pl.BlockSpec((1, STATE, width), lambda i: (at(i), 0, 0))
    return rows, whole, ins, prior


def scan_forward(heads, blocks, operands):
    rows, whole, ins, prior = scan_specs(heads, lambda i: i)
    width = heads * HEADDIM
    return call(
        functools.partial(forward_kernel, heads),
        grid=(blocks,),
        in_specs=ins,
        out_specs=[rows(width), prior],
        out_shape=[
            jax.ShapeDtypeStruct((blocks * SPAN, width), F32),
            jax.ShapeDtypeStruct((blocks, STATE, width), F32),
        ],
        scratch_shapes=[
            pltpu.VMEM((STATE, width), F32),
            pltpu.VMEM((SPAN, width), BF),
            pltpu.VMEM((HALO + SPAN, width), F32),
        ],
        name="scan_forward",
    )(*operands)


def scan_backward(heads, blocks, operands, y, priors, dy):
    rows, whole, ins, prior = scan_specs(heads, lambda i: blocks - 1 - i)
    width = heads * HEADDIM
    return call(
        functools.partial(backward_kernel, heads),
        grid=(blocks,),
        in_specs=ins + [rows(width), prior, rows(width)],
        out_specs=[rows(width), rows(2 * STATE), rows(LANES), whole(1, LANES), whole(8, width)],
        out_shape=[
            jax.ShapeDtypeStruct((blocks * SPAN, width), BF),
            jax.ShapeDtypeStruct((blocks * SPAN, 2 * STATE), F32),
            jax.ShapeDtypeStruct((blocks * SPAN, LANES), F32),
            jax.ShapeDtypeStruct((1, LANES), F32),
            jax.ShapeDtypeStruct((8, width), F32),
        ],
        scratch_shapes=[
            pltpu.VMEM((STATE, width), F32),
            pltpu.VMEM((STATE, width), F32),
            pltpu.VMEM((SPAN, width), BF),
            pltpu.VMEM((SPAN, width), BF),
            pltpu.VMEM((SPAN, width), F32),
            pltpu.VMEM((SPAN, width), F32),
            pltpu.VMEM((HALO + SPAN, width), F32),
            pltpu.VMEM((SPAN + HALO, width), F32),
        ],
        name="scan_backward",
    )(*operands, y, priors, dy)


def level_pieces(groups):
    return [(g, i) for g, count in enumerate(groups) for i in range(count)]


def upper_kernel(plan, lanes, tok, ns, here_ref, coef_ref, q_ref, *refs):
    pieces, (upper_ref, grad_ref, q_turned) = refs[:-3], refs[-3:]

    @pl.when(pl.program_id(0) == 0)
    def _():
        q_turned[...] = q_ref[...].T

    for j, (a, b) in enumerate(lanes):
        for k in range(ns):
            at = here_ref[0] ^ k
            rows = pl.ds(pl.multiple_of(at * tok, tok), tok)
            total = None
            for w, g, i in plan[j]:
                n = j * LEVELS + w
                term = coef_ref[rows, n : n + 1] * pieces[g * ns + k][i].astype(F32)
                total = term if total is None else total + term
            total = total.astype(BF)
            upper_ref[j, rows, :] = total
        grad_ref[a:b, :] = dot(q_turned[a:b, :], upper_ref[j]).astype(BF)


def products_kernel(plan, lanes, tok, ns, here_ref, count_ref, q_ref, w_ref, *refs):
    pieces, (prod_ref, inner_ref, sums) = refs[:-3], refs[-3:]
    step = pl.program_id(0)

    @pl.when(step == 0)
    def _():
        sums[...] = jnp.zeros_like(sums)

    for k in range(ns):
        at = here_ref[0] ^ k
        rows = pl.ds(pl.multiple_of(at * tok, tok), tok)
        for j, (a, b) in enumerate(lanes):
            value = dot(q_ref[rows, a:b], w_ref[a:b, :])
            prod_ref[at, j] = value.astype(BF)
            for w, g, i in plan[j]:
                part = value * (pieces[g * ns + k][i].astype(F32) * count_ref[j, w])
                folded = part[:, :LANES]
                for c in range(LANES, part.shape[1], LANES):
                    folded = folded + part[:, c : c + LANES]
                sums[w, rows, :] += folded

    @pl.when(step == pl.num_programs(0) - 1)
    def _():
        lane = lax.broadcasted_iota(jnp.int32, inner_ref.shape, 1)
        total = jnp.zeros(inner_ref.shape, F32)
        for w in range(LEVELS):
            total = jnp.where(lane == w, jnp.sum(sums[w], axis=1, keepdims=True), total)
        inner_ref[...] = total


def gate_kernel(lanes, upper_ref, w_ref, y_ref, z_ref, gain_ref, coef_ref, dy_ref, dz_ref, grad_ref):
    @pl.when(pl.program_id(0) == 0)
    def _():
        grad_ref[...] = jnp.zeros_like(grad_ref)

    for j, (a, b) in enumerate(lanes):
        upper = upper_ref[j]
        coef = coef_ref[:, j : j + 1]
        wide = TILE if (b - a) % TILE == 0 else LANES
        for c in range(a, b, wide):
            at = slice(c, c + wide)
            grad_t = dot(upper, w_ref[at, :], ((1,), (1,)))
            z = z_ref[:, at].astype(F32)
            sig = jax.nn.sigmoid(z)
            act = z * sig
            y = y_ref[:, at]
            q = y * act
            dq = gain_ref[:, at] * grad_t - q * coef
            dy_ref[:, at] = (dq * act).astype(BF)
            dz_ref[:, at] = (dq * y * (sig * (1.0 + z * (1.0 - sig)))).astype(BF)
            grad_ref[0:1, at] += jnp.sum(q * grad_t, axis=0, keepdims=True)


def mixed_kernel(plan, ns, count_ref, ratio_ref, x_ref, *refs):
    shares, out_ref = refs[:-1], refs[-1]
    x = x_ref[...].astype(F32)
    for w in range(LEVELS):
        total = None
        for k in range(ns):
            for j in plan[w]:
                term = shares[k][j].astype(F32) * count_ref[k, j * LEVELS + w]
                total = term if total is None else total + term
        out_ref[w] = (x + ratio_ref[:, w : w + 1] * total).astype(BF)


def dp_terms(others):
    return [swapped(other, "dp", k + 1) for k, other in enumerate(others)]


def fsdp_half(own, got):
    nf = lax.axis_size("fsdp")
    f = lax.axis_index("fsdp")

    def part(offset):
        total = picked(own, f ^ offset).astype(F32)
        for other in got:
            total = total + picked(other, f ^ offset).astype(F32)
        return total.astype(BF)

    kept = jnp.stack([part(e) for e in range(0, nf, 2)])
    sent = jnp.stack([part(e ^ 1) for e in range(0, nf, 2)])
    return kept, sent


def fsdp_rest(kept, got):
    k = 2
    while k < lax.axis_size("fsdp"):
        total = (kept.astype(F32) + got.astype(F32)).astype(BF)
        kept, sent = total[::2], total[1::2]
        got = swapped(sent, "fsdp", k)
        k *= 2
    return kept[0], got[0]


def shards(
    tokens,
    lengths,
    norm_gain,
    w_in,
    w_dt,
    conv_w,
    conv_b,
    dt_bias,
    a_log,
    skip,
    gate_gain,
    w_out,
    cotangent,
):
    nd, ns, nf = lax.axis_size("dp"), lax.axis_size("seq"), lax.axis_size("fsdp")
    d, s, f = lax.axis_index("dp"), lax.axis_index("seq"), lax.axis_index("fsdp")
    tok = tokens.shape[1]
    length = ns * tok
    blocks = length // SPAN
    heads = HEADS // ns
    run = heads // nd
    width = heads * HEADDIM
    own_bc = 2 * STATE // ns
    used = width + own_bc
    cols = -(-(used + heads) // LANES) * LANES
    rows_in = w_in.shape[0]
    reach = CONV - 1

    levels = np.array(
        [[level_of(dd * (HEADS // nd) + ss * run + i) for dd in range(nd) for i in range(run)] for ss in range(ns)]
    )
    cuts = [0] + [h for h in range(1, heads) if (levels[:, h] != levels[:, h - 1]).any()] + [heads]
    ranges = [(a, b) for a, b in zip(cuts, cuts[1:])]
    range_level = np.array([[levels[ss, a] for a, _ in ranges] for ss in range(ns)])
    counts = (range_level[:, :, None] <= np.arange(LEVELS)[None, None, :]).astype(np.float32)
    counted = picked(jnp.asarray(counts), s)
    lowest = [int(range_level[ss].min()) for ss in range(ns)]

    def by_head(vector):
        lead = vector.shape[:-1]
        per = vector.shape[-1] // HEADS
        cut = vector.reshape(lead + (nd, ns, run * per))
        mine = lax.dynamic_index_in_dim(cut, s, len(lead) + 1, keepdims=False)
        return mine.reshape(lead + (heads * per,))

    def for_groups(matrix):
        per = matrix.shape[1] // HEADS
        cut = matrix.reshape(matrix.shape[0], nd, ns, run * per)
        return jnp.transpose(cut, (2, 0, 1, 3)).reshape(ns, matrix.shape[0], heads * per)

    def from_groups(stack):
        per = stack.shape[2] // heads
        cut = stack.reshape(ns, stack.shape[1], nd, run * per)
        return jnp.transpose(cut, (1, 2, 0, 3)).reshape(stack.shape[1], HEADS * per)

    pad_cols = cols - used - heads
    stack = jnp.concatenate(
        [
            for_groups(w_in[:, INNER : 2 * INNER]),
            w_in[:, 2 * INNER :].reshape(rows_in, ns, own_bc).transpose(1, 0, 2),
            for_groups(w_dt),
            jnp.zeros((ns, rows_in, pad_cols), BF),
            for_groups(w_in[:, :INNER]),
        ],
        axis=2,
    )
    arrived = [picked(stack, s)] + [swapped(picked(stack, s ^ k), "seq", k) for k in range(1, ns)]
    mine = filled((ns, rows_in, stack.shape[2]), [(p, None, (s ^ k, None, None)) for k, p in enumerate(arrived)])
    mine_z = mine[:, :, cols:]

    own_x = tokens[0].astype(F32)
    scale = lax.rsqrt(jnp.mean(own_x * own_x, axis=-1, keepdims=True) + EPS)
    xn_own = (own_x * scale * norm_gain).astype(BF)
    xn_across = swapped(xn_own, "seq", 2)
    xn_pieces = [xn_own, swapped(xn_own, "seq", 1), xn_across, swapped(xn_across, "seq", 1)]
    xn = filled((ns, tok, D), [(p, None, (s ^ k, None, None)) for k, p in enumerate(xn_pieces)])
    xn = xn.reshape(length, D)

    half = width // 2

    def over_fsdp(chunk):
        return lax.all_gather(chunk, "fsdp", axis=0, tiled=False)

    def over_dp(held):
        pieces = [held] + [swapped(held, "dp", j) for j in range(1, nd)]
        moves = [
            (piece, i, (d ^ j, None, i, None, None)) for j, piece in enumerate(pieces) for i in range(nf)
        ]
        return pieces, moves

    held_a = over_fsdp(mine[:, :, :half])
    held_b = over_fsdp(after(mine[:, :, half:cols], held_a))
    pieces_a, moves_a = over_dp(held_a)
    pieces_b, moves_b = over_dp(after(held_b, pieces_a[0]))
    full_a = filled((nd, ns, nf, rows_in, half), moves_a).reshape(D, half)
    full_b = filled((nd, ns, nf, rows_in, cols - half), moves_b).reshape(D, cols - half)
    held_z = over_fsdp(after(mine_z, held_b))
    full_out = lax.all_gather(after(w_out, held_z), ("dp", "fsdp"), axis=0, tiled=True)
    pieces_z, moves_z = over_dp(held_z)
    full_z = filled((nd, ns, nf, rows_in, width), moves_z).reshape(D, width)

    def wants(at, level):
        return lowest[at] <= level

    def chips_of(level):
        return [any(wants(p, level) for p in (at, at ^ 1)) for at in range(ns)]

    groups = []
    for level in range(LEVELS):
        if groups and chips_of(level) == chips_of(level - 1):
            groups[-1][1] = level + 1
        else:
            groups.append([level, level + 1])

    def cotangent_pieces(group, *others):
        chips = chips_of(group[0])
        block = after(cotangent[group[0] : group[1], 0], *others)
        across = swapped(block, "seq", 2, lambda i, j: chips[j])
        beside = swapped(block, "seq", 1, lambda i, j: chips[j])
        far = swapped(across, "seq", 1, lambda i, j: chips[j])
        return [block, beside, across, far]

    cots = [None] * len(groups)
    cots[-1] = cotangent_pieces(groups[-1], xn_across)

    positions = jnp.arange(length, dtype=jnp.int32)
    ends = jnp.cumsum(lengths[0])[:-1]
    seg = jnp.sum((positions[:, None] >= ends[None, :]).astype(jnp.int32), axis=1)
    seg_before = jnp.concatenate([jnp.full((1,), -1, jnp.int32), seg[SPAN - 1 : length - 1 : SPAN]])
    seg_pad = jnp.concatenate([jnp.full((reach,), -1, jnp.int32), seg])
    masks = [(seg_pad[k : k + length] == seg) for k in range(reach)]
    mask_cols = [m.astype(F32) for m in masks]
    mask_cols += [jnp.pad(m, (0, reach - k))[reach - k :] for k, m in enumerate(mask_cols)]
    mask_cols = jnp.pad(jnp.stack(mask_cols, axis=1), ((0, 0), (0, LANES - 2 * reach)))

    weight_s = jnp.concatenate(
        [by_head(conv_w[:, :INNER]), by_head(conv_b[None, :INNER]), jnp.zeros((3, width), F32)]
    )
    weight_r = jnp.pad(
        lax.dynamic_slice_in_dim(conv_w, INNER + s * own_bc, own_bc, 1), ((0, 0), (0, cols - used))
    )
    bias_r = jnp.pad(
        lax.dynamic_slice_in_dim(conv_b, INNER + s * own_bc, own_bc, 0), (0, cols - used)
    )
    bias = by_head(dt_bias)
    rate = -jnp.exp(by_head(a_log))
    skip_own = by_head(skip)
    gain = by_head(gate_gain)

    xn_turned = xn.T
    proj_a = dot(xn, full_a).astype(BF)
    proj_b = dot(xn, after(full_b, proj_a)).astype(BF)
    proj = jnp.concatenate([proj_a, proj_b], axis=1)

    proj_r = proj_b[:, width - half :]
    mixer = jnp.concatenate([jnp.zeros((reach, cols - width), BF), proj_r], axis=0)

    def taken(k):
        rows = mixer[k : k + length].astype(F32)
        return jnp.where(masks[k][:, None], rows, 0.0) if k < reach else rows

    pre_r = bias_r
    for k in range(CONV):
        pre_r = pre_r + taken(k) * weight_r[k]
    bc_own = jax.nn.silu(pre_r).astype(BF)[:, :own_bc]
    bc = [bc_own] + [swapped(bc_own, "seq", k) for k in range(1, ns)]
    for g in range(len(groups) - 1):
        cots[g] = cotangent_pieces(groups[g], *bc)
    bc = reordered_by_xor(bc, s)
    b_in = jnp.concatenate(bc[: ns // 2], axis=1)
    c_out = jnp.concatenate(bc[ns // 2 :], axis=1)

    def padded(rows):
        return jnp.pad(rows, ((0, 0), (0, LANES - rows.shape[1])))

    pre_dt = proj_r[:, own_bc : own_bc + heads].astype(F32) + bias
    steps = jax.nn.softplus(pre_dt)
    tails = proj.reshape(blocks, SPAN, cols)[: blocks - 1, SPAN - HALO :, :width]
    operands = (
        seg_before,
        seg[:, None],
        seg[None, :],
        mask_cols,
        proj,
        jnp.concatenate([jnp.zeros((1, HALO, width), BF), tails]),
        weight_s,
        b_in,
        c_out,
        padded(steps),
        steps.T,
        padded(rate[None, :]),
        rate[:, None],
        jnp.repeat(skip_own, HEADDIM)[None, :],
    )
    y, priors = scan_forward(heads, blocks, operands)
    proj_z = dot(xn, full_z).astype(BF)
    q = y * jax.nn.silu(proj_z.astype(F32))
    q_gain = (q * gain).astype(BF)
    lanes = [(a * HEADDIM, b * HEADDIM) for a, b in ranges]
    squares = jnp.stack([jnp.sum(q[:, a:b] * q[:, a:b], axis=1) for a, b in lanes])
    widths = np.array([[(HEADS >> 3 - w) * HEADDIM] for w in range(LEVELS)], np.float32)
    per_level = jnp.sum(counted[:, :, None] * squares[:, None, :], axis=0)
    ratio = lax.rsqrt(butterfly(per_level, "seq") / widths + EPS)

    order = level_pieces([b - a for a, b in groups])
    plan = [[(w,) + order[w] for w in range(LEVELS) if range_level[:, j].min() <= w] for j in range(len(lanes))]
    here = s.astype(jnp.int32)[None]
    tile = pl.BlockSpec((length, TILE), lambda i: (0, i))
    cot_specs = [
        pl.BlockSpec((b - a, tok, TILE), lambda i: (0, 0, i)) for a, b in groups for _ in range(ns)
    ]
    cot_pieces = [piece for group in cots for piece in group]
    smem = pl.BlockSpec(memory_space=pltpu.SMEM)
    coef = jnp.concatenate([counted[j][:, None] * ratio for j in range(len(lanes))])
    upper, grad_out = call(
        functools.partial(upper_kernel, plan, lanes, tok, ns),
        grid=(D // TILE,),
        in_specs=[
            smem,
            pl.BlockSpec((length, LANES), lambda i: (0, 0)),
            pl.BlockSpec((length, width), lambda i: (0, 0)),
        ]
        + cot_specs,
        out_specs=[
            pl.BlockSpec((len(lanes), length, TILE), lambda i: (0, 0, i)),
            pl.BlockSpec((width, TILE), lambda i: (0, i)),
        ],
        out_shape=[
            jax.ShapeDtypeStruct((len(lanes), length, D), BF),
            jax.ShapeDtypeStruct((width, D), BF),
        ],
        scratch_shapes=[pltpu.VMEM((width, length), BF)],
        name="upper",
    )(here, padded(coef.T), q_gain, *cot_pieces)
    grad_out = grad_out.reshape(nd, nf, width // nd // nf, D)
    out_other = [picked(grad_out, d ^ k) for k in range(1, nd)]
    out_got = dp_terms(out_other)
    out_own = picked(grad_out, d)

    full_out, out_other = together(full_out, out_other)
    products, inner = call(
        functools.partial(products_kernel, plan, lanes, tok, ns),
        grid=(D // TILE,),
        in_specs=[
            smem,
            smem,
            pl.BlockSpec((length, width), lambda i: (0, 0)),
            pl.BlockSpec((width, TILE), lambda i: (0, i)),
        ]
        + cot_specs,
        out_specs=[
            pl.BlockSpec((ns, len(lanes), tok, TILE), lambda i: (0, 0, 0, i)),
            pl.BlockSpec((length, LANES), lambda i: (0, 0)),
        ],
        out_shape=[
            jax.ShapeDtypeStruct((ns, len(lanes), tok, D), BF),
            jax.ShapeDtypeStruct((length, LANES), F32),
        ],
        scratch_shapes=[pltpu.VMEM((LEVELS, length, LANES), F32)],
        name="products",
    )(here, counted, q_gain, full_out, *cot_pieces)
    means = butterfly(inner[:, :LEVELS].T, "seq") / widths
    shares = [picked(products, s ^ k) for k in range(ns)]
    shares[1:3] = [swapped(after(shares[k], means), "seq", k) for k in (1, 2)]

    coef = jnp.sum(counted[:, :, None] * (ratio**3 * means)[None], axis=1)
    rows = pl.BlockSpec((SPAN, width), lambda i: (i, 0))
    dy, dz, grad_gate = call(
        functools.partial(gate_kernel, lanes),
        grid=(blocks,),
        in_specs=[
            pl.BlockSpec((len(lanes), SPAN, D), lambda i: (0, i, 0)),
            pl.BlockSpec((width, D), lambda i: (0, 0)),
            rows,
            rows,
            pl.BlockSpec((1, width), lambda i: (0, 0)),
            pl.BlockSpec((SPAN, LANES), lambda i: (i, 0)),
        ],
        out_specs=[rows, rows, pl.BlockSpec((8, width), lambda i: (0, 0))],
        out_shape=[
            jax.ShapeDtypeStruct((length, width), BF),
            jax.ShapeDtypeStruct((length, width), BF),
            jax.ShapeDtypeStruct((8, width), F32),
        ],
        name="gate_backward",
    )(upper, full_out, y, proj_z, gain[None], padded(coef.T))
    grad_gate = grad_gate[0]

    def in_terms(dproj, at):
        out = row_terms(xn_turned, dproj, at, nd, ns, nf)
        return out.reshape(nf, ns * rows_in, dproj.shape[1])

    z_other = [in_terms(dz, d ^ k) for k in range(1, nd)]
    z_got = dp_terms(z_other)
    out_kept, out_sent = fsdp_half(out_own, out_got)
    dy = after(dy, *z_other, out_sent)
    out_half = swapped(out_sent, "fsdp", 1)

    dproj_s, dbc, ddt, drate, dsum = scan_backward(heads, blocks, operands, y, priors, dy)
    dproj_s, dbc, out_half, shares[1] = together(dproj_s, dbc, out_half, shares[1])
    out_pair = fsdp_rest(out_kept, out_half)
    dbc = dbc.astype(BF)
    dbc_parts = reordered_by_xor([dbc[:, j * own_bc : (j + 1) * own_bc] for j in range(ns)], s)
    dbc_got = [swapped(dbc_parts[k], "seq", k) for k in range(1, ns)]
    cut = width // 2
    left_in = dproj_s[:, :cut]
    left_other = [in_terms(left_in, d ^ k) for k in range(1, nd)]
    left_got = dp_terms(left_other)
    dbc_own = after(dbc_parts[0].astype(F32), *left_other)
    for got in dbc_got:
        dbc_own = dbc_own + got.astype(F32)
    dpre = jnp.pad(dbc_own, ((0, 0), (0, cols - used))) * silu_slope(pre_r)
    grad_b_r = jnp.sum(dpre, axis=0)[:own_bc]
    grad_w_r = jnp.stack([jnp.sum(dpre * taken(k), axis=0) for k in range(CONV)])[:, :own_bc]
    dmixer = dpre * weight_r[reach]
    for k in range(reach):
        back = reach - k
        later = jnp.where(masks[k][:, None], dpre, 0.0)[back:]
        dmixer = dmixer + jnp.pad(later, ((0, back), (0, 0))) * weight_r[k]
    dpre_dt = ddt[:, :heads] * jax.nn.sigmoid(pre_dt)
    dproj_r = jnp.concatenate(
        [dmixer[:, :own_bc].astype(BF), dpre_dt.astype(BF), jnp.zeros((length, pad_cols), BF)], axis=1
    )
    dproj_r, shares[2] = together(dproj_r, shares[2])
    right_in = jnp.concatenate([dproj_s[:, cut:], dproj_r], axis=1)
    right_other = [in_terms(right_in, d ^ k) for k in range(1, nd)]
    right_got = dp_terms(right_other)
    z_kept, z_sent = fsdp_half(after(in_terms(dz, d), *left_other), z_got)
    z_pair = fsdp_rest(z_kept, swapped(z_sent, "fsdp", 1))
    flat = flattened(
        [
            jnp.concatenate([dsum[:CONV], grad_w_r], axis=1).reshape(-1),
            dsum[CONV],
            grad_b_r,
            grad_gate,
            jnp.sum(dpre_dt, axis=0),
            drate[0, :heads] * rate,
            jnp.sum(dsum[CONV + 1].reshape(heads, HEADDIM), axis=1),
        ]
    )
    full_x = jnp.concatenate([full_a, full_b], axis=1)
    dxn = input_grad(dz, dproj_s, after(dproj_r, *right_other), full_z, full_x, ns, tok)
    near = picked(dxn, s).astype(F32) + swapped(picked(dxn, s ^ 1), "seq", 1).astype(F32)
    far = picked(dxn, s ^ 2).astype(F32) + swapped(picked(dxn, s ^ 3), "seq", 1).astype(F32)
    far = far.astype(BF)
    shares[3] = swapped(after(shares[3], far), "seq", 3)
    dxn_own = near + swapped(far, "seq", 2).astype(F32)
    grad_norm = jnp.sum(dxn_own * own_x * scale, axis=0)
    scaled = norm_gain * dxn_own
    dx = scale * scaled - own_x * scale**3 * jnp.mean(own_x * scaled, axis=-1, keepdims=True)
    dx = dx + jnp.sum(cotangent[:, 0].astype(F32), axis=0)

    left_kept, left_sent = fsdp_half(in_terms(after(left_in, far), d), left_got)
    left_pair = fsdp_rest(left_kept, swapped(left_sent, "fsdp", 1))
    right_kept, right_sent = fsdp_half(in_terms(after(right_in, dxn_own), d), right_got)
    right_pair = fsdp_rest(right_kept, swapped(right_sent, "fsdp", 1))

    def to_owner(pair, *others):
        total = after((pair[0].astype(F32) + pair[1].astype(F32)).astype(BF), *others)
        return seq_exchange(total.reshape(ns, rows_in, total.shape[1]), s)

    sum_out = out_pair[0].astype(F32) + out_pair[1].astype(F32)
    got_z = to_owner(z_pair)
    got_x = jnp.concatenate([to_owner(left_pair, right_sent), to_owner(right_pair)], axis=2)

    ratio_own = padded(lax.dynamic_slice_in_dim(ratio, s * tok, tok, 1).T)
    theirs = jnp.stack([picked(jnp.asarray(counts), s ^ k).reshape(-1) for k in range(ns)])
    mixed = call(
        functools.partial(
            mixed_kernel,
            [[j for j in range(len(lanes)) if range_level[:, j].min() <= w] for w in range(LEVELS)],
            ns,
        ),
        grid=(D // TILE,),
        in_specs=[
            smem,
            pl.BlockSpec((tok, LANES), lambda i: (0, 0)),
            pl.BlockSpec((tok, TILE), lambda i: (0, i)),
        ]
        + [pl.BlockSpec((len(lanes), tok, TILE), lambda i: (0, 0, i))] * ns,
        out_specs=pl.BlockSpec((LEVELS, tok, TILE), lambda i: (0, 0, i)),
        out_shape=jax.ShapeDtypeStruct((LEVELS, tok, D), BF),
        name="mixed",
    )(theirs, ratio_own, tokens[0], *shares)[:, None]

    sum_in = jnp.concatenate(
        [
            from_groups(got_z),
            from_groups(got_x[:, :, :width]),
            jnp.transpose(got_x[:, :, width:used], (1, 0, 2)).reshape(rows_in, 2 * STATE),
        ],
        axis=1,
    ).astype(F32)
    sum_dt = from_groups(got_x[:, :, used : used + heads]).astype(F32)

    flat = jnp.concatenate([flat, grad_norm.reshape(-1, LANES)])
    flat = butterfly(butterfly(after(flat, right_sent), "dp"), "fsdp")
    sizes = [CONV * used, used, width, heads, heads, heads]
    filling = -sum(sizes) % 1024
    sizes += [filling, D]
    every = seq_gather(flat, s).reshape(ns, -1)
    starts = np.cumsum([0] + sizes)
    pieces = [every[:, a : a + n] for a, n in zip(starts, sizes)]

    def heads_back(rows):
        lead = rows.shape[1:-1]
        cut = rows.reshape((ns,) + lead + (nd, rows.shape[-1] // nd))
        order = tuple(range(1, 1 + len(lead))) + (1 + len(lead), 0, 2 + len(lead))
        return jnp.transpose(cut, order).reshape(lead + (-1,))

    conv_rows = pieces[0].reshape(ns, CONV, used)
    conv_all = jnp.concatenate(
        [
            heads_back(conv_rows[:, :, :width]),
            jnp.transpose(conv_rows[:, :, width:], (1, 0, 2)).reshape(CONV, 2 * STATE),
        ],
        axis=1,
    )
    bias_all = jnp.concatenate([heads_back(pieces[1][:, :width]), pieces[1][:, width:].reshape(-1)])
    return (
        mixed,
        dx.astype(BF)[None],
        jnp.sum(pieces[7], axis=0),
        sum_in,
        sum_dt,
        conv_all,
        bias_all,
        heads_back(pieces[3]),
        heads_back(pieces[4]),
        heads_back(pieces[5]),
        heads_back(pieces[2]),
        sum_out,
    )


def solution(mesh):
    rows = P(("dp", "seq", "fsdp"), None)
    held = P(("dp", "fsdp"), "seq", None)
    levels = P(None, ("dp", "fsdp"), "seq", None)
    placed = (held, P(("dp", "fsdp"), None), P(), rows, rows, P(), P(), P(), P(), P(), P(), rows, levels)
    return jax.shard_map(
        shards,
        mesh=mesh,
        in_specs=placed,
        out_specs=(levels, held, P(), rows, rows, P(), P(), P(), P(), P(), P(), rows),
        check_vma=False,
    )
```

```python
import functools

import jax
import jax.numpy as jnp
import numpy as np
from jax import lax
from jax.experimental import pallas as pl
from jax.experimental.pallas import tpu as pltpu
from jax.sharding import PartitionSpec as P

D = 2048
HEADS = 64
HEADDIM = 64
STATE = 128
CONV = 4
SPAN = 256
INNER = 4096
EPS = 1e-05
LEVELS = 4
BF = jnp.bfloat16
F32 = jnp.float32
HIGH = lax.Precision.HIGHEST
LANES = 128
HALO = 16
TILE = 256
VMEM_LIMIT = 48 * 1024 * 1024


def dot(a, b, dims=((1,), (0,)), precision=None):
    return lax.dot_general(a, b, (dims, ((), ())), preferred_element_type=F32, precision=precision)


def silu_slope(v):
    sig = jax.nn.sigmoid(v)
    return sig * (1.0 + v * (1.0 - sig))


def level_of(head):
    return 0 if head < 8 else 1 if head < 16 else 2 if head < 32 else 3


def swapped(value, axis, k, keep=None):
    pairs = [(i, i ^ k) for i in range(lax.axis_size(axis))]
    if keep is not None:
        pairs = [p for p in pairs if keep(*p)]
    return lax.ppermute(value, axis, pairs)


def after(value, *others):
    return lax.optimization_barrier((value,) + others)[0]


def together(*values):
    return lax.optimization_barrier(values)


def flattened(vectors):
    flat = jnp.concatenate(vectors)
    return jnp.pad(flat, (0, -flat.shape[0] % 1024)).reshape(-1, LANES)


def butterfly(value, axis):
    k = 1
    while k < lax.axis_size(axis):
        value = value + swapped(value, axis, k)
        k *= 2
    return value


def picked(array, index):
    return lax.dynamic_index_in_dim(array, index, 0, keepdims=False)


def placed_by_xor(pieces, here):
    out = jnp.zeros((len(pieces),) + pieces[0].shape, pieces[0].dtype)
    for k, piece in enumerate(pieces):
        out = lax.dynamic_update_index_in_dim(out, piece, here ^ k, 0)
    return out


def seq_gather(block, here):
    return placed_by_xor([block] + [swapped(block, "seq", k) for k in range(1, 4)], here)


def reordered_by_xor(pieces, here):
    k = 1
    while k < len(pieces):
        flip = (here & k) > 0
        pieces = [jnp.where(flip, pieces[j ^ k], piece) for j, piece in enumerate(pieces)]
        k *= 2
    return pieces


def seq_exchange(pieces, here):
    got = [picked(pieces, here)]
    for k in range(1, pieces.shape[0]):
        got.append(swapped(picked(pieces, here ^ k), "seq", k))
    return placed_by_xor(got, here)


def call(kernel, **kwargs):
    return pl.pallas_call(
        kernel,
        compiler_params=pltpu.CompilerParams(vmem_limit_bytes=VMEM_LIMIT),
        cost_estimate=pl.CostEstimate(flops=1, bytes_accessed=1, transcendentals=0),
        **kwargs,
    )


def filled(shape, moves):
    arrays, plan, rows = [], [], []
    block = tuple(size if index is None else 1 for size, index in zip(shape, moves[0][2]))
    for piece, lead, place in moves:
        at = next((i for i, a in enumerate(arrays) if a is piece), len(arrays))
        if at == len(arrays):
            arrays.append(piece)
        plan.append((at, lead))
        rows.append(jnp.stack([jnp.asarray(0 if n is None else n, jnp.int32) for n in place]))

    def kernel(index_ref, *refs):
        pieces, out = refs[:-1], refs[-1]
        for m, (at, lead) in enumerate(plan):

            @pl.when(pl.program_id(0) == m)
            def _():
                value = pieces[at][...] if lead is None else pieces[at][lead]
                out[...] = value.reshape(block)

    return call(
        kernel,
        grid_spec=pltpu.PrefetchScalarGridSpec(
            num_scalar_prefetch=1,
            grid=(len(plan),),
            in_specs=[
                pl.BlockSpec(a.shape, lambda i, t, n=a.ndim: (0,) * n) for a in arrays
            ],
            out_specs=pl.BlockSpec(
                block, lambda i, t: tuple(t[i, n] for n in range(len(shape)))
            ),
        ),
        out_shape=jax.ShapeDtypeStruct(shape, arrays[0].dtype),
        name="filled",
    )(jnp.stack(rows), *arrays)


def terms_kernel(at_ref, left_ref, right_ref, out_ref):
    value = dot(left_ref[...], right_ref[...]).astype(BF)
    out_ref[...] = value.reshape(out_ref.shape)


def row_terms(turned, right, at, nd, ns, nf):
    depth = turned.shape[1]
    rows = turned.shape[0] // (nd * ns)
    columns = right.shape[1]
    return call(
        terms_kernel,
        grid_spec=pltpu.PrefetchScalarGridSpec(
            num_scalar_prefetch=1,
            grid=(ns,),
            in_specs=[
                pl.BlockSpec((rows, depth), lambda i, t: (t[0] * ns + i, 0)),
                pl.BlockSpec((depth, columns), lambda i, t: (0, 0)),
            ],
            out_specs=pl.BlockSpec((nf, 1, rows // nf, columns), lambda i, t: (0, i, 0, 0)),
        ),
        out_shape=jax.ShapeDtypeStruct((nf, ns, rows // nf, columns), BF),
        name="row_terms",
    )(at.astype(jnp.int32)[None], turned, right)


def input_grad_kernel(dz_ref, ds_ref, dr_ref, wz_ref, wa_ref, wb_ref, out_ref):
    half = wa_ref.shape[1]
    rest = ds_ref.shape[1] - half
    columns = ((1,), (1,))
    total = dot(dz_ref[...], wz_ref[...], columns)
    total = total + dot(ds_ref[:, :half], wa_ref[...], columns)
    total = total + dot(ds_ref[:, half:], wb_ref[:, :rest], columns)
    total = total + dot(dr_ref[...], wb_ref[:, rest:], columns)
    out_ref[0] = total.astype(BF)


def input_grad(dz, ds, dr, wz, wa, wb, blocks, tok):
    def rows(a):
        return pl.BlockSpec((tok, a.shape[1]), lambda i: (i, 0))

    def whole(a):
        return pl.BlockSpec(a.shape, lambda i: (0, 0))

    return call(
        input_grad_kernel,
        grid=(blocks,),
        in_specs=[rows(dz), rows(ds), rows(dr), whole(wz), whole(wa), whole(wb)],
        out_specs=pl.BlockSpec((1, tok, wz.shape[0]), lambda i: (i, 0, 0)),
        out_shape=jax.ShapeDtypeStruct((blocks, tok, wz.shape[0]), BF),
        name="input_grad",
    )(dz, ds, dr, wz, wa, wb)


def tri(rows_first):
    a = lax.broadcasted_iota(jnp.int32, (SPAN, SPAN), 0)
    b = lax.broadcasted_iota(jnp.int32, (SPAN, SPAN), 1)
    return (a >= b) if rows_first else (a <= b)


def pair_of(lo, cols, p):
    return jnp.where(lo, cols[:, 2 * p : 2 * p + 1], cols[:, 2 * p + 1 : 2 * p + 2])


def decays(segc, segr, segp, dt, dtr, rate, rater):
    lower = tri(True).astype(F32)
    upper = tri(False).astype(F32)
    cum = dot(lower, dt * rate, precision=HIGH)
    cumr = dot(dtr * rater, upper, precision=HIGH)
    last = cum[SPAN - 1 : SPAN, :]
    keep = jnp.where(segc == segp, jnp.exp(cum), 0.0)
    to_end = jnp.where(segc == segr[:, SPAN - 1 : SPAN], jnp.exp(last - cum), 0.0)
    return cum, cumr, keep, to_end


def spread_columns(ref, first, count):
    return [jnp.broadcast_to(ref[:, first + k : first + k + 1], (SPAN, LANES)) for k in range(count)]


def taps(ext, masks, at):
    terms = [ext[pl.ds(HALO - CONV + 1 + k, SPAN), at] for k in range(CONV)]
    return [t * m for t, m in zip(terms, masks)] + terms[CONV - 1 :]


def convolved(terms, weight_ref, at):
    total = weight_ref[CONV : CONV + 1, at] + terms[0] * weight_ref[0:1, at]
    for k in range(1, CONV):
        total = total + terms[k] * weight_ref[k : k + 1, at]
    return total


def forward_kernel(
    heads,
    segp_ref,
    segc_ref,
    segr_ref,
    mask_ref,
    in_ref,
    halo_ref,
    weight_ref,
    b_ref,
    c_ref,
    dt_ref,
    dtr_ref,
    rate_ref,
    rater_ref,
    skip_ref,
    y_ref,
    prior_ref,
    carry,
    to_end_u,
    ext,
):
    block = pl.program_id(0)
    width = heads * HEADDIM

    @pl.when(block == 0)
    def _():
        carry[...] = jnp.zeros_like(carry)

    prior_ref[0] = carry[...]
    ext[0:HALO] = halo_ref[0].astype(F32)
    ext[HALO:] = in_ref[...].astype(F32)
    segc, segr = segc_ref[...], segr_ref[...]
    dt = dt_ref[...]
    cum, cumr, keep, to_end = decays(
        segc, segr, segp_ref[block], dt, dtr_ref[...], rate_ref[...], rater_ref[...]
    )
    bm, cm = b_ref[...], c_ref[...]
    mixing = dot(cm, bm, ((1,), (1,)))
    mixing = jnp.where(tri(True) & (segc == segr), mixing, 0.0)
    masks = spread_columns(mask_ref, 0, CONV - 1)
    lo = lax.broadcasted_iota(jnp.int32, (SPAN, LANES), 1) < HEADDIM
    for p in range(heads // 2):
        at = slice(p * LANES, (p + 1) * LANES)
        pre = convolved(taps(ext, masks, at), weight_ref, at)
        x2 = pre * jax.nn.sigmoid(pre)
        u2 = x2 * pair_of(lo, dt, p)
        sides = (jnp.where(lo, u2, 0.0).astype(BF), jnp.where(lo, 0.0, u2).astype(BF))
        total = dot(cm, carry[:, at].astype(BF)) * pair_of(lo, keep, p) + skip_ref[:, at] * x2
        for k in range(2):
            h = 2 * p + k
            decay = jnp.exp(jnp.minimum(cum[:, h : h + 1] - cumr[h : h + 1, :], 0.0))
            total = total + dot((decay * mixing).astype(BF), sides[k])
        y_ref[:, at] = total
        to_end_u[:, at] = (u2 * pair_of(lo, to_end, p)).astype(BF)
    fresh = dot(bm, to_end_u[...], ((0,), (0,)))
    lo_row = lax.broadcasted_iota(jnp.int32, (1, LANES), 1) < HEADDIM
    for p in range(heads // 2):
        at = slice(p * LANES, (p + 1) * LANES)
        factor = pair_of(lo_row, keep[SPAN - 1 : SPAN, :], p)
        carry[:, at] = factor * carry[:, at] + fresh[:, at]


def split_dot(value, ones):
    high = value.astype(BF)
    low = (value - high.astype(F32)).astype(BF)
    return dot(high, ones) + dot(low, ones)


def backward_kernel(
    heads,
    segp_ref,
    segc_ref,
    segr_ref,
    mask_ref,
    in_ref,
    halo_ref,
    weight_ref,
    b_ref,
    c_ref,
    dt_ref,
    dtr_ref,
    rate_ref,
    rater_ref,
    skip_ref,
    y_ref,
    prior_ref,
    dy_ref,
    din_ref,
    dbc_ref,
    ddt_ref,
    drate_ref,
    dsum_ref,
    dcarry,
    after_state,
    keep_dy,
    to_end_u,
    slopes,
    along,
    ext,
    dext,
):
    step = pl.program_id(0)
    block = pl.num_programs(0) - 1 - step

    @pl.when(step == 0)
    def _():
        dcarry[...] = jnp.zeros_like(dcarry)
        after_state[...] = jnp.zeros_like(after_state)
        drate_ref[...] = jnp.zeros_like(drate_ref)
        dsum_ref[...] = jnp.zeros_like(dsum_ref)
        dext[SPAN:] = jnp.zeros((HALO, dext.shape[1]), F32)

    ext[0:HALO] = halo_ref[0].astype(F32)
    ext[HALO:] = in_ref[...].astype(F32)
    segc, segr = segc_ref[...], segr_ref[...]
    dt = dt_ref[...]
    cum, cumr, keep, to_end = decays(
        segc, segr, segp_ref[block], dt, dtr_ref[...], rate_ref[...], rater_ref[...]
    )
    bm, cm = b_ref[...], c_ref[...]
    allowed = tri(False) & (segc == segr)
    mixing = jnp.where(allowed, dot(bm, cm, ((1,), (1,))), 0.0)
    masks = spread_columns(mask_ref, 0, CONV - 1)
    moved = spread_columns(mask_ref, CONV - 1, CONV - 1)
    lo = lax.broadcasted_iota(jnp.int32, (SPAN, LANES), 1) < HEADDIM
    dmixing = jnp.zeros((SPAN, SPAN), F32)
    for p in range(heads // 2):
        at = slice(p * LANES, (p + 1) * LANES)
        terms = taps(ext, masks, at)
        pre = convolved(terms, weight_ref, at)
        sig = jax.nn.sigmoid(pre)
        x2 = pre * sig
        dt2 = pair_of(lo, dt, p)
        u2 = x2 * dt2
        dyb = dy_ref[:, at]
        dy2 = dyb.astype(F32)
        skip = skip_ref[:, at]
        te2 = pair_of(lo, to_end, p)
        u_sides = (jnp.where(lo, u2, 0.0).astype(BF), jnp.where(lo, 0.0, u2).astype(BF))
        dy_sides = (jnp.where(lo, dy2, 0.0).astype(BF), jnp.where(lo, 0.0, dy2).astype(BF))
        du = te2 * dot(bm, dcarry[:, at].astype(BF))
        for k in range(2):
            h = 2 * p + k
            decay = jnp.exp(jnp.minimum(cumr[h : h + 1, :] - cum[:, h : h + 1], 0.0))
            du = du + dot((decay * mixing).astype(BF), dy_sides[k])
            dmixing = dmixing + decay * dot(u_sides[k], dyb, ((1,), (1,)))
        keep_dy[:, at] = (pair_of(lo, keep, p) * dy2).astype(BF)
        to_end_u[:, at] = (te2 * u2).astype(BF)
        slopes[:, at] = dy2 * (y_ref[:, at] - skip * x2) - u2.astype(BF).astype(F32) * du
        along[:, at] = x2 * du
        dpre = (dt2 * du + skip * dy2) * (sig * (1.0 + pre * (1.0 - sig)))
        dext[0:SPAN, at] = dpre
        for k in range(CONV):
            dsum_ref[k : k + 1, at] += jnp.sum(dpre * terms[k], axis=0, keepdims=True)
        dsum_ref[CONV : CONV + 1, at] += jnp.sum(dpre, axis=0, keepdims=True)
        dsum_ref[CONV + 1 : CONV + 2, at] += jnp.sum(dy2 * x2, axis=0, keepdims=True)
        din = dpre * weight_ref[CONV - 1 : CONV, at]
        for k in range(CONV - 1):
            later = dext[pl.ds(CONV - 1 - k, SPAN), at]
            din = din + later * moved[k] * weight_ref[k : k + 1, at]
        din_ref[:, at] = din.astype(BF)
    dext[SPAN:] = dext[0:HALO]
    dmixing = jnp.where(allowed, dmixing, 0.0).astype(BF)
    dstate = dcarry[...].astype(BF)
    prior = prior_ref[0]
    dbc_ref[:, :STATE] = dot(dmixing, cm) + dot(to_end_u[...], dstate, ((1,), (1,)))
    dbc_ref[:, STATE:] = dot(dmixing, bm, ((0,), (0,))) + dot(
        keep_dy[...], prior.astype(BF), ((1,), (1,))
    )
    width = heads * HEADDIM
    ones = (
        lax.broadcasted_iota(jnp.int32, (width, LANES), 0) // HEADDIM
        == lax.broadcasted_iota(jnp.int32, (width, LANES), 1)
    ).astype(BF)
    at_end = jnp.sum(dcarry[...] * after_state[...], axis=0, keepdims=True)
    at_end = split_dot(jnp.broadcast_to(at_end, (16, width)), ones)[:1]
    dcum = split_dot(slopes[...], ones)
    da = dot(tri(False).astype(F32), dcum, precision=HIGH) + at_end
    ddt_ref[...] = rate_ref[...] * da + split_dot(along[...], ones)
    drate_ref[...] += jnp.sum(dt * da, axis=0, keepdims=True)
    fresh = dot(cm, keep_dy[...], ((0,), (0,)))
    lo_row = lax.broadcasted_iota(jnp.int32, (1, LANES), 1) < HEADDIM
    for p in range(heads // 2):
        at = slice(p * LANES, (p + 1) * LANES)
        factor = pair_of(lo_row, keep[SPAN - 1 : SPAN, :], p)
        dcarry[:, at] = factor * dcarry[:, at] + fresh[:, at]
    after_state[...] = prior


def scan_specs(heads, at):
    width = heads * HEADDIM

    def rows(n):
        return pl.BlockSpec((SPAN, n), lambda i: (at(i), 0))

    def whole(*shape):
        return pl.BlockSpec(shape, lambda i: (0,) * len(shape))

    ins = [
        pl.BlockSpec(memory_space=pltpu.SMEM),
        rows(1),
        pl.BlockSpec((1, SPAN), lambda i: (0, at(i))),
        rows(LANES),
        rows(width),
        pl.BlockSpec((1, HALO, width), lambda i: (at(i), 0, 0)),
        whole(8, width),
        rows(STATE),
        rows(STATE),
        rows(LANES),
        pl.BlockSpec((heads, SPAN), lambda i: (0, at(i))),
        whole(1, LANES),
        whole(heads, 1),
        whole(1, width),
    ]
    prior = pl.BlockSpec((1, STATE, width), lambda i: (at(i), 0, 0))
    return rows, whole, ins, prior


def scan_forward(heads, blocks, operands):
    rows, whole, ins, prior = scan_specs(heads, lambda i: i)
    width = heads * HEADDIM
    return call(
        functools.partial(forward_kernel, heads),
        grid=(blocks,),
        in_specs=ins,
        out_specs=[rows(width), prior],
        out_shape=[
            jax.ShapeDtypeStruct((blocks * SPAN, width), F32),
            jax.ShapeDtypeStruct((blocks, STATE, width), F32),
        ],
        scratch_shapes=[
            pltpu.VMEM((STATE, width), F32),
            pltpu.VMEM((SPAN, width), BF),
            pltpu.VMEM((HALO + SPAN, width), F32),
        ],
        name="scan_forward",
    )(*operands)


def scan_backward(heads, blocks, operands, y, priors, dy):
    rows, whole, ins, prior = scan_specs(heads, lambda i: blocks - 1 - i)
    width = heads * HEADDIM
    return call(
        functools.partial(backward_kernel, heads),
        grid=(blocks,),
        in_specs=ins + [rows(width), prior, rows(width)],
        out_specs=[rows(width), rows(2 * STATE), rows(LANES), whole(1, LANES), whole(8, width)],
        out_shape=[
            jax.ShapeDtypeStruct((blocks * SPAN, width), BF),
            jax.ShapeDtypeStruct((blocks * SPAN, 2 * STATE), F32),
            jax.ShapeDtypeStruct((blocks * SPAN, LANES), F32),
            jax.ShapeDtypeStruct((1, LANES), F32),
            jax.ShapeDtypeStruct((8, width), F32),
        ],
        scratch_shapes=[
            pltpu.VMEM((STATE, width), F32),
            pltpu.VMEM((STATE, width), F32),
            pltpu.VMEM((SPAN, width), BF),
            pltpu.VMEM((SPAN, width), BF),
            pltpu.VMEM((SPAN, width), F32),
            pltpu.VMEM((SPAN, width), F32),
            pltpu.VMEM((HALO + SPAN, width), F32),
            pltpu.VMEM((SPAN + HALO, width), F32),
        ],
        name="scan_backward",
    )(*operands, y, priors, dy)


def as_columns(rows):
    few, tokens = rows.shape
    return jnp.concatenate([rows, jnp.zeros((LANES - few, tokens), F32)]).T


def level_block(pieces, spot):
    piece, lead = spot
    return pieces[piece][lead + (slice(None), slice(None))].astype(F32)


def upper_kernel(where, plan, nd, tok, ns, here_ref, range_ref, count_ref, ratio_ref, q_ref, *refs):
    count = 3 + 2 * LEVELS
    pieces, outs = refs[:count], refs[count:]
    upper_ref, grad_refs, q_turned, coefs = outs[0], outs[1 : 1 + nd], outs[1 + nd], outs[2 + nd]

    @pl.when(pl.program_id(0) == 0)
    def _():
        q_turned[...] = q_ref[...].T
        rows = [count_ref[j, w] * ratio_ref[w : w + 1, :] for j in range(len(plan)) for w in range(LEVELS)]
        coefs[...] = as_columns(jnp.concatenate(rows))

    for k in range(ns):
        at = here_ref[0] ^ k
        rows = pl.ds(pl.multiple_of(at * tok, tok), tok)
        levels = [level_block(pieces, where[w][k]) for w in range(LEVELS)]
        for j in range(len(plan)):
            total = None
            for w in plan[j]:
                n = j * LEVELS + w
                term = coefs[rows, n : n + 1] * levels[w]
                total = term if total is None else total + term
            upper_ref[j, rows, :] = total.astype(BF)
    count = q_turned.shape[0] // nd
    for k in range(nd):
        index = here_ref[1] ^ k
        rows = pl.ds(pl.multiple_of(index * count, count), count)
        grad_refs[k][...] = dot(q_turned[rows, :], upper_ref[range_ref[index]]).astype(BF)


def products_kernel(where, plan, lanes, tok, ns, here_ref, count_ref, q_ref, w_ref, *refs):
    count = 3 + 2 * LEVELS
    pieces, outs = refs[:count], refs[count:]
    prod_refs, inner_ref, sums = outs[:ns], outs[ns], outs[ns + 1]
    step = pl.program_id(0)

    @pl.when(step == 0)
    def _():
        sums[...] = jnp.zeros_like(sums)

    for k in range(ns):
        at = here_ref[0] ^ k
        rows = pl.ds(pl.multiple_of(at * tok, tok), tok)
        values = [dot(q_ref[rows, a:b], w_ref[a:b, :]) for a, b in lanes]
        for j, value in enumerate(values):
            prod_refs[k][j] = value.astype(BF)
        for w in range(LEVELS):
            total = None
            for j in range(len(lanes)):
                if w in plan[j]:
                    term = values[j] * count_ref[j, w]
                    total = term if total is None else total + term
            part = total * level_block(pieces, where[w][k])
            folded = part[:, :LANES]
            for c in range(LANES, part.shape[1], LANES):
                folded = folded + part[:, c : c + LANES]
            sums[w, rows, :] += folded

    @pl.when(step == pl.num_programs(0) - 1)
    def _():
        lane = lax.broadcasted_iota(jnp.int32, sums.shape[1:], 1)
        total = jnp.zeros(sums.shape[1:], F32)
        for w in range(LEVELS):
            total = jnp.where(lane == w, jnp.sum(sums[w], axis=1, keepdims=True), total)
        inner_ref[...] = total.T[:LEVELS]


def gate_kernel(
    lanes, count_ref, upper_ref, w_ref, y_ref, z_ref, gain_ref, ratio_ref, mean_ref, dy_ref, dz_ref, grad_ref
):
    @pl.when(pl.program_id(0) == 0)
    def _():
        grad_ref[...] = jnp.zeros_like(grad_ref)

    cubes = ratio_ref[...] * ratio_ref[...] * ratio_ref[...] * mean_ref[...]
    rows = []
    for j in range(len(lanes)):
        total = cubes[0:1] * count_ref[j, 0]
        for w in range(1, LEVELS):
            total = total + cubes[w : w + 1] * count_ref[j, w]
        rows.append(total)
    coefs = as_columns(jnp.concatenate(rows))
    for j, (a, b) in enumerate(lanes):
        upper = upper_ref[j]
        coef = jnp.broadcast_to(coefs[:, j : j + 1], (SPAN, LANES))
        for c in range(a, b, LANES):
            at = slice(c, c + LANES)
            grad_t = dot(upper, w_ref[at, :], ((1,), (1,)))
            z = z_ref[:, at].astype(F32)
            sig = jax.nn.sigmoid(z)
            act = z * sig
            y = y_ref[:, at]
            q = y * act
            dq = gain_ref[:, at] * grad_t - q * coef
            dy_ref[:, at] = (dq * act).astype(BF)
            dz_ref[:, at] = (dq * y * (sig * (1.0 + z * (1.0 - sig)))).astype(BF)
            grad_ref[0:1, at] += jnp.sum(q * grad_t, axis=0, keepdims=True)


def mixed_kernel(plan, ns, count_ref, ratio_ref, x_ref, *refs):
    shares, out_ref = refs[:-1], refs[-1]
    x = x_ref[...].astype(F32)
    for w in range(LEVELS):
        total = None
        for k in range(ns):
            for j in plan[w]:
                term = shares[k][j].astype(F32) * count_ref[k, j * LEVELS + w]
                total = term if total is None else total + term
        out_ref[w] = (x + ratio_ref[:, w : w + 1] * total).astype(BF)


def dp_terms(others):
    return [swapped(other, "dp", k + 1) for k, other in enumerate(others)]


def over_seq(value):
    total = value
    for k in range(1, lax.axis_size("seq")):
        total = total + swapped(value, "seq", k)
    return total


def fsdp_half(own, got):
    nf = lax.axis_size("fsdp")
    f = lax.axis_index("fsdp")

    def part(offset):
        total = picked(own, f ^ offset).astype(F32)
        for other in got:
            total = total + picked(other, f ^ offset).astype(F32)
        return total.astype(BF)

    kept = jnp.stack([part(e) for e in range(0, nf, 2)])
    sent = jnp.stack([part(e ^ 1) for e in range(0, nf, 2)])
    return kept, sent


def fsdp_rest(kept, got):
    k = 2
    while k < lax.axis_size("fsdp"):
        total = (kept.astype(F32) + got.astype(F32)).astype(BF)
        kept, sent = total[::2], total[1::2]
        got = swapped(sent, "fsdp", k)
        k *= 2
    return kept[0], got[0]


def shards(
    tokens,
    lengths,
    norm_gain,
    w_in,
    w_dt,
    conv_w,
    conv_b,
    dt_bias,
    a_log,
    skip,
    gate_gain,
    w_out,
    cotangent,
):
    nd, ns, nf = lax.axis_size("dp"), lax.axis_size("seq"), lax.axis_size("fsdp")
    d, s, f = lax.axis_index("dp"), lax.axis_index("seq"), lax.axis_index("fsdp")
    tok = tokens.shape[1]
    length = ns * tok
    blocks = length // SPAN
    heads = HEADS // ns
    run = heads // nd
    width = heads * HEADDIM
    own_bc = 2 * STATE // ns
    used = width + own_bc
    cols = -(-(used + heads) // LANES) * LANES
    rows_in = w_in.shape[0]
    reach = CONV - 1

    levels = np.array(
        [[level_of(dd * (HEADS // nd) + ss * run + i) for dd in range(nd) for i in range(run)] for ss in range(ns)]
    )
    cuts = [0] + [h for h in range(1, heads) if (levels[:, h] != levels[:, h - 1]).any()] + [heads]
    ranges = [(a, b) for a, b in zip(cuts, cuts[1:])]
    range_level = np.array([[levels[ss, a] for a, _ in ranges] for ss in range(ns)])
    counts = (range_level[:, :, None] <= np.arange(LEVELS)[None, None, :]).astype(np.float32)
    counted = picked(jnp.asarray(counts), s)
    lowest = [int(range_level[ss].min()) for ss in range(ns)]

    def by_head(vector):
        lead = vector.shape[:-1]
        per = vector.shape[-1] // HEADS
        cut = vector.reshape(lead + (nd, ns, run * per))
        mine = lax.dynamic_index_in_dim(cut, s, len(lead) + 1, keepdims=False)
        return mine.reshape(lead + (heads * per,))

    def for_groups(matrix):
        per = matrix.shape[1] // HEADS
        cut = matrix.reshape(matrix.shape[0], nd, ns, run * per)
        return jnp.transpose(cut, (2, 0, 1, 3)).reshape(ns, matrix.shape[0], heads * per)

    def from_groups(stack):
        per = stack.shape[2] // heads
        cut = stack.reshape(ns, stack.shape[1], nd, run * per)
        return jnp.transpose(cut, (1, 2, 0, 3)).reshape(stack.shape[1], HEADS * per)

    pad_cols = cols - used - heads
    stack = jnp.concatenate(
        [
            for_groups(w_in[:, INNER : 2 * INNER]),
            w_in[:, 2 * INNER :].reshape(rows_in, ns, own_bc).transpose(1, 0, 2),
            for_groups(w_dt),
            jnp.zeros((ns, rows_in, pad_cols), BF),
            for_groups(w_in[:, :INNER]),
        ],
        axis=2,
    )
    own_x = tokens[0].astype(F32)
    scale = lax.rsqrt(jnp.mean(own_x * own_x, axis=-1, keepdims=True) + EPS)
    xn_own = (own_x * scale * norm_gain).astype(BF)
    xn_across = swapped(xn_own, "seq", 2)
    xn_pieces = [xn_own, swapped(xn_own, "seq", 1), xn_across, swapped(xn_across, "seq", 1)]
    arrived = [picked(stack, s)] + [swapped(picked(stack, s ^ k), "seq", k) for k in range(1, ns)]
    mine = filled((ns, rows_in, stack.shape[2]), [(p, None, (s ^ k, None, None)) for k, p in enumerate(arrived)])
    mine_z = mine[:, :, cols:]

    def needed(at, level):
        return min(lowest[at], lowest[at ^ 1]) <= level

    def beside(level, *others):
        block = after(cotangent[level : level + 2, 0], *others)
        return swapped(block, "seq", 1, lambda i, j: needed(j, level + 1))

    def across(level, *others):
        block = after(cotangent[level, 0], *others)
        return swapped(block, "seq", 2, lambda i, j: needed(j, level))

    def far(level, block):
        return swapped(block, "seq", 1, lambda i, j: needed(j, level))

    positions = jnp.arange(length, dtype=jnp.int32)
    ends = jnp.cumsum(lengths[0])[:-1]
    seg = jnp.sum((positions[:, None] >= ends[None, :]).astype(jnp.int32), axis=1)
    seg_before = jnp.concatenate([jnp.full((1,), -1, jnp.int32), seg[SPAN - 1 : length - 1 : SPAN]])
    seg_pad = jnp.concatenate([jnp.full((reach,), -1, jnp.int32), seg])
    masks = [(seg_pad[k : k + length] == seg) for k in range(reach)]
    mask_cols = [m.astype(F32) for m in masks]
    mask_cols += [jnp.pad(m, (0, reach - k))[reach - k :] for k, m in enumerate(mask_cols)]
    mask_cols = jnp.pad(jnp.stack(mask_cols, axis=1), ((0, 0), (0, LANES - 2 * reach)))

    def conv_params(s_part, bc_part):
        return by_head(s_part), bc_part

    weight_s = jnp.concatenate(
        [by_head(conv_w[:, :INNER]), by_head(conv_b[None, :INNER]), jnp.zeros((3, width), F32)]
    )
    weight_r = jnp.pad(
        lax.dynamic_slice_in_dim(conv_w, INNER + s * own_bc, own_bc, 1), ((0, 0), (0, cols - used))
    )
    bias_r = jnp.pad(
        lax.dynamic_slice_in_dim(conv_b, INNER + s * own_bc, own_bc, 0), (0, cols - used)
    )
    bias = by_head(dt_bias)
    rate = -jnp.exp(by_head(a_log))
    skip_own = by_head(skip)
    gain = by_head(gate_gain)

    half = width // 2

    def over_fsdp(chunk):
        return lax.all_gather(chunk, "fsdp", axis=0, tiled=False)

    def over_dp(held):
        pieces = [held] + [swapped(held, "dp", j) for j in range(1, nd)]
        moves = [
            (piece, i, (d ^ j, None, i, None, None)) for j, piece in enumerate(pieces) for i in range(nf)
        ]
        return pieces, moves

    held_a = over_fsdp(mine[:, :, :half])
    held_b = over_fsdp(mine[:, :, half:cols])
    small_ones = (seg, seg_before, mask_cols, weight_s, weight_r, bias_r, bias, rate, skip_own, gain)
    held_a, xn_pieces, small_ones = together(held_a, xn_pieces, small_ones)
    seg, seg_before, mask_cols, weight_s, weight_r, bias_r, bias, rate, skip_own, gain = small_ones
    xn = filled((ns, tok, D), [(p, None, (s ^ k, None, None)) for k, p in enumerate(xn_pieces)])
    xn = xn.reshape(length, D)

    near_high, near_low = beside(2, held_a), beside(0, held_a)
    chip3 = across(3, held_a)
    pieces_a, moves_a = over_dp(held_a)
    held_b, moves_a_there, chip3, near_high = together(held_b, [m[0] for m in moves_a], chip3, near_high)
    moves_a = [(p,) + m[1:] for p, m in zip(moves_a_there, moves_a)]
    chip2, far3 = across(2, held_b), far(3, chip3)
    pieces_b, moves_b = over_dp(held_b)
    full_a = filled((nd, ns, nf, rows_in, half), moves_a).reshape(D, half)
    full_b = filled((nd, ns, nf, rows_in, cols - half), moves_b).reshape(D, cols - half)
    held_z = over_fsdp(after(mine_z, held_a))

    xn_turned = xn.T
    proj_a = dot(xn, full_a).astype(BF)
    proj_b = dot(xn, after(full_b, proj_a, xn_turned)).astype(BF)
    proj_b, chip2, far3, near_low, held_z = together(proj_b, chip2, far3, near_low, held_z)
    full_out = lax.all_gather(after(w_out, held_z), ("dp", "fsdp"), axis=0, tiled=True)
    pieces_z, moves_z = over_dp(held_z)
    proj = jnp.concatenate([proj_a, proj_b], axis=1)

    proj_r = proj_b[:, width - half :]
    mixer = jnp.concatenate([jnp.zeros((reach, cols - width), BF), proj_r], axis=0)

    def taken(k):
        rows = mixer[k : k + length].astype(F32)
        return rows * mask_cols[:, k : k + 1] if k < reach else rows

    pre_r = bias_r
    for k in range(CONV):
        pre_r = pre_r + taken(k) * weight_r[k]
    bc_own = jax.nn.silu(pre_r).astype(BF)[:, :own_bc]
    bc = [bc_own] + [swapped(bc_own, "seq", k) for k in range(1, ns)]
    chip1, far2 = across(1, *bc), far(2, chip2)
    bc = reordered_by_xor(bc, s)
    b_in = jnp.concatenate(bc[: ns // 2], axis=1)
    c_out = jnp.concatenate(bc[ns // 2 :], axis=1)

    def padded(rows):
        return jnp.pad(rows, ((0, 0), (0, LANES - rows.shape[1])))

    pre_dt = proj_r[:, own_bc : own_bc + heads].astype(F32) + bias
    steps = jax.nn.softplus(pre_dt)
    tails = proj.reshape(blocks, SPAN, cols)[: blocks - 1, SPAN - HALO :, :width]
    operands = (
        seg_before,
        seg[:, None],
        seg[None, :],
        mask_cols,
        proj,
        jnp.concatenate([jnp.zeros((1, HALO, width), BF), tails]),
        weight_s,
        b_in,
        c_out,
        padded(steps),
        steps.T,
        padded(rate[None, :]),
        rate[:, None],
        jnp.repeat(skip_own, HEADDIM)[None, :],
    )
    y, priors = scan_forward(heads, blocks, operands)
    y, chip1, far2 = together(y, chip1, far2)
    chip0, far1 = across(0, y), far(1, chip1)
    full_z = filled((nd, ns, nf, rows_in, width), moves_z).reshape(D, width)
    proj_z = dot(xn, full_z).astype(BF)
    proj_z, chip0, far1 = together(proj_z, chip0, far1)
    far0 = far(0, chip0)
    q = y * jax.nn.silu(proj_z.astype(F32))
    q_gain = (q * gain).astype(BF)
    lanes = [(a * HEADDIM, b * HEADDIM) for a, b in ranges]
    squares = jnp.stack([jnp.sum(q[:, a:b] * q[:, a:b], axis=1) for a, b in lanes])
    widths = np.array([[(HEADS >> 3 - w) * HEADDIM] for w in range(LEVELS)], np.float32)
    per_level = jnp.sum(counted[:, :, None] * squares[:, None, :], axis=0)
    ratio = lax.rsqrt(over_seq(per_level) / widths + EPS)

    plan = [[w for w in range(LEVELS) if range_level[:, j].min() <= w] for j in range(len(lanes))]
    out_rows = width // nd
    range_of = [next(j for j, (a, b) in enumerate(lanes) if a <= i * out_rows < b) for i in range(nd)]
    here = jnp.stack([s, d]).astype(jnp.int32)
    smem = pl.BlockSpec(memory_space=pltpu.SMEM)
    cot_pieces = [cotangent, near_low, near_high, chip0, chip1, chip2, chip3, far0, far1, far2, far3]
    cot_specs = [pl.BlockSpec((LEVELS, 1, tok, TILE), lambda i: (0, 0, 0, i))]
    cot_specs += [pl.BlockSpec((2, tok, TILE), lambda i: (0, 0, i))] * 2
    cot_specs += [pl.BlockSpec((tok, TILE), lambda i: (0, i))] * (2 * LEVELS)
    where = [[(0, (w, 0)), (1 + w // 2, (w % 2,)), (3 + w, ()), (3 + LEVELS + w, ())] for w in range(LEVELS)]
    upper, *grad_out = call(
        functools.partial(upper_kernel, where, plan, nd, tok, ns),
        grid=(D // TILE,),
        in_specs=[
            smem,
            smem,
            smem,
            pl.BlockSpec((LEVELS, length), lambda i: (0, 0)),
            pl.BlockSpec((length, width), lambda i: (0, 0)),
        ]
        + cot_specs,
        out_specs=[pl.BlockSpec((len(lanes), length, TILE), lambda i: (0, 0, i))]
        + [pl.BlockSpec((out_rows, TILE), lambda i: (0, i))] * nd,
        out_shape=[jax.ShapeDtypeStruct((len(lanes), length, D), BF)]
        + [jax.ShapeDtypeStruct((out_rows, D), BF)] * nd,
        scratch_shapes=[pltpu.VMEM((width, length), BF), pltpu.VMEM((length, LANES), F32)],
        name="upper",
    )(here, jnp.asarray(range_of, jnp.int32), counted, ratio, q_gain, *cot_pieces)
    grad_out = [g.reshape(nf, out_rows // nf, D) for g in grad_out]
    out_got = dp_terms(grad_out[1:])

    full_out, upper = together(full_out, upper)
    *shares, inner = call(
        functools.partial(products_kernel, where, plan, lanes, tok, ns),
        grid=(D // TILE,),
        in_specs=[
            smem,
            smem,
            pl.BlockSpec((length, width), lambda i: (0, 0)),
            pl.BlockSpec((width, TILE), lambda i: (0, i)),
        ]
        + cot_specs,
        out_specs=[pl.BlockSpec((len(lanes), tok, TILE), lambda i: (0, 0, i))] * ns
        + [pl.BlockSpec((LEVELS, length), lambda i: (0, 0))],
        out_shape=[jax.ShapeDtypeStruct((len(lanes), tok, D), BF)] * ns
        + [jax.ShapeDtypeStruct((LEVELS, length), F32)],
        scratch_shapes=[pltpu.VMEM((LEVELS, length, LANES), F32)],
        name="products",
    )(here, counted, q_gain, full_out, *cot_pieces)
    means = over_seq(inner) / widths
    shares = [shares[0]] + [swapped(after(shares[k], means), "seq", k) for k in range(1, ns)]

    rows = pl.BlockSpec((SPAN, width), lambda i: (i, 0))
    scalars = pl.BlockSpec((LEVELS, SPAN), lambda i: (0, i))
    dy, dz, grad_gate = call(
        functools.partial(gate_kernel, lanes),
        grid=(blocks,),
        in_specs=[
            smem,
            pl.BlockSpec((len(lanes), SPAN, D), lambda i: (0, i, 0)),
            pl.BlockSpec((width, D), lambda i: (0, 0)),
            rows,
            rows,
            pl.BlockSpec((1, width), lambda i: (0, 0)),
            scalars,
            scalars,
        ],
        out_specs=[rows, rows, pl.BlockSpec((8, width), lambda i: (0, 0))],
        out_shape=[
            jax.ShapeDtypeStruct((length, width), BF),
            jax.ShapeDtypeStruct((length, width), BF),
            jax.ShapeDtypeStruct((8, width), F32),
        ],
        name="gate_backward",
    )(counted, upper, full_out, y, proj_z, gain[None], ratio, means)
    grad_gate = grad_gate[0]

    def in_terms(dproj, at):
        out = row_terms(xn_turned, dproj, at, nd, ns, nf)
        return out.reshape(nf, ns * rows_in, dproj.shape[1])

    z_other = [in_terms(dz, d ^ k) for k in range(1, nd)]
    z_got = dp_terms(z_other)
    dy, out_got, shares[1] = together(after(dy, *z_other), out_got, shares[1])
    out_kept, out_sent = fsdp_half(grad_out[0], out_got)
    dy = after(dy, out_sent)
    out_half = swapped(out_sent, "fsdp", 1)

    dproj_s, dbc, ddt, drate, dsum = scan_backward(heads, blocks, operands, y, priors, dy)
    dproj_s, dbc, out_half, shares[2] = together(dproj_s, dbc, out_half, shares[2])
    out_pair = fsdp_rest(out_kept, out_half)
    dbc = dbc.astype(BF)
    dbc_parts = reordered_by_xor([dbc[:, j * own_bc : (j + 1) * own_bc] for j in range(ns)], s)
    dbc_got = [swapped(dbc_parts[k], "seq", k) for k in range(1, ns)]
    cut = width // 2
    left_in = dproj_s[:, :cut]
    left_other = [in_terms(left_in, d ^ k) for k in range(1, nd)]
    left_got = dp_terms(left_other)
    dbc_own = after(dbc_parts[0].astype(F32), *left_other)
    for got in dbc_got:
        dbc_own = dbc_own + got.astype(F32)
    dz_late, z_got = together(after(dz, *left_other), z_got)
    z_kept, z_sent = fsdp_half(in_terms(dz_late, d), z_got)
    z_half = swapped(z_sent, "fsdp", 1)
    dpre = jnp.pad(dbc_own, ((0, 0), (0, cols - used))) * silu_slope(pre_r)
    grad_b_r = jnp.sum(dpre, axis=0)[:own_bc]
    grad_w_r = jnp.stack([jnp.sum(dpre * taken(k), axis=0) for k in range(CONV)])[:, :own_bc]
    dmixer = dpre * weight_r[reach]
    for k in range(reach):
        back = reach - k
        later = (dpre * mask_cols[:, k : k + 1])[back:]
        dmixer = dmixer + jnp.pad(later, ((0, back), (0, 0))) * weight_r[k]
    dpre_dt = ddt[:, :heads] * jax.nn.sigmoid(pre_dt)
    dproj_r = jnp.concatenate(
        [dmixer[:, :own_bc].astype(BF), dpre_dt.astype(BF), jnp.zeros((length, pad_cols), BF)], axis=1
    )
    dproj_r, left_got, z_sent = together(dproj_r, left_got, z_sent)
    right_in = jnp.concatenate([dproj_s[:, cut:], dproj_r], axis=1)
    right_other = [in_terms(right_in, d ^ k) for k in range(1, nd)]
    right_got = dp_terms(right_other)
    own_left = in_terms(after(left_in, *right_other), d)
    own_right = in_terms(after(right_in, own_left), d)
    left_kept, left_sent = fsdp_half(own_left, left_got)
    left_half = swapped(left_sent, "fsdp", 1)
    flat = flattened(
        [
            jnp.concatenate([dsum[:CONV], grad_w_r], axis=1).reshape(-1),
            dsum[CONV],
            grad_b_r,
            grad_gate,
            jnp.sum(dpre_dt, axis=0),
            drate[0, :heads] * rate,
            jnp.sum(dsum[CONV + 1].reshape(heads, HEADDIM), axis=1),
        ]
    )
    dxn = input_grad(dz, dproj_s, after(dproj_r, own_right), full_z, full_a, full_b, ns, tok)
    dxn, z_half = together(dxn, z_half)
    near = picked(dxn, s).astype(F32) + swapped(picked(dxn, s ^ 1), "seq", 1).astype(F32)
    far = picked(dxn, s ^ 2).astype(F32) + swapped(picked(dxn, s ^ 3), "seq", 1).astype(F32)
    far = far.astype(BF)
    dxn_across = swapped(far, "seq", 2)
    z_pair = fsdp_rest(z_kept, z_half)
    right_got, left_half, far = together(right_got, left_half, far)
    left_pair = fsdp_rest(left_kept, left_half)
    right_kept, right_sent = fsdp_half(own_right, right_got)
    right_half = swapped(right_sent, "fsdp", 1)

    dxn_own = near + after(dxn_across, right_sent).astype(F32)
    grad_norm = jnp.sum(dxn_own * own_x * scale, axis=0)
    scaled = norm_gain * dxn_own
    dx = scale * scaled - own_x * scale**3 * jnp.mean(own_x * scaled, axis=-1, keepdims=True)
    dx = dx + jnp.sum(after(cotangent, right_sent)[:, 0].astype(F32), axis=0)
    flat = jnp.concatenate([flat, grad_norm.reshape(-1, LANES)])
    flat = butterfly(flat, "dp")

    z_pair, left_pair, right_half, flat = together(z_pair, left_pair, right_half, flat)
    right_pair = fsdp_rest(right_kept, right_half)

    def whole_sum(pair):
        total = (pair[0].astype(F32) + pair[1].astype(F32)).astype(BF)
        return total.reshape(ns, rows_in, total.shape[1])

    early = jnp.concatenate([whole_sum(z_pair), whole_sum(left_pair)], axis=2)
    early_got = [picked(early, s)] + [swapped(picked(early, s ^ k), "seq", k) for k in range(1, ns)]
    early_got, right_pair = together(early_got, right_pair)
    flat = butterfly(flat, "fsdp")
    late = whole_sum(right_pair)
    late_got = [picked(late, s)] + [swapped(picked(late, s ^ k), "seq", k) for k in range(1, ns)]
    early_got, late_got = together(early_got, late_got)
    early = placed_by_xor(early_got, s)
    late = placed_by_xor(late_got, s)
    got_z = early[:, :, :width]
    got_x = jnp.concatenate([early[:, :, width:], late], axis=2)
    sum_out = out_pair[0].astype(F32) + out_pair[1].astype(F32)

    ratio_own = padded(lax.dynamic_slice_in_dim(ratio, s * tok, tok, 1).T)
    theirs = jnp.stack([picked(jnp.asarray(counts), s ^ k).reshape(-1) for k in range(ns)])
    mixed = call(
        functools.partial(
            mixed_kernel,
            [[j for j in range(len(lanes)) if range_level[:, j].min() <= w] for w in range(LEVELS)],
            ns,
        ),
        grid=(D // TILE,),
        in_specs=[
            smem,
            pl.BlockSpec((tok, LANES), lambda i: (0, 0)),
            pl.BlockSpec((tok, TILE), lambda i: (0, i)),
        ]
        + [pl.BlockSpec((len(lanes), tok, TILE), lambda i: (0, 0, i))] * ns,
        out_specs=pl.BlockSpec((LEVELS, tok, TILE), lambda i: (0, 0, i)),
        out_shape=jax.ShapeDtypeStruct((LEVELS, tok, D), BF),
        name="mixed",
    )(theirs, ratio_own, tokens[0], *after(shares, right_sent))[:, None]

    sum_in = jnp.concatenate(
        [
            from_groups(got_z),
            from_groups(got_x[:, :, :width]),
            jnp.transpose(got_x[:, :, width:used], (1, 0, 2)).reshape(rows_in, 2 * STATE),
        ],
        axis=1,
    ).astype(F32)
    sum_dt = from_groups(got_x[:, :, used : used + heads]).astype(F32)

    sizes = [CONV * used, used, width, heads, heads, heads]
    filling = -sum(sizes) % 1024
    sizes += [filling, D]
    every = seq_gather(flat, s).reshape(ns, -1)
    starts = np.cumsum([0] + sizes)
    pieces = [every[:, a : a + n] for a, n in zip(starts, sizes)]

    def heads_back(rows):
        lead = rows.shape[1:-1]
        cut = rows.reshape((ns,) + lead + (nd, rows.shape[-1] // nd))
        order = tuple(range(1, 1 + len(lead))) + (1 + len(lead), 0, 2 + len(lead))
        return jnp.transpose(cut, order).reshape(lead + (-1,))

    conv_rows = pieces[0].reshape(ns, CONV, used)
    conv_all = jnp.concatenate(
        [
            heads_back(conv_rows[:, :, :width]),
            jnp.transpose(conv_rows[:, :, width:], (1, 0, 2)).reshape(CONV, 2 * STATE),
        ],
        axis=1,
    )
    bias_all = jnp.concatenate([heads_back(pieces[1][:, :width]), pieces[1][:, width:].reshape(-1)])
    return (
        mixed,
        dx.astype(BF)[None],
        jnp.sum(pieces[7], axis=0),
        sum_in,
        sum_dt,
        conv_all,
        bias_all,
        heads_back(pieces[3]),
        heads_back(pieces[4]),
        heads_back(pieces[5]),
        heads_back(pieces[2]),
        sum_out,
    )


def solution(mesh):
    rows = P(("dp", "seq", "fsdp"), None)
    held = P(("dp", "fsdp"), "seq", None)
    levels = P(None, ("dp", "fsdp"), "seq", None)
    placed = (held, P(("dp", "fsdp"), None), P(), rows, rows, P(), P(), P(), P(), P(), P(), rows, levels)
    return jax.shard_map(
        shards,
        mesh=mesh,
        in_specs=placed,
        out_specs=(levels, held, P(), rows, rows, P(), P(), P(), P(), P(), P(), rows),
        check_vma=False,
    )
```

```python
import functools

import jax
import jax.numpy as jnp
import numpy as np
from jax import lax
from jax.experimental import pallas as pl
from jax.experimental.pallas import tpu as pltpu
from jax.sharding import PartitionSpec as P

D = 2048
HEADS = 64
HEADDIM = 64
STATE = 128
CONV = 4
SPAN = 256
INNER = 4096
EPS = 1e-05
LEVELS = 4
BF = jnp.bfloat16
F32 = jnp.float32
HIGH = lax.Precision.HIGHEST
LANES = 128
HALO = 16
TILE = 256
VMEM_LIMIT = 48 * 1024 * 1024


def dot(a, b, dims=((1,), (0,)), precision=None):
    return lax.dot_general(a, b, (dims, ((), ())), preferred_element_type=F32, precision=precision)


def silu_slope(v):
    sig = jax.nn.sigmoid(v)
    return sig * (1.0 + v * (1.0 - sig))


def level_of(head):
    return 0 if head < 8 else 1 if head < 16 else 2 if head < 32 else 3


def swapped(value, axis, k, keep=None):
    pairs = [(i, i ^ k) for i in range(lax.axis_size(axis))]
    if keep is not None:
        pairs = [p for p in pairs if keep(*p)]
    return lax.ppermute(value, axis, pairs)


def after(value, *others):
    return lax.optimization_barrier((value,) + others)[0]


def together(*values):
    return lax.optimization_barrier(values)


def flattened(vectors):
    flat = jnp.concatenate(vectors)
    return jnp.pad(flat, (0, -flat.shape[0] % 1024)).reshape(-1, LANES)


def butterfly(value, axis):
    k = 1
    while k < lax.axis_size(axis):
        value = value + swapped(value, axis, k)
        k *= 2
    return value


def picked(array, index):
    return lax.dynamic_index_in_dim(array, index, 0, keepdims=False)


def placed_by_xor(pieces, here):
    out = jnp.zeros((len(pieces),) + pieces[0].shape, pieces[0].dtype)
    for k, piece in enumerate(pieces):
        out = lax.dynamic_update_index_in_dim(out, piece, here ^ k, 0)
    return out


def seq_gather(block, here):
    return placed_by_xor([block] + [swapped(block, "seq", k) for k in range(1, 4)], here)


def reordered_by_xor(pieces, here):
    k = 1
    while k < len(pieces):
        flip = (here & k) > 0
        pieces = [jnp.where(flip, pieces[j ^ k], piece) for j, piece in enumerate(pieces)]
        k *= 2
    return pieces


def seq_exchange(pieces, here):
    got = [picked(pieces, here)]
    for k in range(1, pieces.shape[0]):
        got.append(swapped(picked(pieces, here ^ k), "seq", k))
    return placed_by_xor(got, here)


def call(kernel, **kwargs):
    return pl.pallas_call(
        kernel,
        compiler_params=pltpu.CompilerParams(vmem_limit_bytes=VMEM_LIMIT),
        cost_estimate=pl.CostEstimate(flops=1, bytes_accessed=1, transcendentals=0),
        **kwargs,
    )


def filled(shape, moves):
    arrays, plan, rows = [], [], []
    block = tuple(size if index is None else 1 for size, index in zip(shape, moves[0][2]))
    for piece, lead, place in moves:
        at = next((i for i, a in enumerate(arrays) if a is piece), len(arrays))
        if at == len(arrays):
            arrays.append(piece)
        plan.append((at, lead))
        rows.append(jnp.stack([jnp.asarray(0 if n is None else n, jnp.int32) for n in place]))

    def kernel(index_ref, *refs):
        pieces, out = refs[:-1], refs[-1]
        for m, (at, lead) in enumerate(plan):

            @pl.when(pl.program_id(0) == m)
            def _():
                value = pieces[at][...] if lead is None else pieces[at][lead]
                out[...] = value.reshape(block)

    return call(
        kernel,
        grid_spec=pltpu.PrefetchScalarGridSpec(
            num_scalar_prefetch=1,
            grid=(len(plan),),
            in_specs=[
                pl.BlockSpec(a.shape, lambda i, t, n=a.ndim: (0,) * n) for a in arrays
            ],
            out_specs=pl.BlockSpec(
                block, lambda i, t: tuple(t[i, n] for n in range(len(shape)))
            ),
        ),
        out_shape=jax.ShapeDtypeStruct(shape, arrays[0].dtype),
        name="filled",
    )(jnp.stack(rows), *arrays)


def terms_kernel(ns, nf, at_ref, left_ref, right_ref, out_ref):
    value = dot(left_ref[...], right_ref[...]).astype(BF)
    rows = value.shape[0] // (ns * nf)
    for i in range(ns):
        for k in range(nf):
            out_ref[k, i] = value[(i * nf + k) * rows : (i * nf + k + 1) * rows]


def row_terms(turned, right, at, nd, ns, nf):
    depth = turned.shape[1]
    rows = turned.shape[0] // nd
    columns = right.shape[1]
    wide = TILE if columns % TILE == 0 else LANES
    return call(
        functools.partial(terms_kernel, ns, nf),
        grid_spec=pltpu.PrefetchScalarGridSpec(
            num_scalar_prefetch=1,
            grid=(columns // wide,),
            in_specs=[
                pl.BlockSpec((rows, depth), lambda i, t: (t[0], 0)),
                pl.BlockSpec((depth, wide), lambda i, t: (0, i)),
            ],
            out_specs=pl.BlockSpec((nf, ns, rows // (nf * ns), wide), lambda i, t: (0, 0, 0, i)),
        ),
        out_shape=jax.ShapeDtypeStruct((nf, ns, rows // (nf * ns), columns), BF),
        name="row_terms",
    )(at.astype(jnp.int32)[None], turned, right)


def input_grad_kernel(blocks, dz_ref, ds_ref, dr_ref, wz_ref, wa_ref, wb_ref, out_ref):
    half = wa_ref.shape[1]
    rest = ds_ref.shape[1] - half
    columns = ((1,), (1,))
    total = dot(dz_ref[...], wz_ref[...], columns)
    total = total + dot(ds_ref[:, :half], wa_ref[...], columns)
    total = total + dot(ds_ref[:, half:], wb_ref[:, :rest], columns)
    total = total + dot(dr_ref[...], wb_ref[:, rest:], columns)
    total = total.astype(BF)
    tok = total.shape[0] // blocks
    for i in range(blocks):
        out_ref[i] = total[i * tok : (i + 1) * tok]


def input_grad(dz, ds, dr, wz, wa, wb, blocks, tok):
    def whole(a):
        return pl.BlockSpec(a.shape, lambda i: (0, 0))

    def rows(a):
        return pl.BlockSpec((TILE, a.shape[1]), lambda i: (i, 0))

    return call(
        functools.partial(input_grad_kernel, blocks),
        grid=(wz.shape[0] // TILE,),
        in_specs=[whole(dz), whole(ds), whole(dr), rows(wz), rows(wa), rows(wb)],
        out_specs=pl.BlockSpec((blocks, tok, TILE), lambda i: (0, 0, i)),
        out_shape=jax.ShapeDtypeStruct((blocks, tok, wz.shape[0]), BF),
        name="input_grad",
    )(dz, ds, dr, wz, wa, wb)


def tri(rows_first):
    a = lax.broadcasted_iota(jnp.int32, (SPAN, SPAN), 0)
    b = lax.broadcasted_iota(jnp.int32, (SPAN, SPAN), 1)
    return (a >= b) if rows_first else (a <= b)


def pair_of(lo, cols, p):
    return jnp.where(lo, cols[:, 2 * p : 2 * p + 1], cols[:, 2 * p + 1 : 2 * p + 2])


def decays(segc, segr, segp, dt, dtr, rate, rater):
    lower = tri(True).astype(F32)
    upper = tri(False).astype(F32)
    cum = dot(lower, dt * rate, precision=HIGH)
    cumr = dot(dtr * rater, upper, precision=HIGH)
    last = cum[SPAN - 1 : SPAN, :]
    keep = jnp.where(segc == segp, jnp.exp(cum), 0.0)
    to_end = jnp.where(segc == segr[:, SPAN - 1 : SPAN], jnp.exp(last - cum), 0.0)
    return cum, cumr, keep, to_end


def spread_columns(ref, first, count):
    return [jnp.broadcast_to(ref[:, first + k : first + k + 1], (SPAN, LANES)) for k in range(count)]


def taps(ext, masks, at):
    terms = [ext[pl.ds(HALO - CONV + 1 + k, SPAN), at] for k in range(CONV)]
    return [t * m for t, m in zip(terms, masks)] + terms[CONV - 1 :]


def convolved(terms, weight_ref, at):
    total = weight_ref[CONV : CONV + 1, at] + terms[0] * weight_ref[0:1, at]
    for k in range(1, CONV):
        total = total + terms[k] * weight_ref[k : k + 1, at]
    return total


def forward_kernel(
    heads,
    segp_ref,
    segc_ref,
    segr_ref,
    mask_ref,
    in_ref,
    halo_ref,
    weight_ref,
    b_ref,
    c_ref,
    dt_ref,
    dtr_ref,
    rate_ref,
    rater_ref,
    skip_ref,
    y_ref,
    prior_ref,
    carry,
    to_end_u,
    ext,
):
    block = pl.program_id(0)
    width = heads * HEADDIM

    @pl.when(block == 0)
    def _():
        carry[...] = jnp.zeros_like(carry)

    prior_ref[0] = carry[...]
    ext[0:HALO] = halo_ref[0].astype(F32)
    ext[HALO:] = in_ref[...].astype(F32)
    segc, segr = segc_ref[...], segr_ref[...]
    dt = dt_ref[...]
    cum, cumr, keep, to_end = decays(
        segc, segr, segp_ref[block], dt, dtr_ref[...], rate_ref[...], rater_ref[...]
    )
    bm, cm = b_ref[...], c_ref[...]
    mixing = dot(cm, bm, ((1,), (1,)))
    mixing = jnp.where(tri(True) & (segc == segr), mixing, 0.0)
    masks = spread_columns(mask_ref, 0, CONV - 1)
    lo = lax.broadcasted_iota(jnp.int32, (SPAN, LANES), 1) < HEADDIM
    for p in range(heads // 2):
        at = slice(p * LANES, (p + 1) * LANES)
        pre = convolved(taps(ext, masks, at), weight_ref, at)
        x2 = pre * jax.nn.sigmoid(pre)
        u2 = x2 * pair_of(lo, dt, p)
        sides = (jnp.where(lo, u2, 0.0).astype(BF), jnp.where(lo, 0.0, u2).astype(BF))
        total = dot(cm, carry[:, at].astype(BF)) * pair_of(lo, keep, p) + skip_ref[:, at] * x2
        for k in range(2):
            h = 2 * p + k
            decay = jnp.exp(jnp.minimum(cum[:, h : h + 1] - cumr[h : h + 1, :], 0.0))
            total = total + dot((decay * mixing).astype(BF), sides[k])
        y_ref[:, at] = total
        to_end_u[:, at] = (u2 * pair_of(lo, to_end, p)).astype(BF)
    fresh = dot(bm, to_end_u[...], ((0,), (0,)))
    lo_row = lax.broadcasted_iota(jnp.int32, (1, LANES), 1) < HEADDIM
    for p in range(heads // 2):
        at = slice(p * LANES, (p + 1) * LANES)
        factor = pair_of(lo_row, keep[SPAN - 1 : SPAN, :], p)
        carry[:, at] = factor * carry[:, at] + fresh[:, at]


def split_dot(value, ones):
    high = value.astype(BF)
    low = (value - high.astype(F32)).astype(BF)
    return dot(high, ones) + dot(low, ones)


def backward_kernel(
    heads,
    segp_ref,
    segc_ref,
    segr_ref,
    mask_ref,
    in_ref,
    halo_ref,
    weight_ref,
    b_ref,
    c_ref,
    dt_ref,
    dtr_ref,
    rate_ref,
    rater_ref,
    skip_ref,
    y_ref,
    prior_ref,
    dy_ref,
    din_ref,
    dbc_ref,
    ddt_ref,
    drate_ref,
    dsum_ref,
    dcarry,
    after_state,
    keep_dy,
    to_end_u,
    slopes,
    along,
    ext,
    dext,
):
    step = pl.program_id(0)
    block = pl.num_programs(0) - 1 - step

    @pl.when(step == 0)
    def _():
        dcarry[...] = jnp.zeros_like(dcarry)
        after_state[...] = jnp.zeros_like(after_state)
        drate_ref[...] = jnp.zeros_like(drate_ref)
        dsum_ref[...] = jnp.zeros_like(dsum_ref)
        dext[SPAN:] = jnp.zeros((HALO, dext.shape[1]), F32)

    ext[0:HALO] = halo_ref[0].astype(F32)
    ext[HALO:] = in_ref[...].astype(F32)
    segc, segr = segc_ref[...], segr_ref[...]
    dt = dt_ref[...]
    cum, cumr, keep, to_end = decays(
        segc, segr, segp_ref[block], dt, dtr_ref[...], rate_ref[...], rater_ref[...]
    )
    bm, cm = b_ref[...], c_ref[...]
    allowed = tri(False) & (segc == segr)
    mixing = jnp.where(allowed, dot(bm, cm, ((1,), (1,))), 0.0)
    masks = spread_columns(mask_ref, 0, CONV - 1)
    moved = spread_columns(mask_ref, CONV - 1, CONV - 1)
    lo = lax.broadcasted_iota(jnp.int32, (SPAN, LANES), 1) < HEADDIM
    dmixing = jnp.zeros((SPAN, SPAN), F32)
    for p in range(heads // 2):
        at = slice(p * LANES, (p + 1) * LANES)
        terms = taps(ext, masks, at)
        pre = convolved(terms, weight_ref, at)
        sig = jax.nn.sigmoid(pre)
        x2 = pre * sig
        dt2 = pair_of(lo, dt, p)
        u2 = x2 * dt2
        dyb = dy_ref[:, at]
        dy2 = dyb.astype(F32)
        skip = skip_ref[:, at]
        te2 = pair_of(lo, to_end, p)
        u_sides = (jnp.where(lo, u2, 0.0).astype(BF), jnp.where(lo, 0.0, u2).astype(BF))
        dy_sides = (jnp.where(lo, dy2, 0.0).astype(BF), jnp.where(lo, 0.0, dy2).astype(BF))
        du = te2 * dot(bm, dcarry[:, at].astype(BF))
        for k in range(2):
            h = 2 * p + k
            decay = jnp.exp(jnp.minimum(cumr[h : h + 1, :] - cum[:, h : h + 1], 0.0))
            du = du + dot((decay * mixing).astype(BF), dy_sides[k])
            dmixing = dmixing + decay * dot(u_sides[k], dyb, ((1,), (1,)))
        keep_dy[:, at] = (pair_of(lo, keep, p) * dy2).astype(BF)
        to_end_u[:, at] = (te2 * u2).astype(BF)
        slopes[:, at] = dy2 * (y_ref[:, at] - skip * x2) - u2.astype(BF).astype(F32) * du
        along[:, at] = x2 * du
        dpre = (dt2 * du + skip * dy2) * (sig * (1.0 + pre * (1.0 - sig)))
        dext[0:SPAN, at] = dpre
        for k in range(CONV):
            dsum_ref[k : k + 1, at] += jnp.sum(dpre * terms[k], axis=0, keepdims=True)
        dsum_ref[CONV : CONV + 1, at] += jnp.sum(dpre, axis=0, keepdims=True)
        dsum_ref[CONV + 1 : CONV + 2, at] += jnp.sum(dy2 * x2, axis=0, keepdims=True)
        din = dpre * weight_ref[CONV - 1 : CONV, at]
        for k in range(CONV - 1):
            later = dext[pl.ds(CONV - 1 - k, SPAN), at]
            din = din + later * moved[k] * weight_ref[k : k + 1, at]
        din_ref[:, at] = din.astype(BF)
    dext[SPAN:] = dext[0:HALO]
    dmixing = jnp.where(allowed, dmixing, 0.0).astype(BF)
    dstate = dcarry[...].astype(BF)
    prior = prior_ref[0]
    dbc_ref[:, :STATE] = dot(dmixing, cm) + dot(to_end_u[...], dstate, ((1,), (1,)))
    dbc_ref[:, STATE:] = dot(dmixing, bm, ((0,), (0,))) + dot(
        keep_dy[...], prior.astype(BF), ((1,), (1,))
    )
    width = heads * HEADDIM
    ones = (
        lax.broadcasted_iota(jnp.int32, (width, LANES), 0) // HEADDIM
        == lax.broadcasted_iota(jnp.int32, (width, LANES), 1)
    ).astype(BF)
    at_end = jnp.sum(dcarry[...] * after_state[...], axis=0, keepdims=True)
    at_end = split_dot(jnp.broadcast_to(at_end, (16, width)), ones)[:1]
    dcum = split_dot(slopes[...], ones)
    da = dot(tri(False).astype(F32), dcum, precision=HIGH) + at_end
    ddt_ref[...] = rate_ref[...] * da + split_dot(along[...], ones)
    drate_ref[...] += jnp.sum(dt * da, axis=0, keepdims=True)
    fresh = dot(cm, keep_dy[...], ((0,), (0,)))
    lo_row = lax.broadcasted_iota(jnp.int32, (1, LANES), 1) < HEADDIM
    for p in range(heads // 2):
        at = slice(p * LANES, (p + 1) * LANES)
        factor = pair_of(lo_row, keep[SPAN - 1 : SPAN, :], p)
        dcarry[:, at] = factor * dcarry[:, at] + fresh[:, at]
    after_state[...] = prior


def scan_specs(heads, at):
    width = heads * HEADDIM

    def rows(n):
        return pl.BlockSpec((SPAN, n), lambda i: (at(i), 0))

    def whole(*shape):
        return pl.BlockSpec(shape, lambda i: (0,) * len(shape))

    ins = [
        pl.BlockSpec(memory_space=pltpu.SMEM),
        rows(1),
        pl.BlockSpec((1, SPAN), lambda i: (0, at(i))),
        rows(LANES),
        rows(width),
        pl.BlockSpec((1, HALO, width), lambda i: (at(i), 0, 0)),
        whole(8, width),
        rows(STATE),
        rows(STATE),
        rows(LANES),
        pl.BlockSpec((heads, SPAN), lambda i: (0, at(i))),
        whole(1, LANES),
        whole(heads, 1),
        whole(1, width),
    ]
    prior = pl.BlockSpec((1, STATE, width), lambda i: (at(i), 0, 0))
    return rows, whole, ins, prior


def scan_forward(heads, blocks, operands):
    rows, whole, ins, prior = scan_specs(heads, lambda i: i)
    width = heads * HEADDIM
    return call(
        functools.partial(forward_kernel, heads),
        grid=(blocks,),
        in_specs=ins,
        out_specs=[rows(width), prior],
        out_shape=[
            jax.ShapeDtypeStruct((blocks * SPAN, width), F32),
            jax.ShapeDtypeStruct((blocks, STATE, width), F32),
        ],
        scratch_shapes=[
            pltpu.VMEM((STATE, width), F32),
            pltpu.VMEM((SPAN, width), BF),
            pltpu.VMEM((HALO + SPAN, width), F32),
        ],
        name="scan_forward",
    )(*operands)


def scan_backward(heads, blocks, operands, y, priors, dy):
    rows, whole, ins, prior = scan_specs(heads, lambda i: blocks - 1 - i)
    width = heads * HEADDIM
    return call(
        functools.partial(backward_kernel, heads),
        grid=(blocks,),
        in_specs=ins + [rows(width), prior, rows(width)],
        out_specs=[rows(width), rows(2 * STATE), rows(LANES), whole(1, LANES), whole(8, width)],
        out_shape=[
            jax.ShapeDtypeStruct((blocks * SPAN, width), BF),
            jax.ShapeDtypeStruct((blocks * SPAN, 2 * STATE), F32),
            jax.ShapeDtypeStruct((blocks * SPAN, LANES), F32),
            jax.ShapeDtypeStruct((1, LANES), F32),
            jax.ShapeDtypeStruct((8, width), F32),
        ],
        scratch_shapes=[
            pltpu.VMEM((STATE, width), F32),
            pltpu.VMEM((STATE, width), F32),
            pltpu.VMEM((SPAN, width), BF),
            pltpu.VMEM((SPAN, width), BF),
            pltpu.VMEM((SPAN, width), F32),
            pltpu.VMEM((SPAN, width), F32),
            pltpu.VMEM((HALO + SPAN, width), F32),
            pltpu.VMEM((SPAN + HALO, width), F32),
        ],
        name="scan_backward",
    )(*operands, y, priors, dy)


def as_columns(rows):
    few, tokens = rows.shape
    return jnp.concatenate([rows, jnp.zeros((LANES - few, tokens), F32)]).T


def level_block(pieces, spot):
    piece, lead = spot
    return pieces[piece][lead + (slice(None), slice(None))].astype(F32)


def upper_kernel(where, plan, nd, tok, ns, here_ref, range_ref, count_ref, ratio_ref, q_turned, *refs):
    count = 3 + 2 * LEVELS
    pieces, outs = refs[:count], refs[count:]
    upper_ref, grad_refs, coefs = outs[0], outs[1 : 1 + nd], outs[1 + nd]

    @pl.when(pl.program_id(0) == 0)
    def _():
        rows = [count_ref[j, w] * ratio_ref[w : w + 1, :] for j in range(len(plan)) for w in range(LEVELS)]
        coefs[...] = as_columns(jnp.concatenate(rows))

    for k in range(ns):
        at = here_ref[0] ^ k
        rows = pl.ds(pl.multiple_of(at * tok, tok), tok)
        levels = [level_block(pieces, where[w][k]) for w in range(LEVELS)]
        for j in range(len(plan)):
            total = None
            for w in plan[j]:
                n = j * LEVELS + w
                term = coefs[rows, n : n + 1] * levels[w]
                total = term if total is None else total + term
            upper_ref[j, rows, :] = total.astype(BF)
    count = q_turned.shape[0] // nd
    for k in range(nd):
        index = here_ref[1] ^ k
        rows = pl.ds(pl.multiple_of(index * count, count), count)
        grad_refs[k][...] = dot(q_turned[rows, :], upper_ref[range_ref[index]]).astype(BF)


def products_kernel(where, plan, lanes, tok, ns, here_ref, count_ref, q_ref, w_ref, *refs):
    count = 3 + 2 * LEVELS
    pieces, outs = refs[:count], refs[count:]
    prod_refs, inner_ref, sums = outs[:ns], outs[ns], outs[ns + 1]
    step = pl.program_id(0)

    @pl.when(step == 0)
    def _():
        sums[...] = jnp.zeros_like(sums)

    for k in range(ns):
        at = here_ref[0] ^ k
        rows = pl.ds(pl.multiple_of(at * tok, tok), tok)
        values = [dot(q_ref[rows, a:b], w_ref[a:b, :]) for a, b in lanes]
        for j, value in enumerate(values):
            prod_refs[k][j] = value.astype(BF)
        for w in range(LEVELS):
            total = None
            for j in range(len(lanes)):
                if w in plan[j]:
                    term = values[j] * count_ref[j, w]
                    total = term if total is None else total + term
            part = total * level_block(pieces, where[w][k])
            folded = part[:, :LANES]
            for c in range(LANES, part.shape[1], LANES):
                folded = folded + part[:, c : c + LANES]
            sums[w, rows, :] += folded

    @pl.when(step == pl.num_programs(0) - 1)
    def _():
        lane = lax.broadcasted_iota(jnp.int32, sums.shape[1:], 1)
        total = jnp.zeros(sums.shape[1:], F32)
        for w in range(LEVELS):
            total = jnp.where(lane == w, jnp.sum(sums[w], axis=1, keepdims=True), total)
        inner_ref[...] = total.T[:LEVELS]


def gate_kernel(
    starts, wide, count_ref, upper_ref, w_ref, y_ref, z_ref, gain_ref, ratio_ref, mean_ref, dy_ref, dz_ref, grad_ref, coefs
):
    step = pl.program_id(0)

    @pl.when(step == 0)
    def _():
        cubes = ratio_ref[...] * ratio_ref[...] * ratio_ref[...] * mean_ref[...]
        rows = []
        for j in range(len(starts)):
            total = cubes[0:1] * count_ref[j, 0]
            for w in range(1, LEVELS):
                total = total + cubes[w : w + 1] * count_ref[j, w]
            rows.append(total)
        columns = as_columns(jnp.concatenate(rows))
        for j in range(len(starts)):
            coefs[j] = jnp.broadcast_to(columns[:, j : j + 1], coefs.shape[1:])

    grad_all = dot(upper_ref[0], w_ref[...], ((1,), (1,)))
    coef = coefs[tile_range(starts, wide, step)]
    for c in range(0, wide, LANES):
        at = slice(c, c + LANES)
        grad_t = grad_all[:, at]
        z = z_ref[:, at].astype(F32)
        sig = jax.nn.sigmoid(z)
        act = z * sig
        y = y_ref[:, at]
        q = y * act
        dq = gain_ref[:, at] * grad_t - q * coef
        dy_ref[:, at] = (dq * act).astype(BF)
        dz_ref[:, at] = (dq * y * (sig * (1.0 + z * (1.0 - sig)))).astype(BF)
        grad_ref[0:1, at] = jnp.sum(q * grad_t, axis=0, keepdims=True)


def tile_range(starts, wide, step):
    index = 0
    for start in starts[1:]:
        index = index + jnp.where(step * wide >= start, 1, 0)
    return index


def mixed_kernel(plan, ns, tok, here_ref, count_ref, ratio_ref, x_ref, *refs):
    shares, out_ref = refs[:-1], refs[-1]
    at = pl.ds(pl.multiple_of(here_ref[0] * tok, tok), tok)
    ratios = as_columns(ratio_ref[:, at])
    x = x_ref[...].astype(F32)
    for w in range(LEVELS):
        total = None
        for k in range(ns):
            for j in plan[w]:
                term = shares[k][j].astype(F32) * count_ref[k, j * LEVELS + w]
                total = term if total is None else total + term
        out_ref[w] = (x + ratios[:, w : w + 1] * total).astype(BF)


def dp_terms(others):
    return [swapped(other, "dp", k + 1) for k, other in enumerate(others)]


def over_seq(value):
    dense = value.reshape(-1, LANES)
    total = dense
    for k in range(1, lax.axis_size("seq")):
        total = total + swapped(dense, "seq", k)
    return total.reshape(value.shape)


def fsdp_half(own, got):
    nf = lax.axis_size("fsdp")
    f = lax.axis_index("fsdp")

    def part(offset):
        total = picked(own, f ^ offset).astype(F32)
        for other in got:
            total = total + picked(other, f ^ offset).astype(F32)
        return total.astype(BF)

    kept = jnp.stack([part(e) for e in range(0, nf, 2)])
    sent = jnp.stack([part(e ^ 1) for e in range(0, nf, 2)])
    return kept, sent


def fsdp_rest(kept, got):
    k = 2
    while k < lax.axis_size("fsdp"):
        total = (kept.astype(F32) + got.astype(F32)).astype(BF)
        kept, sent = total[::2], total[1::2]
        got = swapped(sent, "fsdp", k)
        k *= 2
    return kept[0], got[0]


def shards(
    tokens,
    lengths,
    norm_gain,
    w_in,
    w_dt,
    conv_w,
    conv_b,
    dt_bias,
    a_log,
    skip,
    gate_gain,
    w_out,
    cotangent,
):
    nd, ns, nf = lax.axis_size("dp"), lax.axis_size("seq"), lax.axis_size("fsdp")
    d, s, f = lax.axis_index("dp"), lax.axis_index("seq"), lax.axis_index("fsdp")
    tok = tokens.shape[1]
    length = ns * tok
    blocks = length // SPAN
    heads = HEADS // ns
    run = heads // nd
    width = heads * HEADDIM
    own_bc = 2 * STATE // ns
    used = width + own_bc
    cols = -(-(used + heads) // LANES) * LANES
    rows_in = w_in.shape[0]
    reach = CONV - 1

    levels = np.array(
        [[level_of(dd * (HEADS // nd) + ss * run + i) for dd in range(nd) for i in range(run)] for ss in range(ns)]
    )
    cuts = [0] + [h for h in range(1, heads) if (levels[:, h] != levels[:, h - 1]).any()] + [heads]
    ranges = [(a, b) for a, b in zip(cuts, cuts[1:])]
    range_level = np.array([[levels[ss, a] for a, _ in ranges] for ss in range(ns)])
    counts = (range_level[:, :, None] <= np.arange(LEVELS)[None, None, :]).astype(np.float32)
    counted = picked(jnp.asarray(counts), s)
    theirs = picked(
        jnp.asarray(np.stack([[counts[i ^ k].reshape(-1) for k in range(ns)] for i in range(ns)])), s
    )
    lowest = [int(range_level[ss].min()) for ss in range(ns)]

    def by_head(vector):
        lead = vector.shape[:-1]
        per = vector.shape[-1] // HEADS
        cut = vector.reshape(lead + (nd, ns, run * per))
        mine = lax.dynamic_index_in_dim(cut, s, len(lead) + 1, keepdims=False)
        return mine.reshape(lead + (heads * per,))

    def for_groups(matrix):
        per = matrix.shape[1] // HEADS
        cut = matrix.reshape(matrix.shape[0], nd, ns, run * per)
        return jnp.transpose(cut, (2, 0, 1, 3)).reshape(ns, matrix.shape[0], heads * per)

    def from_groups(stack):
        per = stack.shape[2] // heads
        cut = stack.reshape(ns, stack.shape[1], nd, run * per)
        return jnp.transpose(cut, (1, 2, 0, 3)).reshape(stack.shape[1], HEADS * per)

    pad_cols = cols - used - heads
    stack = jnp.concatenate(
        [
            for_groups(w_in[:, INNER : 2 * INNER]),
            w_in[:, 2 * INNER :].reshape(rows_in, ns, own_bc).transpose(1, 0, 2),
            for_groups(w_dt),
            jnp.zeros((ns, rows_in, pad_cols), BF),
            for_groups(w_in[:, :INNER]),
        ],
        axis=2,
    )
    own_x = tokens[0].astype(F32)
    scale = lax.rsqrt(jnp.mean(own_x * own_x, axis=-1, keepdims=True) + EPS)
    xn_own = (own_x * scale * norm_gain).astype(BF)
    xn_across = swapped(xn_own, "seq", 2)
    xn_pieces = [xn_own, swapped(xn_own, "seq", 1), xn_across, swapped(xn_across, "seq", 1)]
    arrived = [picked(stack, s)] + [swapped(picked(stack, s ^ k), "seq", k) for k in range(1, ns)]
    mine = filled((ns, rows_in, stack.shape[2]), [(p, None, (s ^ k, None, None)) for k, p in enumerate(arrived)])
    mine_z = mine[:, :, cols:]

    def needed(at, level):
        return min(lowest[at], lowest[at ^ 1]) <= level

    halves = [cotangent[w : w + 2, 0] for w in range(0, LEVELS, 2)]
    singles = [cotangent[w, 0] for w in range(LEVELS)]

    def beside(level, *others):
        block = after(halves[level // 2], *others)
        return swapped(block, "seq", 1, lambda i, j: needed(j, level + 1))

    def across(level, *others):
        block = after(singles[level], *others)
        return swapped(block, "seq", 2, lambda i, j: needed(j, level))

    def far(level, block):
        return swapped(block, "seq", 1, lambda i, j: needed(j, level))

    positions = jnp.arange(length, dtype=jnp.int32)
    ends = jnp.cumsum(lengths[0])[:-1]
    seg = jnp.sum((positions[:, None] >= ends[None, :]).astype(jnp.int32), axis=1)
    seg_before = jnp.concatenate([jnp.full((1,), -1, jnp.int32), seg[SPAN - 1 : length - 1 : SPAN]])
    seg_pad = jnp.concatenate([jnp.full((reach,), -1, jnp.int32), seg])
    masks = [(seg_pad[k : k + length] == seg) for k in range(reach)]
    mask_cols = [m.astype(F32) for m in masks]
    mask_cols += [jnp.pad(m, (0, reach - k))[reach - k :] for k, m in enumerate(mask_cols)]
    mask_cols = jnp.pad(jnp.stack(mask_cols, axis=1), ((0, 0), (0, LANES - 2 * reach)))

    def conv_params(s_part, bc_part):
        return by_head(s_part), bc_part

    weight_s = jnp.concatenate(
        [by_head(conv_w[:, :INNER]), by_head(conv_b[None, :INNER]), jnp.zeros((3, width), F32)]
    )
    weight_r = jnp.pad(
        lax.dynamic_slice_in_dim(conv_w, INNER + s * own_bc, own_bc, 1), ((0, 0), (0, cols - used))
    )
    bias_r = jnp.pad(
        lax.dynamic_slice_in_dim(conv_b, INNER + s * own_bc, own_bc, 0), (0, cols - used)
    )
    bias = by_head(dt_bias)
    rate = -jnp.exp(by_head(a_log))
    skip_own = by_head(skip)
    gain = by_head(gate_gain)

    half = width // 2

    def over_fsdp(chunk):
        return lax.all_gather(chunk, "fsdp", axis=0, tiled=False)

    def over_dp(held):
        pieces = [held] + [swapped(held, "dp", j) for j in range(1, nd)]
        moves = [
            (piece, i, (d ^ j, None, i, None, None)) for j, piece in enumerate(pieces) for i in range(nf)
        ]
        return pieces, moves

    held_a = over_fsdp(mine[:, :, :half])
    held_b = over_fsdp(mine[:, :, half:cols])
    small_ones = (seg, seg_before, mask_cols, weight_s, weight_r, bias_r, bias, rate, skip_own, gain, theirs)
    held_a, small_ones, halves, singles = together(held_a, small_ones, halves, singles)
    seg, seg_before, mask_cols, weight_s, weight_r, bias_r, bias, rate, skip_own, gain, theirs = small_ones
    near_high, near_low = beside(2, held_a), beside(0, held_a)
    chip3 = across(3, held_a)
    pieces_a, moves_a = over_dp(held_a)
    held_b, moves_a_there, chip3, near_high, xn_pieces = together(
        held_b, [m[0] for m in moves_a], chip3, near_high, xn_pieces
    )
    xn = filled((ns, tok, D), [(p, None, (s ^ k, None, None)) for k, p in enumerate(xn_pieces)])
    xn = xn.reshape(length, D)

    moves_a = [(p,) + m[1:] for p, m in zip(moves_a_there, moves_a)]
    chip2, far3 = across(2, held_b), far(3, chip3)
    pieces_b, moves_b = over_dp(held_b)
    full_a = filled((nd, ns, nf, rows_in, half), moves_a).reshape(D, half)
    full_b = filled((nd, ns, nf, rows_in, cols - half), moves_b).reshape(D, cols - half)
    held_z = over_fsdp(after(mine_z, held_a))

    xn_turned = xn.T
    proj_a = dot(xn, full_a).astype(BF)
    proj_b = dot(xn, after(full_b, proj_a, xn_turned)).astype(BF)
    proj_b, chip2, far3, near_low, held_z = together(proj_b, chip2, far3, near_low, held_z)
    held_out = over_fsdp(after(w_out, held_z))
    pieces_z, moves_z = over_dp(held_z)
    proj = jnp.concatenate([proj_a, proj_b], axis=1)

    proj_r = proj_b[:, width - half :]
    mixer = jnp.concatenate([jnp.zeros((reach, cols - width), BF), proj_r], axis=0)

    def taken(k):
        rows = mixer[k : k + length].astype(F32)
        return rows * mask_cols[:, k : k + 1] if k < reach else rows

    pre_r = bias_r
    for k in range(CONV):
        pre_r = pre_r + taken(k) * weight_r[k]
    bc_own = jax.nn.silu(pre_r).astype(BF)[:, :own_bc]
    bc = [bc_own] + [swapped(bc_own, "seq", k) for k in range(1, ns)]
    chip1, far2 = across(1, *bc), far(2, chip2)
    bc = reordered_by_xor(bc, s)
    b_in = jnp.concatenate(bc[: ns // 2], axis=1)
    c_out = jnp.concatenate(bc[ns // 2 :], axis=1)

    def padded(rows):
        return jnp.pad(rows, ((0, 0), (0, LANES - rows.shape[1])))

    pre_dt = proj_r[:, own_bc : own_bc + heads].astype(F32) + bias
    steps = jax.nn.softplus(pre_dt)
    tails = proj.reshape(blocks, SPAN, cols)[: blocks - 1, SPAN - HALO :, :width]
    operands = (
        seg_before,
        seg[:, None],
        seg[None, :],
        mask_cols,
        proj,
        jnp.concatenate([jnp.zeros((1, HALO, width), BF), tails]),
        weight_s,
        b_in,
        c_out,
        padded(steps),
        steps.T,
        padded(rate[None, :]),
        rate[:, None],
        jnp.repeat(skip_own, HEADDIM)[None, :],
    )
    y, priors = scan_forward(heads, blocks, operands)
    y, chip1, far2, held_out = together(y, chip1, far2, held_out)
    chip0, far1 = across(0, y), far(1, chip1)
    full_z = filled((nd, ns, nf, rows_in, width), moves_z).reshape(D, width)
    moves_out = [(p, i, place[:1] + place[2:]) for p, i, place in over_dp(held_out)[1]]
    proj_z = dot(xn, full_z).astype(BF)
    proj_z, chip0, far1 = together(proj_z, chip0, far1)
    far0 = far(0, chip0)
    q = y * jax.nn.silu(proj_z.astype(F32))
    q_gain = (q * gain).astype(BF)
    lanes = [(a * HEADDIM, b * HEADDIM) for a, b in ranges]
    squares = jnp.stack([jnp.sum(q[:, a:b] * q[:, a:b], axis=1) for a, b in lanes])
    widths = np.array([[(HEADS >> 3 - w) * HEADDIM] for w in range(LEVELS)], np.float32)
    per_level = jnp.sum(counted[:, :, None] * squares[:, None, :], axis=0)
    ratio = lax.rsqrt(over_seq(per_level) / widths + EPS)

    plan = [[w for w in range(LEVELS) if range_level[:, j].min() <= w] for j in range(len(lanes))]
    out_rows = width // nd
    range_of = [next(j for j, (a, b) in enumerate(lanes) if a <= i * out_rows < b) for i in range(nd)]
    here = jnp.stack([s, d]).astype(jnp.int32)
    smem = pl.BlockSpec(memory_space=pltpu.SMEM)
    cot_pieces = [cotangent, near_low, near_high, chip0, chip1, chip2, chip3, far0, far1, far2, far3]
    cot_specs = [pl.BlockSpec((LEVELS, 1, tok, TILE), lambda i: (0, 0, 0, i))]
    cot_specs += [pl.BlockSpec((2, tok, TILE), lambda i: (0, 0, i))] * 2
    cot_specs += [pl.BlockSpec((tok, TILE), lambda i: (0, i))] * (2 * LEVELS)
    where = [[(0, (w, 0)), (1 + w // 2, (w % 2,)), (3 + w, ()), (3 + LEVELS + w, ())] for w in range(LEVELS)]
    upper, *grad_out = call(
        functools.partial(upper_kernel, where, plan, nd, tok, ns),
        grid=(D // TILE,),
        in_specs=[
            smem,
            smem,
            smem,
            pl.BlockSpec((LEVELS, length), lambda i: (0, 0)),
            pl.BlockSpec((width, length), lambda i: (0, 0)),
        ]
        + cot_specs,
        out_specs=[pl.BlockSpec((len(lanes), length, TILE), lambda i: (0, 0, i))]
        + [pl.BlockSpec((out_rows, TILE), lambda i: (0, i))] * nd,
        out_shape=[jax.ShapeDtypeStruct((len(lanes), length, D), BF)]
        + [jax.ShapeDtypeStruct((out_rows, D), BF)] * nd,
        scratch_shapes=[pltpu.VMEM((length, LANES), F32)],
        name="upper",
    )(here, jnp.asarray(range_of, jnp.int32), counted, ratio, q_gain.T, *cot_pieces)
    grad_out = [g.reshape(nf, out_rows // nf, D) for g in grad_out]
    out_got = dp_terms(grad_out[1:])

    full_out = filled((nd, nf) + w_out.shape, moves_out).reshape(width, D)
    full_out, upper = together(full_out, upper)
    *shares, inner = call(
        functools.partial(products_kernel, where, plan, lanes, tok, ns),
        grid=(D // TILE,),
        in_specs=[
            smem,
            smem,
            pl.BlockSpec((length, width), lambda i: (0, 0)),
            pl.BlockSpec((width, TILE), lambda i: (0, i)),
        ]
        + cot_specs,
        out_specs=[pl.BlockSpec((len(lanes), tok, TILE), lambda i: (0, 0, i))] * ns
        + [pl.BlockSpec((LEVELS, length), lambda i: (0, 0))],
        out_shape=[jax.ShapeDtypeStruct((len(lanes), tok, D), BF)] * ns
        + [jax.ShapeDtypeStruct((LEVELS, length), F32)],
        scratch_shapes=[pltpu.VMEM((LEVELS, length, LANES), F32)],
        name="products",
    )(here, counted, q_gain, full_out, *cot_pieces)
    means = over_seq(inner) / widths
    shares = [shares[0]] + [swapped(after(shares[k], means), "seq", k) for k in range(1, ns)]

    starts = [a for a, _ in lanes]
    wide = min(min(b - a for a, b in lanes), TILE)
    cols_of = pl.BlockSpec((length, wide), lambda i: (0, i))
    scalars = pl.BlockSpec((LEVELS, length), lambda i: (0, 0))
    dy, dz, grad_gate = call(
        functools.partial(gate_kernel, starts, wide),
        grid=(width // wide,),
        in_specs=[
            smem,
            pl.BlockSpec((1, length, D), lambda i: (tile_range(starts, wide, i), 0, 0)),
            pl.BlockSpec((wide, D), lambda i: (i, 0)),
            cols_of,
            cols_of,
            pl.BlockSpec((1, wide), lambda i: (0, i)),
            scalars,
            scalars,
        ],
        out_specs=[cols_of, cols_of, pl.BlockSpec((8, wide), lambda i: (0, i))],
        out_shape=[
            jax.ShapeDtypeStruct((length, width), BF),
            jax.ShapeDtypeStruct((length, width), BF),
            jax.ShapeDtypeStruct((8, width), F32),
        ],
        scratch_shapes=[pltpu.VMEM((len(lanes), length, LANES), F32)],
        name="gate_backward",
    )(counted, upper, full_out, y, proj_z, gain[None], ratio, means)
    grad_gate = grad_gate[0]

    def in_terms(dproj, at):
        out = row_terms(xn_turned, dproj, at, nd, ns, nf)
        return out.reshape(nf, ns * rows_in, dproj.shape[1])

    z_other = [in_terms(dz, d ^ k) for k in range(1, nd)]
    z_got = dp_terms(z_other)
    dy, out_got, shares[1] = together(after(dy, *z_other), out_got, shares[1])
    out_kept, out_sent = fsdp_half(grad_out[0], out_got)
    dy = after(dy, out_sent)
    out_half = swapped(out_sent, "fsdp", 1)

    dproj_s, dbc, ddt, drate, dsum = scan_backward(heads, blocks, operands, y, priors, dy)
    dproj_s, dbc, out_half, shares[2] = together(dproj_s, dbc, out_half, shares[2])
    out_pair = fsdp_rest(out_kept, out_half)
    dbc = dbc.astype(BF)
    dbc_parts = reordered_by_xor([dbc[:, j * own_bc : (j + 1) * own_bc] for j in range(ns)], s)
    dbc_got = [swapped(dbc_parts[k], "seq", k) for k in range(1, ns)]
    cut = width // 2
    left_in = dproj_s[:, :cut]
    left_other = [in_terms(left_in, d ^ k) for k in range(1, nd)]
    left_got = dp_terms(left_other)
    dbc_own = after(dbc_parts[0].astype(F32), *left_other)
    for got in dbc_got:
        dbc_own = dbc_own + got.astype(F32)
    dz_late, z_got = together(after(dz, *left_other), z_got)
    z_kept, z_sent = fsdp_half(in_terms(dz_late, d), z_got)
    z_half = swapped(z_sent, "fsdp", 1)
    dpre = jnp.pad(dbc_own, ((0, 0), (0, cols - used))) * silu_slope(pre_r)
    grad_b_r = jnp.sum(dpre, axis=0)[:own_bc]
    grad_w_r = jnp.stack([jnp.sum(dpre * taken(k), axis=0) for k in range(CONV)])[:, :own_bc]
    dmixer = dpre * weight_r[reach]
    for k in range(reach):
        back = reach - k
        later = (dpre * mask_cols[:, k : k + 1])[back:]
        dmixer = dmixer + jnp.pad(later, ((0, back), (0, 0))) * weight_r[k]
    dpre_dt = ddt[:, :heads] * jax.nn.sigmoid(pre_dt)
    dproj_r = jnp.concatenate(
        [dmixer[:, :own_bc].astype(BF), dpre_dt.astype(BF), jnp.zeros((length, pad_cols), BF)], axis=1
    )
    dxn = input_grad(dz, dproj_s, after(dproj_r, z_sent), full_z, full_a, full_b, ns, tok)
    beside_near = swapped(picked(dxn, s ^ 1), "seq", 1)
    beside_far = swapped(picked(dxn, s ^ 3), "seq", 1)

    dproj_r, left_got, dxn, out_pair = together(dproj_r, left_got, dxn, out_pair)
    right_in = jnp.concatenate([dproj_s[:, cut:], dproj_r], axis=1)
    right_other = [in_terms(right_in, d ^ k) for k in range(1, nd)]
    right_got = dp_terms(right_other)
    own_left = in_terms(after(left_in, *right_other), d)
    own_right = in_terms(after(right_in, own_left), d)
    left_kept, left_sent = fsdp_half(own_left, left_got)
    left_half = swapped(left_sent, "fsdp", 1)
    flat = flattened(
        [
            jnp.concatenate([dsum[:CONV], grad_w_r], axis=1).reshape(-1),
            dsum[CONV],
            grad_b_r,
            grad_gate,
            jnp.sum(dpre_dt, axis=0),
            drate[0, :heads] * rate,
            jnp.sum(dsum[CONV + 1].reshape(heads, HEADDIM), axis=1),
        ]
    )
    near = picked(dxn, s).astype(F32) + beside_near.astype(F32)
    far = (picked(dxn, s ^ 2).astype(F32) + after(beside_far, own_right).astype(F32)).astype(BF)
    dxn_across = swapped(far, "seq", 2)
    far, z_half = together(far, z_half)
    z_pair = fsdp_rest(z_kept, z_half)
    right_got, left_half = together(right_got, left_half)
    left_pair = fsdp_rest(left_kept, left_half)
    right_kept, right_sent = fsdp_half(own_right, right_got)
    right_half = swapped(right_sent, "fsdp", 1)

    dxn_own = near + after(dxn_across, right_sent).astype(F32)
    grad_norm = jnp.sum(dxn_own * own_x * scale, axis=0)
    scaled = norm_gain * dxn_own
    dx = scale * scaled - own_x * scale**3 * jnp.mean(own_x * scaled, axis=-1, keepdims=True)
    dx = dx + jnp.sum(after(cotangent, right_sent)[:, 0].astype(F32), axis=0)
    flat = jnp.concatenate([flat, grad_norm.reshape(-1, LANES)])
    flat = butterfly(flat, "dp")
    dx = dx.astype(BF)

    z_pair, left_pair, right_half, flat, dx = together(z_pair, left_pair, right_half, flat, dx)
    right_pair = fsdp_rest(right_kept, right_half)

    def whole_sum(pair):
        total = (pair[0].astype(F32) + pair[1].astype(F32)).astype(BF)
        return total.reshape(ns, rows_in, total.shape[1])

    early = jnp.concatenate([whole_sum(z_pair), whole_sum(left_pair)], axis=2)
    early_got = [picked(early, s)] + [swapped(picked(early, s ^ k), "seq", k) for k in range(1, ns)]
    mixed = call(
        functools.partial(
            mixed_kernel,
            [[j for j in range(len(lanes)) if range_level[:, j].min() <= w] for w in range(LEVELS)],
            ns,
            tok,
        ),
        grid=(D // TILE,),
        in_specs=[
            smem,
            smem,
            pl.BlockSpec((LEVELS, length), lambda i: (0, 0)),
            pl.BlockSpec((tok, TILE), lambda i: (0, i)),
        ]
        + [pl.BlockSpec((len(lanes), tok, TILE), lambda i: (0, 0, i))] * ns,
        out_specs=pl.BlockSpec((LEVELS, tok, TILE), lambda i: (0, 0, i)),
        out_shape=jax.ShapeDtypeStruct((LEVELS, tok, D), BF),
        name="mixed",
    )(here, theirs, ratio, tokens[0], *after(shares, right_half))[:, None]
    flat = butterfly(flat, "fsdp")
    early_got, right_pair, mixed = together(early_got, right_pair, mixed)
    late = whole_sum(right_pair)
    late_got = [picked(late, s)] + [swapped(picked(late, s ^ k), "seq", k) for k in range(1, ns)]
    early_got, late_got = together(early_got, late_got)
    early = placed_by_xor(early_got, s)
    late = placed_by_xor(late_got, s)
    got_z = early[:, :, :width]
    got_x = jnp.concatenate([early[:, :, width:], late], axis=2)
    sum_out = out_pair[0].astype(F32) + out_pair[1].astype(F32)


    sum_in = jnp.concatenate(
        [
            from_groups(got_z),
            from_groups(got_x[:, :, :width]),
            jnp.transpose(got_x[:, :, width:used], (1, 0, 2)).reshape(rows_in, 2 * STATE),
        ],
        axis=1,
    ).astype(F32)
    sum_dt = from_groups(got_x[:, :, used : used + heads]).astype(F32)

    sizes = [CONV * used, used, width, heads, heads, heads]
    filling = -sum(sizes) % 1024
    sizes += [filling, D]
    every = seq_gather(flat, s).reshape(ns, -1)
    starts = np.cumsum([0] + sizes)
    pieces = [every[:, a : a + n] for a, n in zip(starts, sizes)]

    def heads_back(rows):
        lead = rows.shape[1:-1]
        cut = rows.reshape((ns,) + lead + (nd, rows.shape[-1] // nd))
        order = tuple(range(1, 1 + len(lead))) + (1 + len(lead), 0, 2 + len(lead))
        return jnp.transpose(cut, order).reshape(lead + (-1,))

    conv_rows = pieces[0].reshape(ns, CONV, used)
    conv_all = jnp.concatenate(
        [
            heads_back(conv_rows[:, :, :width]),
            jnp.transpose(conv_rows[:, :, width:], (1, 0, 2)).reshape(CONV, 2 * STATE),
        ],
        axis=1,
    )
    bias_all = jnp.concatenate([heads_back(pieces[1][:, :width]), pieces[1][:, width:].reshape(-1)])
    return (
        mixed,
        dx[None],
        jnp.sum(pieces[7], axis=0),
        sum_in,
        sum_dt,
        conv_all,
        bias_all,
        heads_back(pieces[3]),
        heads_back(pieces[4]),
        heads_back(pieces[5]),
        heads_back(pieces[2]),
        sum_out,
    )


def solution(mesh):
    rows = P(("dp", "seq", "fsdp"), None)
    held = P(("dp", "fsdp"), "seq", None)
    levels = P(None, ("dp", "fsdp"), "seq", None)
    placed = (held, P(("dp", "fsdp"), None), P(), rows, rows, P(), P(), P(), P(), P(), P(), rows, levels)
    return jax.shard_map(
        shards,
        mesh=mesh,
        in_specs=placed,
        out_specs=(levels, held, P(), rows, rows, P(), P(), P(), P(), P(), P(), rows),
        check_vma=False,
    )
```

```python
import functools

import jax
import jax.numpy as jnp
import numpy as np
from jax import lax
from jax.experimental import pallas as pl
from jax.experimental.pallas import tpu as pltpu
from jax.sharding import PartitionSpec as P

D = 2048
HEADS = 64
HEADDIM = 64
STATE = 128
CONV = 4
SPAN = 128
INNER = 4096
EPS = 1e-05
LEVELS = 4
BF = jnp.bfloat16
F32 = jnp.float32
HIGH = lax.Precision.HIGHEST
LANES = 128
HALO = 16
TILE = 256
VMEM_LIMIT = 48 * 1024 * 1024


def dot(a, b, dims=((1,), (0,)), precision=None):
    return lax.dot_general(a, b, (dims, ((), ())), preferred_element_type=F32, precision=precision)


def silu_slope(v):
    sig = jax.nn.sigmoid(v)
    return sig * (1.0 + v * (1.0 - sig))


def level_of(head):
    return 0 if head < 8 else 1 if head < 16 else 2 if head < 32 else 3


def swapped(value, axis, k, keep=None):
    pairs = [(i, i ^ k) for i in range(lax.axis_size(axis))]
    if keep is not None:
        pairs = [p for p in pairs if keep(*p)]
    return lax.ppermute(value, axis, pairs)


def after(value, *others):
    return lax.optimization_barrier((value,) + others)[0]


def together(*values):
    return lax.optimization_barrier(values)


def flattened(vectors):
    flat = jnp.concatenate(vectors)
    return jnp.pad(flat, (0, -flat.shape[0] % 1024)).reshape(-1, LANES)


def butterfly(value, axis):
    k = 1
    while k < lax.axis_size(axis):
        value = value + swapped(value, axis, k)
        k *= 2
    return value


def picked(array, index):
    return lax.dynamic_index_in_dim(array, index, 0, keepdims=False)


def placed_by_xor(pieces, here):
    out = jnp.zeros((len(pieces),) + pieces[0].shape, pieces[0].dtype)
    for k, piece in enumerate(pieces):
        out = lax.dynamic_update_index_in_dim(out, piece, here ^ k, 0)
    return out


def seq_gather(block, here):
    return placed_by_xor([block] + [swapped(block, "seq", k) for k in range(1, 4)], here)


def reordered_by_xor(pieces, here):
    k = 1
    while k < len(pieces):
        flip = (here & k) > 0
        pieces = [jnp.where(flip, pieces[j ^ k], piece) for j, piece in enumerate(pieces)]
        k *= 2
    return pieces


def seq_exchange(pieces, here):
    got = [picked(pieces, here)]
    for k in range(1, pieces.shape[0]):
        got.append(swapped(picked(pieces, here ^ k), "seq", k))
    return placed_by_xor(got, here)


def call(kernel, **kwargs):
    return pl.pallas_call(
        kernel,
        compiler_params=pltpu.CompilerParams(vmem_limit_bytes=VMEM_LIMIT),
        cost_estimate=pl.CostEstimate(flops=1, bytes_accessed=1, transcendentals=0),
        **kwargs,
    )


def filled(shape, moves):
    arrays, plan, rows = [], [], []
    block = tuple(size if index is None else 1 for size, index in zip(shape, moves[0][2]))
    for piece, lead, place in moves:
        at = next((i for i, a in enumerate(arrays) if a is piece), len(arrays))
        if at == len(arrays):
            arrays.append(piece)
        plan.append((at, lead))
        rows.append(jnp.stack([jnp.asarray(0 if n is None else n, jnp.int32) for n in place]))

    def kernel(index_ref, *refs):
        pieces, out = refs[:-1], refs[-1]
        for m, (at, lead) in enumerate(plan):

            @pl.when(pl.program_id(0) == m)
            def _():
                value = pieces[at][...] if lead is None else pieces[at][lead]
                out[...] = value.reshape(block)

    return call(
        kernel,
        grid_spec=pltpu.PrefetchScalarGridSpec(
            num_scalar_prefetch=1,
            grid=(len(plan),),
            in_specs=[
                pl.BlockSpec(a.shape, lambda i, t, n=a.ndim: (0,) * n) for a in arrays
            ],
            out_specs=pl.BlockSpec(
                block, lambda i, t: tuple(t[i, n] for n in range(len(shape)))
            ),
        ),
        out_shape=jax.ShapeDtypeStruct(shape, arrays[0].dtype),
        name="filled",
    )(jnp.stack(rows), *arrays)


def terms_kernel(ns, nf, at_ref, left_ref, right_ref, out_ref):
    value = dot(left_ref[...], right_ref[...]).astype(BF)
    rows = value.shape[0] // (ns * nf)
    for i in range(ns):
        for k in range(nf):
            out_ref[k, i] = value[(i * nf + k) * rows : (i * nf + k + 1) * rows]


def row_terms(turned, right, at, nd, ns, nf, first, columns):
    depth = turned.shape[1]
    rows = turned.shape[0] // nd
    wide = TILE if columns % TILE == 0 else LANES
    return call(
        functools.partial(terms_kernel, ns, nf),
        grid_spec=pltpu.PrefetchScalarGridSpec(
            num_scalar_prefetch=1,
            grid=(columns // wide,),
            in_specs=[
                pl.BlockSpec((rows, depth), lambda i, t: (t[0], 0)),
                pl.BlockSpec((depth, wide), lambda i, t: (0, i + first // wide)),
            ],
            out_specs=pl.BlockSpec((nf, ns, rows // (nf * ns), wide), lambda i, t: (0, 0, 0, i)),
        ),
        out_shape=jax.ShapeDtypeStruct((nf, ns, rows // (nf * ns), columns), BF),
        name="row_terms",
    )(at.astype(jnp.int32)[None], turned, right)


def input_grad_kernel(blocks, dz_ref, ds_ref, dr_ref, wz_ref, wa_ref, wb_ref, out_ref):
    half = wa_ref.shape[1]
    rest = ds_ref.shape[1] - half
    columns = ((1,), (1,))
    total = dot(dz_ref[...], wz_ref[...], columns)
    total = total + dot(ds_ref[:, :half], wa_ref[...], columns)
    total = total + dot(ds_ref[:, half:], wb_ref[:, :rest], columns)
    total = total + dot(dr_ref[...], wb_ref[:, rest:], columns)
    total = total.astype(BF)
    tok = total.shape[0] // blocks
    for i in range(blocks):
        out_ref[i] = total[i * tok : (i + 1) * tok]


def input_grad(dz, ds, dr, wz, wa, wb, blocks, tok):
    def whole(a):
        return pl.BlockSpec(a.shape, lambda i: (0, 0))

    def rows(a):
        return pl.BlockSpec((TILE, a.shape[1]), lambda i: (i, 0))

    return call(
        functools.partial(input_grad_kernel, blocks),
        grid=(wz.shape[0] // TILE,),
        in_specs=[whole(dz), whole(ds), whole(dr), rows(wz), rows(wa), rows(wb)],
        out_specs=pl.BlockSpec((blocks, tok, TILE), lambda i: (0, 0, i)),
        out_shape=jax.ShapeDtypeStruct((blocks, tok, wz.shape[0]), BF),
        name="input_grad",
    )(dz, ds, dr, wz, wa, wb)


def tri(rows_first):
    a = lax.broadcasted_iota(jnp.int32, (SPAN, SPAN), 0)
    b = lax.broadcasted_iota(jnp.int32, (SPAN, SPAN), 1)
    return (a >= b) if rows_first else (a <= b)


def pair_of(lo, cols, p):
    return jnp.where(lo, cols[:, 2 * p : 2 * p + 1], cols[:, 2 * p + 1 : 2 * p + 2])


def decays(segc, segr, segp, dt, rate):
    cum = dot(tri(True).astype(F32), dt * rate, precision=HIGH)
    last = cum[SPAN - 1 : SPAN, :]
    keep = jnp.where(segc == segp, jnp.exp(cum), 0.0)
    to_end = jnp.where(segc == segr[:, SPAN - 1 : SPAN], jnp.exp(last - cum), 0.0)
    return cum, cum.T, keep, to_end


def spread_columns(ref, first, count):
    return [jnp.broadcast_to(ref[:, first + k : first + k + 1], (SPAN, LANES)) for k in range(count)]


def taps(ext, masks, at):
    terms = [ext[pl.ds(HALO - CONV + 1 + k, SPAN), at] for k in range(CONV)]
    return [t * m for t, m in zip(terms, masks)] + terms[CONV - 1 :]


def convolved(terms, weight_ref, at):
    total = weight_ref[CONV : CONV + 1, at] + terms[0] * weight_ref[0:1, at]
    for k in range(1, CONV):
        total = total + terms[k] * weight_ref[k : k + 1, at]
    return total


def forward_kernel(
    heads,
    segp_ref,
    segc_ref,
    segr_ref,
    mask_ref,
    in_a_ref,
    in_b_ref,
    halo_ref,
    weight_ref,
    b_ref,
    c_ref,
    dt_ref,
    rate_ref,
    skip_ref,
    y_ref,
    prior_ref,
    carry,
    to_end_u,
    ext,
):
    block = pl.program_id(0)
    width = heads * HEADDIM

    @pl.when(block == 0)
    def _():
        carry[...] = jnp.zeros_like(carry)

    prior_ref[0] = carry[...]
    ext[0:HALO] = halo_ref[0].astype(F32)
    half = in_a_ref.shape[1]
    ext[HALO:, :half] = in_a_ref[...].astype(F32)
    ext[HALO:, half:] = in_b_ref[:, : ext.shape[1] - half].astype(F32)
    segc, segr = segc_ref[...], segr_ref[...]
    dt = dt_ref[...]
    cum, cumr, keep, to_end = decays(segc, segr, segp_ref[block], dt, rate_ref[...])
    bm, cm = b_ref[...], c_ref[...]
    mixing = dot(cm, bm, ((1,), (1,)))
    mixing = jnp.where(tri(True) & (segc == segr), mixing, 0.0)
    masks = spread_columns(mask_ref, 0, CONV - 1)
    lo = lax.broadcasted_iota(jnp.int32, (SPAN, LANES), 1) < HEADDIM
    for p in range(heads // 2):
        at = slice(p * LANES, (p + 1) * LANES)
        pre = convolved(taps(ext, masks, at), weight_ref, at)
        x2 = pre * jax.nn.sigmoid(pre)
        u2 = x2 * pair_of(lo, dt, p)
        sides = (jnp.where(lo, u2, 0.0).astype(BF), jnp.where(lo, 0.0, u2).astype(BF))
        total = dot(cm, carry[:, at].astype(BF)) * pair_of(lo, keep, p) + skip_ref[:, at] * x2
        for k in range(2):
            h = 2 * p + k
            decay = jnp.exp(jnp.minimum(cum[:, h : h + 1] - cumr[h : h + 1, :], 0.0))
            total = total + dot((decay * mixing).astype(BF), sides[k])
        y_ref[:, at] = total
        to_end_u[:, at] = (u2 * pair_of(lo, to_end, p)).astype(BF)
    fresh = dot(bm, to_end_u[...], ((0,), (0,)))
    lo_row = lax.broadcasted_iota(jnp.int32, (1, LANES), 1) < HEADDIM
    for p in range(heads // 2):
        at = slice(p * LANES, (p + 1) * LANES)
        factor = pair_of(lo_row, keep[SPAN - 1 : SPAN, :], p)
        carry[:, at] = factor * carry[:, at] + fresh[:, at]


def split_dot(value, ones):
    high = value.astype(BF)
    low = (value - high.astype(F32)).astype(BF)
    return dot(high, ones) + dot(low, ones)


def backward_kernel(
    heads,
    segp_ref,
    segc_ref,
    segr_ref,
    mask_ref,
    in_a_ref,
    in_b_ref,
    halo_ref,
    weight_ref,
    b_ref,
    c_ref,
    dt_ref,
    rate_ref,
    skip_ref,
    y_ref,
    prior_ref,
    dy_ref,
    din_ref,
    dbc_ref,
    ddt_ref,
    drate_ref,
    dsum_ref,
    dcarry,
    after_state,
    keep_dy,
    to_end_u,
    slopes,
    along,
    ext,
    dext,
):
    step = pl.program_id(0)
    block = pl.num_programs(0) - 1 - step

    @pl.when(step == 0)
    def _():
        dcarry[...] = jnp.zeros_like(dcarry)
        after_state[...] = jnp.zeros_like(after_state)
        drate_ref[...] = jnp.zeros_like(drate_ref)
        dsum_ref[...] = jnp.zeros_like(dsum_ref)
        dext[SPAN:] = jnp.zeros((HALO, dext.shape[1]), F32)

    ext[0:HALO] = halo_ref[0].astype(F32)
    half = in_a_ref.shape[1]
    ext[HALO:, :half] = in_a_ref[...].astype(F32)
    ext[HALO:, half:] = in_b_ref[:, : ext.shape[1] - half].astype(F32)
    segc, segr = segc_ref[...], segr_ref[...]
    dt = dt_ref[...]
    cum, cumr, keep, to_end = decays(segc, segr, segp_ref[block], dt, rate_ref[...])
    bm, cm = b_ref[...], c_ref[...]
    allowed = tri(False) & (segc == segr)
    mixing = jnp.where(allowed, dot(bm, cm, ((1,), (1,))), 0.0)
    masks = spread_columns(mask_ref, 0, CONV - 1)
    moved = spread_columns(mask_ref, CONV - 1, CONV - 1)
    lo = lax.broadcasted_iota(jnp.int32, (SPAN, LANES), 1) < HEADDIM
    dmixing = jnp.zeros((SPAN, SPAN), F32)
    for p in range(heads // 2):
        at = slice(p * LANES, (p + 1) * LANES)
        terms = taps(ext, masks, at)
        pre = convolved(terms, weight_ref, at)
        sig = jax.nn.sigmoid(pre)
        x2 = pre * sig
        dt2 = pair_of(lo, dt, p)
        u2 = x2 * dt2
        dyb = dy_ref[:, at]
        dy2 = dyb.astype(F32)
        skip = skip_ref[:, at]
        te2 = pair_of(lo, to_end, p)
        u_sides = (jnp.where(lo, u2, 0.0).astype(BF), jnp.where(lo, 0.0, u2).astype(BF))
        dy_sides = (jnp.where(lo, dy2, 0.0).astype(BF), jnp.where(lo, 0.0, dy2).astype(BF))
        du = te2 * dot(bm, dcarry[:, at].astype(BF))
        for k in range(2):
            h = 2 * p + k
            decay = jnp.exp(jnp.minimum(cumr[h : h + 1, :] - cum[:, h : h + 1], 0.0))
            du = du + dot((decay * mixing).astype(BF), dy_sides[k])
            dmixing = dmixing + decay * dot(u_sides[k], dyb, ((1,), (1,)))
        keep_dy[:, at] = (pair_of(lo, keep, p) * dy2).astype(BF)
        to_end_u[:, at] = (te2 * u2).astype(BF)
        slopes[:, at] = dy2 * (y_ref[:, at] - skip * x2) - u2.astype(BF).astype(F32) * du
        along[:, at] = x2 * du
        dpre = (dt2 * du + skip * dy2) * (sig * (1.0 + pre * (1.0 - sig)))
        dext[0:SPAN, at] = dpre
        for k in range(CONV):
            dsum_ref[k : k + 1, at] += jnp.sum(dpre * terms[k], axis=0, keepdims=True)
        dsum_ref[CONV : CONV + 1, at] += jnp.sum(dpre, axis=0, keepdims=True)
        dsum_ref[CONV + 1 : CONV + 2, at] += jnp.sum(dy2 * x2, axis=0, keepdims=True)
        din = dpre * weight_ref[CONV - 1 : CONV, at]
        for k in range(CONV - 1):
            later = dext[pl.ds(CONV - 1 - k, SPAN), at]
            din = din + later * moved[k] * weight_ref[k : k + 1, at]
        din_ref[:, at] = din.astype(BF)
    dext[SPAN:] = dext[0:HALO]
    dmixing = jnp.where(allowed, dmixing, 0.0).astype(BF)
    dstate = dcarry[...].astype(BF)
    prior = prior_ref[0]
    dbc_ref[:, :STATE] = dot(dmixing, cm) + dot(to_end_u[...], dstate, ((1,), (1,)))
    dbc_ref[:, STATE:] = dot(dmixing, bm, ((0,), (0,))) + dot(
        keep_dy[...], prior.astype(BF), ((1,), (1,))
    )
    width = heads * HEADDIM
    ones = (
        lax.broadcasted_iota(jnp.int32, (width, LANES), 0) // HEADDIM
        == lax.broadcasted_iota(jnp.int32, (width, LANES), 1)
    ).astype(BF)
    at_end = jnp.sum(dcarry[...] * after_state[...], axis=0, keepdims=True)
    at_end = split_dot(jnp.broadcast_to(at_end, (16, width)), ones)[:1]
    dcum = split_dot(slopes[...], ones)
    da = dot(tri(False).astype(F32), dcum, precision=HIGH) + at_end
    ddt_ref[...] = rate_ref[...] * da + split_dot(along[...], ones)
    drate_ref[...] += jnp.sum(dt * da, axis=0, keepdims=True)
    fresh = dot(cm, keep_dy[...], ((0,), (0,)))
    lo_row = lax.broadcasted_iota(jnp.int32, (1, LANES), 1) < HEADDIM
    for p in range(heads // 2):
        at = slice(p * LANES, (p + 1) * LANES)
        factor = pair_of(lo_row, keep[SPAN - 1 : SPAN, :], p)
        dcarry[:, at] = factor * dcarry[:, at] + fresh[:, at]
    after_state[...] = prior


def scan_specs(heads, at, in_widths):
    width = heads * HEADDIM

    def rows(n):
        return pl.BlockSpec((SPAN, n), lambda i: (at(i), 0))

    def whole(*shape):
        return pl.BlockSpec(shape, lambda i: (0,) * len(shape))

    ins = [
        pl.BlockSpec(memory_space=pltpu.SMEM),
        rows(1),
        pl.BlockSpec((1, SPAN), lambda i: (0, at(i))),
        rows(LANES),
        rows(in_widths[0]),
        rows(in_widths[1]),
        pl.BlockSpec((1, HALO, width), lambda i: (at(i), 0, 0)),
        whole(8, width),
        rows(STATE),
        rows(STATE),
        rows(LANES),
        whole(1, LANES),
        whole(1, width),
    ]
    prior = pl.BlockSpec((1, STATE, width), lambda i: (at(i), 0, 0))
    return rows, whole, ins, prior


def scan_forward(heads, blocks, operands):
    rows, whole, ins, prior = scan_specs(heads, lambda i: i, [operands[n].shape[1] for n in (4, 5)])
    width = heads * HEADDIM
    return call(
        functools.partial(forward_kernel, heads),
        grid=(blocks,),
        in_specs=ins,
        out_specs=[rows(width), prior],
        out_shape=[
            jax.ShapeDtypeStruct((blocks * SPAN, width), F32),
            jax.ShapeDtypeStruct((blocks, STATE, width), F32),
        ],
        scratch_shapes=[
            pltpu.VMEM((STATE, width), F32),
            pltpu.VMEM((SPAN, width), BF),
            pltpu.VMEM((HALO + SPAN, width), F32),
        ],
        name="scan_forward",
    )(*operands)


def scan_backward(heads, blocks, operands, y, priors, dy):
    rows, whole, ins, prior = scan_specs(
        heads, lambda i: blocks - 1 - i, [operands[n].shape[1] for n in (4, 5)]
    )
    width = heads * HEADDIM
    return call(
        functools.partial(backward_kernel, heads),
        grid=(blocks,),
        in_specs=ins + [rows(width), prior, rows(width)],
        out_specs=[rows(width), rows(2 * STATE), rows(LANES), whole(1, LANES), whole(8, width)],
        out_shape=[
            jax.ShapeDtypeStruct((blocks * SPAN, width), BF),
            jax.ShapeDtypeStruct((blocks * SPAN, 2 * STATE), F32),
            jax.ShapeDtypeStruct((blocks * SPAN, LANES), F32),
            jax.ShapeDtypeStruct((1, LANES), F32),
            jax.ShapeDtypeStruct((8, width), F32),
        ],
        scratch_shapes=[
            pltpu.VMEM((STATE, width), F32),
            pltpu.VMEM((STATE, width), F32),
            pltpu.VMEM((SPAN, width), BF),
            pltpu.VMEM((SPAN, width), BF),
            pltpu.VMEM((SPAN, width), F32),
            pltpu.VMEM((SPAN, width), F32),
            pltpu.VMEM((HALO + SPAN, width), F32),
            pltpu.VMEM((SPAN + HALO, width), F32),
        ],
        name="scan_backward",
    )(*operands, y, priors, dy)


def as_columns(rows):
    few, tokens = rows.shape
    return jnp.concatenate([rows, jnp.zeros((LANES - few, tokens), F32)]).T


def level_block(pieces, spot):
    piece, lead = spot
    return pieces[piece][lead + (slice(None), slice(None))].astype(F32)


def upper_kernel(where, plan, nd, tok, ns, here_ref, range_ref, count_ref, ratio_ref, q_turned, *refs):
    count = 3 + 2 * LEVELS
    pieces, outs = refs[:count], refs[count:]
    upper_ref, grad_refs, coefs = outs[0], outs[1 : 2 * nd], outs[2 * nd]

    @pl.when(pl.program_id(0) == 0)
    def _():
        rows = [count_ref[j, w] * ratio_ref[w : w + 1, :] for j in range(len(plan)) for w in range(LEVELS)]
        coefs[...] = as_columns(jnp.concatenate(rows))

    for k in range(ns):
        at = here_ref[0] ^ k
        rows = pl.ds(pl.multiple_of(at * tok, tok), tok)
        levels = [level_block(pieces, where[w][k]) for w in range(LEVELS)]
        for j in range(len(plan)):
            total = None
            for w in plan[j]:
                n = j * LEVELS + w
                term = coefs[rows, n : n + 1] * levels[w]
                total = term if total is None else total + term
            upper_ref[j, rows, :] = total.astype(BF)
    count = q_turned.shape[0] // nd
    for k in range(nd):
        index = here_ref[1] ^ k
        rows = pl.ds(pl.multiple_of(index * count, count), count)
        value = dot(q_turned[rows, :], upper_ref[range_ref[index]]).astype(BF)
        if k:
            grad_refs[2 * k - 1][...] = value[: count // 2]
            grad_refs[2 * k][...] = value[count // 2 :]
        else:
            grad_refs[0][...] = value


def products_kernel(where, plan, lanes, tok, ns, nd, here_ref, count_ref, q_ref, *refs):
    count = 3 + 2 * LEVELS
    parts, pieces, outs = refs[:nd], refs[nd : nd + count], refs[nd + count :]
    prod_refs, inner_ref, w_ref, sums = outs[:ns], outs[ns], outs[ns + 1], outs[ns + 2]
    step = pl.program_id(0)
    rows_of = w_ref.shape[0] // nd
    for k, part in enumerate(parts):
        at = pl.multiple_of((here_ref[1] ^ k) * rows_of, rows_of)
        w_ref[pl.ds(at, rows_of), :] = part[...].reshape(rows_of, w_ref.shape[1])

    @pl.when(step == 0)
    def _():
        sums[...] = jnp.zeros_like(sums)

    for k in range(ns):
        at = here_ref[0] ^ k
        rows = pl.ds(pl.multiple_of(at * tok, tok), tok)
        values = [dot(q_ref[rows, a:b], w_ref[a:b, :]) for a, b in lanes]
        for j, value in enumerate(values):
            prod_refs[k][j] = value.astype(BF)
        for w in range(LEVELS):
            total = None
            for j in range(len(lanes)):
                if w in plan[j]:
                    term = values[j] * count_ref[j, w]
                    total = term if total is None else total + term
            part = total * level_block(pieces, where[w][k])
            folded = part[:, :LANES]
            for c in range(LANES, part.shape[1], LANES):
                folded = folded + part[:, c : c + LANES]
            sums[w, rows, :] += folded

    @pl.when(step == pl.num_programs(0) - 1)
    def _():
        lane = lax.broadcasted_iota(jnp.int32, sums.shape[1:], 1)
        total = jnp.zeros(sums.shape[1:], F32)
        for w in range(LEVELS):
            total = jnp.where(lane == w, jnp.sum(sums[w], axis=1, keepdims=True), total)
        inner_ref[...] = total.T[:LEVELS]


def gate_kernel(
    starts, wide, count_ref, upper_ref, w_ref, y_ref, z_ref, gain_ref, ratio_ref, mean_ref, dy_ref, dz_ref, grad_ref, coefs
):
    step = pl.program_id(0)

    @pl.when(step == 0)
    def _():
        cubes = ratio_ref[...] * ratio_ref[...] * ratio_ref[...] * mean_ref[...]
        rows = []
        for j in range(len(starts)):
            total = cubes[0:1] * count_ref[j, 0]
            for w in range(1, LEVELS):
                total = total + cubes[w : w + 1] * count_ref[j, w]
            rows.append(total)
        columns = as_columns(jnp.concatenate(rows))
        for j in range(len(starts)):
            coefs[j] = jnp.broadcast_to(columns[:, j : j + 1], coefs.shape[1:])

    grad_all = dot(upper_ref[0], w_ref[...], ((1,), (1,)))
    coef = coefs[tile_range(starts, wide, step)]
    for c in range(0, wide, LANES):
        at = slice(c, c + LANES)
        grad_t = grad_all[:, at]
        z = z_ref[:, at].astype(F32)
        sig = jax.nn.sigmoid(z)
        act = z * sig
        y = y_ref[:, at]
        q = y * act
        dq = gain_ref[:, at] * grad_t - q * coef
        dy_ref[:, at] = (dq * act).astype(BF)
        dz_ref[:, at] = (dq * y * (sig * (1.0 + z * (1.0 - sig)))).astype(BF)
        grad_ref[0:1, at] = jnp.sum(q * grad_t, axis=0, keepdims=True)


def tile_range(starts, wide, step):
    index = 0
    for start in starts[1:]:
        index = index + jnp.where(step * wide >= start, 1, 0)
    return index


def mixed_kernel(plan, ns, tok, here_ref, count_ref, ratio_ref, x_ref, *refs):
    shares, out_ref = refs[:-1], refs[-1]
    at = pl.ds(pl.multiple_of(here_ref[0] * tok, tok), tok)
    ratios = as_columns(ratio_ref[:, at])
    x = x_ref[...].astype(F32)
    for w in range(LEVELS):
        total = None
        for k in range(ns):
            for j in plan[w]:
                term = shares[k][j].astype(F32) * count_ref[k, j * LEVELS + w]
                total = term if total is None else total + term
        out_ref[w] = (x + ratios[:, w : w + 1] * total).astype(BF)


def dp_terms(others):
    return [swapped(other, "dp", k + 1) for k, other in enumerate(others)]


def over_seq(value):
    dense = value.reshape(-1, LANES)
    total = dense
    for k in range(1, lax.axis_size("seq")):
        total = total + swapped(dense, "seq", k)
    return total.reshape(value.shape)


def fsdp_half(own, got):
    nf = lax.axis_size("fsdp")
    f = lax.axis_index("fsdp")

    def part(offset):
        total = picked(own, f ^ offset).astype(F32)
        for other in got:
            total = total + picked(other, f ^ offset).astype(F32)
        return total.astype(BF)

    kept = jnp.stack([part(e) for e in range(0, nf, 2)])
    sent = jnp.stack([part(e ^ 1) for e in range(0, nf, 2)])
    return kept, sent


def fsdp_rest(kept, got):
    k = 2
    while k < lax.axis_size("fsdp"):
        total = (kept.astype(F32) + got.astype(F32)).astype(BF)
        kept, sent = total[::2], total[1::2]
        got = swapped(sent, "fsdp", k)
        k *= 2
    return kept[0], got[0]


def shards(
    tokens,
    lengths,
    norm_gain,
    w_in,
    w_dt,
    conv_w,
    conv_b,
    dt_bias,
    a_log,
    skip,
    gate_gain,
    w_out,
    cotangent,
):
    nd, ns, nf = lax.axis_size("dp"), lax.axis_size("seq"), lax.axis_size("fsdp")
    d, s, f = lax.axis_index("dp"), lax.axis_index("seq"), lax.axis_index("fsdp")
    tok = tokens.shape[1]
    length = ns * tok
    blocks = length // SPAN
    heads = HEADS // ns
    run = heads // nd
    width = heads * HEADDIM
    own_bc = 2 * STATE // ns
    used = width + own_bc
    cols = -(-(used + heads) // LANES) * LANES
    rows_in = w_in.shape[0]
    reach = CONV - 1

    levels = np.array(
        [[level_of(dd * (HEADS // nd) + ss * run + i) for dd in range(nd) for i in range(run)] for ss in range(ns)]
    )
    cuts = [0] + [h for h in range(1, heads) if (levels[:, h] != levels[:, h - 1]).any()] + [heads]
    ranges = [(a, b) for a, b in zip(cuts, cuts[1:])]
    range_level = np.array([[levels[ss, a] for a, _ in ranges] for ss in range(ns)])
    counts = (range_level[:, :, None] <= np.arange(LEVELS)[None, None, :]).astype(np.float32)
    counted = picked(jnp.asarray(counts), s)
    theirs = picked(
        jnp.asarray(np.stack([[counts[i ^ k].reshape(-1) for k in range(ns)] for i in range(ns)])), s
    )
    lowest = [int(range_level[ss].min()) for ss in range(ns)]

    def by_head(vector):
        lead = vector.shape[:-1]
        per = vector.shape[-1] // HEADS
        cut = vector.reshape(lead + (nd, ns, run * per))
        mine = lax.dynamic_index_in_dim(cut, s, len(lead) + 1, keepdims=False)
        return mine.reshape(lead + (heads * per,))

    def for_groups(matrix):
        per = matrix.shape[1] // HEADS
        cut = matrix.reshape(matrix.shape[0], nd, ns, run * per)
        return jnp.transpose(cut, (2, 0, 1, 3)).reshape(ns, matrix.shape[0], heads * per)

    def from_groups(stack):
        per = stack.shape[2] // heads
        cut = stack.reshape(ns, stack.shape[1], nd, run * per)
        return jnp.transpose(cut, (1, 2, 0, 3)).reshape(stack.shape[1], HEADS * per)

    pad_cols = cols - used - heads
    stack = jnp.concatenate(
        [
            for_groups(w_in[:, INNER : 2 * INNER]),
            w_in[:, 2 * INNER :].reshape(rows_in, ns, own_bc).transpose(1, 0, 2),
            for_groups(w_dt),
            jnp.zeros((ns, rows_in, pad_cols), BF),
            for_groups(w_in[:, :INNER]),
        ],
        axis=2,
    )
    own_x = tokens[0].astype(F32)
    scale = lax.rsqrt(jnp.mean(own_x * own_x, axis=-1, keepdims=True) + EPS)
    xn_own = (own_x * scale * norm_gain).astype(BF)
    xn_across = swapped(xn_own, "seq", 2)
    xn_pieces = [xn_own, swapped(xn_own, "seq", 1), xn_across, swapped(xn_across, "seq", 1)]
    arrived = [picked(stack, s)] + [swapped(picked(stack, s ^ k), "seq", k) for k in range(1, ns)]
    mine = filled((ns, rows_in, stack.shape[2]), [(p, None, (s ^ k, None, None)) for k, p in enumerate(arrived)])
    mine_z = mine[:, :, cols:]

    def needed(at, level):
        return min(lowest[at], lowest[at ^ 1]) <= level

    halves = [cotangent[w : w + 2, 0] for w in range(0, LEVELS, 2)]
    singles = [cotangent[w, 0] for w in range(LEVELS)]

    def beside(level, *others):
        block = after(halves[level // 2], *others)
        return swapped(block, "seq", 1, lambda i, j: needed(j, level + 1))

    def across(level, *others):
        block = after(singles[level], *others)
        return swapped(block, "seq", 2, lambda i, j: needed(j, level))

    def far(level, block):
        return swapped(block, "seq", 1, lambda i, j: needed(j, level))

    positions = jnp.arange(length, dtype=jnp.int32)
    ends = jnp.cumsum(lengths[0])[:-1]
    seg = jnp.sum((positions[:, None] >= ends[None, :]).astype(jnp.int32), axis=1)
    seg_before = jnp.concatenate([jnp.full((1,), -1, jnp.int32), seg[SPAN - 1 : length - 1 : SPAN]])
    seg_pad = jnp.concatenate([jnp.full((reach,), -1, jnp.int32), seg])
    masks = [(seg_pad[k : k + length] == seg) for k in range(reach)]
    mask_cols = [m.astype(F32) for m in masks]
    mask_cols += [jnp.pad(m, (0, reach - k))[reach - k :] for k, m in enumerate(mask_cols)]
    mask_cols = jnp.pad(jnp.stack(mask_cols, axis=1), ((0, 0), (0, LANES - 2 * reach)))

    def conv_params(s_part, bc_part):
        return by_head(s_part), bc_part

    weight_s = jnp.concatenate(
        [by_head(conv_w[:, :INNER]), by_head(conv_b[None, :INNER]), jnp.zeros((3, width), F32)]
    )
    weight_r = jnp.pad(
        lax.dynamic_slice_in_dim(conv_w, INNER + s * own_bc, own_bc, 1), ((0, 0), (0, cols - used))
    )
    bias_r = jnp.pad(
        lax.dynamic_slice_in_dim(conv_b, INNER + s * own_bc, own_bc, 0), (0, cols - used)
    )
    bias = by_head(dt_bias)
    rate = -jnp.exp(by_head(a_log))
    skip_own = by_head(skip)
    gain = by_head(gate_gain)

    half = width // 2

    def over_fsdp(chunk):
        return lax.all_gather(chunk, "fsdp", axis=0, tiled=False)

    def over_dp(held):
        pieces = [held] + [swapped(held, "dp", j) for j in range(1, nd)]
        moves = [
            (piece, i, (d ^ j, None, i, None, None)) for j, piece in enumerate(pieces) for i in range(nf)
        ]
        return pieces, moves

    held_a = over_fsdp(mine[:, :, :half])
    held_b = over_fsdp(mine[:, :, half:cols])
    small_ones = (seg, seg_before, mask_cols, weight_s, weight_r, bias_r, bias, rate, skip_own, gain, theirs)
    held_a, small_ones, halves, singles = together(held_a, small_ones, halves, singles)
    seg, seg_before, mask_cols, weight_s, weight_r, bias_r, bias, rate, skip_own, gain, theirs = small_ones
    near_high, near_low = beside(2, held_a), beside(0, held_a)
    chip3 = across(3, held_a)
    pieces_a, moves_a = over_dp(held_a)
    held_b, moves_a_there, chip3, near_high, xn_pieces = together(
        held_b, [m[0] for m in moves_a], chip3, near_high, xn_pieces
    )
    xn = filled((ns, tok, D), [(p, None, (s ^ k, None, None)) for k, p in enumerate(xn_pieces)])
    xn = xn.reshape(length, D)

    moves_a = [(p,) + m[1:] for p, m in zip(moves_a_there, moves_a)]
    chip2, far3 = across(2, held_b), far(3, chip3)
    pieces_b, moves_b = over_dp(held_b)
    full_a = filled((nd, ns, nf, rows_in, half), moves_a).reshape(D, half)
    full_b = filled((nd, ns, nf, rows_in, cols - half), moves_b).reshape(D, cols - half)
    held_z = over_fsdp(after(mine_z, held_a))

    xn_turned = xn.T
    proj_a = dot(xn, full_a).astype(BF)
    proj_b = dot(xn, after(full_b, proj_a, xn_turned)).astype(BF)
    proj_b, chip2, far3, near_low, held_z = together(proj_b, chip2, far3, near_low, held_z)
    held_out = over_fsdp(after(w_out, held_z))
    pieces_z, moves_z = over_dp(held_z)

    proj_r = proj_b[:, width - half :]
    mixer = jnp.concatenate([jnp.zeros((reach, cols - width), BF), proj_r], axis=0)

    def taken(k):
        rows = mixer[k : k + length].astype(F32)
        return rows * mask_cols[:, k : k + 1] if k < reach else rows

    pre_r = bias_r
    for k in range(CONV):
        pre_r = pre_r + taken(k) * weight_r[k]
    bc_own = jax.nn.silu(pre_r).astype(BF)[:, :own_bc]
    bc_across = swapped(bc_own, "seq", 2)
    bc = [bc_own, swapped(bc_own, "seq", 1), bc_across, swapped(bc_across, "seq", 1)]
    chip1, chip0, far2 = across(1, bc_across), across(0, bc_across), far(2, chip2)
    bc = reordered_by_xor(bc, s)
    b_in = jnp.concatenate(bc[: ns // 2], axis=1)
    c_out = jnp.concatenate(bc[ns // 2 :], axis=1)

    def padded(rows):
        return jnp.pad(rows, ((0, 0), (0, LANES - rows.shape[1])))

    pre_dt = proj_r[:, own_bc : own_bc + heads].astype(F32) + bias
    steps = jax.nn.softplus(pre_dt)
    tails = [
        p.reshape(blocks, SPAN, p.shape[1])[: blocks - 1, SPAN - HALO :, :half] for p in (proj_a, proj_b)
    ]
    operands = (
        seg_before,
        seg[:, None],
        seg[None, :],
        mask_cols,
        proj_a,
        proj_b,
        jnp.concatenate([jnp.zeros((1, HALO, width), BF), jnp.concatenate(tails, axis=2)]),
        weight_s,
        b_in,
        c_out,
        padded(steps),
        padded(rate[None, :]),
        jnp.repeat(skip_own, HEADDIM)[None, :],
    )
    y, priors = scan_forward(heads, blocks, operands)
    y, chip1, far2, held_out = together(y, chip1, far2, held_out)
    far1 = far(1, chip1)
    full_z = filled((nd, ns, nf, rows_in, width), moves_z).reshape(D, width)
    pieces_out = over_dp(held_out)[0]
    proj_z = dot(xn, full_z).astype(BF)
    proj_z, chip0, far1 = together(proj_z, chip0, far1)
    far0 = far(0, chip0)
    q = y * jax.nn.silu(proj_z.astype(F32))
    q_gain = (q * gain).astype(BF)
    lanes = [(a * HEADDIM, b * HEADDIM) for a, b in ranges]
    squares = jnp.stack([jnp.sum(q[:, a:b] * q[:, a:b], axis=1) for a, b in lanes])
    widths = np.array([[(HEADS >> 3 - w) * HEADDIM] for w in range(LEVELS)], np.float32)
    per_level = jnp.sum(counted[:, :, None] * squares[:, None, :], axis=0)
    ratio = lax.rsqrt(over_seq(per_level) / widths + EPS)

    plan = [[w for w in range(LEVELS) if range_level[:, j].min() <= w] for j in range(len(lanes))]
    out_rows = width // nd
    range_of = [next(j for j, (a, b) in enumerate(lanes) if a <= i * out_rows < b) for i in range(nd)]
    here = jnp.stack([s, d]).astype(jnp.int32)
    smem = pl.BlockSpec(memory_space=pltpu.SMEM)
    cot_pieces = [cotangent, near_low, near_high, chip0, chip1, chip2, chip3, far0, far1, far2, far3]
    cot_specs = [pl.BlockSpec((LEVELS, 1, tok, TILE), lambda i: (0, 0, 0, i))]
    cot_specs += [pl.BlockSpec((2, tok, TILE), lambda i: (0, 0, i))] * 2
    cot_specs += [pl.BlockSpec((tok, TILE), lambda i: (0, i))] * (2 * LEVELS)
    where = [[(0, (w, 0)), (1 + w // 2, (w % 2,)), (3 + w, ()), (3 + LEVELS + w, ())] for w in range(LEVELS)]
    upper, *grad_out = call(
        functools.partial(upper_kernel, where, plan, nd, tok, ns),
        grid=(D // TILE,),
        in_specs=[
            smem,
            smem,
            smem,
            pl.BlockSpec((LEVELS, length), lambda i: (0, 0)),
            pl.BlockSpec((width, length), lambda i: (0, 0)),
        ]
        + cot_specs,
        out_specs=[pl.BlockSpec((len(lanes), length, TILE), lambda i: (0, 0, i))]
        + [pl.BlockSpec((out_rows, TILE), lambda i: (0, i))]
        + [pl.BlockSpec((out_rows // 2, TILE), lambda i: (0, i))] * (2 * nd - 2),
        out_shape=[jax.ShapeDtypeStruct((len(lanes), length, D), BF)]
        + [jax.ShapeDtypeStruct((out_rows, D), BF)]
        + [jax.ShapeDtypeStruct((out_rows // 2, D), BF)] * (2 * nd - 2),
        scratch_shapes=[pltpu.VMEM((length, LANES), F32)],
        name="upper",
    )(here, jnp.asarray(range_of, jnp.int32), counted, ratio, q_gain.T, *cot_pieces)
    out_first, out_second = dp_terms(grad_out[1::2]), dp_terms(grad_out[2::2])

    pieces_out, upper = together(pieces_out, upper)
    *shares, inner, full_out = call(
        functools.partial(products_kernel, where, plan, lanes, tok, ns, nd),
        grid=(D // TILE,),
        in_specs=[
            smem,
            smem,
            pl.BlockSpec((length, width), lambda i: (0, 0)),
        ]
        + [pl.BlockSpec((nf, w_out.shape[0], TILE), lambda i: (0, 0, i))] * nd
        + cot_specs,
        out_specs=[pl.BlockSpec((len(lanes), tok, TILE), lambda i: (0, 0, i))] * ns
        + [pl.BlockSpec((LEVELS, length), lambda i: (0, 0))]
        + [pl.BlockSpec((width, TILE), lambda i: (0, i))],
        out_shape=[jax.ShapeDtypeStruct((len(lanes), tok, D), BF)] * ns
        + [jax.ShapeDtypeStruct((LEVELS, length), F32)]
        + [jax.ShapeDtypeStruct((width, D), BF)],
        scratch_shapes=[pltpu.VMEM((LEVELS, length, LANES), F32)],
        name="products",
    )(here, counted, q_gain, *pieces_out, *cot_pieces)
    means, out_first = together(over_seq(inner) / widths, out_first)
    shares = [shares[0]] + [swapped(after(shares[k], means), "seq", k) for k in range(1, ns)]

    starts = [a for a, _ in lanes]
    wide = min(min(b - a for a, b in lanes), TILE)
    cols_of = pl.BlockSpec((length, wide), lambda i: (0, i))
    scalars = pl.BlockSpec((LEVELS, length), lambda i: (0, 0))
    dy, dz, grad_gate = call(
        functools.partial(gate_kernel, starts, wide),
        grid=(width // wide,),
        in_specs=[
            smem,
            pl.BlockSpec((1, length, D), lambda i: (tile_range(starts, wide, i), 0, 0)),
            pl.BlockSpec((wide, D), lambda i: (i, 0)),
            cols_of,
            cols_of,
            pl.BlockSpec((1, wide), lambda i: (0, i)),
            scalars,
            scalars,
        ],
        out_specs=[cols_of, cols_of, pl.BlockSpec((8, wide), lambda i: (0, i))],
        out_shape=[
            jax.ShapeDtypeStruct((length, width), BF),
            jax.ShapeDtypeStruct((length, width), BF),
            jax.ShapeDtypeStruct((8, width), F32),
        ],
        scratch_shapes=[pltpu.VMEM((len(lanes), length, LANES), F32)],
        name="gate_backward",
    )(counted, upper, full_out, y, proj_z, gain[None], ratio, means)
    grad_gate = grad_gate[0]

    def in_terms(dproj, at, first=0, columns=None):
        columns = columns or dproj.shape[1]
        out = row_terms(xn_turned, dproj, at, nd, ns, nf, first, columns)
        return out.reshape(nf, ns * rows_in, columns)

    z_other = [in_terms(dz, d ^ k) for k in range(1, nd)]
    z_got = dp_terms(z_other)
    dy, out_second, shares[1] = together(after(dy, *z_other), out_second, shares[1])
    chunk = (nf, out_rows // nf, D)
    out_got = [jnp.concatenate([u, v]).reshape(chunk) for u, v in zip(out_first, out_second)]
    out_kept, out_sent = fsdp_half(grad_out[0].reshape(chunk), out_got)
    dy = after(dy, out_sent)
    out_half = swapped(out_sent, "fsdp", 1)

    dproj_s, dbc, ddt, drate, dsum = scan_backward(heads, blocks, operands, y, priors, dy)
    dproj_s, dbc, out_half, shares[2] = together(dproj_s, dbc, out_half, shares[2])
    out_pair = fsdp_rest(out_kept, out_half)
    dbc = dbc.astype(BF)
    dbc_parts = reordered_by_xor([dbc[:, j * own_bc : (j + 1) * own_bc] for j in range(ns)], s)
    dbc_got = [swapped(dbc_parts[k], "seq", k) for k in range(1, ns)]
    left_other = [in_terms(dproj_s, d ^ k, 0, half) for k in range(1, nd)]
    left_got = dp_terms(left_other)
    late_s = after(dproj_s, *left_other)
    middle_other = [in_terms(late_s, d ^ k, half, half) for k in range(1, nd)]
    middle_got = dp_terms(middle_other)
    dbc_own = after(dbc_parts[0].astype(F32), *middle_other)
    for got in dbc_got:
        dbc_own = dbc_own + got.astype(F32)
    dz_late, z_got = together(after(dz, *middle_other), z_got)
    z_kept, z_sent = fsdp_half(in_terms(dz_late, d), z_got)
    z_half = swapped(z_sent, "fsdp", 1)
    dpre = jnp.pad(dbc_own, ((0, 0), (0, cols - used))) * silu_slope(pre_r)
    grad_b_r = jnp.sum(dpre, axis=0)[:own_bc]
    grad_w_r = jnp.stack([jnp.sum(dpre * taken(k), axis=0) for k in range(CONV)])[:, :own_bc]
    dmixer = dpre * weight_r[reach]
    for k in range(reach):
        back = reach - k
        later = (dpre * mask_cols[:, k : k + 1])[back:]
        dmixer = dmixer + jnp.pad(later, ((0, back), (0, 0))) * weight_r[k]
    dpre_dt = ddt[:, :heads] * jax.nn.sigmoid(pre_dt)
    dproj_r = jnp.concatenate(
        [dmixer[:, :own_bc].astype(BF), dpre_dt.astype(BF), jnp.zeros((length, pad_cols), BF)], axis=1
    )
    dproj_r, out_pair = together(after(dproj_r, z_sent), out_pair)
    right_other = [in_terms(dproj_r, d ^ k) for k in range(1, nd)]
    right_got = dp_terms(right_other)
    own_s = in_terms(after(dproj_s, *right_other), d)
    own_r = in_terms(after(dproj_r, own_s), d)

    dxn = input_grad(dz, dproj_s, after(dproj_r, own_r), full_z, full_a, full_b, ns, tok)
    beside_near = swapped(picked(dxn, s ^ 1), "seq", 1)
    beside_far = swapped(picked(dxn, s ^ 3), "seq", 1)
    dxn, left_got, z_half = together(dxn, left_got, z_half)
    left_kept, left_sent = fsdp_half(own_s[:, :, :half], left_got)
    left_half = swapped(left_sent, "fsdp", 1)
    z_pair = fsdp_rest(z_kept, z_half)
    flat = flattened(
        [
            jnp.concatenate([dsum[:CONV], grad_w_r], axis=1).reshape(-1),
            dsum[CONV],
            grad_b_r,
            grad_gate,
            jnp.sum(dpre_dt, axis=0),
            drate[0, :heads] * rate,
            jnp.sum(dsum[CONV + 1].reshape(heads, HEADDIM), axis=1),
        ]
    )
    near = picked(dxn, s).astype(F32) + beside_near.astype(F32)
    far = (picked(dxn, s ^ 2).astype(F32) + beside_far.astype(F32)).astype(BF)
    dxn_across = swapped(far, "seq", 2)
    middle_got, right_got, far = together(middle_got, right_got, far)
    kept_m, sent_m = fsdp_half(own_s[:, :, half:], middle_got)
    kept_r, sent_r = fsdp_half(own_r, right_got)
    right_kept = jnp.concatenate([kept_m, kept_r], axis=2)
    right_sent = jnp.concatenate([sent_m, sent_r], axis=2)
    left_half, right_sent = together(left_half, right_sent)
    left_pair = fsdp_rest(left_kept, left_half)
    right_half = swapped(right_sent, "fsdp", 1)

    dxn_own = near + after(dxn_across, right_sent).astype(F32)
    grad_norm = jnp.sum(dxn_own * own_x * scale, axis=0)
    scaled = norm_gain * dxn_own
    dx = scale * scaled - own_x * scale**3 * jnp.mean(own_x * scaled, axis=-1, keepdims=True)
    dx = dx + jnp.sum(after(cotangent, right_sent)[:, 0].astype(F32), axis=0)
    flat = jnp.concatenate([flat, grad_norm.reshape(-1, LANES)])
    flat = butterfly(flat, "dp")
    dx = dx.astype(BF)

    z_pair, left_pair, right_half, flat, dx = together(z_pair, left_pair, right_half, flat, dx)
    right_pair = fsdp_rest(right_kept, right_half)

    def whole_sum(pair):
        total = (pair[0].astype(F32) + pair[1].astype(F32)).astype(BF)
        return total.reshape(ns, rows_in, total.shape[1])

    early = jnp.concatenate([whole_sum(z_pair), whole_sum(left_pair)], axis=2)
    early_got = [picked(early, s)] + [swapped(picked(early, s ^ k), "seq", k) for k in range(1, ns)]
    mixed = call(
        functools.partial(
            mixed_kernel,
            [[j for j in range(len(lanes)) if range_level[:, j].min() <= w] for w in range(LEVELS)],
            ns,
            tok,
        ),
        grid=(D // TILE,),
        in_specs=[
            smem,
            smem,
            pl.BlockSpec((LEVELS, length), lambda i: (0, 0)),
            pl.BlockSpec((tok, TILE), lambda i: (0, i)),
        ]
        + [pl.BlockSpec((len(lanes), tok, TILE), lambda i: (0, 0, i))] * ns,
        out_specs=pl.BlockSpec((LEVELS, tok, TILE), lambda i: (0, 0, i)),
        out_shape=jax.ShapeDtypeStruct((LEVELS, tok, D), BF),
        name="mixed",
    )(here, theirs, ratio, tokens[0], *after(shares, right_half))[:, None]
    flat = butterfly(flat, "fsdp")
    early_got, right_pair, mixed = together(early_got, right_pair, mixed)
    late = whole_sum(right_pair)
    late_got = [picked(late, s)] + [swapped(picked(late, s ^ k), "seq", k) for k in range(1, ns)]
    early_got, late_got = together(early_got, late_got)
    early = placed_by_xor(early_got, s)
    late = placed_by_xor(late_got, s)
    got_z = early[:, :, :width]
    got_x = jnp.concatenate([early[:, :, width:], late], axis=2)
    sum_out = out_pair[0].astype(F32) + out_pair[1].astype(F32)


    sum_in = jnp.concatenate(
        [
            from_groups(got_z),
            from_groups(got_x[:, :, :width]),
            jnp.transpose(got_x[:, :, width:used], (1, 0, 2)).reshape(rows_in, 2 * STATE),
        ],
        axis=1,
    ).astype(F32)
    sum_dt = from_groups(got_x[:, :, used : used + heads]).astype(F32)

    sizes = [CONV * used, used, width, heads, heads, heads]
    filling = -sum(sizes) % 1024
    sizes += [filling, D]
    every = seq_gather(flat, s).reshape(ns, -1)
    starts = np.cumsum([0] + sizes)
    pieces = [every[:, a : a + n] for a, n in zip(starts, sizes)]

    def heads_back(rows):
        lead = rows.shape[1:-1]
        cut = rows.reshape((ns,) + lead + (nd, rows.shape[-1] // nd))
        order = tuple(range(1, 1 + len(lead))) + (1 + len(lead), 0, 2 + len(lead))
        return jnp.transpose(cut, order).reshape(lead + (-1,))

    conv_rows = pieces[0].reshape(ns, CONV, used)
    conv_all = jnp.concatenate(
        [
            heads_back(conv_rows[:, :, :width]),
            jnp.transpose(conv_rows[:, :, width:], (1, 0, 2)).reshape(CONV, 2 * STATE),
        ],
        axis=1,
    )
    bias_all = jnp.concatenate([heads_back(pieces[1][:, :width]), pieces[1][:, width:].reshape(-1)])
    return (
        mixed,
        dx[None],
        jnp.sum(pieces[7], axis=0),
        sum_in,
        sum_dt,
        conv_all,
        bias_all,
        heads_back(pieces[3]),
        heads_back(pieces[4]),
        heads_back(pieces[5]),
        heads_back(pieces[2]),
        sum_out,
    )


def solution(mesh):
    rows = P(("dp", "seq", "fsdp"), None)
    held = P(("dp", "fsdp"), "seq", None)
    levels = P(None, ("dp", "fsdp"), "seq", None)
    placed = (held, P(("dp", "fsdp"), None), P(), rows, rows, P(), P(), P(), P(), P(), P(), rows, levels)
    return jax.shard_map(
        shards,
        mesh=mesh,
        in_specs=placed,
        out_specs=(levels, held, P(), rows, rows, P(), P(), P(), P(), P(), P(), rows),
        check_vma=False,
    )
```

```python
import functools

import jax
import jax.numpy as jnp
import numpy as np
from jax import lax
from jax.experimental import pallas as pl
from jax.experimental.pallas import tpu as pltpu
from jax.sharding import PartitionSpec as P

D = 2048
HEADS = 64
HEADDIM = 64
STATE = 128
CONV = 4
SPAN = 128
INNER = 4096
EPS = 1e-05
LEVELS = 4
BF = jnp.bfloat16
F32 = jnp.float32
HIGH = lax.Precision.HIGHEST
LANES = 128
HALO = 16
TILE = 256
VMEM_LIMIT = 48 * 1024 * 1024


def dot(a, b, dims=((1,), (0,)), precision=None):
    return lax.dot_general(a, b, (dims, ((), ())), preferred_element_type=F32, precision=precision)


def silu_slope(v):
    sig = jax.nn.sigmoid(v)
    return sig * (1.0 + v * (1.0 - sig))


def level_of(head):
    return 0 if head < 8 else 1 if head < 16 else 2 if head < 32 else 3


def swapped(value, axis, k, keep=None):
    pairs = [(i, i ^ k) for i in range(lax.axis_size(axis))]
    if keep is not None:
        pairs = [p for p in pairs if keep(*p)]
    return lax.ppermute(value, axis, pairs)


def after(value, *others):
    return lax.optimization_barrier((value,) + others)[0]


def together(*values):
    return lax.optimization_barrier(values)


def flattened(vectors):
    flat = jnp.concatenate(vectors)
    return jnp.pad(flat, (0, -flat.shape[0] % 1024)).reshape(-1, LANES)


def butterfly(value, axis):
    k = 1
    while k < lax.axis_size(axis):
        value = value + swapped(value, axis, k)
        k *= 2
    return value


def picked(array, index):
    return lax.dynamic_index_in_dim(array, index, 0, keepdims=False)


def seq_gather(block, here):
    return jnp.stack(reordered_by_xor([block] + [swapped(block, "seq", k) for k in range(1, 4)], here))


def reordered_by_xor(pieces, here):
    k = 1
    while k < len(pieces):
        flip = (here & k) > 0
        pieces = [jnp.where(flip, pieces[j ^ k], piece) for j, piece in enumerate(pieces)]
        k *= 2
    return pieces


def call(kernel, **kwargs):
    return pl.pallas_call(
        kernel,
        compiler_params=pltpu.CompilerParams(vmem_limit_bytes=VMEM_LIMIT),
        cost_estimate=pl.CostEstimate(flops=1, bytes_accessed=1, transcendentals=0),
        **kwargs,
    )


def filled(shape, moves):
    arrays, plan, rows = [], [], []
    block = tuple(size if index is None else 1 for size, index in zip(shape, moves[0][2]))
    for piece, lead, place in moves:
        at = next((i for i, a in enumerate(arrays) if a is piece), len(arrays))
        if at == len(arrays):
            arrays.append(piece)
        plan.append((at, lead))
        rows.append(jnp.stack([jnp.asarray(0 if n is None else n, jnp.int32) for n in place]))

    def kernel(index_ref, *refs):
        pieces, out = refs[:-1], refs[-1]
        for m, (at, lead) in enumerate(plan):

            @pl.when(pl.program_id(0) == m)
            def _():
                value = pieces[at][...] if lead is None else pieces[at][lead]
                out[...] = value.reshape(block)

    return call(
        kernel,
        grid_spec=pltpu.PrefetchScalarGridSpec(
            num_scalar_prefetch=1,
            grid=(len(plan),),
            in_specs=[
                pl.BlockSpec(a.shape, lambda i, t, n=a.ndim: (0,) * n) for a in arrays
            ],
            out_specs=pl.BlockSpec(
                block, lambda i, t: tuple(t[i, n] for n in range(len(shape)))
            ),
        ),
        out_shape=jax.ShapeDtypeStruct(shape, arrays[0].dtype),
        name="filled",
    )(jnp.stack(rows), *arrays)


def terms_kernel(ns, nf, at_ref, left_ref, right_ref, out_ref):
    value = dot(left_ref[...], right_ref[...]).astype(BF)
    rows = value.shape[0] // (ns * nf)
    for i in range(ns):
        for k in range(nf):
            out_ref[k, i] = value[(i * nf + k) * rows : (i * nf + k + 1) * rows]


def row_terms(turned, right, at, nd, ns, nf, first, columns):
    depth = turned.shape[1]
    rows = turned.shape[0] // nd
    wide = TILE if columns % TILE == 0 else LANES
    return call(
        functools.partial(terms_kernel, ns, nf),
        grid_spec=pltpu.PrefetchScalarGridSpec(
            num_scalar_prefetch=1,
            grid=(columns // wide,),
            in_specs=[
                pl.BlockSpec((rows, depth), lambda i, t: (t[0], 0)),
                pl.BlockSpec((depth, wide), lambda i, t: (0, i + first // wide)),
            ],
            out_specs=pl.BlockSpec((nf, ns, rows // (nf * ns), wide), lambda i, t: (0, 0, 0, i)),
        ),
        out_shape=jax.ShapeDtypeStruct((nf, ns, rows // (nf * ns), columns), BF),
        name="row_terms",
    )(at.astype(jnp.int32)[None], turned, right)


def input_grad_kernel(blocks, dz_ref, ds_ref, dr_ref, wz_ref, wa_ref, wb_ref, out_ref):
    half = wb_ref.shape[1]
    columns = ((1,), (1,))
    total = dot(dz_ref[...], wz_ref[...], columns)
    total = total + dot(ds_ref[:, :half], wa_ref[:, :half], columns)
    total = total + dot(ds_ref[:, half:], wb_ref[...], columns)
    total = total + dot(dr_ref[...], wa_ref[:, half:], columns)
    total = total.astype(BF)
    tok = total.shape[0] // blocks
    for i in range(blocks):
        out_ref[i] = total[i * tok : (i + 1) * tok]


def input_grad(dz, ds, dr, wz, wa, wb, blocks, tok):
    def whole(a):
        return pl.BlockSpec(a.shape, lambda i: (0, 0))

    def rows(a):
        return pl.BlockSpec((TILE, a.shape[1]), lambda i: (i, 0))

    return call(
        functools.partial(input_grad_kernel, blocks),
        grid=(wz.shape[0] // TILE,),
        in_specs=[whole(dz), whole(ds), whole(dr), rows(wz), rows(wa), rows(wb)],
        out_specs=pl.BlockSpec((blocks, tok, TILE), lambda i: (0, 0, i)),
        out_shape=jax.ShapeDtypeStruct((blocks, tok, wz.shape[0]), BF),
        name="input_grad",
    )(dz, ds, dr, wz, wa, wb)


def tri(rows_first):
    a = lax.broadcasted_iota(jnp.int32, (SPAN, SPAN), 0)
    b = lax.broadcasted_iota(jnp.int32, (SPAN, SPAN), 1)
    return (a >= b) if rows_first else (a <= b)


def pair_of(lo, cols, p):
    return jnp.where(lo, cols[:, 2 * p : 2 * p + 1], cols[:, 2 * p + 1 : 2 * p + 2])


def decays(segc, segr, segp, dt, rate):
    cum = dot(tri(True).astype(F32), dt * rate, precision=HIGH)
    last = cum[SPAN - 1 : SPAN, :]
    keep = jnp.where(segc == segp, jnp.exp(cum), 0.0)
    to_end = jnp.where(segc == segr[:, SPAN - 1 : SPAN], jnp.exp(last - cum), 0.0)
    return cum, cum.T, keep, to_end


def spread_columns(ref, first, count):
    return [jnp.broadcast_to(ref[:, first + k : first + k + 1], (SPAN, LANES)) for k in range(count)]


def taps(ext, masks, at):
    terms = [ext[pl.ds(HALO - CONV + 1 + k, SPAN), at] for k in range(CONV)]
    return [t * m for t, m in zip(terms, masks)] + terms[CONV - 1 :]


def convolved(terms, weight_ref, at):
    total = weight_ref[CONV : CONV + 1, at] + terms[0] * weight_ref[0:1, at]
    for k in range(1, CONV):
        total = total + terms[k] * weight_ref[k : k + 1, at]
    return total


def forward_kernel(
    heads,
    segp_ref,
    segc_ref,
    segr_ref,
    mask_ref,
    in_a_ref,
    in_b_ref,
    halo_ref,
    weight_ref,
    b_ref,
    c_ref,
    dt_ref,
    rate_ref,
    skip_ref,
    y_ref,
    prior_ref,
    carry,
    to_end_u,
    ext,
):
    block = pl.program_id(0)
    width = heads * HEADDIM

    @pl.when(block == 0)
    def _():
        carry[...] = jnp.zeros_like(carry)

    prior_ref[0] = carry[...]
    ext[0:HALO] = halo_ref[0].astype(F32)
    half = in_b_ref.shape[1]
    ext[HALO:, :half] = in_a_ref[:, :half].astype(F32)
    ext[HALO:, half:] = in_b_ref[...].astype(F32)
    segc, segr = segc_ref[...], segr_ref[...]
    dt = dt_ref[...]
    cum, cumr, keep, to_end = decays(segc, segr, segp_ref[block], dt, rate_ref[...])
    bm, cm = b_ref[...], c_ref[...]
    mixing = dot(cm, bm, ((1,), (1,)))
    mixing = jnp.where(tri(True) & (segc == segr), mixing, 0.0)
    masks = spread_columns(mask_ref, 0, CONV - 1)
    lo = lax.broadcasted_iota(jnp.int32, (SPAN, LANES), 1) < HEADDIM
    for p in range(heads // 2):
        at = slice(p * LANES, (p + 1) * LANES)
        pre = convolved(taps(ext, masks, at), weight_ref, at)
        x2 = pre * jax.nn.sigmoid(pre)
        u2 = x2 * pair_of(lo, dt, p)
        ub = u2.astype(BF)
        total = dot(cm, carry[:, at].astype(BF)) * pair_of(lo, keep, p) + skip_ref[:, at] * x2
        inner = []
        for h in (2 * p, 2 * p + 1):
            decay = jnp.exp(jnp.minimum(cum[:, h : h + 1] - cumr[h : h + 1, :], 0.0))
            inner.append(dot((decay * mixing).astype(BF), ub))
        y_ref[:, at] = total + jnp.where(lo, inner[0], inner[1])
        to_end_u[:, at] = (u2 * pair_of(lo, to_end, p)).astype(BF)
    fresh = dot(bm, to_end_u[...], ((0,), (0,)))
    lo_row = lax.broadcasted_iota(jnp.int32, (1, LANES), 1) < HEADDIM
    for p in range(heads // 2):
        at = slice(p * LANES, (p + 1) * LANES)
        factor = pair_of(lo_row, keep[SPAN - 1 : SPAN, :], p)
        carry[:, at] = factor * carry[:, at] + fresh[:, at]


def split_dot(value, ones):
    high = value.astype(BF)
    low = (value - high.astype(F32)).astype(BF)
    return dot(high, ones) + dot(low, ones)


def backward_kernel(
    heads,
    segp_ref,
    segc_ref,
    segr_ref,
    mask_ref,
    in_a_ref,
    in_b_ref,
    halo_ref,
    weight_ref,
    b_ref,
    c_ref,
    dt_ref,
    rate_ref,
    skip_ref,
    y_ref,
    prior_ref,
    dy_ref,
    din_ref,
    dbc_ref,
    ddt_ref,
    drate_ref,
    dsum_ref,
    dcarry,
    after_state,
    keep_dy,
    to_end_u,
    slopes,
    along,
    ext,
    dext,
):
    step = pl.program_id(0)
    block = pl.num_programs(0) - 1 - step

    @pl.when(step == 0)
    def _():
        dcarry[...] = jnp.zeros_like(dcarry)
        after_state[...] = jnp.zeros_like(after_state)
        drate_ref[...] = jnp.zeros_like(drate_ref)
        dsum_ref[...] = jnp.zeros_like(dsum_ref)
        dext[SPAN:] = jnp.zeros((HALO, dext.shape[1]), F32)

    ext[0:HALO] = halo_ref[0].astype(F32)
    half = in_b_ref.shape[1]
    ext[HALO:, :half] = in_a_ref[:, :half].astype(F32)
    ext[HALO:, half:] = in_b_ref[...].astype(F32)
    segc, segr = segc_ref[...], segr_ref[...]
    dt = dt_ref[...]
    cum, cumr, keep, to_end = decays(segc, segr, segp_ref[block], dt, rate_ref[...])
    bm, cm = b_ref[...], c_ref[...]
    allowed = tri(False) & (segc == segr)
    mixing = jnp.where(allowed, dot(bm, cm, ((1,), (1,))), 0.0)
    masks = spread_columns(mask_ref, 0, CONV - 1)
    moved = spread_columns(mask_ref, CONV - 1, CONV - 1)
    lo = lax.broadcasted_iota(jnp.int32, (SPAN, LANES), 1) < HEADDIM
    dmixing = jnp.zeros((SPAN, SPAN), F32)
    for p in range(heads // 2):
        at = slice(p * LANES, (p + 1) * LANES)
        terms = taps(ext, masks, at)
        pre = convolved(terms, weight_ref, at)
        sig = jax.nn.sigmoid(pre)
        x2 = pre * sig
        dt2 = pair_of(lo, dt, p)
        u2 = x2 * dt2
        dyb = dy_ref[:, at]
        dy2 = dyb.astype(F32)
        skip = skip_ref[:, at]
        te2 = pair_of(lo, to_end, p)
        u_sides = (jnp.where(lo, u2, 0.0).astype(BF), jnp.where(lo, 0.0, u2).astype(BF))
        du = te2 * dot(bm, dcarry[:, at].astype(BF))
        inner = []
        for k in range(2):
            h = 2 * p + k
            decay = jnp.exp(jnp.minimum(cumr[h : h + 1, :] - cum[:, h : h + 1], 0.0))
            inner.append(dot((decay * mixing).astype(BF), dyb))
            dmixing = dmixing + decay * dot(u_sides[k], dyb, ((1,), (1,)))
        du = du + jnp.where(lo, inner[0], inner[1])
        keep_dy[:, at] = (pair_of(lo, keep, p) * dy2).astype(BF)
        to_end_u[:, at] = (te2 * u2).astype(BF)
        slopes[:, at] = dy2 * (y_ref[:, at] - skip * x2) - u2.astype(BF).astype(F32) * du
        along[:, at] = x2 * du
        dpre = (dt2 * du + skip * dy2) * (sig * (1.0 + pre * (1.0 - sig)))
        dext[0:SPAN, at] = dpre
        for k in range(CONV):
            dsum_ref[k : k + 1, at] += jnp.sum(dpre * terms[k], axis=0, keepdims=True)
        dsum_ref[CONV : CONV + 1, at] += jnp.sum(dpre, axis=0, keepdims=True)
        dsum_ref[CONV + 1 : CONV + 2, at] += jnp.sum(dy2 * x2, axis=0, keepdims=True)
        din = dpre * weight_ref[CONV - 1 : CONV, at]
        for k in range(CONV - 1):
            later = dext[pl.ds(CONV - 1 - k, SPAN), at]
            din = din + later * moved[k] * weight_ref[k : k + 1, at]
        din_ref[:, at] = din.astype(BF)
    dext[SPAN:] = dext[0:HALO]
    dmixing = jnp.where(allowed, dmixing, 0.0).astype(BF)
    dstate = dcarry[...].astype(BF)
    prior = prior_ref[0]
    dbc_ref[:, :STATE] = dot(dmixing, cm) + dot(to_end_u[...], dstate, ((1,), (1,)))
    dbc_ref[:, STATE:] = dot(dmixing, bm, ((0,), (0,))) + dot(
        keep_dy[...], prior.astype(BF), ((1,), (1,))
    )
    width = heads * HEADDIM
    ones = (
        lax.broadcasted_iota(jnp.int32, (width, LANES), 0) // HEADDIM
        == lax.broadcasted_iota(jnp.int32, (width, LANES), 1)
    ).astype(BF)
    at_end = jnp.sum(dcarry[...] * after_state[...], axis=0, keepdims=True)
    at_end = split_dot(jnp.broadcast_to(at_end, (16, width)), ones)[:1]
    dcum = split_dot(slopes[...], ones)
    da = dot(tri(False).astype(F32), dcum, precision=HIGH) + at_end
    ddt_ref[...] = rate_ref[...] * da + split_dot(along[...], ones)
    drate_ref[...] += jnp.sum(dt * da, axis=0, keepdims=True)
    fresh = dot(cm, keep_dy[...], ((0,), (0,)))
    lo_row = lax.broadcasted_iota(jnp.int32, (1, LANES), 1) < HEADDIM
    for p in range(heads // 2):
        at = slice(p * LANES, (p + 1) * LANES)
        factor = pair_of(lo_row, keep[SPAN - 1 : SPAN, :], p)
        dcarry[:, at] = factor * dcarry[:, at] + fresh[:, at]
    after_state[...] = prior


def scan_specs(heads, at, in_widths):
    width = heads * HEADDIM

    def rows(n):
        return pl.BlockSpec((SPAN, n), lambda i: (at(i), 0))

    def whole(*shape):
        return pl.BlockSpec(shape, lambda i: (0,) * len(shape))

    ins = [
        pl.BlockSpec(memory_space=pltpu.SMEM),
        rows(1),
        pl.BlockSpec((1, SPAN), lambda i: (0, at(i))),
        rows(LANES),
        rows(in_widths[0]),
        rows(in_widths[1]),
        pl.BlockSpec((1, HALO, width), lambda i: (at(i), 0, 0)),
        whole(8, width),
        rows(STATE),
        rows(STATE),
        rows(LANES),
        whole(1, LANES),
        whole(1, width),
    ]
    prior = pl.BlockSpec((1, STATE, width), lambda i: (at(i), 0, 0))
    return rows, whole, ins, prior


def scan_forward(heads, blocks, operands):
    rows, whole, ins, prior = scan_specs(heads, lambda i: i, [operands[n].shape[1] for n in (4, 5)])
    width = heads * HEADDIM
    return call(
        functools.partial(forward_kernel, heads),
        grid=(blocks,),
        in_specs=ins,
        out_specs=[rows(width), prior],
        out_shape=[
            jax.ShapeDtypeStruct((blocks * SPAN, width), F32),
            jax.ShapeDtypeStruct((blocks, STATE, width), F32),
        ],
        scratch_shapes=[
            pltpu.VMEM((STATE, width), F32),
            pltpu.VMEM((SPAN, width), BF),
            pltpu.VMEM((HALO + SPAN, width), F32),
        ],
        name="scan_forward",
    )(*operands)


def scan_backward(heads, blocks, operands, y, priors, dy):
    rows, whole, ins, prior = scan_specs(
        heads, lambda i: blocks - 1 - i, [operands[n].shape[1] for n in (4, 5)]
    )
    width = heads * HEADDIM
    return call(
        functools.partial(backward_kernel, heads),
        grid=(blocks,),
        in_specs=ins + [rows(width), prior, rows(width)],
        out_specs=[rows(width), rows(2 * STATE), rows(LANES), whole(1, LANES), whole(8, width)],
        out_shape=[
            jax.ShapeDtypeStruct((blocks * SPAN, width), BF),
            jax.ShapeDtypeStruct((blocks * SPAN, 2 * STATE), F32),
            jax.ShapeDtypeStruct((blocks * SPAN, LANES), F32),
            jax.ShapeDtypeStruct((1, LANES), F32),
            jax.ShapeDtypeStruct((8, width), F32),
        ],
        scratch_shapes=[
            pltpu.VMEM((STATE, width), F32),
            pltpu.VMEM((STATE, width), F32),
            pltpu.VMEM((SPAN, width), BF),
            pltpu.VMEM((SPAN, width), BF),
            pltpu.VMEM((SPAN, width), F32),
            pltpu.VMEM((SPAN, width), F32),
            pltpu.VMEM((HALO + SPAN, width), F32),
            pltpu.VMEM((SPAN + HALO, width), F32),
        ],
        name="scan_backward",
    )(*operands, y, priors, dy)


def as_columns(rows):
    few, tokens = rows.shape
    return jnp.concatenate([rows, jnp.zeros((LANES - few, tokens), F32)]).T


def level_block(pieces, spot):
    piece, lead = spot
    return pieces[piece][lead + (slice(None), slice(None))].astype(F32)


def upper_kernel(where, plan, nd, tok, ns, here_ref, range_ref, count_ref, ratio_ref, q_turned, *refs):
    count = 3 + 2 * LEVELS
    pieces, outs = refs[:count], refs[count:]
    upper_ref, grad_refs, coefs = outs[0], outs[1 : 2 * nd], outs[2 * nd]

    @pl.when(pl.program_id(0) == 0)
    def _():
        rows = [count_ref[j, w] * ratio_ref[w : w + 1, :] for j in range(len(plan)) for w in range(LEVELS)]
        coefs[...] = as_columns(jnp.concatenate(rows))

    for k in range(ns):
        at = here_ref[0] ^ k
        rows = pl.ds(pl.multiple_of(at * tok, tok), tok)
        levels = [level_block(pieces, where[w][k]) for w in range(LEVELS)]
        for j in range(len(plan)):
            total = None
            for w in plan[j]:
                n = j * LEVELS + w
                term = coefs[rows, n : n + 1] * levels[w]
                total = term if total is None else total + term
            upper_ref[j, rows, :] = total.astype(BF)
    count = q_turned.shape[0] // nd
    for k in range(nd):
        index = here_ref[1] ^ k
        rows = pl.ds(pl.multiple_of(index * count, count), count)
        value = dot(q_turned[rows, :], upper_ref[range_ref[index]]).astype(BF)
        if k:
            grad_refs[2 * k - 1][...] = value[: count // 2]
            grad_refs[2 * k][...] = value[count // 2 :]
        else:
            grad_refs[0][...] = value


def products_kernel(where, plan, lanes, tok, ns, nd, here_ref, count_ref, q_ref, *refs):
    count = 3 + 2 * LEVELS
    held_ref, pieces, outs = refs[0], refs[1 : 1 + count], refs[1 + count :]
    prod_refs, inner_ref, w_ref, sums = outs[:ns], outs[ns], outs[ns + 1], outs[ns + 2]
    step = pl.program_id(0)
    rows_of = w_ref.shape[0] // nd
    for k in range(nd):
        at = pl.multiple_of((here_ref[1] ^ k) * rows_of, rows_of)
        w_ref[pl.ds(at, rows_of), :] = held_ref[:, k].reshape(rows_of, w_ref.shape[1])

    @pl.when(step == 0)
    def _():
        sums[...] = jnp.zeros_like(sums)

    for k in range(ns):
        at = here_ref[0] ^ k
        rows = pl.ds(pl.multiple_of(at * tok, tok), tok)
        values = [dot(q_ref[rows, a:b], w_ref[a:b, :]) for a, b in lanes]
        for j, value in enumerate(values):
            prod_refs[k][j] = value.astype(BF)
        for w in range(LEVELS):
            total = None
            for j in range(len(lanes)):
                if w in plan[j]:
                    term = values[j] * count_ref[j, w]
                    total = term if total is None else total + term
            part = total * level_block(pieces, where[w][k])
            folded = part[:, :LANES]
            for c in range(LANES, part.shape[1], LANES):
                folded = folded + part[:, c : c + LANES]
            sums[w, rows, :] += folded

    @pl.when(step == pl.num_programs(0) - 1)
    def _():
        lane = lax.broadcasted_iota(jnp.int32, sums.shape[1:], 1)
        total = jnp.zeros(sums.shape[1:], F32)
        for w in range(LEVELS):
            total = jnp.where(lane == w, jnp.sum(sums[w], axis=1, keepdims=True), total)
        inner_ref[...] = total.T[:LEVELS]


def gate_kernel(
    starts, wide, count_ref, upper_ref, w_ref, y_ref, z_ref, gain_ref, ratio_ref, mean_ref, dy_ref, dz_ref, grad_ref, coefs
):
    step = pl.program_id(0)

    @pl.when(step == 0)
    def _():
        cubes = ratio_ref[...] * ratio_ref[...] * ratio_ref[...] * mean_ref[...]
        rows = []
        for j in range(len(starts)):
            total = cubes[0:1] * count_ref[j, 0]
            for w in range(1, LEVELS):
                total = total + cubes[w : w + 1] * count_ref[j, w]
            rows.append(total)
        columns = as_columns(jnp.concatenate(rows))
        for j in range(len(starts)):
            coefs[j] = jnp.broadcast_to(columns[:, j : j + 1], coefs.shape[1:])

    grad_all = dot(upper_ref[0], w_ref[...], ((1,), (1,)))
    coef = coefs[tile_range(starts, wide, step)]
    for c in range(0, wide, LANES):
        at = slice(c, c + LANES)
        grad_t = grad_all[:, at]
        z = z_ref[:, at].astype(F32)
        sig = jax.nn.sigmoid(z)
        act = z * sig
        y = y_ref[:, at]
        q = y * act
        dq = gain_ref[:, at] * grad_t - q * coef
        dy_ref[:, at] = (dq * act).astype(BF)
        dz_ref[:, at] = (dq * y * (sig * (1.0 + z * (1.0 - sig)))).astype(BF)
        grad_ref[0:1, at] = jnp.sum(q * grad_t, axis=0, keepdims=True)


def tile_range(starts, wide, step):
    index = 0
    for start in starts[1:]:
        index = index + jnp.where(step * wide >= start, 1, 0)
    return index


def mixed_kernel(plan, ns, tok, here_ref, count_ref, ratio_ref, x_ref, *refs):
    shares, out_ref = refs[:-1], refs[-1]
    at = pl.ds(pl.multiple_of(here_ref[0] * tok, tok), tok)
    ratios = as_columns(ratio_ref[:, at])
    x = x_ref[...].astype(F32)
    for w in range(LEVELS):
        total = None
        for k in range(ns):
            for j in plan[w]:
                term = shares[k][j].astype(F32) * count_ref[k, j * LEVELS + w]
                total = term if total is None else total + term
        out_ref[w] = (x + ratios[:, w : w + 1] * total).astype(BF)


def dp_terms(others):
    return [swapped(other, "dp", k + 1) for k, other in enumerate(others)]


def over_seq(value):
    dense = value.reshape(-1, LANES)
    total = dense
    for k in range(1, lax.axis_size("seq")):
        total = total + swapped(dense, "seq", k)
    return total.reshape(value.shape)


def fsdp_half(own, got):
    nf = lax.axis_size("fsdp")
    f = lax.axis_index("fsdp")

    def part(offset):
        total = picked(own, f ^ offset).astype(F32)
        for other in got:
            total = total + picked(other, f ^ offset).astype(F32)
        return total.astype(BF)

    kept = jnp.stack([part(e) for e in range(0, nf, 2)])
    sent = jnp.stack([part(e ^ 1) for e in range(0, nf, 2)])
    return kept, sent


def fsdp_rest(kept, got):
    k = 2
    while k < lax.axis_size("fsdp"):
        total = (kept.astype(F32) + got.astype(F32)).astype(BF)
        kept, sent = total[::2], total[1::2]
        got = swapped(sent, "fsdp", k)
        k *= 2
    return kept[0], got[0]


def shards(
    tokens,
    lengths,
    norm_gain,
    w_in,
    w_dt,
    conv_w,
    conv_b,
    dt_bias,
    a_log,
    skip,
    gate_gain,
    w_out,
    cotangent,
):
    nd, ns, nf = lax.axis_size("dp"), lax.axis_size("seq"), lax.axis_size("fsdp")
    d, s, f = lax.axis_index("dp"), lax.axis_index("seq"), lax.axis_index("fsdp")
    tok = tokens.shape[1]
    length = ns * tok
    blocks = length // SPAN
    heads = HEADS // ns
    run = heads // nd
    width = heads * HEADDIM
    own_bc = 2 * STATE // ns
    used = width + own_bc
    cols = -(-(used + heads) // LANES) * LANES
    rows_in = w_in.shape[0]
    reach = CONV - 1

    levels = np.array(
        [[level_of(dd * (HEADS // nd) + ss * run + i) for dd in range(nd) for i in range(run)] for ss in range(ns)]
    )
    cuts = [0] + [h for h in range(1, heads) if (levels[:, h] != levels[:, h - 1]).any()] + [heads]
    ranges = [(a, b) for a, b in zip(cuts, cuts[1:])]
    range_level = np.array([[levels[ss, a] for a, _ in ranges] for ss in range(ns)])
    counts = (range_level[:, :, None] <= np.arange(LEVELS)[None, None, :]).astype(np.float32)
    counted = picked(jnp.asarray(counts), s)
    theirs = picked(
        jnp.asarray(np.stack([[counts[i ^ k].reshape(-1) for k in range(ns)] for i in range(ns)])), s
    )
    lowest = [int(range_level[ss].min()) for ss in range(ns)]

    def by_head(vector):
        lead = vector.shape[:-1]
        per = vector.shape[-1] // HEADS
        cut = vector.reshape(lead + (nd, ns, run * per))
        mine = lax.dynamic_index_in_dim(cut, s, len(lead) + 1, keepdims=False)
        return mine.reshape(lead + (heads * per,))

    def for_groups(matrix):
        per = matrix.shape[1] // HEADS
        cut = matrix.reshape(matrix.shape[0], nd, ns, run * per)
        return jnp.transpose(cut, (2, 0, 1, 3)).reshape(ns, matrix.shape[0], heads * per)

    def from_groups(stack):
        per = stack.shape[2] // heads
        cut = stack.reshape(ns, stack.shape[1], nd, run * per)
        return jnp.transpose(cut, (1, 2, 0, 3)).reshape(stack.shape[1], HEADS * per)

    pad_cols = cols - used - heads
    half = width // 2
    first = half + cols - width
    group_x = for_groups(w_in[:, INNER : 2 * INNER])
    stack = jnp.concatenate(
        [
            group_x[:, :, :half],
            w_in[:, 2 * INNER :].reshape(rows_in, ns, own_bc).transpose(1, 0, 2),
            for_groups(w_dt),
            jnp.zeros((ns, rows_in, pad_cols), BF),
            group_x[:, :, half:],
            for_groups(w_in[:, :INNER]),
        ],
        axis=2,
    )
    own_x = tokens[0].astype(F32)
    scale = lax.rsqrt(jnp.mean(own_x * own_x, axis=-1, keepdims=True) + EPS)
    xn_own = (own_x * scale * norm_gain).astype(BF)
    xn_across = swapped(xn_own, "seq", 2)
    xn_pieces = [xn_own, swapped(xn_own, "seq", 1), xn_across, swapped(xn_across, "seq", 1)]
    arrived = [picked(stack, s)] + [swapped(picked(stack, s ^ k), "seq", k) for k in range(1, ns)]
    mine = filled((ns, rows_in, stack.shape[2]), [(p, None, (s ^ k, None, None)) for k, p in enumerate(arrived)])
    mine_z = mine[:, :, cols:]

    def needed(at, level):
        return min(lowest[at], lowest[at ^ 1]) <= level

    halves = [cotangent[w : w + 2, 0] for w in range(0, LEVELS, 2)]
    singles = [cotangent[w, 0] for w in range(LEVELS)]

    def beside(level, *others):
        block = after(halves[level // 2], *others)
        return swapped(block, "seq", 1, lambda i, j: needed(j, level + 1))

    def across(level, *others):
        block = after(singles[level], *others)
        return swapped(block, "seq", 2, lambda i, j: needed(j, level))

    def far(level, block):
        return swapped(block, "seq", 1, lambda i, j: needed(j, level))

    positions = jnp.arange(length, dtype=jnp.int32)
    ends = jnp.cumsum(lengths[0])[:-1]
    seg = jnp.sum((positions[:, None] >= ends[None, :]).astype(jnp.int32), axis=1)
    seg_before = jnp.concatenate([jnp.full((1,), -1, jnp.int32), seg[SPAN - 1 : length - 1 : SPAN]])
    seg_pad = jnp.concatenate([jnp.full((reach,), -1, jnp.int32), seg])
    masks = [(seg_pad[k : k + length] == seg) for k in range(reach)]
    mask_cols = [m.astype(F32) for m in masks]
    mask_cols += [jnp.pad(m, (0, reach - k))[reach - k :] for k, m in enumerate(mask_cols)]
    mask_cols = jnp.pad(jnp.stack(mask_cols, axis=1), ((0, 0), (0, LANES - 2 * reach)))

    def conv_params(s_part, bc_part):
        return by_head(s_part), bc_part

    weight_s = jnp.concatenate(
        [by_head(conv_w[:, :INNER]), by_head(conv_b[None, :INNER]), jnp.zeros((3, width), F32)]
    )
    weight_r = jnp.pad(
        lax.dynamic_slice_in_dim(conv_w, INNER + s * own_bc, own_bc, 1), ((0, 0), (0, cols - used))
    )
    bias_r = jnp.pad(
        lax.dynamic_slice_in_dim(conv_b, INNER + s * own_bc, own_bc, 0), (0, cols - used)
    )
    bias = by_head(dt_bias)
    rate = -jnp.exp(by_head(a_log))
    skip_own = by_head(skip)
    gain = by_head(gate_gain)

    def over_fsdp(chunk):
        return lax.all_gather(chunk, "fsdp", axis=0, tiled=False)

    def over_dp(held):
        pieces = [held] + [swapped(held, "dp", j) for j in range(1, nd)]
        moves = [
            (piece, i, (d ^ j, None, i, None, None)) for j, piece in enumerate(pieces) for i in range(nf)
        ]
        return pieces, moves

    held_a = over_fsdp(mine[:, :, :first])
    held_b = over_fsdp(mine[:, :, first:cols])
    other_out = [swapped(w_out, "dp", j) for j in range(1, nd)]
    held_a, other_out = together(held_a, other_out)
    small_ones = (seg, seg_before, mask_cols, weight_s, weight_r, bias_r, bias, rate, skip_own, gain, theirs)
    held_a, small_ones, halves, singles = together(held_a, small_ones, halves, singles)
    seg, seg_before, mask_cols, weight_s, weight_r, bias_r, bias, rate, skip_own, gain, theirs = small_ones
    near_high, near_low = beside(2, held_a), beside(0, held_a)
    chip3 = across(3, held_a)
    pieces_a, moves_a = over_dp(held_a)
    held_b, moves_a_there, chip3, near_high, xn_pieces = together(
        held_b, [m[0] for m in moves_a], chip3, near_high, xn_pieces
    )
    xn = filled((ns, tok, D), [(p, None, (s ^ k, None, None)) for k, p in enumerate(xn_pieces)])
    xn = xn.reshape(length, D)

    moves_a = [(p,) + m[1:] for p, m in zip(moves_a_there, moves_a)]
    far3 = far(3, chip3)
    pieces_b, moves_b = over_dp(held_b)
    full_a = filled((nd, ns, nf, rows_in, first), moves_a).reshape(D, first)
    full_b = filled((nd, ns, nf, rows_in, half), moves_b).reshape(D, half)
    parts_z = mine_z.reshape(ns, 2, rows_in // 2, width)
    held_z = over_fsdp(after(parts_z[:, 0], held_a))
    late_z = over_fsdp(after(parts_z[:, 1], held_b))
    held_out = over_fsdp(after(jnp.stack([w_out] + other_out), held_z))

    xn_turned = xn.T
    proj_a = dot(xn, full_a).astype(BF)

    proj_r = proj_a[:, half:]
    mixer = jnp.concatenate([jnp.zeros((reach, cols - width), BF), proj_r], axis=0)

    def taken(k):
        rows = mixer[k : k + length].astype(F32)
        return rows * mask_cols[:, k : k + 1] if k < reach else rows

    pre_r = bias_r
    for k in range(CONV):
        pre_r = pre_r + taken(k) * weight_r[k]
    bc_own = jax.nn.silu(pre_r).astype(BF)[:, :own_bc]
    bc_across = swapped(bc_own, "seq", 2)
    bc = [bc_own, swapped(bc_own, "seq", 1), bc_across, swapped(bc_across, "seq", 1)]
    chip2, chip1 = across(2, bc_across), across(1, bc_across)
    proj_b = dot(xn, after(full_b, proj_a, xn_turned, bc_across)).astype(BF)
    proj_b, far3, near_low, held_z = together(proj_b, far3, near_low, held_z)
    pieces_z = over_dp(held_z)[0]
    bc = reordered_by_xor(bc, s)
    b_in = jnp.concatenate(bc[: ns // 2], axis=1)
    c_out = jnp.concatenate(bc[ns // 2 :], axis=1)

    def padded(rows):
        return jnp.pad(rows, ((0, 0), (0, LANES - rows.shape[1])))

    pre_dt = proj_r[:, own_bc : own_bc + heads].astype(F32) + bias
    steps = jax.nn.softplus(pre_dt)
    tails = [
        p.reshape(blocks, SPAN, p.shape[1])[: blocks - 1, SPAN - HALO :, :half] for p in (proj_a, proj_b)
    ]
    operands = (
        seg_before,
        seg[:, None],
        seg[None, :],
        mask_cols,
        proj_a,
        proj_b,
        jnp.concatenate([jnp.zeros((1, HALO, width), BF), jnp.concatenate(tails, axis=2)]),
        weight_s,
        b_in,
        c_out,
        padded(steps),
        padded(rate[None, :]),
        jnp.repeat(skip_own, HEADDIM)[None, :],
    )
    y, priors = scan_forward(heads, blocks, operands)
    y, chip2, late_z = together(y, chip2, late_z)
    far2, chip0 = far(2, chip2), across(0, y)
    moves_z = [
        (piece, i, (d ^ j, None, i, h, None, None))
        for h, pieces in enumerate([pieces_z, over_dp(late_z)[0]])
        for j, piece in enumerate(pieces)
        for i in range(nf)
    ]
    full_z = filled((nd, ns, nf, 2, rows_in // 2, width), moves_z).reshape(D, width)
    proj_z = dot(xn, full_z).astype(BF)
    proj_z, chip1 = together(proj_z, chip1)
    far1 = far(1, chip1)
    q = y * jax.nn.silu(proj_z.astype(F32))
    q_gain = (q * gain).astype(BF)
    lanes = [(a * HEADDIM, b * HEADDIM) for a, b in ranges]
    squares = jnp.stack([jnp.sum(q[:, a:b] * q[:, a:b], axis=1) for a, b in lanes])
    widths = np.array([[(HEADS >> 3 - w) * HEADDIM] for w in range(LEVELS)], np.float32)
    per_level = jnp.sum(counted[:, :, None] * squares[:, None, :], axis=0)
    ratio, chip0 = together(lax.rsqrt(over_seq(per_level) / widths + EPS), chip0)
    far0 = far(0, chip0)

    plan = [[w for w in range(LEVELS) if range_level[:, j].min() <= w] for j in range(len(lanes))]
    out_rows = width // nd
    range_of = [next(j for j, (a, b) in enumerate(lanes) if a <= i * out_rows < b) for i in range(nd)]
    here = jnp.stack([s, d]).astype(jnp.int32)
    smem = pl.BlockSpec(memory_space=pltpu.SMEM)
    cot_pieces = [cotangent, near_low, near_high, chip0, chip1, chip2, chip3, far0, far1, far2, far3]
    cot_specs = [pl.BlockSpec((LEVELS, 1, tok, TILE), lambda i: (0, 0, 0, i))]
    cot_specs += [pl.BlockSpec((2, tok, TILE), lambda i: (0, 0, i))] * 2
    cot_specs += [pl.BlockSpec((tok, TILE), lambda i: (0, i))] * (2 * LEVELS)
    where = [[(0, (w, 0)), (1 + w // 2, (w % 2,)), (3 + w, ()), (3 + LEVELS + w, ())] for w in range(LEVELS)]
    upper, *grad_out = call(
        functools.partial(upper_kernel, where, plan, nd, tok, ns),
        grid=(D // TILE,),
        in_specs=[
            smem,
            smem,
            smem,
            pl.BlockSpec((LEVELS, length), lambda i: (0, 0)),
            pl.BlockSpec((width, length), lambda i: (0, 0)),
        ]
        + cot_specs,
        out_specs=[pl.BlockSpec((len(lanes), length, TILE), lambda i: (0, 0, i))]
        + [pl.BlockSpec((out_rows, TILE), lambda i: (0, i))]
        + [pl.BlockSpec((out_rows // 2, TILE), lambda i: (0, i))] * (2 * nd - 2),
        out_shape=[jax.ShapeDtypeStruct((len(lanes), length, D), BF)]
        + [jax.ShapeDtypeStruct((out_rows, D), BF)]
        + [jax.ShapeDtypeStruct((out_rows // 2, D), BF)] * (2 * nd - 2),
        scratch_shapes=[pltpu.VMEM((length, LANES), F32)],
        name="upper",
    )(here, jnp.asarray(range_of, jnp.int32), counted, ratio, q_gain.T, *cot_pieces)
    out_first, out_second = dp_terms(grad_out[1::2]), dp_terms(grad_out[2::2])

    held_out, upper = together(held_out, upper)
    *shares, inner, full_out = call(
        functools.partial(products_kernel, where, plan, lanes, tok, ns, nd),
        grid=(D // TILE,),
        in_specs=[
            smem,
            smem,
            pl.BlockSpec((length, width), lambda i: (0, 0)),
        ]
        + [pl.BlockSpec((nf, nd, w_out.shape[0], TILE), lambda i: (0, 0, 0, i))]
        + cot_specs,
        out_specs=[pl.BlockSpec((len(lanes), tok, TILE), lambda i: (0, 0, i))] * ns
        + [pl.BlockSpec((LEVELS, length), lambda i: (0, 0))]
        + [pl.BlockSpec((width, TILE), lambda i: (0, i))],
        out_shape=[jax.ShapeDtypeStruct((len(lanes), tok, D), BF)] * ns
        + [jax.ShapeDtypeStruct((LEVELS, length), F32)]
        + [jax.ShapeDtypeStruct((width, D), BF)],
        scratch_shapes=[pltpu.VMEM((LEVELS, length, LANES), F32)],
        name="products",
    )(here, counted, q_gain, held_out, *cot_pieces)
    means, out_first = together(over_seq(inner) / widths, out_first)
    shares = [shares[0]] + [swapped(after(shares[k], means), "seq", k) for k in range(1, ns)]

    starts = [a for a, _ in lanes]
    wide = min(min(b - a for a, b in lanes), TILE)
    cols_of = pl.BlockSpec((length, wide), lambda i: (0, i))
    scalars = pl.BlockSpec((LEVELS, length), lambda i: (0, 0))
    dy, dz, grad_gate = call(
        functools.partial(gate_kernel, starts, wide),
        grid=(width // wide,),
        in_specs=[
            smem,
            pl.BlockSpec((1, length, D), lambda i: (tile_range(starts, wide, i), 0, 0)),
            pl.BlockSpec((wide, D), lambda i: (i, 0)),
            cols_of,
            cols_of,
            pl.BlockSpec((1, wide), lambda i: (0, i)),
            scalars,
            scalars,
        ],
        out_specs=[cols_of, cols_of, pl.BlockSpec((8, wide), lambda i: (0, i))],
        out_shape=[
            jax.ShapeDtypeStruct((length, width), BF),
            jax.ShapeDtypeStruct((length, width), BF),
            jax.ShapeDtypeStruct((8, width), F32),
        ],
        scratch_shapes=[pltpu.VMEM((len(lanes), length, LANES), F32)],
        name="gate_backward",
    )(counted, upper, full_out, y, proj_z, gain[None], ratio, means)
    grad_gate = grad_gate[0]

    def in_terms(dproj, at, first=0, columns=None):
        columns = columns or dproj.shape[1]
        out = row_terms(xn_turned, dproj, at, nd, ns, nf, first, columns)
        return out.reshape(nf, ns * rows_in, columns)

    z_other = [in_terms(dz, d ^ k) for k in range(1, nd)]
    z_got = dp_terms(z_other)
    dy, out_second, shares[1] = together(after(dy, *z_other), out_second, shares[1])
    chunk = (nf, out_rows // nf, D)
    out_got = [jnp.concatenate([u, v]).reshape(chunk) for u, v in zip(out_first, out_second)]
    out_kept, out_sent = fsdp_half(grad_out[0].reshape(chunk), out_got)
    dy = after(dy, out_sent)
    out_half = swapped(out_sent, "fsdp", 1)

    dproj_s, dbc, ddt, drate, dsum = scan_backward(heads, blocks, operands, y, priors, dy)
    dproj_s, dbc, out_half, shares[2] = together(dproj_s, dbc, out_half, shares[2])
    dbc = dbc.astype(BF)
    dbc_parts = reordered_by_xor([dbc[:, j * own_bc : (j + 1) * own_bc] for j in range(ns)], s)
    dbc_got = [swapped(dbc_parts[k], "seq", k) for k in range(1, ns)]
    left_other = [in_terms(dproj_s, d ^ k, 0, half) for k in range(1, nd)]
    left_got = dp_terms(left_other)
    late_s = after(dproj_s, *left_other)
    middle_other = [in_terms(late_s, d ^ k, half, half) for k in range(1, nd)]
    middle_got = dp_terms(middle_other)
    dz_late, z_got = together(after(dz, *middle_other), z_got)
    z_kept, z_sent = fsdp_half(in_terms(dz_late, d), z_got)
    z_half = swapped(z_sent, "fsdp", 1)
    own_s = in_terms(after(dproj_s, z_sent), d)
    own_s, left_got, dbc_got = together(own_s, left_got, dbc_got)
    left_kept, left_sent = fsdp_half(own_s[:, :, :half], left_got)
    left_half = swapped(left_sent, "fsdp", 1)
    dbc_own = after(dbc_parts[0].astype(F32), left_sent)
    for got in dbc_got:
        dbc_own = dbc_own + got.astype(F32)
    dpre = jnp.pad(dbc_own, ((0, 0), (0, cols - used))) * silu_slope(pre_r)
    grad_b_r = jnp.sum(dpre, axis=0)[:own_bc]
    grad_w_r = jnp.stack([jnp.sum(dpre * taken(k), axis=0) for k in range(CONV)])[:, :own_bc]
    dmixer = dpre * weight_r[reach]
    for k in range(reach):
        back = reach - k
        later = (dpre * mask_cols[:, k : k + 1])[back:]
        dmixer = dmixer + jnp.pad(later, ((0, back), (0, 0))) * weight_r[k]
    dpre_dt = ddt[:, :heads] * jax.nn.sigmoid(pre_dt)
    dproj_r = jnp.concatenate(
        [dmixer[:, :own_bc].astype(BF), dpre_dt.astype(BF), jnp.zeros((length, pad_cols), BF)], axis=1
    )
    dproj_r, z_half = together(dproj_r, z_half)
    z_pair = fsdp_rest(z_kept, z_half)
    right_other = [in_terms(dproj_r, d ^ k) for k in range(1, nd)]
    right_got = dp_terms(right_other)
    own_r = in_terms(after(dproj_r, *right_other), d)

    dxn = input_grad(dz, dproj_s, after(dproj_r, own_r), full_z, full_a, full_b, ns, tok)
    beside_near = swapped(picked(dxn, s ^ 1), "seq", 1)
    beside_far = swapped(picked(dxn, s ^ 3), "seq", 1)
    out_pair = fsdp_rest(out_kept, after(out_half, own_r))
    dxn, left_half, z_pair = together(dxn, left_half, z_pair)
    left_pair = fsdp_rest(left_kept, left_half)
    flat = flattened(
        [
            jnp.concatenate([dsum[:CONV], grad_w_r], axis=1).reshape(-1),
            dsum[CONV],
            grad_b_r,
            grad_gate,
            jnp.sum(dpre_dt, axis=0),
            drate[0, :heads] * rate,
            jnp.sum(dsum[CONV + 1].reshape(heads, HEADDIM), axis=1),
        ]
    )
    near = picked(dxn, s).astype(F32) + beside_near.astype(F32)
    far = (picked(dxn, s ^ 2).astype(F32) + beside_far.astype(F32)).astype(BF)
    dxn_across = swapped(far, "seq", 2)
    middle_got, right_got, far, out_pair = together(middle_got, right_got, far, out_pair)
    kept_m, sent_m = fsdp_half(own_s[:, :, half:], middle_got)
    kept_r, sent_r = fsdp_half(own_r, right_got)
    right_kept = jnp.concatenate([kept_m, kept_r], axis=2)
    right_sent = jnp.concatenate([sent_m, sent_r], axis=2)
    right_half = swapped(right_sent, "fsdp", 1)

    dxn_own = near + after(dxn_across, right_sent).astype(F32)
    grad_norm = jnp.sum(dxn_own * own_x * scale, axis=0)
    scaled = norm_gain * dxn_own
    dx = scale * scaled - own_x * scale**3 * jnp.mean(own_x * scaled, axis=-1, keepdims=True)
    dx = dx + jnp.sum(after(cotangent, right_sent)[:, 0].astype(F32), axis=0)
    flat = jnp.concatenate([flat, grad_norm.reshape(-1, LANES)])
    flat = butterfly(flat, "dp")
    dx = dx.astype(BF)

    z_pair, left_pair, right_half, flat, dx = together(z_pair, left_pair, right_half, flat, dx)
    right_pair = fsdp_rest(right_kept, right_half)

    def whole_sum(pair):
        total = (pair[0].astype(F32) + pair[1].astype(F32)).astype(BF)
        return total.reshape(ns, rows_in, total.shape[1])

    early = jnp.concatenate([whole_sum(z_pair), whole_sum(left_pair)], axis=2)
    early_got = [picked(early, s)] + [swapped(picked(early, s ^ k), "seq", k) for k in range(1, ns)]
    mixed = call(
        functools.partial(
            mixed_kernel,
            [[j for j in range(len(lanes)) if range_level[:, j].min() <= w] for w in range(LEVELS)],
            ns,
            tok,
        ),
        grid=(D // TILE,),
        in_specs=[
            smem,
            smem,
            pl.BlockSpec((LEVELS, length), lambda i: (0, 0)),
            pl.BlockSpec((tok, TILE), lambda i: (0, i)),
        ]
        + [pl.BlockSpec((len(lanes), tok, TILE), lambda i: (0, 0, i))] * ns,
        out_specs=pl.BlockSpec((LEVELS, tok, TILE), lambda i: (0, 0, i)),
        out_shape=jax.ShapeDtypeStruct((LEVELS, tok, D), BF),
        name="mixed",
    )(here, theirs, ratio, tokens[0], *after(shares, right_half))[:, None]
    flat = butterfly(flat, "fsdp")
    early_got, right_pair, mixed = together(early_got, right_pair, mixed)
    late = whole_sum(right_pair)
    late_got = [picked(late, s)] + [swapped(picked(late, s ^ k), "seq", k) for k in range(1, ns)]
    early = jnp.stack(reordered_by_xor(early_got, s))
    late = jnp.stack(reordered_by_xor(late_got, s))
    got_z = early[:, :, :width]
    got_x = jnp.concatenate([early[:, :, width:], late], axis=2)
    sum_out = out_pair[0].astype(F32) + out_pair[1].astype(F32)


    sum_in = jnp.concatenate(
        [
            from_groups(got_z),
            from_groups(got_x[:, :, :width]),
            jnp.transpose(got_x[:, :, width:used], (1, 0, 2)).reshape(rows_in, 2 * STATE),
        ],
        axis=1,
    ).astype(F32)
    sum_dt = from_groups(got_x[:, :, used : used + heads]).astype(F32)

    sizes = [CONV * used, used, width, heads, heads, heads]
    filling = -sum(sizes) % 1024
    sizes += [filling, D]
    every = seq_gather(flat, s).reshape(ns, -1)
    starts = np.cumsum([0] + sizes)
    pieces = [every[:, a : a + n] for a, n in zip(starts, sizes)]

    def heads_back(rows):
        lead = rows.shape[1:-1]
        cut = rows.reshape((ns,) + lead + (nd, rows.shape[-1] // nd))
        order = tuple(range(1, 1 + len(lead))) + (1 + len(lead), 0, 2 + len(lead))
        return jnp.transpose(cut, order).reshape(lead + (-1,))

    conv_rows = pieces[0].reshape(ns, CONV, used)
    conv_all = jnp.concatenate(
        [
            heads_back(conv_rows[:, :, :width]),
            jnp.transpose(conv_rows[:, :, width:], (1, 0, 2)).reshape(CONV, 2 * STATE),
        ],
        axis=1,
    )
    bias_all = jnp.concatenate([heads_back(pieces[1][:, :width]), pieces[1][:, width:].reshape(-1)])
    return (
        mixed,
        dx[None],
        jnp.sum(pieces[7], axis=0),
        sum_in,
        sum_dt,
        conv_all,
        bias_all,
        heads_back(pieces[3]),
        heads_back(pieces[4]),
        heads_back(pieces[5]),
        heads_back(pieces[2]),
        sum_out,
    )


def solution(mesh):
    rows = P(("dp", "seq", "fsdp"), None)
    held = P(("dp", "fsdp"), "seq", None)
    levels = P(None, ("dp", "fsdp"), "seq", None)
    placed = (held, P(("dp", "fsdp"), None), P(), rows, rows, P(), P(), P(), P(), P(), P(), rows, levels)
    return jax.shard_map(
        shards,
        mesh=mesh,
        in_specs=placed,
        out_specs=(levels, held, P(), rows, rows, P(), P(), P(), P(), P(), P(), rows),
        check_vma=False,
    )
```

```python
import functools

import jax
import jax.numpy as jnp
import numpy as np
from jax import lax
from jax.experimental import pallas as pl
from jax.experimental.pallas import tpu as pltpu
from jax.sharding import PartitionSpec as P

D = 2048
HEADS = 64
HEADDIM = 64
STATE = 128
CONV = 4
SPAN = 128
INNER = 4096
EPS = 1e-05
LEVELS = 4
BF = jnp.bfloat16
F32 = jnp.float32
HIGH = lax.Precision.HIGHEST
LANES = 128
HALO = 16
TILE = 256
VMEM_LIMIT = 48 * 1024 * 1024


def dot(a, b, dims=((1,), (0,)), precision=None):
    return lax.dot_general(a, b, (dims, ((), ())), preferred_element_type=F32, precision=precision)


def silu_slope(v):
    sig = jax.nn.sigmoid(v)
    return sig * (1.0 + v * (1.0 - sig))


def level_of(head):
    return 0 if head < 8 else 1 if head < 16 else 2 if head < 32 else 3


def swapped(value, axis, k, keep=None):
    pairs = [(i, i ^ k) for i in range(lax.axis_size(axis))]
    if keep is not None:
        pairs = [p for p in pairs if keep(*p)]
    return lax.ppermute(value, axis, pairs)


def after(value, *others):
    return lax.optimization_barrier((value,) + others)[0]


def together(*values):
    return lax.optimization_barrier(values)


def flattened(vectors):
    flat = jnp.concatenate(vectors)
    return jnp.pad(flat, (0, -flat.shape[0] % 1024)).reshape(-1, LANES)


def butterfly(value, axis):
    k = 1
    while k < lax.axis_size(axis):
        value = value + swapped(value, axis, k)
        k *= 2
    return value


def picked(array, index):
    return lax.dynamic_index_in_dim(array, index, 0, keepdims=False)


def seq_gather(block, here):
    return jnp.stack(reordered_by_xor([block] + [swapped(block, "seq", k) for k in range(1, 4)], here))


def reordered_by_xor(pieces, here):
    k = 1
    while k < len(pieces):
        flip = (here & k) > 0
        pieces = [jnp.where(flip, pieces[j ^ k], piece) for j, piece in enumerate(pieces)]
        k *= 2
    return pieces


def call(kernel, **kwargs):
    return pl.pallas_call(
        kernel,
        compiler_params=pltpu.CompilerParams(vmem_limit_bytes=VMEM_LIMIT),
        cost_estimate=pl.CostEstimate(flops=1, bytes_accessed=1, transcendentals=0),
        **kwargs,
    )


def filled(shape, moves):
    arrays, plan, rows = [], [], []
    block = tuple(size if index is None else 1 for size, index in zip(shape, moves[0][2]))
    for piece, lead, place in moves:
        at = next((i for i, a in enumerate(arrays) if a is piece), len(arrays))
        if at == len(arrays):
            arrays.append(piece)
        plan.append((at, lead))
        rows.append(jnp.stack([jnp.asarray(0 if n is None else n, jnp.int32) for n in place]))

    def kernel(index_ref, *refs):
        pieces, out = refs[:-1], refs[-1]
        for m, (at, lead) in enumerate(plan):

            @pl.when(pl.program_id(0) == m)
            def _():
                value = pieces[at][...] if lead is None else pieces[at][lead]
                out[...] = value.reshape(block)

    return call(
        kernel,
        grid_spec=pltpu.PrefetchScalarGridSpec(
            num_scalar_prefetch=1,
            grid=(len(plan),),
            in_specs=[
                pl.BlockSpec(a.shape, lambda i, t, n=a.ndim: (0,) * n) for a in arrays
            ],
            out_specs=pl.BlockSpec(
                block, lambda i, t: tuple(t[i, n] for n in range(len(shape)))
            ),
        ),
        out_shape=jax.ShapeDtypeStruct(shape, arrays[0].dtype),
        name="filled",
    )(jnp.stack(rows), *arrays)


def terms_kernel(ns, nf, at_ref, left_ref, right_ref, out_ref):
    value = dot(left_ref[...], right_ref[...]).astype(BF)
    rows = value.shape[0] // (ns * nf)
    for i in range(ns):
        for k in range(nf):
            out_ref[k, i] = value[(i * nf + k) * rows : (i * nf + k + 1) * rows]


def row_terms(turned, right, at, nd, ns, nf, first, columns):
    depth = turned.shape[1]
    rows = turned.shape[0] // nd
    wide = TILE if columns % TILE == 0 else LANES
    return call(
        functools.partial(terms_kernel, ns, nf),
        grid_spec=pltpu.PrefetchScalarGridSpec(
            num_scalar_prefetch=1,
            grid=(columns // wide,),
            in_specs=[
                pl.BlockSpec((rows, depth), lambda i, t: (t[0], 0)),
                pl.BlockSpec((depth, wide), lambda i, t: (0, i + first // wide)),
            ],
            out_specs=pl.BlockSpec((nf, ns, rows // (nf * ns), wide), lambda i, t: (0, 0, 0, i)),
        ),
        out_shape=jax.ShapeDtypeStruct((nf, ns, rows // (nf * ns), columns), BF),
        name="row_terms",
    )(at.astype(jnp.int32)[None], turned, right)


def small_back_kernel(
    width, pre_ref, dbc_ref, in_ref, mask_ref, weight_ref, ddt_ref, pre_dt_ref, out_ref, sum_ref, ext, dext
):
    rows = pre_ref.shape[0]
    ext[0:HALO] = jnp.zeros((HALO, LANES), F32)
    ext[HALO:] = in_ref[...].astype(F32)
    pre = pre_ref[...]
    sig = jax.nn.sigmoid(pre)
    dpre = dbc_ref[...] * (sig * (1.0 + pre * (1.0 - sig)))
    dext[0:rows] = dpre
    dext[rows:] = jnp.zeros((HALO, LANES), F32)
    total = dpre * weight_ref[CONV - 1 : CONV, :]
    for k in range(CONV):
        term = ext[pl.ds(HALO - CONV + 1 + k, rows), :]
        if k < CONV - 1:
            term = term * mask_ref[:, k : k + 1]
            later = dext[pl.ds(CONV - 1 - k, rows), :] * mask_ref[:, CONV - 1 + k : CONV + k]
            total = total + later * weight_ref[k : k + 1, :]
        sum_ref[k : k + 1, :] = jnp.sum(dpre * term, axis=0, keepdims=True)
    sum_ref[CONV : CONV + 1, :] = jnp.sum(dpre, axis=0, keepdims=True)
    draw = ddt_ref[...] * jax.nn.sigmoid(pre_dt_ref[...])
    sum_ref[CONV + 1 : CONV + 2, :] = jnp.sum(draw, axis=0, keepdims=True)
    out_ref[...] = (total + pltpu.roll(draw, width, axis=1)).astype(BF)


def small_back(width, pre, dbc, proj, masks, weight, ddt, pre_dt):
    rows = pre.shape[0]
    return call(
        functools.partial(small_back_kernel, width),
        out_shape=[
            jax.ShapeDtypeStruct((rows, LANES), BF),
            jax.ShapeDtypeStruct((8, LANES), F32),
        ],
        scratch_shapes=[pltpu.VMEM((HALO + rows, LANES), F32), pltpu.VMEM((rows + HALO, LANES), F32)],
        name="small_back",
    )(pre, dbc, proj, masks, weight, ddt, pre_dt)


def input_grad_kernel(blocks, dz_ref, ds_ref, dr_ref, wz_ref, wa_ref, wb_ref, out_ref):
    half = wb_ref.shape[1]
    columns = ((1,), (1,))
    total = dot(dz_ref[...], wz_ref[...], columns)
    total = total + dot(ds_ref[:, :half], wa_ref[:, :half], columns)
    total = total + dot(ds_ref[:, half:], wb_ref[...], columns)
    total = total + dot(dr_ref[...], wa_ref[:, half:], columns)
    total = total.astype(BF)
    tok = total.shape[0] // blocks
    for i in range(blocks):
        out_ref[i] = total[i * tok : (i + 1) * tok]


def input_grad(dz, ds, dr, wz, wa, wb, blocks, tok):
    def whole(a):
        return pl.BlockSpec(a.shape, lambda i: (0, 0))

    def rows(a):
        return pl.BlockSpec((TILE, a.shape[1]), lambda i: (i, 0))

    return call(
        functools.partial(input_grad_kernel, blocks),
        grid=(wz.shape[0] // TILE,),
        in_specs=[whole(dz), whole(ds), whole(dr), rows(wz), rows(wa), rows(wb)],
        out_specs=pl.BlockSpec((blocks, tok, TILE), lambda i: (0, 0, i)),
        out_shape=jax.ShapeDtypeStruct((blocks, tok, wz.shape[0]), BF),
        name="input_grad",
    )(dz, ds, dr, wz, wa, wb)


def assembled(here_ref, pieces, nd, full_ref):
    halves = len(pieces) // nd
    nf, ns, rows = pieces[0].shape[:3]
    for n, piece in enumerate(pieces):
        h, j = divmod(n, nd)
        for k in range(nf):
            for i in range(ns):
                block = ((here_ref[1] ^ j) * ns + i) * nf + k
                at = pl.multiple_of((block * halves + h) * rows, rows)
                full_ref[pl.ds(at, rows), :] = piece[k, i]


def project_kernel(nd, count, here_ref, xn_ref, *refs):
    pieces, (out_ref, full_ref) = refs[:count], refs[count:]
    if nd:
        assembled(here_ref, pieces, nd, full_ref)
    else:
        full_ref[...] = pieces[0][...]
    out_ref[...] = dot(xn_ref[...], full_ref[...]).astype(BF)


def gated_kernel(nd, count, starts, wide, here_ref, xn_ref, y_ref, gain_ref, *refs):
    pieces, (out_ref, full_ref, gated_ref, turned_ref, squares_ref, sums) = refs[:count], refs[count:]
    step = pl.program_id(0)

    @pl.when(step == 0)
    def _():
        sums[...] = jnp.zeros_like(sums)

    if nd:
        assembled(here_ref, pieces, nd, full_ref)
    else:
        full_ref[...] = pieces[0][...]
    value = dot(xn_ref[...], full_ref[...]).astype(BF)
    out_ref[...] = value
    where = tile_range(starts, wide, step)
    for c in range(0, wide, LANES):
        at = slice(c, c + LANES)
        z = value[:, at].astype(F32)
        q = y_ref[:, at] * (z * jax.nn.sigmoid(z))
        gated = (q * gain_ref[:, at]).astype(BF)
        gated_ref[:, at] = gated
        turned_ref[at, :] = gated.T
        sums[where] += q * q

    @pl.when(step == pl.num_programs(0) - 1)
    def _():
        lane = lax.broadcasted_iota(jnp.int32, sums.shape[1:], 1)
        total = jnp.zeros(sums.shape[1:], F32)
        for j in range(len(starts)):
            total = jnp.where(lane == j, jnp.sum(sums[j], axis=1, keepdims=True), total)
        squares_ref[...] = total.T[: squares_ref.shape[0]]


def projections(here, xn, pieces, nd, rows, columns, gate=None):
    if pieces[0].ndim == 2:
        nd = 0
    wide = TILE if columns % TILE == 0 else LANES
    if gate is not None:
        y, gain, starts, wide = gate
    tokens, depth = xn.shape
    outs = [pl.BlockSpec((tokens, wide), lambda i: (0, i)), pl.BlockSpec((depth, wide), lambda i: (0, i))]
    shapes = [jax.ShapeDtypeStruct((tokens, columns), BF), jax.ShapeDtypeStruct((depth, columns), BF)]
    ins = [pl.BlockSpec(memory_space=pltpu.SMEM), pl.BlockSpec((tokens, depth), lambda i: (0, 0))]
    operands = [here, xn]
    scratch = []
    kernel = functools.partial(project_kernel, nd, len(pieces))
    if gate is not None:
        kernel = functools.partial(gated_kernel, nd, len(pieces), starts, wide)
        operands += [y, gain]
        ins += [outs[0], pl.BlockSpec((1, wide), lambda i: (0, i))]
        outs += [
            outs[0],
            pl.BlockSpec((wide, tokens), lambda i: (i, 0)),
            pl.BlockSpec((8, tokens), lambda i: (0, 0)),
        ]
        shapes += [
            shapes[0],
            jax.ShapeDtypeStruct((columns, tokens), BF),
            jax.ShapeDtypeStruct((8, tokens), F32),
        ]
        scratch = [pltpu.VMEM((len(starts), tokens, LANES), F32)]
    for piece in pieces:
        lead = piece.shape[:-1]
        ins.append(pl.BlockSpec(lead + (wide,), lambda i, n=len(lead): (0,) * n + (i,)))
    return call(
        kernel,
        grid=(columns // wide,),
        in_specs=ins,
        out_specs=outs,
        out_shape=shapes,
        scratch_shapes=scratch,
        name="gated" if gate is not None else "project",
    )(*operands, *pieces)


def tri(rows_first):
    a = lax.broadcasted_iota(jnp.int32, (SPAN, SPAN), 0)
    b = lax.broadcasted_iota(jnp.int32, (SPAN, SPAN), 1)
    return (a >= b) if rows_first else (a <= b)


def pair_of(lo, cols, p):
    return jnp.where(lo, cols[:, 2 * p : 2 * p + 1], cols[:, 2 * p + 1 : 2 * p + 2])


def decays(segc, segr, segp, dt, rate):
    cum = dot(tri(True).astype(F32), dt * rate, precision=HIGH)
    last = cum[SPAN - 1 : SPAN, :]
    keep = jnp.where(segc == segp, jnp.exp(cum), 0.0)
    to_end = jnp.where(segc == segr[:, SPAN - 1 : SPAN], jnp.exp(last - cum), 0.0)
    return cum, cum.T, keep, to_end


def spread_columns(ref, first, count):
    return [jnp.broadcast_to(ref[:, first + k : first + k + 1], (SPAN, LANES)) for k in range(count)]


def taps(ext, masks, at):
    terms = [ext[pl.ds(HALO - CONV + 1 + k, SPAN), at] for k in range(CONV)]
    return [t * m for t, m in zip(terms, masks)] + terms[CONV - 1 :]


def convolved(terms, weight_ref, at):
    total = weight_ref[CONV : CONV + 1, at] + terms[0] * weight_ref[0:1, at]
    for k in range(1, CONV):
        total = total + terms[k] * weight_ref[k : k + 1, at]
    return total


def forward_kernel(
    heads,
    segp_ref,
    segc_ref,
    segr_ref,
    mask_ref,
    in_a_ref,
    in_b_ref,
    halo_ref,
    weight_ref,
    b_ref,
    c_ref,
    dt_ref,
    rate_ref,
    skip_ref,
    y_ref,
    prior_ref,
    carry,
    to_end_u,
    ext,
):
    block = pl.program_id(0)
    width = heads * HEADDIM

    @pl.when(block == 0)
    def _():
        carry[...] = jnp.zeros_like(carry)

    prior_ref[0] = carry[...]
    ext[0:HALO] = halo_ref[0].astype(F32)
    half = in_b_ref.shape[1]
    ext[HALO:, :half] = in_a_ref[:, :half].astype(F32)
    ext[HALO:, half:] = in_b_ref[...].astype(F32)
    segc, segr = segc_ref[...], segr_ref[...]
    dt = dt_ref[...]
    cum, cumr, keep, to_end = decays(segc, segr, segp_ref[block], dt, rate_ref[...])
    bm, cm = b_ref[...], c_ref[...]
    mixing = dot(cm, bm, ((1,), (1,)))
    mixing = jnp.where(tri(True) & (segc == segr), mixing, 0.0)
    masks = spread_columns(mask_ref, 0, CONV - 1)
    lo = lax.broadcasted_iota(jnp.int32, (SPAN, LANES), 1) < HEADDIM
    for p in range(heads // 2):
        at = slice(p * LANES, (p + 1) * LANES)
        pre = convolved(taps(ext, masks, at), weight_ref, at)
        x2 = pre * jax.nn.sigmoid(pre)
        u2 = x2 * pair_of(lo, dt, p)
        ub = u2.astype(BF)
        total = dot(cm, carry[:, at].astype(BF)) * pair_of(lo, keep, p) + skip_ref[:, at] * x2
        inner = []
        for h in (2 * p, 2 * p + 1):
            decay = jnp.exp(jnp.minimum(cum[:, h : h + 1] - cumr[h : h + 1, :], 0.0))
            inner.append(dot((decay * mixing).astype(BF), ub))
        y_ref[:, at] = total + jnp.where(lo, inner[0], inner[1])
        to_end_u[:, at] = (u2 * pair_of(lo, to_end, p)).astype(BF)
    fresh = dot(bm, to_end_u[...], ((0,), (0,)))
    lo_row = lax.broadcasted_iota(jnp.int32, (1, LANES), 1) < HEADDIM
    for p in range(heads // 2):
        at = slice(p * LANES, (p + 1) * LANES)
        factor = pair_of(lo_row, keep[SPAN - 1 : SPAN, :], p)
        carry[:, at] = factor * carry[:, at] + fresh[:, at]


def split_dot(value, ones):
    high = value.astype(BF)
    low = (value - high.astype(F32)).astype(BF)
    return dot(high, ones) + dot(low, ones)


def backward_kernel(
    heads,
    segp_ref,
    segc_ref,
    segr_ref,
    mask_ref,
    in_a_ref,
    in_b_ref,
    halo_ref,
    weight_ref,
    b_ref,
    c_ref,
    dt_ref,
    rate_ref,
    skip_ref,
    y_ref,
    prior_ref,
    dy_ref,
    din_ref,
    dbc_ref,
    ddt_ref,
    drate_ref,
    dsum_ref,
    dcarry,
    after_state,
    keep_dy,
    to_end_u,
    slopes,
    along,
    ext,
    dext,
):
    step = pl.program_id(0)
    block = pl.num_programs(0) - 1 - step

    @pl.when(step == 0)
    def _():
        dcarry[...] = jnp.zeros_like(dcarry)
        after_state[...] = jnp.zeros_like(after_state)
        drate_ref[...] = jnp.zeros_like(drate_ref)
        dsum_ref[...] = jnp.zeros_like(dsum_ref)
        dext[SPAN:] = jnp.zeros((HALO, dext.shape[1]), F32)

    ext[0:HALO] = halo_ref[0].astype(F32)
    half = in_b_ref.shape[1]
    ext[HALO:, :half] = in_a_ref[:, :half].astype(F32)
    ext[HALO:, half:] = in_b_ref[...].astype(F32)
    segc, segr = segc_ref[...], segr_ref[...]
    dt = dt_ref[...]
    cum, cumr, keep, to_end = decays(segc, segr, segp_ref[block], dt, rate_ref[...])
    bm, cm = b_ref[...], c_ref[...]
    allowed = tri(False) & (segc == segr)
    mixing = jnp.where(allowed, dot(bm, cm, ((1,), (1,))), 0.0)
    masks = spread_columns(mask_ref, 0, CONV - 1)
    moved = spread_columns(mask_ref, CONV - 1, CONV - 1)
    lo = lax.broadcasted_iota(jnp.int32, (SPAN, LANES), 1) < HEADDIM
    dmixing = jnp.zeros((SPAN, SPAN), F32)
    for p in range(heads // 2):
        at = slice(p * LANES, (p + 1) * LANES)
        terms = taps(ext, masks, at)
        pre = convolved(terms, weight_ref, at)
        sig = jax.nn.sigmoid(pre)
        x2 = pre * sig
        dt2 = pair_of(lo, dt, p)
        u2 = x2 * dt2
        dyb = dy_ref[:, at]
        dy2 = dyb.astype(F32)
        skip = skip_ref[:, at]
        te2 = pair_of(lo, to_end, p)
        u_sides = (jnp.where(lo, u2, 0.0).astype(BF), jnp.where(lo, 0.0, u2).astype(BF))
        du = te2 * dot(bm, dcarry[:, at].astype(BF))
        inner = []
        for k in range(2):
            h = 2 * p + k
            decay = jnp.exp(jnp.minimum(cumr[h : h + 1, :] - cum[:, h : h + 1], 0.0))
            inner.append(dot((decay * mixing).astype(BF), dyb))
            dmixing = dmixing + decay * dot(u_sides[k], dyb, ((1,), (1,)))
        du = du + jnp.where(lo, inner[0], inner[1])
        keep_dy[:, at] = (pair_of(lo, keep, p) * dy2).astype(BF)
        to_end_u[:, at] = (te2 * u2).astype(BF)
        slopes[:, at] = dy2 * (y_ref[:, at] - skip * x2) - u2.astype(BF).astype(F32) * du
        along[:, at] = x2 * du
        dpre = (dt2 * du + skip * dy2) * (sig * (1.0 + pre * (1.0 - sig)))
        dext[0:SPAN, at] = dpre
        for k in range(CONV):
            dsum_ref[k : k + 1, at] += jnp.sum(dpre * terms[k], axis=0, keepdims=True)
        dsum_ref[CONV : CONV + 1, at] += jnp.sum(dpre, axis=0, keepdims=True)
        dsum_ref[CONV + 1 : CONV + 2, at] += jnp.sum(dy2 * x2, axis=0, keepdims=True)
        din = dpre * weight_ref[CONV - 1 : CONV, at]
        for k in range(CONV - 1):
            later = dext[pl.ds(CONV - 1 - k, SPAN), at]
            din = din + later * moved[k] * weight_ref[k : k + 1, at]
        din_ref[:, at] = din.astype(BF)
    dext[SPAN:] = dext[0:HALO]
    dmixing = jnp.where(allowed, dmixing, 0.0).astype(BF)
    dstate = dcarry[...].astype(BF)
    prior = prior_ref[0]
    dbc_ref[:, :STATE] = dot(dmixing, cm) + dot(to_end_u[...], dstate, ((1,), (1,)))
    dbc_ref[:, STATE:] = dot(dmixing, bm, ((0,), (0,))) + dot(
        keep_dy[...], prior.astype(BF), ((1,), (1,))
    )
    width = heads * HEADDIM
    ones = (
        lax.broadcasted_iota(jnp.int32, (width, LANES), 0) // HEADDIM
        == lax.broadcasted_iota(jnp.int32, (width, LANES), 1)
    ).astype(BF)
    at_end = jnp.sum(dcarry[...] * after_state[...], axis=0, keepdims=True)
    at_end = split_dot(jnp.broadcast_to(at_end, (16, width)), ones)[:1]
    dcum = split_dot(slopes[...], ones)
    da = dot(tri(False).astype(F32), dcum, precision=HIGH) + at_end
    ddt_ref[...] = rate_ref[...] * da + split_dot(along[...], ones)
    drate_ref[...] += jnp.sum(dt * da, axis=0, keepdims=True)
    fresh = dot(cm, keep_dy[...], ((0,), (0,)))
    lo_row = lax.broadcasted_iota(jnp.int32, (1, LANES), 1) < HEADDIM
    for p in range(heads // 2):
        at = slice(p * LANES, (p + 1) * LANES)
        factor = pair_of(lo_row, keep[SPAN - 1 : SPAN, :], p)
        dcarry[:, at] = factor * dcarry[:, at] + fresh[:, at]
    after_state[...] = prior


def scan_specs(heads, at, in_widths):
    width = heads * HEADDIM

    def rows(n):
        return pl.BlockSpec((SPAN, n), lambda i: (at(i), 0))

    def whole(*shape):
        return pl.BlockSpec(shape, lambda i: (0,) * len(shape))

    ins = [
        pl.BlockSpec(memory_space=pltpu.SMEM),
        rows(1),
        pl.BlockSpec((1, SPAN), lambda i: (0, at(i))),
        rows(LANES),
        rows(in_widths[0]),
        rows(in_widths[1]),
        pl.BlockSpec((1, HALO, width), lambda i: (at(i), 0, 0)),
        whole(8, width),
        rows(STATE),
        rows(STATE),
        rows(LANES),
        whole(1, LANES),
        whole(1, width),
    ]
    prior = pl.BlockSpec((1, STATE, width), lambda i: (at(i), 0, 0))
    return rows, whole, ins, prior


def scan_forward(heads, blocks, operands):
    rows, whole, ins, prior = scan_specs(heads, lambda i: i, [operands[n].shape[1] for n in (4, 5)])
    width = heads * HEADDIM
    return call(
        functools.partial(forward_kernel, heads),
        grid=(blocks,),
        in_specs=ins,
        out_specs=[rows(width), prior],
        out_shape=[
            jax.ShapeDtypeStruct((blocks * SPAN, width), F32),
            jax.ShapeDtypeStruct((blocks, STATE, width), F32),
        ],
        scratch_shapes=[
            pltpu.VMEM((STATE, width), F32),
            pltpu.VMEM((SPAN, width), BF),
            pltpu.VMEM((HALO + SPAN, width), F32),
        ],
        name="scan_forward",
    )(*operands)


def scan_backward(heads, blocks, operands, y, priors, dy):
    rows, whole, ins, prior = scan_specs(
        heads, lambda i: blocks - 1 - i, [operands[n].shape[1] for n in (4, 5)]
    )
    width = heads * HEADDIM
    return call(
        functools.partial(backward_kernel, heads),
        grid=(blocks,),
        in_specs=ins + [rows(width), prior, rows(width)],
        out_specs=[rows(width), rows(2 * STATE), rows(LANES), whole(1, LANES), whole(8, width)],
        out_shape=[
            jax.ShapeDtypeStruct((blocks * SPAN, width), BF),
            jax.ShapeDtypeStruct((blocks * SPAN, 2 * STATE), F32),
            jax.ShapeDtypeStruct((blocks * SPAN, LANES), F32),
            jax.ShapeDtypeStruct((1, LANES), F32),
            jax.ShapeDtypeStruct((8, width), F32),
        ],
        scratch_shapes=[
            pltpu.VMEM((STATE, width), F32),
            pltpu.VMEM((STATE, width), F32),
            pltpu.VMEM((SPAN, width), BF),
            pltpu.VMEM((SPAN, width), BF),
            pltpu.VMEM((SPAN, width), F32),
            pltpu.VMEM((SPAN, width), F32),
            pltpu.VMEM((HALO + SPAN, width), F32),
            pltpu.VMEM((SPAN + HALO, width), F32),
        ],
        name="scan_backward",
    )(*operands, y, priors, dy)


def as_columns(rows):
    few, tokens = rows.shape
    return jnp.concatenate([rows, jnp.zeros((LANES - few, tokens), F32)]).T


def level_block(pieces, spot):
    piece, lead = spot
    return pieces[piece][lead + (slice(None), slice(None))].astype(F32)


def upper_kernel(where, plan, nd, tok, ns, here_ref, range_ref, count_ref, ratio_ref, q_turned, *refs):
    count = 3 + 2 * LEVELS
    pieces, outs = refs[:count], refs[count:]
    upper_ref, grad_refs, coefs = outs[0], outs[1 : 2 * nd], outs[2 * nd]

    @pl.when(pl.program_id(0) == 0)
    def _():
        rows = [count_ref[j, w] * ratio_ref[w : w + 1, :] for j in range(len(plan)) for w in range(LEVELS)]
        coefs[...] = as_columns(jnp.concatenate(rows))

    for k in range(ns):
        at = here_ref[0] ^ k
        rows = pl.ds(pl.multiple_of(at * tok, tok), tok)
        levels = [level_block(pieces, where[w][k]) for w in range(LEVELS)]
        for j in range(len(plan)):
            total = None
            for w in plan[j]:
                n = j * LEVELS + w
                term = coefs[rows, n : n + 1] * levels[w]
                total = term if total is None else total + term
            upper_ref[j, rows, :] = total.astype(BF)
    count = q_turned.shape[0] // nd
    for k in range(nd):
        index = here_ref[1] ^ k
        rows = pl.ds(pl.multiple_of(index * count, count), count)
        value = dot(q_turned[rows, :], upper_ref[range_ref[index]]).astype(BF)
        if k:
            grad_refs[2 * k - 1][...] = value[: count // 2]
            grad_refs[2 * k][...] = value[count // 2 :]
        else:
            grad_refs[0][...] = value


def products_kernel(where, plan, lanes, tok, ns, nd, here_ref, count_ref, q_ref, *refs):
    count = 3 + 2 * LEVELS
    held_ref, pieces, outs = refs[0], refs[1 : 1 + count], refs[1 + count :]
    prod_refs, inner_ref, w_ref, sums = outs[:ns], outs[ns], outs[ns + 1], outs[ns + 2]
    step = pl.program_id(0)
    rows_of = w_ref.shape[0] // nd
    for k in range(nd):
        at = pl.multiple_of((here_ref[1] ^ k) * rows_of, rows_of)
        w_ref[pl.ds(at, rows_of), :] = held_ref[:, k].reshape(rows_of, w_ref.shape[1])

    @pl.when(step == 0)
    def _():
        sums[...] = jnp.zeros_like(sums)

    for k in range(ns):
        at = here_ref[0] ^ k
        rows = pl.ds(pl.multiple_of(at * tok, tok), tok)
        values = [dot(q_ref[rows, a:b], w_ref[a:b, :]) for a, b in lanes]
        for j, value in enumerate(values):
            prod_refs[k][j] = value.astype(BF)
        for w in range(LEVELS):
            total = None
            for j in range(len(lanes)):
                if w in plan[j]:
                    term = values[j] * count_ref[j, w]
                    total = term if total is None else total + term
            part = total * level_block(pieces, where[w][k])
            folded = part[:, :LANES]
            for c in range(LANES, part.shape[1], LANES):
                folded = folded + part[:, c : c + LANES]
            sums[w, rows, :] += folded

    @pl.when(step == pl.num_programs(0) - 1)
    def _():
        lane = lax.broadcasted_iota(jnp.int32, sums.shape[1:], 1)
        total = jnp.zeros(sums.shape[1:], F32)
        for w in range(LEVELS):
            total = jnp.where(lane == w, jnp.sum(sums[w], axis=1, keepdims=True), total)
        inner_ref[...] = total.T[:LEVELS]


def gate_kernel(
    starts, wide, count_ref, upper_ref, w_ref, y_ref, z_ref, gain_ref, ratio_ref, mean_ref, dy_ref, dz_ref, grad_ref, coefs
):
    step = pl.program_id(0)

    @pl.when(step == 0)
    def _():
        cubes = ratio_ref[...] * ratio_ref[...] * ratio_ref[...] * mean_ref[...]
        rows = []
        for j in range(len(starts)):
            total = cubes[0:1] * count_ref[j, 0]
            for w in range(1, LEVELS):
                total = total + cubes[w : w + 1] * count_ref[j, w]
            rows.append(total)
        columns = as_columns(jnp.concatenate(rows))
        for j in range(len(starts)):
            coefs[j] = jnp.broadcast_to(columns[:, j : j + 1], coefs.shape[1:])

    grad_all = dot(upper_ref[0], w_ref[...], ((1,), (1,)))
    coef = coefs[tile_range(starts, wide, step)]
    for c in range(0, wide, LANES):
        at = slice(c, c + LANES)
        grad_t = grad_all[:, at]
        z = z_ref[:, at].astype(F32)
        sig = jax.nn.sigmoid(z)
        act = z * sig
        y = y_ref[:, at]
        q = y * act
        dq = gain_ref[:, at] * grad_t - q * coef
        dy_ref[:, at] = (dq * act).astype(BF)
        dz_ref[:, at] = (dq * y * (sig * (1.0 + z * (1.0 - sig)))).astype(BF)
        grad_ref[0:1, at] = jnp.sum(q * grad_t, axis=0, keepdims=True)


def tile_range(starts, wide, step):
    index = 0
    for start in starts[1:]:
        index = index + jnp.where(step * wide >= start, 1, 0)
    return index


def mixed_kernel(plan, ns, tok, here_ref, count_ref, ratio_ref, x_ref, *refs):
    shares, out_ref = refs[:-1], refs[-1]
    at = pl.ds(pl.multiple_of(here_ref[0] * tok, tok), tok)
    ratios = as_columns(ratio_ref[:, at])
    x = x_ref[...].astype(F32)
    for w in range(LEVELS):
        total = None
        for k in range(ns):
            for j in plan[w]:
                term = shares[k][j].astype(F32) * count_ref[k, j * LEVELS + w]
                total = term if total is None else total + term
        out_ref[w] = (x + ratios[:, w : w + 1] * total).astype(BF)


def dp_terms(others):
    return [swapped(other, "dp", k + 1) for k, other in enumerate(others)]


def over_seq(value):
    dense = value.reshape(-1, LANES)
    total = dense
    for k in range(1, lax.axis_size("seq")):
        total = total + swapped(dense, "seq", k)
    return total.reshape(value.shape)


def fsdp_half(own, got):
    nf = lax.axis_size("fsdp")
    f = lax.axis_index("fsdp")

    def part(offset):
        total = picked(own, f ^ offset).astype(F32)
        for other in got:
            total = total + picked(other, f ^ offset).astype(F32)
        return total.astype(BF)

    kept = jnp.stack([part(e) for e in range(0, nf, 2)])
    sent = jnp.stack([part(e ^ 1) for e in range(0, nf, 2)])
    return kept, sent


def fsdp_rest(kept, got):
    k = 2
    while k < lax.axis_size("fsdp"):
        total = (kept.astype(F32) + got.astype(F32)).astype(BF)
        kept, sent = total[::2], total[1::2]
        got = swapped(sent, "fsdp", k)
        k *= 2
    return kept[0], got[0]


def shards(
    tokens,
    lengths,
    norm_gain,
    w_in,
    w_dt,
    conv_w,
    conv_b,
    dt_bias,
    a_log,
    skip,
    gate_gain,
    w_out,
    cotangent,
):
    nd, ns, nf = lax.axis_size("dp"), lax.axis_size("seq"), lax.axis_size("fsdp")
    d, s, f = lax.axis_index("dp"), lax.axis_index("seq"), lax.axis_index("fsdp")
    tok = tokens.shape[1]
    length = ns * tok
    blocks = length // SPAN
    heads = HEADS // ns
    run = heads // nd
    width = heads * HEADDIM
    own_bc = 2 * STATE // ns
    used = width + own_bc
    cols = -(-(used + heads) // LANES) * LANES
    rows_in = w_in.shape[0]
    reach = CONV - 1

    levels = np.array(
        [[level_of(dd * (HEADS // nd) + ss * run + i) for dd in range(nd) for i in range(run)] for ss in range(ns)]
    )
    cuts = [0] + [h for h in range(1, heads) if (levels[:, h] != levels[:, h - 1]).any()] + [heads]
    ranges = [(a, b) for a, b in zip(cuts, cuts[1:])]
    range_level = np.array([[levels[ss, a] for a, _ in ranges] for ss in range(ns)])
    counts = (range_level[:, :, None] <= np.arange(LEVELS)[None, None, :]).astype(np.float32)
    counted = picked(jnp.asarray(counts), s)
    theirs = picked(
        jnp.asarray(np.stack([[counts[i ^ k].reshape(-1) for k in range(ns)] for i in range(ns)])), s
    )
    lowest = [int(range_level[ss].min()) for ss in range(ns)]

    def by_head(vector):
        lead = vector.shape[:-1]
        per = vector.shape[-1] // HEADS
        cut = vector.reshape(lead + (nd, ns, run * per))
        mine = lax.dynamic_index_in_dim(cut, s, len(lead) + 1, keepdims=False)
        return mine.reshape(lead + (heads * per,))

    def for_groups(matrix):
        per = matrix.shape[1] // HEADS
        cut = matrix.reshape(matrix.shape[0], nd, ns, run * per)
        return jnp.transpose(cut, (2, 0, 1, 3)).reshape(ns, matrix.shape[0], heads * per)

    def from_groups(stack):
        per = stack.shape[2] // heads
        cut = stack.reshape(ns, stack.shape[1], nd, run * per)
        return jnp.transpose(cut, (1, 2, 0, 3)).reshape(stack.shape[1], HEADS * per)

    pad_cols = cols - used - heads
    half = width // 2
    first = half + cols - width
    group_x = for_groups(w_in[:, INNER : 2 * INNER])
    stack = jnp.concatenate(
        [
            group_x[:, :, :half],
            w_in[:, 2 * INNER :].reshape(rows_in, ns, own_bc).transpose(1, 0, 2),
            for_groups(w_dt),
            jnp.zeros((ns, rows_in, pad_cols), BF),
            group_x[:, :, half:],
            for_groups(w_in[:, :INNER]),
        ],
        axis=2,
    )
    own_x = tokens[0].astype(F32)
    scale = lax.rsqrt(jnp.mean(own_x * own_x, axis=-1, keepdims=True) + EPS)
    xn_own = (own_x * scale * norm_gain).astype(BF)
    xn_across = swapped(xn_own, "seq", 2)
    xn_pieces = [xn_own, swapped(xn_own, "seq", 1), xn_across, swapped(xn_across, "seq", 1)]
    arrived = [picked(stack, s)] + [swapped(picked(stack, s ^ k), "seq", k) for k in range(1, ns)]
    mine = filled((ns, rows_in, stack.shape[2]), [(p, None, (s ^ k, None, None)) for k, p in enumerate(arrived)])
    mine_z = mine[:, :, cols:]

    def needed(at, level):
        return min(lowest[at], lowest[at ^ 1]) <= level

    halves = [cotangent[w : w + 2, 0] for w in range(0, LEVELS, 2)]
    singles = [cotangent[w, 0] for w in range(LEVELS)]

    def beside(level, *others):
        block = after(halves[level // 2], *others)
        return swapped(block, "seq", 1, lambda i, j: needed(j, level + 1))

    def across(level, *others):
        block = after(singles[level], *others)
        return swapped(block, "seq", 2, lambda i, j: needed(j, level))

    def far(level, block):
        return swapped(block, "seq", 1, lambda i, j: needed(j, level))

    positions = jnp.arange(length, dtype=jnp.int32)
    ends = jnp.cumsum(lengths[0])[:-1]
    seg = jnp.sum((positions[:, None] >= ends[None, :]).astype(jnp.int32), axis=1)
    seg_before = jnp.concatenate([jnp.full((1,), -1, jnp.int32), seg[SPAN - 1 : length - 1 : SPAN]])
    seg_pad = jnp.concatenate([jnp.full((reach,), -1, jnp.int32), seg])
    masks = [(seg_pad[k : k + length] == seg) for k in range(reach)]
    mask_cols = [m.astype(F32) for m in masks]
    mask_cols += [jnp.pad(m, (0, reach - k))[reach - k :] for k, m in enumerate(mask_cols)]
    mask_cols = jnp.pad(jnp.stack(mask_cols, axis=1), ((0, 0), (0, LANES - 2 * reach)))

    def conv_params(s_part, bc_part):
        return by_head(s_part), bc_part

    weight_s = jnp.concatenate(
        [by_head(conv_w[:, :INNER]), by_head(conv_b[None, :INNER]), jnp.zeros((3, width), F32)]
    )
    weight_r = jnp.pad(
        lax.dynamic_slice_in_dim(conv_w, INNER + s * own_bc, own_bc, 1), ((0, 0), (0, cols - used))
    )
    bias_r = jnp.pad(
        lax.dynamic_slice_in_dim(conv_b, INNER + s * own_bc, own_bc, 0), (0, cols - used)
    )
    bias = by_head(dt_bias)
    rate = -jnp.exp(by_head(a_log))
    skip_own = by_head(skip)
    gain = by_head(gate_gain)

    def over_fsdp(chunk):
        return lax.all_gather(chunk, "fsdp", axis=0, tiled=False)

    def over_dp(held):
        return [held] + [swapped(held, "dp", j) for j in range(1, nd)]

    row_halves = 2 if rows_in % 32 == 0 else 1

    def ready(parts, columns):
        if rows_in % 16 == 0:
            return [piece for pieces in parts for piece in pieces]
        moves = [
            (piece, i, (d ^ j, None, i, h, None, None))
            for h, pieces in enumerate(parts)
            for j, piece in enumerate(pieces)
            for i in range(nf)
        ]
        return [filled((nd, ns, nf, len(parts), rows_in // len(parts), columns), moves).reshape(D, columns)]

    held_a = over_fsdp(mine[:, :, :first])
    held_b = over_fsdp(mine[:, :, first:cols])
    other_out = [swapped(w_out, "dp", j) for j in range(1, nd)]
    held_a, other_out = together(held_a, other_out)
    small_ones = (seg, seg_before, mask_cols, weight_s, weight_r, bias_r, bias, rate, skip_own, gain, theirs)
    held_a, small_ones, halves, singles = together(held_a, small_ones, halves, singles)
    seg, seg_before, mask_cols, weight_s, weight_r, bias_r, bias, rate, skip_own, gain, theirs = small_ones
    near_high, near_low = beside(2, held_a), beside(0, held_a)
    chip3 = across(3, held_a)
    pieces_a = over_dp(held_a)
    held_b, pieces_a, chip3, near_high, xn_pieces = together(
        held_b, pieces_a, chip3, near_high, xn_pieces
    )
    xn = filled((ns, tok, D), [(p, None, (s ^ k, None, None)) for k, p in enumerate(xn_pieces)])
    xn = xn.reshape(length, D)

    far3 = far(3, chip3)
    pieces_b = over_dp(held_b)
    parts_z = mine_z.reshape(ns, row_halves, rows_in // row_halves, width)
    held_z = over_fsdp(after(parts_z[:, 0], held_a))
    late_z = [over_fsdp(after(parts_z[:, h], held_b)) for h in range(1, row_halves)]
    held_out = over_fsdp(after(jnp.stack([w_out] + other_out), held_z))

    xn_turned = xn.T
    here = jnp.stack([s, d]).astype(jnp.int32)
    proj_a, full_a = projections(here, xn, ready([pieces_a], first), nd, rows_in, first)

    proj_r = proj_a[:, half:]
    mixer = jnp.concatenate([jnp.zeros((reach, cols - width), BF), proj_r], axis=0)

    def taken(k):
        rows = mixer[k : k + length].astype(F32)
        return rows * mask_cols[:, k : k + 1] if k < reach else rows

    pre_r = bias_r
    for k in range(CONV):
        pre_r = pre_r + taken(k) * weight_r[k]
    bc_own = jax.nn.silu(pre_r).astype(BF)[:, :own_bc]
    bc_across = swapped(bc_own, "seq", 2)
    bc = [bc_own, swapped(bc_own, "seq", 1), bc_across, swapped(bc_across, "seq", 1)]
    bc, held_z = together(bc, held_z)
    chip2, chip1 = across(2, bc[2]), across(1, bc[2])
    pieces_z = over_dp(held_z)
    pieces_b, xn_turned = together(pieces_b, xn_turned)
    proj_b, full_b = projections(here, xn, ready([pieces_b], half), nd, rows_in, half)
    proj_b, far3, near_low = together(proj_b, far3, near_low)
    bc = reordered_by_xor(bc, s)
    b_in = jnp.concatenate(bc[: ns // 2], axis=1)
    c_out = jnp.concatenate(bc[ns // 2 :], axis=1)

    def padded(rows):
        return jnp.pad(rows, ((0, 0), (0, LANES - rows.shape[1])))

    pre_dt = proj_r[:, own_bc : own_bc + heads].astype(F32) + bias
    steps = jax.nn.softplus(pre_dt)
    tails = [
        p.reshape(blocks, SPAN, p.shape[1])[: blocks - 1, SPAN - HALO :, :half] for p in (proj_a, proj_b)
    ]
    operands = (
        seg_before,
        seg[:, None],
        seg[None, :],
        mask_cols,
        proj_a,
        proj_b,
        jnp.concatenate([jnp.zeros((1, HALO, width), BF), jnp.concatenate(tails, axis=2)]),
        weight_s,
        b_in,
        c_out,
        padded(steps),
        padded(rate[None, :]),
        jnp.repeat(skip_own, HEADDIM)[None, :],
    )
    y, priors = scan_forward(heads, blocks, operands)
    y, chip2, late_z = together(y, chip2, late_z)
    far2, chip0 = far(2, chip2), across(0, y)
    parts = [pieces_z] + [over_dp(piece) for piece in late_z]
    lanes = [(a * HEADDIM, b * HEADDIM) for a, b in ranges]
    starts = [a for a, _ in lanes]
    wide = min(min(b - a for a, b in lanes), TILE)
    proj_z, full_z, q_gain, q_turned, squares = projections(
        here, xn, ready(parts, width), nd, rows_in, width, (y, gain[None], starts, wide)
    )
    squares, chip1 = together(squares[: len(lanes)], chip1)
    far1 = far(1, chip1)
    widths = np.array([[(HEADS >> 3 - w) * HEADDIM] for w in range(LEVELS)], np.float32)
    per_level = jnp.sum(counted[:, :, None] * squares[:, None, :], axis=0)
    ratio, chip0 = together(lax.rsqrt(over_seq(per_level) / widths + EPS), chip0)
    far0 = far(0, chip0)

    plan = [[w for w in range(LEVELS) if range_level[:, j].min() <= w] for j in range(len(lanes))]
    out_rows = width // nd
    range_of = [next(j for j, (a, b) in enumerate(lanes) if a <= i * out_rows < b) for i in range(nd)]
    smem = pl.BlockSpec(memory_space=pltpu.SMEM)
    cot_pieces = [cotangent, near_low, near_high, chip0, chip1, chip2, chip3, far0, far1, far2, far3]
    cot_specs = [pl.BlockSpec((LEVELS, 1, tok, TILE), lambda i: (0, 0, 0, i))]
    cot_specs += [pl.BlockSpec((2, tok, TILE), lambda i: (0, 0, i))] * 2
    cot_specs += [pl.BlockSpec((tok, TILE), lambda i: (0, i))] * (2 * LEVELS)
    where = [[(0, (w, 0)), (1 + w // 2, (w % 2,)), (3 + w, ()), (3 + LEVELS + w, ())] for w in range(LEVELS)]
    upper, *grad_out = call(
        functools.partial(upper_kernel, where, plan, nd, tok, ns),
        grid=(D // TILE,),
        in_specs=[
            smem,
            smem,
            smem,
            pl.BlockSpec((LEVELS, length), lambda i: (0, 0)),
            pl.BlockSpec((width, length), lambda i: (0, 0)),
        ]
        + cot_specs,
        out_specs=[pl.BlockSpec((len(lanes), length, TILE), lambda i: (0, 0, i))]
        + [pl.BlockSpec((out_rows, TILE), lambda i: (0, i))]
        + [pl.BlockSpec((out_rows // 2, TILE), lambda i: (0, i))] * (2 * nd - 2),
        out_shape=[jax.ShapeDtypeStruct((len(lanes), length, D), BF)]
        + [jax.ShapeDtypeStruct((out_rows, D), BF)]
        + [jax.ShapeDtypeStruct((out_rows // 2, D), BF)] * (2 * nd - 2),
        scratch_shapes=[pltpu.VMEM((length, LANES), F32)],
        name="upper",
    )(here, jnp.asarray(range_of, jnp.int32), counted, ratio, q_turned, *cot_pieces)
    out_first, out_second = dp_terms(grad_out[1::2]), dp_terms(grad_out[2::2])

    held_out, upper = together(held_out, upper)
    *shares, inner, full_out = call(
        functools.partial(products_kernel, where, plan, lanes, tok, ns, nd),
        grid=(D // TILE,),
        in_specs=[
            smem,
            smem,
            pl.BlockSpec((length, width), lambda i: (0, 0)),
        ]
        + [pl.BlockSpec((nf, nd, w_out.shape[0], TILE), lambda i: (0, 0, 0, i))]
        + cot_specs,
        out_specs=[pl.BlockSpec((len(lanes), tok, TILE), lambda i: (0, 0, i))] * ns
        + [pl.BlockSpec((LEVELS, length), lambda i: (0, 0))]
        + [pl.BlockSpec((width, TILE), lambda i: (0, i))],
        out_shape=[jax.ShapeDtypeStruct((len(lanes), tok, D), BF)] * ns
        + [jax.ShapeDtypeStruct((LEVELS, length), F32)]
        + [jax.ShapeDtypeStruct((width, D), BF)],
        scratch_shapes=[pltpu.VMEM((LEVELS, length, LANES), F32)],
        name="products",
    )(here, counted, q_gain, held_out, *cot_pieces)
    means, out_first = together(over_seq(inner) / widths, out_first)
    shares[1:3] = [swapped(after(shares[k], means), "seq", k) for k in (1, 2)]
    split = (len(lanes) + 1) // 2
    third = [swapped(after(shares[3][:split], shares[1]), "seq", 3), shares[3][split:]]

    cols_of = pl.BlockSpec((length, wide), lambda i: (0, i))
    scalars = pl.BlockSpec((LEVELS, length), lambda i: (0, 0))
    dy, dz, grad_gate = call(
        functools.partial(gate_kernel, starts, wide),
        grid=(width // wide,),
        in_specs=[
            smem,
            pl.BlockSpec((1, length, D), lambda i: (tile_range(starts, wide, i), 0, 0)),
            pl.BlockSpec((wide, D), lambda i: (i, 0)),
            cols_of,
            cols_of,
            pl.BlockSpec((1, wide), lambda i: (0, i)),
            scalars,
            scalars,
        ],
        out_specs=[cols_of, cols_of, pl.BlockSpec((8, wide), lambda i: (0, i))],
        out_shape=[
            jax.ShapeDtypeStruct((length, width), BF),
            jax.ShapeDtypeStruct((length, width), BF),
            jax.ShapeDtypeStruct((8, width), F32),
        ],
        scratch_shapes=[pltpu.VMEM((len(lanes), length, LANES), F32)],
        name="gate_backward",
    )(counted, upper, full_out, y, proj_z, gain[None], ratio, means)
    grad_gate = grad_gate[0]

    def in_terms(dproj, at, first=0, columns=None):
        columns = columns or dproj.shape[1]
        out = row_terms(xn_turned, dproj, at, nd, ns, nf, first, columns)
        return out.reshape(nf, ns * rows_in, columns)

    z_other = [in_terms(dz, d ^ k) for k in range(1, nd)]
    z_got = dp_terms(z_other)
    dy, out_second, shares[1] = together(after(dy, *z_other), out_second, shares[1])
    chunk = (nf, out_rows // nf, D)
    out_got = [jnp.concatenate([u, v]).reshape(chunk) for u, v in zip(out_first, out_second)]
    out_kept, out_sent = fsdp_half(grad_out[0].reshape(chunk), out_got)
    dy = after(dy, out_sent)
    out_half = swapped(out_sent, "fsdp", 1)

    dproj_s, dbc, ddt, drate, dsum = scan_backward(heads, blocks, operands, y, priors, dy)
    dproj_s, dbc, out_half, shares[2], third = together(dproj_s, dbc, out_half, shares[2], third)
    out_pair = fsdp_rest(out_kept, out_half)

    dbc = dbc.astype(BF)
    slices = reordered_by_xor([dbc[:, j * own_bc : (j + 1) * own_bc] for j in range(ns)], s)
    beside_bc = swapped(jnp.concatenate([slices[1], slices[3]], axis=1), "seq", 1)
    sum_bc = jnp.concatenate([slices[0], slices[2]], axis=1).astype(F32) + beside_bc.astype(F32)
    across_bc = swapped(sum_bc[:, own_bc:].astype(BF), "seq", 2)

    z_own = in_terms(after(dz, dproj_s), d)
    z_own, z_got = together(z_own, z_got)
    z_kept, z_sent = fsdp_half(z_own, z_got)
    z_half = swapped(z_sent, "fsdp", 1)
    late_s = after(dproj_s, z_sent)
    left_other = [in_terms(late_s, d ^ k, 0, half) for k in range(1, nd)]
    left_got = dp_terms(left_other)
    third[1] = swapped(after(third[1], across_bc), "seq", 3)
    dbc_own = sum_bc[:, :own_bc] + across_bc.astype(F32)
    dproj_r, small_sums = small_back(
        own_bc,
        pre_r,
        padded(after(dbc_own, *left_other)),
        proj_r,
        mask_cols,
        weight_r,
        ddt,
        padded(pre_dt),
    )

    dxn = input_grad(dz, dproj_s, dproj_r, full_z, full_a, full_b, ns, tok)
    pair = swapped(jnp.stack([picked(dxn, s ^ 1), picked(dxn, s ^ 3)]), "seq", 1)

    late_s, late_r = together(dproj_s, after(dproj_r, dxn))
    right_other = [
        jnp.concatenate([in_terms(late_s, d ^ k, half, half), in_terms(late_r, d ^ k)], axis=2)
        for k in range(1, nd)
    ]
    right_other, z_half, left_got, out_pair = together(right_other, z_half, left_got, out_pair)
    right_got = dp_terms(right_other)
    z_pair = fsdp_rest(z_kept, z_half)
    own_s = in_terms(after(dproj_s, *right_other), d)
    left_kept, left_sent = fsdp_half(own_s[:, :, :half], left_got)
    left_half = swapped(left_sent, "fsdp", 1)
    own_r = in_terms(after(dproj_r, left_sent), d)
    flat = flattened(
        [
            jnp.concatenate([dsum[:CONV], small_sums[:CONV, :own_bc]], axis=1).reshape(-1),
            dsum[CONV],
            small_sums[CONV, :own_bc],
            grad_gate,
            small_sums[CONV + 1, :heads],
            drate[0, :heads] * rate,
            jnp.sum(dsum[CONV + 1].reshape(heads, HEADDIM), axis=1),
        ]
    )
    near = picked(dxn, s).astype(F32) + pair[0].astype(F32)
    far_sum = (picked(dxn, s ^ 2).astype(F32) + pair[1].astype(F32)).astype(BF)
    dxn_across = swapped(far_sum, "seq", 2)
    right_got, far_sum, left_half = together(right_got, far_sum, left_half)
    left_pair = fsdp_rest(left_kept, left_half)
    own_right = jnp.concatenate([own_s[:, :, half:], own_r], axis=2)
    right_kept, right_sent = fsdp_half(own_right, right_got)
    right_half = swapped(right_sent, "fsdp", 1)

    mixed = call(
        functools.partial(
            mixed_kernel,
            [[j for j in range(len(lanes)) if range_level[:, j].min() <= w] for w in range(LEVELS)],
            ns,
            tok,
        ),
        grid=(D // TILE,),
        in_specs=[
            smem,
            smem,
            pl.BlockSpec((LEVELS, length), lambda i: (0, 0)),
            pl.BlockSpec((tok, TILE), lambda i: (0, i)),
        ]
        + [pl.BlockSpec((len(lanes), tok, TILE), lambda i: (0, 0, i))] * ns,
        out_specs=pl.BlockSpec((LEVELS, tok, TILE), lambda i: (0, 0, i)),
        out_shape=jax.ShapeDtypeStruct((LEVELS, tok, D), BF),
        name="mixed",
    )(here, theirs, ratio, tokens[0], *after(shares[:3] + [jnp.concatenate(third)], right_sent))[:, None]
    right_half, mixed, dxn_across = together(right_half, mixed, dxn_across)
    right_kept = after(right_kept, mixed)
    right_pair = fsdp_rest(right_kept, right_half)
    dxn_own = near + dxn_across.astype(F32)
    grad_norm = jnp.sum(dxn_own * own_x * scale, axis=0)
    scaled = norm_gain * dxn_own
    dx = scale * scaled - own_x * scale**3 * jnp.mean(own_x * scaled, axis=-1, keepdims=True)
    dx = (dx + jnp.sum(after(cotangent, mixed)[:, 0].astype(F32), axis=0)).astype(BF)
    flat = jnp.concatenate([flat, grad_norm.reshape(-1, LANES)])
    flat = butterfly(flat, "dp")

    def whole_sum(pair):
        total = (pair[0].astype(F32) + pair[1].astype(F32)).astype(BF)
        return total.reshape(ns, rows_in, total.shape[1])

    z_pair, left_pair = together(z_pair, left_pair)
    early = jnp.concatenate([whole_sum(z_pair), whole_sum(left_pair)], axis=2)
    early_got = [picked(early, s)] + [swapped(picked(early, s ^ k), "seq", k) for k in range(1, ns)]
    early_got, right_pair, flat = together(early_got, right_pair, flat)
    flat = butterfly(flat, "fsdp")
    late = whole_sum(right_pair)
    late_got = [picked(late, s)] + [swapped(picked(late, s ^ k), "seq", k) for k in range(1, ns)]
    early = jnp.stack(reordered_by_xor(early_got, s))
    late = jnp.stack(reordered_by_xor(late_got, s))
    got_z = early[:, :, :width]
    got_x = jnp.concatenate([early[:, :, width:], late], axis=2)
    sum_out = out_pair[0].astype(F32) + out_pair[1].astype(F32)


    sum_in = jnp.concatenate(
        [
            from_groups(got_z),
            from_groups(got_x[:, :, :width]),
            jnp.transpose(got_x[:, :, width:used], (1, 0, 2)).reshape(rows_in, 2 * STATE),
        ],
        axis=1,
    ).astype(F32)
    sum_dt = from_groups(got_x[:, :, used : used + heads]).astype(F32)

    sizes = [CONV * used, used, width, heads, heads, heads]
    filling = -sum(sizes) % 1024
    sizes += [filling, D]
    every = seq_gather(flat, s).reshape(ns, -1)
    starts = np.cumsum([0] + sizes)
    pieces = [every[:, a : a + n] for a, n in zip(starts, sizes)]

    def heads_back(rows):
        lead = rows.shape[1:-1]
        cut = rows.reshape((ns,) + lead + (nd, rows.shape[-1] // nd))
        order = tuple(range(1, 1 + len(lead))) + (1 + len(lead), 0, 2 + len(lead))
        return jnp.transpose(cut, order).reshape(lead + (-1,))

    conv_rows = pieces[0].reshape(ns, CONV, used)
    conv_all = jnp.concatenate(
        [
            heads_back(conv_rows[:, :, :width]),
            jnp.transpose(conv_rows[:, :, width:], (1, 0, 2)).reshape(CONV, 2 * STATE),
        ],
        axis=1,
    )
    bias_all = jnp.concatenate([heads_back(pieces[1][:, :width]), pieces[1][:, width:].reshape(-1)])
    return (
        mixed,
        dx[None],
        jnp.sum(pieces[7], axis=0),
        sum_in,
        sum_dt,
        conv_all,
        bias_all,
        heads_back(pieces[3]),
        heads_back(pieces[4]),
        heads_back(pieces[5]),
        heads_back(pieces[2]),
        sum_out,
    )


def solution(mesh):
    rows = P(("dp", "seq", "fsdp"), None)
    held = P(("dp", "fsdp"), "seq", None)
    levels = P(None, ("dp", "fsdp"), "seq", None)
    placed = (held, P(("dp", "fsdp"), None), P(), rows, rows, P(), P(), P(), P(), P(), P(), rows, levels)
    return jax.shard_map(
        shards,
        mesh=mesh,
        in_specs=placed,
        out_specs=(levels, held, P(), rows, rows, P(), P(), P(), P(), P(), P(), rows),
        check_vma=False,
    )
```

```python
import functools

import jax
import jax.numpy as jnp
import numpy as np
from jax import lax
from jax.experimental import pallas as pl
from jax.experimental.pallas import tpu as pltpu
from jax.sharding import PartitionSpec as P

D = 2048
HEADS = 64
HEADDIM = 64
STATE = 128
CONV = 4
SPAN = 128
INNER = 4096
EPS = 1e-05
LEVELS = 4
BF = jnp.bfloat16
F32 = jnp.float32
HIGH = lax.Precision.HIGHEST
LANES = 128
HALO = 16
TILE = 256
WIDE = 512
VMEM_LIMIT = 48 * 1024 * 1024


def dot(a, b, dims=((1,), (0,)), precision=None):
    return lax.dot_general(a, b, (dims, ((), ())), preferred_element_type=F32, precision=precision)


def silu_slope(v):
    sig = jax.nn.sigmoid(v)
    return sig * (1.0 + v * (1.0 - sig))


def level_of(head):
    return 0 if head < 8 else 1 if head < 16 else 2 if head < 32 else 3


def swapped(value, axis, k, keep=None):
    pairs = [(i, i ^ k) for i in range(lax.axis_size(axis))]
    if keep is not None:
        pairs = [p for p in pairs if keep(*p)]
    return lax.ppermute(value, axis, pairs)


def after(value, *others):
    return lax.optimization_barrier((value,) + others)[0]


def together(*values):
    return lax.optimization_barrier(values)


def flattened(vectors):
    flat = jnp.concatenate(vectors)
    return jnp.pad(flat, (0, -flat.shape[0] % 1024)).reshape(-1, LANES)


def butterfly(value, axis):
    k = 1
    while k < lax.axis_size(axis):
        value = value + swapped(value, axis, k)
        k *= 2
    return value


def picked(array, index):
    return lax.dynamic_index_in_dim(array, index, 0, keepdims=False)


def seq_gather(block, here):
    return jnp.stack(reordered_by_xor([block] + [swapped(block, "seq", k) for k in range(1, 4)], here))


def reordered_by_xor(pieces, here):
    k = 1
    while k < len(pieces):
        flip = (here & k) > 0
        pieces = [jnp.where(flip, pieces[j ^ k], piece) for j, piece in enumerate(pieces)]
        k *= 2
    return pieces


def call(kernel, flops=1, **kwargs):
    return pl.pallas_call(
        kernel,
        compiler_params=pltpu.CompilerParams(vmem_limit_bytes=VMEM_LIMIT),
        cost_estimate=pl.CostEstimate(flops=flops, bytes_accessed=1, transcendentals=0),
        **kwargs,
    )


def filled(shape, moves):
    arrays, plan, rows = [], [], []
    block = tuple(size if index is None else 1 for size, index in zip(shape, moves[0][2]))
    for piece, lead, place in moves:
        at = next((i for i, a in enumerate(arrays) if a is piece), len(arrays))
        if at == len(arrays):
            arrays.append(piece)
        plan.append((at, lead))
        rows.append(jnp.stack([jnp.asarray(0 if n is None else n, jnp.int32) for n in place]))

    def kernel(index_ref, *refs):
        pieces, out = refs[:-1], refs[-1]
        for m, (at, lead) in enumerate(plan):

            @pl.when(pl.program_id(0) == m)
            def _():
                value = pieces[at][...] if lead is None else pieces[at][lead]
                out[...] = value.reshape(block)

    return call(
        kernel,
        flops=5 * 10**9,
        grid_spec=pltpu.PrefetchScalarGridSpec(
            num_scalar_prefetch=1,
            grid=(len(plan),),
            in_specs=[
                pl.BlockSpec(a.shape, lambda i, t, n=a.ndim: (0,) * n) for a in arrays
            ],
            out_specs=pl.BlockSpec(
                block, lambda i, t: tuple(t[i, n] for n in range(len(shape)))
            ),
        ),
        out_shape=jax.ShapeDtypeStruct(shape, arrays[0].dtype),
        name="filled",
    )(jnp.stack(rows), *arrays)


def terms_kernel(ns, nf, at_ref, left_ref, right_ref, out_ref):
    value = dot(left_ref[...], right_ref[...]).astype(BF)
    rows = value.shape[0] // (ns * nf)
    for i in range(ns):
        for k in range(nf):
            out_ref[k, i] = value[(i * nf + k) * rows : (i * nf + k + 1) * rows]


def row_terms(turned, right, at, nd, ns, nf, first, columns):
    depth = turned.shape[1]
    rows = turned.shape[0] // nd
    wide = TILE if columns % TILE == 0 else LANES
    return call(
        functools.partial(terms_kernel, ns, nf),
        grid_spec=pltpu.PrefetchScalarGridSpec(
            num_scalar_prefetch=1,
            grid=(columns // wide,),
            in_specs=[
                pl.BlockSpec((rows, depth), lambda i, t: (t[0], 0)),
                pl.BlockSpec((depth, wide), lambda i, t: (0, i + first // wide)),
            ],
            out_specs=pl.BlockSpec((nf, ns, rows // (nf * ns), wide), lambda i, t: (0, 0, 0, i)),
        ),
        out_shape=jax.ShapeDtypeStruct((nf, ns, rows // (nf * ns), columns), BF),
        name="row_terms",
    )(at.astype(jnp.int32)[None], turned, right)


def small_back_kernel(
    width, pre_ref, dbc_ref, in_ref, mask_ref, weight_ref, ddt_ref, pre_dt_ref, out_ref, sum_ref, ext, dext
):
    rows = pre_ref.shape[0]
    ext[0:HALO] = jnp.zeros((HALO, LANES), F32)
    ext[HALO:] = in_ref[...].astype(F32)
    pre = pre_ref[...]
    sig = jax.nn.sigmoid(pre)
    dpre = dbc_ref[...] * (sig * (1.0 + pre * (1.0 - sig)))
    dext[0:rows] = dpre
    dext[rows:] = jnp.zeros((HALO, LANES), F32)
    total = dpre * weight_ref[CONV - 1 : CONV, :]
    for k in range(CONV):
        term = ext[pl.ds(HALO - CONV + 1 + k, rows), :]
        if k < CONV - 1:
            term = term * mask_ref[:, k : k + 1]
            later = dext[pl.ds(CONV - 1 - k, rows), :] * mask_ref[:, CONV - 1 + k : CONV + k]
            total = total + later * weight_ref[k : k + 1, :]
        sum_ref[k : k + 1, :] = jnp.sum(dpre * term, axis=0, keepdims=True)
    sum_ref[CONV : CONV + 1, :] = jnp.sum(dpre, axis=0, keepdims=True)
    draw = ddt_ref[...] * jax.nn.sigmoid(pre_dt_ref[...])
    sum_ref[CONV + 1 : CONV + 2, :] = jnp.sum(draw, axis=0, keepdims=True)
    out_ref[...] = (total + pltpu.roll(draw, width, axis=1)).astype(BF)


def small_back(width, pre, dbc, proj, masks, weight, ddt, pre_dt):
    rows = pre.shape[0]
    return call(
        functools.partial(small_back_kernel, width),
        out_shape=[
            jax.ShapeDtypeStruct((rows, LANES), BF),
            jax.ShapeDtypeStruct((8, LANES), F32),
        ],
        scratch_shapes=[pltpu.VMEM((HALO + rows, LANES), F32), pltpu.VMEM((rows + HALO, LANES), F32)],
        name="small_back",
    )(pre, dbc, proj, masks, weight, ddt, pre_dt)


def input_grad_kernel(blocks, dz_ref, ds_ref, dr_ref, wz_ref, wa_ref, wb_ref, out_ref):
    half = wb_ref.shape[1]
    columns = ((1,), (1,))
    total = dot(dz_ref[...], wz_ref[...], columns)
    total = total + dot(ds_ref[:, :half], wa_ref[:, :half], columns)
    total = total + dot(ds_ref[:, half:], wb_ref[...], columns)
    total = total + dot(dr_ref[...], wa_ref[:, half:], columns)
    total = total.astype(BF)
    tok = total.shape[0] // blocks
    for i in range(blocks):
        out_ref[i] = total[i * tok : (i + 1) * tok]


def input_grad(dz, ds, dr, wz, wa, wb, blocks, tok):
    def whole(a):
        return pl.BlockSpec(a.shape, lambda i: (0, 0))

    def rows(a):
        return pl.BlockSpec((TILE, a.shape[1]), lambda i: (i, 0))

    return call(
        functools.partial(input_grad_kernel, blocks),
        grid=(wz.shape[0] // TILE,),
        in_specs=[whole(dz), whole(ds), whole(dr), rows(wz), rows(wa), rows(wb)],
        out_specs=pl.BlockSpec((blocks, tok, TILE), lambda i: (0, 0, i)),
        out_shape=jax.ShapeDtypeStruct((blocks, tok, wz.shape[0]), BF),
        name="input_grad",
    )(dz, ds, dr, wz, wa, wb)


def assembled(here_ref, pieces, nd, full_ref):
    halves = len(pieces) // nd
    nf, ns, rows = pieces[0].shape[:3]
    for n, piece in enumerate(pieces):
        h, j = divmod(n, nd)
        for k in range(nf):
            for i in range(ns):
                block = ((here_ref[1] ^ j) * ns + i) * nf + k
                at = pl.multiple_of((block * halves + h) * rows, rows)
                full_ref[pl.ds(at, rows), :] = piece[k, i]


def project_kernel(nd, count, here_ref, xn_ref, *refs):
    pieces, (out_ref, full_ref) = refs[:count], refs[count:]
    if nd:
        assembled(here_ref, pieces, nd, full_ref)
    else:
        full_ref[...] = pieces[0][...]
    out_ref[...] = dot(xn_ref[...], full_ref[...]).astype(BF)


def gated_kernel(nd, count, starts, wide, here_ref, xn_ref, y_ref, gain_ref, *refs):
    pieces, (out_ref, full_ref, gated_ref, turned_ref, squares_ref, sums) = refs[:count], refs[count:]
    step = pl.program_id(0)

    @pl.when(step == 0)
    def _():
        sums[...] = jnp.zeros_like(sums)

    if nd:
        assembled(here_ref, pieces, nd, full_ref)
    else:
        full_ref[...] = pieces[0][...]
    value = dot(xn_ref[...], full_ref[...]).astype(BF)
    out_ref[...] = value
    where = tile_range(starts, wide, step)
    for c in range(0, wide, LANES):
        at = slice(c, c + LANES)
        z = value[:, at].astype(F32)
        q = y_ref[:, at] * (z * jax.nn.sigmoid(z))
        gated = (q * gain_ref[:, at]).astype(BF)
        gated_ref[:, at] = gated
        turned_ref[at, :] = gated.T
        sums[where] += q * q

    @pl.when(step == pl.num_programs(0) - 1)
    def _():
        lane = lax.broadcasted_iota(jnp.int32, sums.shape[1:], 1)
        total = jnp.zeros(sums.shape[1:], F32)
        for j in range(len(starts)):
            total = jnp.where(lane == j, jnp.sum(sums[j], axis=1, keepdims=True), total)
        squares_ref[...] = total.T[: squares_ref.shape[0]]


def projections(here, xn, pieces, nd, rows, columns, gate=None):
    if pieces[0].ndim == 2:
        nd = 0
    wide = TILE if columns % TILE == 0 else columns
    if gate is not None:
        y, gain, starts, wide = gate
    tokens, depth = xn.shape
    outs = [pl.BlockSpec((tokens, wide), lambda i: (0, i)), pl.BlockSpec((depth, wide), lambda i: (0, i))]
    shapes = [jax.ShapeDtypeStruct((tokens, columns), BF), jax.ShapeDtypeStruct((depth, columns), BF)]
    ins = [pl.BlockSpec(memory_space=pltpu.SMEM), pl.BlockSpec((tokens, depth), lambda i: (0, 0))]
    operands = [here, xn]
    scratch = []
    kernel = functools.partial(project_kernel, nd, len(pieces))
    if gate is not None:
        kernel = functools.partial(gated_kernel, nd, len(pieces), starts, wide)
        operands += [y, gain]
        ins += [outs[0], pl.BlockSpec((1, wide), lambda i: (0, i))]
        outs += [
            outs[0],
            pl.BlockSpec((wide, tokens), lambda i: (i, 0)),
            pl.BlockSpec((8, tokens), lambda i: (0, 0)),
        ]
        shapes += [
            shapes[0],
            jax.ShapeDtypeStruct((columns, tokens), BF),
            jax.ShapeDtypeStruct((8, tokens), F32),
        ]
        scratch = [pltpu.VMEM((len(starts), tokens, LANES), F32)]
    for piece in pieces:
        lead = piece.shape[:-1]
        ins.append(pl.BlockSpec(lead + (wide,), lambda i, n=len(lead): (0,) * n + (i,)))
    return call(
        kernel,
        flops=2 * tokens * depth * columns if gate is None else 1,
        grid=(columns // wide,),
        in_specs=ins,
        out_specs=outs,
        out_shape=shapes,
        scratch_shapes=scratch,
        name="gated" if gate is not None else "project",
    )(*operands, *pieces)


def tri(rows_first):
    a = lax.broadcasted_iota(jnp.int32, (SPAN, SPAN), 0)
    b = lax.broadcasted_iota(jnp.int32, (SPAN, SPAN), 1)
    return (a >= b) if rows_first else (a <= b)


def pair_of(lo, cols, p):
    return jnp.where(lo, cols[:, 2 * p : 2 * p + 1], cols[:, 2 * p + 1 : 2 * p + 2])


def decays(segc, segr, segp, dt, rate):
    cum = dot(tri(True).astype(F32), dt * rate, precision=HIGH)
    last = cum[SPAN - 1 : SPAN, :]
    keep = jnp.where(segc == segp, jnp.exp(cum), 0.0)
    to_end = jnp.where(segc == segr[:, SPAN - 1 : SPAN], jnp.exp(last - cum), 0.0)
    return cum, cum.T, keep, to_end


def spread_columns(ref, first, count):
    return [jnp.broadcast_to(ref[:, first + k : first + k + 1], (SPAN, LANES)) for k in range(count)]


def taps(ext, masks, at):
    terms = [ext[pl.ds(HALO - CONV + 1 + k, SPAN), at] for k in range(CONV)]
    return [t * m for t, m in zip(terms, masks)] + terms[CONV - 1 :]


def convolved(terms, weight_ref, at):
    total = weight_ref[CONV : CONV + 1, at] + terms[0] * weight_ref[0:1, at]
    for k in range(1, CONV):
        total = total + terms[k] * weight_ref[k : k + 1, at]
    return total


def forward_kernel(
    heads,
    segp_ref,
    segc_ref,
    segr_ref,
    mask_ref,
    in_a_ref,
    in_b_ref,
    halo_ref,
    weight_ref,
    b_ref,
    c_ref,
    dt_ref,
    rate_ref,
    skip_ref,
    y_ref,
    prior_ref,
    carry,
    to_end_u,
    ext,
):
    block = pl.program_id(0)
    width = heads * HEADDIM

    @pl.when(block == 0)
    def _():
        carry[...] = jnp.zeros_like(carry)

    prior_ref[0] = carry[...]
    ext[0:HALO] = halo_ref[0].astype(F32)
    half = in_b_ref.shape[1]
    ext[HALO:, :half] = in_a_ref[:, :half].astype(F32)
    ext[HALO:, half:] = in_b_ref[...].astype(F32)
    segc, segr = segc_ref[...], segr_ref[...]
    dt = dt_ref[...]
    cum, cumr, keep, to_end = decays(segc, segr, segp_ref[block], dt, rate_ref[...])
    bm, cm = b_ref[...], c_ref[...]
    mixing = dot(cm, bm, ((1,), (1,)))
    mixing = jnp.where(tri(True) & (segc == segr), mixing, 0.0)
    masks = spread_columns(mask_ref, 0, CONV - 1)
    lo = lax.broadcasted_iota(jnp.int32, (SPAN, LANES), 1) < HEADDIM
    for p in range(heads // 2):
        at = slice(p * LANES, (p + 1) * LANES)
        pre = convolved(taps(ext, masks, at), weight_ref, at)
        x2 = pre * jax.nn.sigmoid(pre)
        u2 = x2 * pair_of(lo, dt, p)
        ub = u2.astype(BF)
        total = dot(cm, carry[:, at].astype(BF)) * pair_of(lo, keep, p) + skip_ref[:, at] * x2
        inner = []
        for h in (2 * p, 2 * p + 1):
            decay = jnp.exp(jnp.minimum(cum[:, h : h + 1] - cumr[h : h + 1, :], 0.0))
            inner.append(dot((decay * mixing).astype(BF), ub))
        y_ref[:, at] = total + jnp.where(lo, inner[0], inner[1])
        to_end_u[:, at] = (u2 * pair_of(lo, to_end, p)).astype(BF)
    fresh = dot(bm, to_end_u[...], ((0,), (0,)))
    lo_row = lax.broadcasted_iota(jnp.int32, (1, LANES), 1) < HEADDIM
    for p in range(heads // 2):
        at = slice(p * LANES, (p + 1) * LANES)
        factor = pair_of(lo_row, keep[SPAN - 1 : SPAN, :], p)
        carry[:, at] = factor * carry[:, at] + fresh[:, at]


def split_dot(value, ones):
    high = value.astype(BF)
    low = (value - high.astype(F32)).astype(BF)
    return dot(high, ones) + dot(low, ones)


def backward_kernel(
    heads,
    segp_ref,
    segc_ref,
    segr_ref,
    mask_ref,
    in_a_ref,
    in_b_ref,
    halo_ref,
    weight_ref,
    b_ref,
    c_ref,
    dt_ref,
    rate_ref,
    skip_ref,
    y_ref,
    prior_ref,
    dy_ref,
    din_ref,
    dbc_ref,
    ddt_ref,
    drate_ref,
    dsum_ref,
    dcarry,
    after_state,
    keep_dy,
    to_end_u,
    slopes,
    along,
    ext,
    dext,
):
    step = pl.program_id(0)
    block = pl.num_programs(0) - 1 - step

    @pl.when(step == 0)
    def _():
        dcarry[...] = jnp.zeros_like(dcarry)
        after_state[...] = jnp.zeros_like(after_state)
        drate_ref[...] = jnp.zeros_like(drate_ref)
        dsum_ref[...] = jnp.zeros_like(dsum_ref)
        dext[SPAN:] = jnp.zeros((HALO, dext.shape[1]), F32)

    ext[0:HALO] = halo_ref[0].astype(F32)
    half = in_b_ref.shape[1]
    ext[HALO:, :half] = in_a_ref[:, :half].astype(F32)
    ext[HALO:, half:] = in_b_ref[...].astype(F32)
    segc, segr = segc_ref[...], segr_ref[...]
    dt = dt_ref[...]
    cum, cumr, keep, to_end = decays(segc, segr, segp_ref[block], dt, rate_ref[...])
    bm, cm = b_ref[...], c_ref[...]
    allowed = tri(False) & (segc == segr)
    mixing = jnp.where(allowed, dot(bm, cm, ((1,), (1,))), 0.0)
    masks = spread_columns(mask_ref, 0, CONV - 1)
    moved = spread_columns(mask_ref, CONV - 1, CONV - 1)
    lo = lax.broadcasted_iota(jnp.int32, (SPAN, LANES), 1) < HEADDIM
    dmixing = jnp.zeros((SPAN, SPAN), F32)
    for p in range(heads // 2):
        at = slice(p * LANES, (p + 1) * LANES)
        terms = taps(ext, masks, at)
        pre = convolved(terms, weight_ref, at)
        sig = jax.nn.sigmoid(pre)
        x2 = pre * sig
        dt2 = pair_of(lo, dt, p)
        u2 = x2 * dt2
        dyb = dy_ref[:, at]
        dy2 = dyb.astype(F32)
        skip = skip_ref[:, at]
        te2 = pair_of(lo, to_end, p)
        u_sides = (jnp.where(lo, u2, 0.0).astype(BF), jnp.where(lo, 0.0, u2).astype(BF))
        du = te2 * dot(bm, dcarry[:, at].astype(BF))
        inner = []
        for k in range(2):
            h = 2 * p + k
            decay = jnp.exp(jnp.minimum(cumr[h : h + 1, :] - cum[:, h : h + 1], 0.0))
            inner.append(dot((decay * mixing).astype(BF), dyb))
            dmixing = dmixing + decay * dot(u_sides[k], dyb, ((1,), (1,)))
        du = du + jnp.where(lo, inner[0], inner[1])
        keep_dy[:, at] = (pair_of(lo, keep, p) * dy2).astype(BF)
        to_end_u[:, at] = (te2 * u2).astype(BF)
        slopes[:, at] = dy2 * (y_ref[:, at] - skip * x2) - u2.astype(BF).astype(F32) * du
        along[:, at] = x2 * du
        dpre = (dt2 * du + skip * dy2) * (sig * (1.0 + pre * (1.0 - sig)))
        dext[0:SPAN, at] = dpre
        for k in range(CONV):
            dsum_ref[k : k + 1, at] += jnp.sum(dpre * terms[k], axis=0, keepdims=True)
        dsum_ref[CONV : CONV + 1, at] += jnp.sum(dpre, axis=0, keepdims=True)
        dsum_ref[CONV + 1 : CONV + 2, at] += jnp.sum(dy2 * x2, axis=0, keepdims=True)
        din = dpre * weight_ref[CONV - 1 : CONV, at]
        for k in range(CONV - 1):
            later = dext[pl.ds(CONV - 1 - k, SPAN), at]
            din = din + later * moved[k] * weight_ref[k : k + 1, at]
        din_ref[:, at] = din.astype(BF)
    dext[SPAN:] = dext[0:HALO]
    dmixing = jnp.where(allowed, dmixing, 0.0).astype(BF)
    dstate = dcarry[...].astype(BF)
    prior = prior_ref[0]
    dbc_ref[:, :STATE] = dot(dmixing, cm) + dot(to_end_u[...], dstate, ((1,), (1,)))
    dbc_ref[:, STATE:] = dot(dmixing, bm, ((0,), (0,))) + dot(
        keep_dy[...], prior.astype(BF), ((1,), (1,))
    )
    width = heads * HEADDIM
    ones = (
        lax.broadcasted_iota(jnp.int32, (width, LANES), 0) // HEADDIM
        == lax.broadcasted_iota(jnp.int32, (width, LANES), 1)
    ).astype(BF)
    at_end = jnp.sum(dcarry[...] * after_state[...], axis=0, keepdims=True)
    at_end = split_dot(jnp.broadcast_to(at_end, (16, width)), ones)[:1]
    dcum = split_dot(slopes[...], ones)
    da = dot(tri(False).astype(F32), dcum, precision=HIGH) + at_end
    ddt_ref[...] = rate_ref[...] * da + split_dot(along[...], ones)
    drate_ref[...] += jnp.sum(dt * da, axis=0, keepdims=True)
    fresh = dot(cm, keep_dy[...], ((0,), (0,)))
    lo_row = lax.broadcasted_iota(jnp.int32, (1, LANES), 1) < HEADDIM
    for p in range(heads // 2):
        at = slice(p * LANES, (p + 1) * LANES)
        factor = pair_of(lo_row, keep[SPAN - 1 : SPAN, :], p)
        dcarry[:, at] = factor * dcarry[:, at] + fresh[:, at]
    after_state[...] = prior


def scan_specs(heads, at, in_widths):
    width = heads * HEADDIM

    def rows(n):
        return pl.BlockSpec((SPAN, n), lambda i: (at(i), 0))

    def whole(*shape):
        return pl.BlockSpec(shape, lambda i: (0,) * len(shape))

    ins = [
        pl.BlockSpec(memory_space=pltpu.SMEM),
        rows(1),
        pl.BlockSpec((1, SPAN), lambda i: (0, at(i))),
        rows(LANES),
        rows(in_widths[0]),
        rows(in_widths[1]),
        pl.BlockSpec((1, HALO, width), lambda i: (at(i), 0, 0)),
        whole(8, width),
        rows(STATE),
        rows(STATE),
        rows(LANES),
        whole(1, LANES),
        whole(1, width),
    ]
    prior = pl.BlockSpec((1, STATE, width), lambda i: (at(i), 0, 0))
    return rows, whole, ins, prior


def scan_forward(heads, blocks, operands):
    rows, whole, ins, prior = scan_specs(heads, lambda i: i, [operands[n].shape[1] for n in (4, 5)])
    width = heads * HEADDIM
    return call(
        functools.partial(forward_kernel, heads),
        grid=(blocks,),
        in_specs=ins,
        out_specs=[rows(width), prior],
        out_shape=[
            jax.ShapeDtypeStruct((blocks * SPAN, width), F32),
            jax.ShapeDtypeStruct((blocks, STATE, width), F32),
        ],
        scratch_shapes=[
            pltpu.VMEM((STATE, width), F32),
            pltpu.VMEM((SPAN, width), BF),
            pltpu.VMEM((HALO + SPAN, width), F32),
        ],
        name="scan_forward",
    )(*operands)


def scan_backward(heads, blocks, operands, y, priors, dy):
    rows, whole, ins, prior = scan_specs(
        heads, lambda i: blocks - 1 - i, [operands[n].shape[1] for n in (4, 5)]
    )
    width = heads * HEADDIM
    return call(
        functools.partial(backward_kernel, heads),
        grid=(blocks,),
        in_specs=ins + [rows(width), prior, rows(width)],
        out_specs=[rows(width), rows(2 * STATE), rows(LANES), whole(1, LANES), whole(8, width)],
        out_shape=[
            jax.ShapeDtypeStruct((blocks * SPAN, width), BF),
            jax.ShapeDtypeStruct((blocks * SPAN, 2 * STATE), F32),
            jax.ShapeDtypeStruct((blocks * SPAN, LANES), F32),
            jax.ShapeDtypeStruct((1, LANES), F32),
            jax.ShapeDtypeStruct((8, width), F32),
        ],
        scratch_shapes=[
            pltpu.VMEM((STATE, width), F32),
            pltpu.VMEM((STATE, width), F32),
            pltpu.VMEM((SPAN, width), BF),
            pltpu.VMEM((SPAN, width), BF),
            pltpu.VMEM((SPAN, width), F32),
            pltpu.VMEM((SPAN, width), F32),
            pltpu.VMEM((HALO + SPAN, width), F32),
            pltpu.VMEM((SPAN + HALO, width), F32),
        ],
        name="scan_backward",
    )(*operands, y, priors, dy)


def as_columns(rows):
    few, tokens = rows.shape
    return jnp.concatenate([rows, jnp.zeros((LANES - few, tokens), F32)]).T


def level_block(pieces, spot):
    piece, lead = spot
    return pieces[piece][lead + (slice(None), slice(None))].astype(F32)


def upper_kernel(where, plan, nd, tok, ns, here_ref, range_ref, count_ref, ratio_ref, q_turned, *refs):
    count = 3 + 2 * LEVELS
    pieces, outs = refs[:count], refs[count:]
    upper_ref, grad_refs, coefs = outs[0], outs[1 : 2 * nd], outs[2 * nd]

    @pl.when(pl.program_id(0) == 0)
    def _():
        rows = [count_ref[j, w] * ratio_ref[w : w + 1, :] for j in range(len(plan)) for w in range(LEVELS)]
        coefs[...] = as_columns(jnp.concatenate(rows))

    for k in range(ns):
        at = here_ref[0] ^ k
        rows = pl.ds(pl.multiple_of(at * tok, tok), tok)
        levels = [level_block(pieces, where[w][k]) for w in range(LEVELS)]
        for j in range(len(plan)):
            total = None
            for w in plan[j]:
                n = j * LEVELS + w
                term = coefs[rows, n : n + 1] * levels[w]
                total = term if total is None else total + term
            upper_ref[j, rows, :] = total.astype(BF)
    count = q_turned.shape[0] // nd
    for k in range(nd):
        index = here_ref[1] ^ k
        rows = pl.ds(pl.multiple_of(index * count, count), count)
        value = dot(q_turned[rows, :], upper_ref[range_ref[index]]).astype(BF)
        if k:
            grad_refs[2 * k - 1][...] = value[: count // 2]
            grad_refs[2 * k][...] = value[count // 2 :]
        else:
            grad_refs[0][...] = value


def products_kernel(where, plan, lanes, tok, ns, nd, here_ref, count_ref, q_ref, *refs):
    count = 3 + 2 * LEVELS
    held_ref, pieces, outs = refs[0], refs[1 : 1 + count], refs[1 + count :]
    prod_refs, inner_ref, w_ref, sums = outs[:ns], outs[ns], outs[ns + 1], outs[ns + 2]
    step = pl.program_id(0)
    rows_of = w_ref.shape[0] // nd
    for k in range(nd):
        at = pl.multiple_of((here_ref[1] ^ k) * rows_of, rows_of)
        w_ref[pl.ds(at, rows_of), :] = held_ref[:, k].reshape(rows_of, w_ref.shape[1])

    @pl.when(step == 0)
    def _():
        sums[...] = jnp.zeros_like(sums)

    for k in range(ns):
        at = here_ref[0] ^ k
        rows = pl.ds(pl.multiple_of(at * tok, tok), tok)
        values = [dot(q_ref[rows, a:b], w_ref[a:b, :]) for a, b in lanes]
        for j, value in enumerate(values):
            prod_refs[k][j] = value.astype(BF)
        for w in range(LEVELS):
            total = None
            for j in range(len(lanes)):
                if w in plan[j]:
                    term = values[j] * count_ref[j, w]
                    total = term if total is None else total + term
            part = total * level_block(pieces, where[w][k])
            folded = part[:, :LANES]
            for c in range(LANES, part.shape[1], LANES):
                folded = folded + part[:, c : c + LANES]
            sums[w, rows, :] += folded

    @pl.when(step == pl.num_programs(0) - 1)
    def _():
        lane = lax.broadcasted_iota(jnp.int32, sums.shape[1:], 1)
        total = jnp.zeros(sums.shape[1:], F32)
        for w in range(LEVELS):
            total = jnp.where(lane == w, jnp.sum(sums[w], axis=1, keepdims=True), total)
        inner_ref[...] = total.T[:LEVELS]


def gate_kernel(
    starts, wide, count_ref, upper_ref, w_ref, y_ref, z_ref, gain_ref, ratio_ref, mean_ref, dy_ref, dz_ref, grad_ref, coefs
):
    step = pl.program_id(0)

    @pl.when(step == 0)
    def _():
        cubes = ratio_ref[...] * ratio_ref[...] * ratio_ref[...] * mean_ref[...]
        rows = []
        for j in range(len(starts)):
            total = cubes[0:1] * count_ref[j, 0]
            for w in range(1, LEVELS):
                total = total + cubes[w : w + 1] * count_ref[j, w]
            rows.append(total)
        columns = as_columns(jnp.concatenate(rows))
        for j in range(len(starts)):
            coefs[j] = jnp.broadcast_to(columns[:, j : j + 1], coefs.shape[1:])

    grad_all = dot(upper_ref[0], w_ref[...], ((1,), (1,)))
    coef = coefs[tile_range(starts, wide, step)]
    for c in range(0, wide, LANES):
        at = slice(c, c + LANES)
        grad_t = grad_all[:, at]
        z = z_ref[:, at].astype(F32)
        sig = jax.nn.sigmoid(z)
        act = z * sig
        y = y_ref[:, at]
        q = y * act
        dq = gain_ref[:, at] * grad_t - q * coef
        dy_ref[:, at] = (dq * act).astype(BF)
        dz_ref[:, at] = (dq * y * (sig * (1.0 + z * (1.0 - sig)))).astype(BF)
        grad_ref[0:1, at] = jnp.sum(q * grad_t, axis=0, keepdims=True)


def tile_range(starts, wide, step):
    index = 0
    for start in starts[1:]:
        index = index + jnp.where(step * wide >= start, 1, 0)
    return index


def mixed_kernel(plan, split, ns, tok, here_ref, count_ref, ratio_ref, x_ref, *refs):
    shares, out_ref = refs[:-1], refs[-1]
    at = pl.ds(pl.multiple_of(here_ref[0] * tok, tok), tok)
    ratios = as_columns(ratio_ref[:, at])
    x = x_ref[...].astype(F32)
    for w in range(LEVELS):
        total = None
        for k in range(ns):
            for j in plan[w]:
                at = (k, j) if k < 3 or j < split else (k + 1, j - split)
                term = shares[at[0]][at[1]].astype(F32) * count_ref[k, j * LEVELS + w]
                total = term if total is None else total + term
        out_ref[w] = (x + ratios[:, w : w + 1] * total).astype(BF)


def dp_terms(others):
    return [swapped(other, "dp", k + 1) for k, other in enumerate(others)]


def over_seq(value):
    dense = value.reshape(-1, LANES)
    total = dense
    for k in range(1, lax.axis_size("seq")):
        total = total + swapped(dense, "seq", k)
    return total.reshape(value.shape)


def fsdp_half(own, got):
    nf = lax.axis_size("fsdp")
    f = lax.axis_index("fsdp")

    def part(offset):
        total = picked(own, f ^ offset).astype(F32)
        for other in got:
            total = total + picked(other, f ^ offset).astype(F32)
        return total.astype(BF)

    kept = jnp.stack([part(e) for e in range(0, nf, 2)])
    sent = jnp.stack([part(e ^ 1) for e in range(0, nf, 2)])
    return kept, sent


def fsdp_rest(kept, got):
    k = 2
    while k < lax.axis_size("fsdp"):
        total = (kept.astype(F32) + got.astype(F32)).astype(BF)
        kept, sent = total[::2], total[1::2]
        got = swapped(sent, "fsdp", k)
        k *= 2
    return kept[0], got[0]


def shards(
    tokens,
    lengths,
    norm_gain,
    w_in,
    w_dt,
    conv_w,
    conv_b,
    dt_bias,
    a_log,
    skip,
    gate_gain,
    w_out,
    cotangent,
):
    nd, ns, nf = lax.axis_size("dp"), lax.axis_size("seq"), lax.axis_size("fsdp")
    d, s, f = lax.axis_index("dp"), lax.axis_index("seq"), lax.axis_index("fsdp")
    tok = tokens.shape[1]
    length = ns * tok
    blocks = length // SPAN
    heads = HEADS // ns
    run = heads // nd
    width = heads * HEADDIM
    own_bc = 2 * STATE // ns
    used = width + own_bc
    cols = -(-(used + heads) // LANES) * LANES
    rows_in = w_in.shape[0]
    reach = CONV - 1

    levels = np.array(
        [[level_of(dd * (HEADS // nd) + ss * run + i) for dd in range(nd) for i in range(run)] for ss in range(ns)]
    )
    cuts = [0] + [h for h in range(1, heads) if (levels[:, h] != levels[:, h - 1]).any()] + [heads]
    ranges = [(a, b) for a, b in zip(cuts, cuts[1:])]
    range_level = np.array([[levels[ss, a] for a, _ in ranges] for ss in range(ns)])
    counts = (range_level[:, :, None] <= np.arange(LEVELS)[None, None, :]).astype(np.float32)
    counted = picked(jnp.asarray(counts), s)
    theirs = picked(
        jnp.asarray(np.stack([[counts[i ^ k].reshape(-1) for k in range(ns)] for i in range(ns)])), s
    )
    lowest = [int(range_level[ss].min()) for ss in range(ns)]

    def by_head(vector):
        lead = vector.shape[:-1]
        per = vector.shape[-1] // HEADS
        cut = vector.reshape(lead + (nd, ns, run * per))
        mine = lax.dynamic_index_in_dim(cut, s, len(lead) + 1, keepdims=False)
        return mine.reshape(lead + (heads * per,))

    def for_groups(matrix):
        per = matrix.shape[1] // HEADS
        cut = matrix.reshape(matrix.shape[0], nd, ns, run * per)
        return jnp.transpose(cut, (2, 0, 1, 3)).reshape(ns, matrix.shape[0], heads * per)

    def from_groups(stack):
        per = stack.shape[2] // heads
        cut = stack.reshape(ns, stack.shape[1], nd, run * per)
        return jnp.transpose(cut, (1, 2, 0, 3)).reshape(stack.shape[1], HEADS * per)

    pad_cols = cols - used - heads
    half = width // 2
    first = half + cols - width
    group_x = for_groups(w_in[:, INNER : 2 * INNER])
    stack = jnp.concatenate(
        [
            group_x[:, :, :half],
            w_in[:, 2 * INNER :].reshape(rows_in, ns, own_bc).transpose(1, 0, 2),
            for_groups(w_dt),
            jnp.zeros((ns, rows_in, pad_cols), BF),
            group_x[:, :, half:],
            for_groups(w_in[:, :INNER]),
        ],
        axis=2,
    )
    own_x = tokens[0].astype(F32)
    scale = lax.rsqrt(jnp.mean(own_x * own_x, axis=-1, keepdims=True) + EPS)
    xn_own = (own_x * scale * norm_gain).astype(BF)
    xn_across = swapped(xn_own, "seq", 2)
    xn_pieces = [xn_own, swapped(xn_own, "seq", 1), xn_across, swapped(xn_across, "seq", 1)]
    arrived = [picked(stack, s)] + [swapped(picked(stack, s ^ k), "seq", k) for k in range(1, ns)]
    mine = filled((ns, rows_in, stack.shape[2]), [(p, None, (s ^ k, None, None)) for k, p in enumerate(arrived)])
    mine_z = mine[:, :, cols:]

    def needed(at, level):
        return min(lowest[at], lowest[at ^ 1]) <= level

    halves = [cotangent[w : w + 2, 0] for w in range(0, LEVELS, 2)]
    singles = [cotangent[w, 0] for w in range(LEVELS)]

    def beside(level, *others):
        block = after(halves[level // 2], *others)
        return swapped(block, "seq", 1, lambda i, j: needed(j, level + 1))

    def across(level, *others):
        block = after(singles[level], *others)
        return swapped(block, "seq", 2, lambda i, j: needed(j, level))

    def far(level, block):
        return swapped(block, "seq", 1, lambda i, j: needed(j, level))

    positions = jnp.arange(length, dtype=jnp.int32)
    ends = jnp.cumsum(lengths[0])[:-1]
    seg = jnp.sum((positions[:, None] >= ends[None, :]).astype(jnp.int32), axis=1)
    seg_before = jnp.concatenate([jnp.full((1,), -1, jnp.int32), seg[SPAN - 1 : length - 1 : SPAN]])
    seg_pad = jnp.concatenate([jnp.full((reach,), -1, jnp.int32), seg])
    masks = [(seg_pad[k : k + length] == seg) for k in range(reach)]
    mask_cols = [m.astype(F32) for m in masks]
    mask_cols += [jnp.pad(m, (0, reach - k))[reach - k :] for k, m in enumerate(mask_cols)]
    mask_cols = jnp.pad(jnp.stack(mask_cols, axis=1), ((0, 0), (0, LANES - 2 * reach)))

    def conv_params(s_part, bc_part):
        return by_head(s_part), bc_part

    weight_s = jnp.concatenate(
        [by_head(conv_w[:, :INNER]), by_head(conv_b[None, :INNER]), jnp.zeros((3, width), F32)]
    )
    weight_r = jnp.pad(
        lax.dynamic_slice_in_dim(conv_w, INNER + s * own_bc, own_bc, 1), ((0, 0), (0, cols - used))
    )
    bias_r = jnp.pad(
        lax.dynamic_slice_in_dim(conv_b, INNER + s * own_bc, own_bc, 0), (0, cols - used)
    )
    bias = by_head(dt_bias)
    rate = -jnp.exp(by_head(a_log))
    skip_own = by_head(skip)
    gain = by_head(gate_gain)

    def over_fsdp(chunk):
        return lax.all_gather(chunk, "fsdp", axis=0, tiled=False)

    def over_dp(held):
        return [held] + [swapped(held, "dp", j) for j in range(1, nd)]

    row_halves = 2 if rows_in % 32 == 0 else 1

    def ready(parts, columns):
        if rows_in % 16 == 0:
            return [piece for pieces in parts for piece in pieces]
        moves = [
            (piece, i, (d ^ j, None, i, h, None, None))
            for h, pieces in enumerate(parts)
            for j, piece in enumerate(pieces)
            for i in range(nf)
        ]
        return [filled((nd, ns, nf, len(parts), rows_in // len(parts), columns), moves).reshape(D, columns)]

    held_a = over_fsdp(mine[:, :, :first])
    held_b = over_fsdp(mine[:, :, first:cols])
    other_out = [swapped(w_out, "dp", j) for j in range(1, nd)]
    held_a, other_out = together(held_a, other_out)
    small_ones = (seg, seg_before, mask_cols, weight_s, weight_r, bias_r, bias, rate, skip_own, gain, theirs)
    held_a, small_ones, halves, singles = together(held_a, small_ones, halves, singles)
    seg, seg_before, mask_cols, weight_s, weight_r, bias_r, bias, rate, skip_own, gain, theirs = small_ones
    near_high, near_low = beside(2, held_a), beside(0, held_a)
    chip3 = across(3, held_a)
    pieces_a = over_dp(held_a)
    xn = filled((ns, tok, D), [(p, None, (s ^ k, None, None)) for k, p in enumerate(xn_pieces)])
    xn = xn.reshape(length, D)
    held_b, pieces_a, chip3, near_high, xn = together(held_b, pieces_a, chip3, near_high, xn)

    far3 = far(3, chip3)
    pieces_b = over_dp(held_b)
    parts_z = mine_z.reshape(ns, row_halves, rows_in // row_halves, width)
    held_z = over_fsdp(after(parts_z[:, 0], held_a))
    late_z = [over_fsdp(after(parts_z[:, h], held_b)) for h in range(1, row_halves)]
    held_out = over_fsdp(after(jnp.stack([w_out] + other_out), held_z))

    xn_turned = xn.T
    here = jnp.stack([s, d]).astype(jnp.int32)
    proj_a, full_a = projections(here, xn, ready([pieces_a], first), nd, rows_in, first)

    proj_r = proj_a[:, half:]
    mixer = jnp.concatenate([jnp.zeros((reach, cols - width), BF), proj_r], axis=0)

    def taken(k):
        rows = mixer[k : k + length].astype(F32)
        return rows * mask_cols[:, k : k + 1] if k < reach else rows

    pre_r = bias_r
    for k in range(CONV):
        pre_r = pre_r + taken(k) * weight_r[k]
    bc_own = jax.nn.silu(pre_r).astype(BF)[:, :own_bc]
    bc_across = swapped(bc_own, "seq", 2)
    bc = [bc_own, swapped(bc_own, "seq", 1), bc_across, swapped(bc_across, "seq", 1)]
    chip2, chip1 = across(2, bc[2]), across(1, bc[2])
    pieces_b, xn_turned = together(pieces_b, xn_turned)
    proj_b, full_b = projections(here, after(xn, bc[2]), ready([pieces_b], half), nd, rows_in, half)
    proj_b, far3, near_low, held_z = together(proj_b, far3, near_low, held_z)
    pieces_z = over_dp(held_z)
    bc = reordered_by_xor(bc, s)
    b_in = jnp.concatenate(bc[: ns // 2], axis=1)
    c_out = jnp.concatenate(bc[ns // 2 :], axis=1)

    def padded(rows):
        return jnp.pad(rows, ((0, 0), (0, LANES - rows.shape[1])))

    pre_dt = proj_r[:, own_bc : own_bc + heads].astype(F32) + bias
    steps = jax.nn.softplus(pre_dt)
    tails = [
        p.reshape(blocks, SPAN, p.shape[1])[: blocks - 1, SPAN - HALO :, :half] for p in (proj_a, proj_b)
    ]
    operands = (
        seg_before,
        seg[:, None],
        seg[None, :],
        mask_cols,
        proj_a,
        proj_b,
        jnp.concatenate([jnp.zeros((1, HALO, width), BF), jnp.concatenate(tails, axis=2)]),
        weight_s,
        b_in,
        c_out,
        padded(steps),
        padded(rate[None, :]),
        jnp.repeat(skip_own, HEADDIM)[None, :],
    )
    y, priors = scan_forward(heads, blocks, operands)
    y, chip2, late_z = together(y, chip2, late_z)
    far2, chip0 = far(2, chip2), across(0, y)
    parts = [pieces_z] + [over_dp(piece) for piece in late_z]
    lanes = [(a * HEADDIM, b * HEADDIM) for a, b in ranges]
    starts = [a for a, _ in lanes]
    wide = min(min(b - a for a, b in lanes), TILE)
    proj_z, full_z, q_gain, q_turned, squares = projections(
        here, xn, ready(parts, width), nd, rows_in, width, (y, gain[None], starts, wide)
    )
    squares, chip1 = together(squares[: len(lanes)], chip1)
    far1 = far(1, chip1)
    widths = np.array([[(HEADS >> 3 - w) * HEADDIM] for w in range(LEVELS)], np.float32)
    per_level = jnp.sum(counted[:, :, None] * squares[:, None, :], axis=0)
    ratio, chip0 = together(lax.rsqrt(over_seq(per_level) / widths + EPS), chip0)
    far0 = far(0, chip0)

    plan = [[w for w in range(LEVELS) if range_level[:, j].min() <= w] for j in range(len(lanes))]
    out_rows = width // nd
    range_of = [next(j for j, (a, b) in enumerate(lanes) if a <= i * out_rows < b) for i in range(nd)]
    smem = pl.BlockSpec(memory_space=pltpu.SMEM)
    cot_pieces = [cotangent, near_low, near_high, chip0, chip1, chip2, chip3, far0, far1, far2, far3]
    cot_specs = [pl.BlockSpec((LEVELS, 1, tok, WIDE), lambda i: (0, 0, 0, i))]
    cot_specs += [pl.BlockSpec((2, tok, WIDE), lambda i: (0, 0, i))] * 2
    cot_specs += [pl.BlockSpec((tok, WIDE), lambda i: (0, i))] * (2 * LEVELS)
    where = [[(0, (w, 0)), (1 + w // 2, (w % 2,)), (3 + w, ()), (3 + LEVELS + w, ())] for w in range(LEVELS)]
    upper, *grad_out = call(
        functools.partial(upper_kernel, where, plan, nd, tok, ns),
        grid=(D // WIDE,),
        in_specs=[
            smem,
            smem,
            smem,
            pl.BlockSpec((LEVELS, length), lambda i: (0, 0)),
            pl.BlockSpec((width, length), lambda i: (0, 0)),
        ]
        + cot_specs,
        out_specs=[pl.BlockSpec((len(lanes), length, WIDE), lambda i: (0, 0, i))]
        + [pl.BlockSpec((out_rows, WIDE), lambda i: (0, i))]
        + [pl.BlockSpec((out_rows // 2, WIDE), lambda i: (0, i))] * (2 * nd - 2),
        out_shape=[jax.ShapeDtypeStruct((len(lanes), length, D), BF)]
        + [jax.ShapeDtypeStruct((out_rows, D), BF)]
        + [jax.ShapeDtypeStruct((out_rows // 2, D), BF)] * (2 * nd - 2),
        scratch_shapes=[pltpu.VMEM((length, LANES), F32)],
        name="upper",
    )(here, jnp.asarray(range_of, jnp.int32), counted, ratio, q_turned, *cot_pieces)
    out_first, out_second = dp_terms(grad_out[1::2]), dp_terms(grad_out[2::2])

    held_out, upper = together(held_out, upper)
    *shares, inner, full_out = call(
        functools.partial(products_kernel, where, plan, lanes, tok, ns, nd),
        grid=(D // WIDE,),
        in_specs=[
            smem,
            smem,
            pl.BlockSpec((length, width), lambda i: (0, 0)),
        ]
        + [pl.BlockSpec((nf, nd, w_out.shape[0], WIDE), lambda i: (0, 0, 0, i))]
        + cot_specs,
        out_specs=[pl.BlockSpec((len(lanes), tok, WIDE), lambda i: (0, 0, i))] * ns
        + [pl.BlockSpec((LEVELS, length), lambda i: (0, 0))]
        + [pl.BlockSpec((width, WIDE), lambda i: (0, i))],
        out_shape=[jax.ShapeDtypeStruct((len(lanes), tok, D), BF)] * ns
        + [jax.ShapeDtypeStruct((LEVELS, length), F32)]
        + [jax.ShapeDtypeStruct((width, D), BF)],
        scratch_shapes=[pltpu.VMEM((LEVELS, length, LANES), F32)],
        name="products",
    )(here, counted, q_gain, held_out, *cot_pieces)
    means, out_first = together(over_seq(inner) / widths, out_first)
    shares[1:3] = [swapped(after(shares[k], means), "seq", k) for k in (1, 2)]
    split = (len(lanes) + 1) // 2
    third = [swapped(after(shares[3][:split], shares[1]), "seq", 3), shares[3][split:]]

    cols_of = pl.BlockSpec((length, wide), lambda i: (0, i))
    scalars = pl.BlockSpec((LEVELS, length), lambda i: (0, 0))
    dy, dz, grad_gate = call(
        functools.partial(gate_kernel, starts, wide),
        grid=(width // wide,),
        in_specs=[
            smem,
            pl.BlockSpec((1, length, D), lambda i: (tile_range(starts, wide, i), 0, 0)),
            pl.BlockSpec((wide, D), lambda i: (i, 0)),
            cols_of,
            cols_of,
            pl.BlockSpec((1, wide), lambda i: (0, i)),
            scalars,
            scalars,
        ],
        out_specs=[cols_of, cols_of, pl.BlockSpec((8, wide), lambda i: (0, i))],
        out_shape=[
            jax.ShapeDtypeStruct((length, width), BF),
            jax.ShapeDtypeStruct((length, width), BF),
            jax.ShapeDtypeStruct((8, width), F32),
        ],
        scratch_shapes=[pltpu.VMEM((len(lanes), length, LANES), F32)],
        name="gate_backward",
    )(counted, upper, full_out, y, proj_z, gain[None], ratio, means)
    grad_gate = grad_gate[0]

    def in_terms(dproj, at, first=0, columns=None):
        columns = columns or dproj.shape[1]
        out = row_terms(xn_turned, dproj, at, nd, ns, nf, first, columns)
        return out.reshape(nf, ns * rows_in, columns)

    z_other = [in_terms(dz, d ^ k) for k in range(1, nd)]
    z_got = dp_terms(z_other)
    dy, out_second, shares[1] = together(after(dy, *z_other), out_second, shares[1])
    chunk = (nf, out_rows // nf, D)
    out_got = [jnp.concatenate([u, v]).reshape(chunk) for u, v in zip(out_first, out_second)]
    out_kept, out_sent = fsdp_half(grad_out[0].reshape(chunk), out_got)
    dy = after(dy, out_sent)
    out_half = swapped(out_sent, "fsdp", 1)

    dproj_s, dbc, ddt, drate, dsum = scan_backward(heads, blocks, operands, y, priors, dy)
    dproj_s, dbc, out_half, shares[2], third = together(dproj_s, dbc, out_half, shares[2], third)
    out_pair = fsdp_rest(out_kept, out_half)

    dbc = dbc.astype(BF)
    slices = reordered_by_xor([dbc[:, j * own_bc : (j + 1) * own_bc] for j in range(ns)], s)
    beside_bc = swapped(jnp.concatenate([slices[1], slices[3]], axis=1), "seq", 1)
    sum_bc = jnp.concatenate([slices[0], slices[2]], axis=1).astype(F32) + beside_bc.astype(F32)
    across_bc = swapped(sum_bc[:, own_bc:].astype(BF), "seq", 2)

    z_own = in_terms(after(dz, dproj_s), d)
    z_own, z_got = together(z_own, z_got)
    z_kept, z_sent = fsdp_half(z_own, z_got)
    z_half = swapped(z_sent, "fsdp", 1)
    late_s = after(dproj_s, z_sent)
    left_other = [in_terms(late_s, d ^ k, 0, half) for k in range(1, nd)]
    left_got = dp_terms(left_other)
    third[1] = swapped(after(third[1], across_bc), "seq", 3)
    dbc_own = sum_bc[:, :own_bc] + across_bc.astype(F32)
    dproj_r, small_sums = small_back(
        own_bc,
        pre_r,
        padded(after(dbc_own, *left_other)),
        proj_r,
        mask_cols,
        weight_r,
        ddt,
        padded(pre_dt),
    )

    dxn = input_grad(dz, dproj_s, dproj_r, full_z, full_a, full_b, ns, tok)
    pair = swapped(jnp.stack([picked(dxn, s ^ 1), picked(dxn, s ^ 3)]), "seq", 1)

    late_s, late_r, z_half = together(dproj_s, after(dproj_r, dxn), z_half)
    z_pair = fsdp_rest(z_kept, z_half)
    right_other = [
        jnp.concatenate([in_terms(late_s, d ^ k, half, half), in_terms(late_r, d ^ k)], axis=2)
        for k in range(1, nd)
    ]
    right_other, left_got, out_pair = together(right_other, left_got, out_pair)
    right_got = dp_terms(right_other)
    near = picked(dxn, s).astype(F32) + pair[0].astype(F32)
    far_sum = (picked(dxn, s ^ 2).astype(F32) + pair[1].astype(F32)).astype(BF)
    dxn_across = swapped(far_sum, "seq", 2)
    own_s = in_terms(after(dproj_s, far_sum, *right_other), d)
    left_kept, left_sent = fsdp_half(own_s[:, :, :half], left_got)
    left_sent, z_pair = together(left_sent, z_pair)
    left_half = swapped(left_sent, "fsdp", 1)
    own_r = in_terms(after(dproj_r, left_sent), d)
    flat = flattened(
        [
            jnp.concatenate([dsum[:CONV], small_sums[:CONV, :own_bc]], axis=1).reshape(-1),
            dsum[CONV],
            small_sums[CONV, :own_bc],
            grad_gate,
            small_sums[CONV + 1, :heads],
            drate[0, :heads] * rate,
            jnp.sum(dsum[CONV + 1].reshape(heads, HEADDIM), axis=1),
        ]
    )
    right_got, left_half = together(right_got, left_half)
    left_pair = fsdp_rest(left_kept, left_half)
    own_right = jnp.concatenate([own_s[:, :, half:], own_r], axis=2)
    right_kept, right_sent = fsdp_half(own_right, right_got)
    right_half = swapped(right_sent, "fsdp", 1)

    mixed = call(
        functools.partial(
            mixed_kernel,
            [[j for j in range(len(lanes)) if range_level[:, j].min() <= w] for w in range(LEVELS)],
            split,
            ns,
            tok,
        ),
        grid=(D // WIDE,),
        in_specs=[
            smem,
            smem,
            pl.BlockSpec((LEVELS, length), lambda i: (0, 0)),
            pl.BlockSpec((tok, WIDE), lambda i: (0, i)),
        ]
        + [pl.BlockSpec((p.shape[0], tok, WIDE), lambda i: (0, 0, i)) for p in shares[:3] + third],
        out_specs=pl.BlockSpec((LEVELS, tok, WIDE), lambda i: (0, 0, i)),
        out_shape=jax.ShapeDtypeStruct((LEVELS, tok, D), BF),
        name="mixed",
    )(here, theirs, ratio, tokens[0], *after(shares[:3] + third, right_sent))[:, None]
    right_half, mixed, dxn_across = together(right_half, mixed, dxn_across)
    right_kept = after(right_kept, mixed)
    right_pair = fsdp_rest(right_kept, right_half)
    dxn_own = near + dxn_across.astype(F32)
    grad_norm = jnp.sum(dxn_own * own_x * scale, axis=0)
    scaled = norm_gain * dxn_own
    dx = scale * scaled - own_x * scale**3 * jnp.mean(own_x * scaled, axis=-1, keepdims=True)
    dx = (dx + jnp.sum(after(cotangent, mixed)[:, 0].astype(F32), axis=0)).astype(BF)
    flat = jnp.concatenate([flat, grad_norm.reshape(-1, LANES)])
    flat = butterfly(flat, "dp")

    def whole_sum(pair):
        total = (pair[0].astype(F32) + pair[1].astype(F32)).astype(BF)
        return total.reshape(ns, rows_in, total.shape[1])

    z_pair, left_pair = together(z_pair, left_pair)
    early = jnp.concatenate([whole_sum(z_pair), whole_sum(left_pair)], axis=2)
    early_got = [picked(early, s)] + [swapped(picked(early, s ^ k), "seq", k) for k in range(1, ns)]
    early_got, right_pair, flat = together(early_got, right_pair, flat)
    flat = butterfly(flat, "fsdp")
    late = whole_sum(right_pair)
    late_got = [picked(late, s)] + [swapped(picked(late, s ^ k), "seq", k) for k in range(1, ns)]
    early = jnp.stack(reordered_by_xor(early_got, s))
    late = jnp.stack(reordered_by_xor(late_got, s))
    got_z = early[:, :, :width]
    got_x = jnp.concatenate([early[:, :, width:], late], axis=2)
    sum_out = out_pair[0].astype(F32) + out_pair[1].astype(F32)


    sum_in = jnp.concatenate(
        [
            from_groups(got_z),
            from_groups(got_x[:, :, :width]),
            jnp.transpose(got_x[:, :, width:used], (1, 0, 2)).reshape(rows_in, 2 * STATE),
        ],
        axis=1,
    ).astype(F32)
    sum_dt = from_groups(got_x[:, :, used : used + heads]).astype(F32)

    sizes = [CONV * used, used, width, heads, heads, heads]
    filling = -sum(sizes) % 1024
    sizes += [filling, D]
    every = seq_gather(flat, s).reshape(ns, -1)
    starts = np.cumsum([0] + sizes)
    pieces = [every[:, a : a + n] for a, n in zip(starts, sizes)]

    def heads_back(rows):
        lead = rows.shape[1:-1]
        cut = rows.reshape((ns,) + lead + (nd, rows.shape[-1] // nd))
        order = tuple(range(1, 1 + len(lead))) + (1 + len(lead), 0, 2 + len(lead))
        return jnp.transpose(cut, order).reshape(lead + (-1,))

    conv_rows = pieces[0].reshape(ns, CONV, used)
    conv_all = jnp.concatenate(
        [
            heads_back(conv_rows[:, :, :width]),
            jnp.transpose(conv_rows[:, :, width:], (1, 0, 2)).reshape(CONV, 2 * STATE),
        ],
        axis=1,
    )
    bias_all = jnp.concatenate([heads_back(pieces[1][:, :width]), pieces[1][:, width:].reshape(-1)])
    return (
        mixed,
        dx[None],
        jnp.sum(pieces[7], axis=0),
        sum_in,
        sum_dt,
        conv_all,
        bias_all,
        heads_back(pieces[3]),
        heads_back(pieces[4]),
        heads_back(pieces[5]),
        heads_back(pieces[2]),
        sum_out,
    )


def solution(mesh):
    rows = P(("dp", "seq", "fsdp"), None)
    held = P(("dp", "fsdp"), "seq", None)
    levels = P(None, ("dp", "fsdp"), "seq", None)
    placed = (held, P(("dp", "fsdp"), None), P(), rows, rows, P(), P(), P(), P(), P(), P(), rows, levels)
    return jax.shard_map(
        shards,
        mesh=mesh,
        in_specs=placed,
        out_specs=(levels, held, P(), rows, rows, P(), P(), P(), P(), P(), P(), rows),
        check_vma=False,
    )
```

```python
import functools

import jax
import jax.numpy as jnp
import numpy as np
from jax import lax
from jax.experimental import pallas as pl
from jax.experimental.pallas import tpu as pltpu
from jax.sharding import PartitionSpec as P

D = 2048
HEADS = 64
HEADDIM = 64
STATE = 128
CONV = 4
SPAN = 128
INNER = 4096
EPS = 1e-05
LEVELS = 4
BF = jnp.bfloat16
F32 = jnp.float32
HIGH = lax.Precision.HIGHEST
LANES = 128
HALO = 16
TILE = 256
WIDE = 512
VMEM_LIMIT = 48 * 1024 * 1024


def dot(a, b, dims=((1,), (0,)), precision=None):
    return lax.dot_general(a, b, (dims, ((), ())), preferred_element_type=F32, precision=precision)


def silu_slope(v):
    sig = jax.nn.sigmoid(v)
    return sig * (1.0 + v * (1.0 - sig))


def level_of(head):
    return 0 if head < 8 else 1 if head < 16 else 2 if head < 32 else 3


def swapped(value, axis, k, keep=None):
    pairs = [(i, i ^ k) for i in range(lax.axis_size(axis))]
    if keep is not None:
        pairs = [p for p in pairs if keep(*p)]
    return lax.ppermute(value, axis, pairs)


def after(value, *others):
    return lax.optimization_barrier((value,) + others)[0]


def together(*values):
    return lax.optimization_barrier(values)


def flattened(vectors):
    flat = jnp.concatenate(vectors)
    return jnp.pad(flat, (0, -flat.shape[0] % 1024)).reshape(-1, LANES)


def butterfly(value, axis):
    k = 1
    while k < lax.axis_size(axis):
        value = value + swapped(value, axis, k)
        k *= 2
    return value


def picked(array, index):
    return lax.dynamic_index_in_dim(array, index, 0, keepdims=False)


def seq_gather(block, here):
    return jnp.stack(reordered_by_xor([block] + [swapped(block, "seq", k) for k in range(1, 4)], here))


def reordered_by_xor(pieces, here):
    k = 1
    while k < len(pieces):
        flip = (here & k) > 0
        pieces = [jnp.where(flip, pieces[j ^ k], piece) for j, piece in enumerate(pieces)]
        k *= 2
    return pieces


def call(kernel, **kwargs):
    return pl.pallas_call(
        kernel,
        compiler_params=pltpu.CompilerParams(vmem_limit_bytes=VMEM_LIMIT),
        cost_estimate=pl.CostEstimate(flops=1, bytes_accessed=1, transcendentals=0),
        **kwargs,
    )


def filled(shape, moves):
    arrays, plan, rows = [], [], []
    block = tuple(size if index is None else 1 for size, index in zip(shape, moves[0][2]))
    for piece, lead, place in moves:
        at = next((i for i, a in enumerate(arrays) if a is piece), len(arrays))
        if at == len(arrays):
            arrays.append(piece)
        plan.append((at, lead))
        rows.append(jnp.stack([jnp.asarray(0 if n is None else n, jnp.int32) for n in place]))

    def kernel(index_ref, *refs):
        pieces, out = refs[:-1], refs[-1]
        for m, (at, lead) in enumerate(plan):

            @pl.when(pl.program_id(0) == m)
            def _():
                value = pieces[at][...] if lead is None else pieces[at][lead]
                out[...] = value.reshape(block)

    return call(
        kernel,
        grid_spec=pltpu.PrefetchScalarGridSpec(
            num_scalar_prefetch=1,
            grid=(len(plan),),
            in_specs=[
                pl.BlockSpec(a.shape, lambda i, t, n=a.ndim: (0,) * n) for a in arrays
            ],
            out_specs=pl.BlockSpec(
                block, lambda i, t: tuple(t[i, n] for n in range(len(shape)))
            ),
        ),
        out_shape=jax.ShapeDtypeStruct(shape, arrays[0].dtype),
        name="filled",
    )(jnp.stack(rows), *arrays)


def terms_kernel(ns, nf, at_ref, left_ref, right_ref, out_ref):
    value = dot(left_ref[...], right_ref[...]).astype(BF)
    rows = value.shape[0] // (ns * nf)
    for i in range(ns):
        for k in range(nf):
            out_ref[k, i] = value[(i * nf + k) * rows : (i * nf + k + 1) * rows]


def row_terms(turned, right, at, nd, ns, nf, first, columns):
    depth = turned.shape[1]
    rows = turned.shape[0] // nd
    wide = TILE if columns % TILE == 0 else LANES
    return call(
        functools.partial(terms_kernel, ns, nf),
        grid_spec=pltpu.PrefetchScalarGridSpec(
            num_scalar_prefetch=1,
            grid=(columns // wide,),
            in_specs=[
                pl.BlockSpec((rows, depth), lambda i, t: (t[0], 0)),
                pl.BlockSpec((depth, wide), lambda i, t: (0, i + first // wide)),
            ],
            out_specs=pl.BlockSpec((nf, ns, rows // (nf * ns), wide), lambda i, t: (0, 0, 0, i)),
        ),
        out_shape=jax.ShapeDtypeStruct((nf, ns, rows // (nf * ns), columns), BF),
        name="row_terms",
    )(at.astype(jnp.int32)[None], turned, right)


def small_back_kernel(
    width, pre_ref, dbc_ref, in_ref, mask_ref, weight_ref, ddt_ref, pre_dt_ref, out_ref, sum_ref, ext, dext
):
    rows = pre_ref.shape[0]
    ext[0:HALO] = jnp.zeros((HALO, LANES), F32)
    ext[HALO:] = in_ref[...].astype(F32)
    pre = pre_ref[...]
    sig = jax.nn.sigmoid(pre)
    dpre = dbc_ref[...] * (sig * (1.0 + pre * (1.0 - sig)))
    dext[0:rows] = dpre
    dext[rows:] = jnp.zeros((HALO, LANES), F32)
    total = dpre * weight_ref[CONV - 1 : CONV, :]
    for k in range(CONV):
        term = ext[pl.ds(HALO - CONV + 1 + k, rows), :]
        if k < CONV - 1:
            term = term * mask_ref[:, k : k + 1]
            later = dext[pl.ds(CONV - 1 - k, rows), :] * mask_ref[:, CONV - 1 + k : CONV + k]
            total = total + later * weight_ref[k : k + 1, :]
        sum_ref[k : k + 1, :] = jnp.sum(dpre * term, axis=0, keepdims=True)
    sum_ref[CONV : CONV + 1, :] = jnp.sum(dpre, axis=0, keepdims=True)
    draw = ddt_ref[...] * jax.nn.sigmoid(pre_dt_ref[...])
    sum_ref[CONV + 1 : CONV + 2, :] = jnp.sum(draw, axis=0, keepdims=True)
    out_ref[...] = (total + pltpu.roll(draw, width, axis=1)).astype(BF)


def small_back(width, pre, dbc, proj, masks, weight, ddt, pre_dt):
    rows = pre.shape[0]
    return call(
        functools.partial(small_back_kernel, width),
        out_shape=[
            jax.ShapeDtypeStruct((rows, LANES), BF),
            jax.ShapeDtypeStruct((8, LANES), F32),
        ],
        scratch_shapes=[pltpu.VMEM((HALO + rows, LANES), F32), pltpu.VMEM((rows + HALO, LANES), F32)],
        name="small_back",
    )(pre, dbc, proj, masks, weight, ddt, pre_dt)


def input_grad_kernel(blocks, dz_ref, ds_ref, dr_ref, wz_ref, wa_ref, wb_ref, out_ref):
    half = wb_ref.shape[1]
    columns = ((1,), (1,))
    total = dot(dz_ref[...], wz_ref[...], columns)
    total = total + dot(ds_ref[:, :half], wa_ref[:, :half], columns)
    total = total + dot(ds_ref[:, half:], wb_ref[...], columns)
    total = total + dot(dr_ref[...], wa_ref[:, half:], columns)
    total = total.astype(BF)
    tok = total.shape[0] // blocks
    for i in range(blocks):
        out_ref[i] = total[i * tok : (i + 1) * tok]


def input_grad(dz, ds, dr, wz, wa, wb, blocks, tok):
    def whole(a):
        return pl.BlockSpec(a.shape, lambda i: (0, 0))

    def rows(a):
        return pl.BlockSpec((TILE, a.shape[1]), lambda i: (i, 0))

    return call(
        functools.partial(input_grad_kernel, blocks),
        grid=(wz.shape[0] // TILE,),
        in_specs=[whole(dz), whole(ds), whole(dr), rows(wz), rows(wa), rows(wb)],
        out_specs=pl.BlockSpec((blocks, tok, TILE), lambda i: (0, 0, i)),
        out_shape=jax.ShapeDtypeStruct((blocks, tok, wz.shape[0]), BF),
        name="input_grad",
    )(dz, ds, dr, wz, wa, wb)


def assembled(here_ref, pieces, nd, full_ref):
    halves = len(pieces) // nd
    nf, ns, rows = pieces[0].shape[:3]
    for n, piece in enumerate(pieces):
        h, j = divmod(n, nd)
        for k in range(nf):
            for i in range(ns):
                block = ((here_ref[1] ^ j) * ns + i) * nf + k
                at = pl.multiple_of((block * halves + h) * rows, rows)
                full_ref[pl.ds(at, rows), :] = piece[k, i]


def gated_kernel(nd, count, starts, wide, here_ref, xn_ref, y_ref, gain_ref, *refs):
    pieces, (out_ref, full_ref, gated_ref, turned_ref, squares_ref, sums) = refs[:count], refs[count:]
    step = pl.program_id(0)

    @pl.when(step == 0)
    def _():
        sums[...] = jnp.zeros_like(sums)

    if nd:
        assembled(here_ref, pieces, nd, full_ref)
    else:
        full_ref[...] = pieces[0][...]
    value = dot(xn_ref[...], full_ref[...]).astype(BF)
    out_ref[...] = value
    where = tile_range(starts, wide, step)
    for c in range(0, wide, LANES):
        at = slice(c, c + LANES)
        z = value[:, at].astype(F32)
        q = y_ref[:, at] * (z * jax.nn.sigmoid(z))
        gated = (q * gain_ref[:, at]).astype(BF)
        gated_ref[:, at] = gated
        turned_ref[at, :] = gated.T
        sums[where] += q * q

    @pl.when(step == pl.num_programs(0) - 1)
    def _():
        lane = lax.broadcasted_iota(jnp.int32, sums.shape[1:], 1)
        total = jnp.zeros(sums.shape[1:], F32)
        for j in range(len(starts)):
            total = jnp.where(lane == j, jnp.sum(sums[j], axis=1, keepdims=True), total)
        squares_ref[...] = total.T[: squares_ref.shape[0]]


def gated_projection(here, xn, pieces, nd, columns, y, gain, starts, wide):
    if pieces[0].ndim == 2:
        nd = 0
    tokens, depth = xn.shape
    tile = pl.BlockSpec((tokens, wide), lambda i: (0, i))
    ins = [
        pl.BlockSpec(memory_space=pltpu.SMEM),
        pl.BlockSpec((tokens, depth), lambda i: (0, 0)),
        tile,
        pl.BlockSpec((1, wide), lambda i: (0, i)),
    ]
    for piece in pieces:
        lead = piece.shape[:-1]
        ins.append(pl.BlockSpec(lead + (wide,), lambda i, n=len(lead): (0,) * n + (i,)))
    return call(
        functools.partial(gated_kernel, nd, len(pieces), starts, wide),
        grid=(columns // wide,),
        in_specs=ins,
        out_specs=[
            tile,
            pl.BlockSpec((depth, wide), lambda i: (0, i)),
            tile,
            pl.BlockSpec((wide, tokens), lambda i: (i, 0)),
            pl.BlockSpec((8, tokens), lambda i: (0, 0)),
        ],
        out_shape=[
            jax.ShapeDtypeStruct((tokens, columns), BF),
            jax.ShapeDtypeStruct((depth, columns), BF),
            jax.ShapeDtypeStruct((tokens, columns), BF),
            jax.ShapeDtypeStruct((columns, tokens), BF),
            jax.ShapeDtypeStruct((8, tokens), F32),
        ],
        scratch_shapes=[pltpu.VMEM((len(starts), tokens, LANES), F32)],
        name="gated",
    )(here, xn, y, gain, *pieces)


def tri(rows_first):
    a = lax.broadcasted_iota(jnp.int32, (SPAN, SPAN), 0)
    b = lax.broadcasted_iota(jnp.int32, (SPAN, SPAN), 1)
    return (a >= b) if rows_first else (a <= b)


def pair_of(lo, cols, p):
    return jnp.where(lo, cols[:, 2 * p : 2 * p + 1], cols[:, 2 * p + 1 : 2 * p + 2])


def decays(segc, segr, segp, dt, rate):
    cum = dot(tri(True).astype(F32), dt * rate, precision=HIGH)
    last = cum[SPAN - 1 : SPAN, :]
    keep = jnp.where(segc == segp, jnp.exp(cum), 0.0)
    to_end = jnp.where(segc == segr[:, SPAN - 1 : SPAN], jnp.exp(last - cum), 0.0)
    return cum, cum.T, keep, to_end


def spread_columns(ref, first, count):
    return [jnp.broadcast_to(ref[:, first + k : first + k + 1], (SPAN, LANES)) for k in range(count)]


def taps(ext, masks, at):
    terms = [ext[pl.ds(HALO - CONV + 1 + k, SPAN), at] for k in range(CONV)]
    return [t * m for t, m in zip(terms, masks)] + terms[CONV - 1 :]


def convolved(terms, weight_ref, at):
    total = weight_ref[CONV : CONV + 1, at] + terms[0] * weight_ref[0:1, at]
    for k in range(1, CONV):
        total = total + terms[k] * weight_ref[k : k + 1, at]
    return total


def forward_kernel(
    heads,
    segp_ref,
    segc_ref,
    segr_ref,
    mask_ref,
    in_a_ref,
    in_b_ref,
    halo_ref,
    weight_ref,
    b_ref,
    c_ref,
    dt_ref,
    rate_ref,
    skip_ref,
    y_ref,
    prior_ref,
    carry,
    to_end_u,
    ext,
):
    block = pl.program_id(0)
    width = heads * HEADDIM

    @pl.when(block == 0)
    def _():
        carry[...] = jnp.zeros_like(carry)

    prior_ref[0] = carry[...]
    ext[0:HALO] = halo_ref[0].astype(F32)
    half = in_b_ref.shape[1]
    ext[HALO:, :half] = in_a_ref[:, :half].astype(F32)
    ext[HALO:, half:] = in_b_ref[...].astype(F32)
    segc, segr = segc_ref[...], segr_ref[...]
    dt = dt_ref[...]
    cum, cumr, keep, to_end = decays(segc, segr, segp_ref[block], dt, rate_ref[...])
    bm, cm = b_ref[...], c_ref[...]
    mixing = dot(cm, bm, ((1,), (1,)))
    mixing = jnp.where(tri(True) & (segc == segr), mixing, 0.0)
    masks = spread_columns(mask_ref, 0, CONV - 1)
    lo = lax.broadcasted_iota(jnp.int32, (SPAN, LANES), 1) < HEADDIM
    for p in range(heads // 2):
        at = slice(p * LANES, (p + 1) * LANES)
        pre = convolved(taps(ext, masks, at), weight_ref, at)
        x2 = pre * jax.nn.sigmoid(pre)
        u2 = x2 * pair_of(lo, dt, p)
        ub = u2.astype(BF)
        total = dot(cm, carry[:, at].astype(BF)) * pair_of(lo, keep, p) + skip_ref[:, at] * x2
        inner = []
        for h in (2 * p, 2 * p + 1):
            decay = jnp.exp(jnp.minimum(cum[:, h : h + 1] - cumr[h : h + 1, :], 0.0))
            inner.append(dot((decay * mixing).astype(BF), ub))
        y_ref[:, at] = total + jnp.where(lo, inner[0], inner[1])
        to_end_u[:, at] = (u2 * pair_of(lo, to_end, p)).astype(BF)
    fresh = dot(bm, to_end_u[...], ((0,), (0,)))
    lo_row = lax.broadcasted_iota(jnp.int32, (1, LANES), 1) < HEADDIM
    for p in range(heads // 2):
        at = slice(p * LANES, (p + 1) * LANES)
        factor = pair_of(lo_row, keep[SPAN - 1 : SPAN, :], p)
        carry[:, at] = factor * carry[:, at] + fresh[:, at]


def split_dot(value, ones):
    high = value.astype(BF)
    low = (value - high.astype(F32)).astype(BF)
    return dot(high, ones) + dot(low, ones)


def backward_kernel(
    heads,
    segp_ref,
    segc_ref,
    segr_ref,
    mask_ref,
    in_a_ref,
    in_b_ref,
    halo_ref,
    weight_ref,
    b_ref,
    c_ref,
    dt_ref,
    rate_ref,
    skip_ref,
    y_ref,
    prior_ref,
    dy_ref,
    din_ref,
    dbc_ref,
    ddt_ref,
    drate_ref,
    dsum_ref,
    dcarry,
    after_state,
    keep_dy,
    to_end_u,
    slopes,
    along,
    ext,
    dext,
):
    step = pl.program_id(0)
    block = pl.num_programs(0) - 1 - step

    @pl.when(step == 0)
    def _():
        dcarry[...] = jnp.zeros_like(dcarry)
        after_state[...] = jnp.zeros_like(after_state)
        drate_ref[...] = jnp.zeros_like(drate_ref)
        dsum_ref[...] = jnp.zeros_like(dsum_ref)
        dext[SPAN:] = jnp.zeros((HALO, dext.shape[1]), F32)

    ext[0:HALO] = halo_ref[0].astype(F32)
    half = in_b_ref.shape[1]
    ext[HALO:, :half] = in_a_ref[:, :half].astype(F32)
    ext[HALO:, half:] = in_b_ref[...].astype(F32)
    segc, segr = segc_ref[...], segr_ref[...]
    dt = dt_ref[...]
    cum, cumr, keep, to_end = decays(segc, segr, segp_ref[block], dt, rate_ref[...])
    bm, cm = b_ref[...], c_ref[...]
    allowed = tri(False) & (segc == segr)
    mixing = jnp.where(allowed, dot(bm, cm, ((1,), (1,))), 0.0)
    masks = spread_columns(mask_ref, 0, CONV - 1)
    moved = spread_columns(mask_ref, CONV - 1, CONV - 1)
    lo = lax.broadcasted_iota(jnp.int32, (SPAN, LANES), 1) < HEADDIM
    dmixing = jnp.zeros((SPAN, SPAN), F32)
    for p in range(heads // 2):
        at = slice(p * LANES, (p + 1) * LANES)
        terms = taps(ext, masks, at)
        pre = convolved(terms, weight_ref, at)
        sig = jax.nn.sigmoid(pre)
        x2 = pre * sig
        dt2 = pair_of(lo, dt, p)
        u2 = x2 * dt2
        dyb = dy_ref[:, at]
        dy2 = dyb.astype(F32)
        skip = skip_ref[:, at]
        te2 = pair_of(lo, to_end, p)
        u_sides = (jnp.where(lo, u2, 0.0).astype(BF), jnp.where(lo, 0.0, u2).astype(BF))
        du = te2 * dot(bm, dcarry[:, at].astype(BF))
        inner = []
        for k in range(2):
            h = 2 * p + k
            decay = jnp.exp(jnp.minimum(cumr[h : h + 1, :] - cum[:, h : h + 1], 0.0))
            inner.append(dot((decay * mixing).astype(BF), dyb))
            dmixing = dmixing + decay * dot(u_sides[k], dyb, ((1,), (1,)))
        du = du + jnp.where(lo, inner[0], inner[1])
        keep_dy[:, at] = (pair_of(lo, keep, p) * dy2).astype(BF)
        to_end_u[:, at] = (te2 * u2).astype(BF)
        slopes[:, at] = dy2 * (y_ref[:, at] - skip * x2) - u2.astype(BF).astype(F32) * du
        along[:, at] = x2 * du
        dpre = (dt2 * du + skip * dy2) * (sig * (1.0 + pre * (1.0 - sig)))
        dext[0:SPAN, at] = dpre
        for k in range(CONV):
            dsum_ref[k : k + 1, at] += jnp.sum(dpre * terms[k], axis=0, keepdims=True)
        dsum_ref[CONV : CONV + 1, at] += jnp.sum(dpre, axis=0, keepdims=True)
        dsum_ref[CONV + 1 : CONV + 2, at] += jnp.sum(dy2 * x2, axis=0, keepdims=True)
        din = dpre * weight_ref[CONV - 1 : CONV, at]
        for k in range(CONV - 1):
            later = dext[pl.ds(CONV - 1 - k, SPAN), at]
            din = din + later * moved[k] * weight_ref[k : k + 1, at]
        din_ref[:, at] = din.astype(BF)
    dext[SPAN:] = dext[0:HALO]
    dmixing = jnp.where(allowed, dmixing, 0.0).astype(BF)
    dstate = dcarry[...].astype(BF)
    prior = prior_ref[0]
    dbc_ref[:, :STATE] = dot(dmixing, cm) + dot(to_end_u[...], dstate, ((1,), (1,)))
    dbc_ref[:, STATE:] = dot(dmixing, bm, ((0,), (0,))) + dot(
        keep_dy[...], prior.astype(BF), ((1,), (1,))
    )
    width = heads * HEADDIM
    ones = (
        lax.broadcasted_iota(jnp.int32, (width, LANES), 0) // HEADDIM
        == lax.broadcasted_iota(jnp.int32, (width, LANES), 1)
    ).astype(BF)
    at_end = jnp.sum(dcarry[...] * after_state[...], axis=0, keepdims=True)
    at_end = split_dot(jnp.broadcast_to(at_end, (16, width)), ones)[:1]
    dcum = split_dot(slopes[...], ones)
    da = dot(tri(False).astype(F32), dcum, precision=HIGH) + at_end
    ddt_ref[...] = rate_ref[...] * da + split_dot(along[...], ones)
    drate_ref[...] += jnp.sum(dt * da, axis=0, keepdims=True)
    fresh = dot(cm, keep_dy[...], ((0,), (0,)))
    lo_row = lax.broadcasted_iota(jnp.int32, (1, LANES), 1) < HEADDIM
    for p in range(heads // 2):
        at = slice(p * LANES, (p + 1) * LANES)
        factor = pair_of(lo_row, keep[SPAN - 1 : SPAN, :], p)
        dcarry[:, at] = factor * dcarry[:, at] + fresh[:, at]
    after_state[...] = prior


def scan_specs(heads, at, in_widths):
    width = heads * HEADDIM

    def rows(n):
        return pl.BlockSpec((SPAN, n), lambda i: (at(i), 0))

    def whole(*shape):
        return pl.BlockSpec(shape, lambda i: (0,) * len(shape))

    ins = [
        pl.BlockSpec(memory_space=pltpu.SMEM),
        rows(1),
        pl.BlockSpec((1, SPAN), lambda i: (0, at(i))),
        rows(LANES),
        rows(in_widths[0]),
        rows(in_widths[1]),
        pl.BlockSpec((1, HALO, width), lambda i: (at(i), 0, 0)),
        whole(8, width),
        rows(STATE),
        rows(STATE),
        rows(LANES),
        whole(1, LANES),
        whole(1, width),
    ]
    prior = pl.BlockSpec((1, STATE, width), lambda i: (at(i), 0, 0))
    return rows, whole, ins, prior


def scan_forward(heads, blocks, operands):
    rows, whole, ins, prior = scan_specs(heads, lambda i: i, [operands[n].shape[1] for n in (4, 5)])
    width = heads * HEADDIM
    return call(
        functools.partial(forward_kernel, heads),
        grid=(blocks,),
        in_specs=ins,
        out_specs=[rows(width), prior],
        out_shape=[
            jax.ShapeDtypeStruct((blocks * SPAN, width), F32),
            jax.ShapeDtypeStruct((blocks, STATE, width), F32),
        ],
        scratch_shapes=[
            pltpu.VMEM((STATE, width), F32),
            pltpu.VMEM((SPAN, width), BF),
            pltpu.VMEM((HALO + SPAN, width), F32),
        ],
        name="scan_forward",
    )(*operands)


def scan_backward(heads, blocks, operands, y, priors, dy):
    rows, whole, ins, prior = scan_specs(
        heads, lambda i: blocks - 1 - i, [operands[n].shape[1] for n in (4, 5)]
    )
    width = heads * HEADDIM
    return call(
        functools.partial(backward_kernel, heads),
        grid=(blocks,),
        in_specs=ins + [rows(width), prior, rows(width)],
        out_specs=[rows(width), rows(2 * STATE), rows(LANES), whole(1, LANES), whole(8, width)],
        out_shape=[
            jax.ShapeDtypeStruct((blocks * SPAN, width), BF),
            jax.ShapeDtypeStruct((blocks * SPAN, 2 * STATE), F32),
            jax.ShapeDtypeStruct((blocks * SPAN, LANES), F32),
            jax.ShapeDtypeStruct((1, LANES), F32),
            jax.ShapeDtypeStruct((8, width), F32),
        ],
        scratch_shapes=[
            pltpu.VMEM((STATE, width), F32),
            pltpu.VMEM((STATE, width), F32),
            pltpu.VMEM((SPAN, width), BF),
            pltpu.VMEM((SPAN, width), BF),
            pltpu.VMEM((SPAN, width), F32),
            pltpu.VMEM((SPAN, width), F32),
            pltpu.VMEM((HALO + SPAN, width), F32),
            pltpu.VMEM((SPAN + HALO, width), F32),
        ],
        name="scan_backward",
    )(*operands, y, priors, dy)


def as_columns(rows):
    few, tokens = rows.shape
    return jnp.concatenate([rows, jnp.zeros((LANES - few, tokens), F32)]).T


def level_block(pieces, spot):
    piece, lead = spot
    return pieces[piece][lead + (slice(None), slice(None))].astype(F32)


def upper_kernel(where, plan, nd, tok, ns, here_ref, range_ref, count_ref, ratio_ref, q_turned, *refs):
    count = 3 + 2 * LEVELS
    pieces, outs = refs[:count], refs[count:]
    upper_ref, grad_refs, coefs = outs[0], outs[1 : 2 * nd], outs[2 * nd]

    @pl.when(pl.program_id(0) == 0)
    def _():
        rows = [count_ref[j, w] * ratio_ref[w : w + 1, :] for j in range(len(plan)) for w in range(LEVELS)]
        coefs[...] = as_columns(jnp.concatenate(rows))

    for k in range(ns):
        at = here_ref[0] ^ k
        rows = pl.ds(pl.multiple_of(at * tok, tok), tok)
        levels = [level_block(pieces, where[w][k]) for w in range(LEVELS)]
        for j in range(len(plan)):
            total = None
            for w in plan[j]:
                n = j * LEVELS + w
                term = coefs[rows, n : n + 1] * levels[w]
                total = term if total is None else total + term
            upper_ref[j, rows, :] = total.astype(BF)
    count = q_turned.shape[0] // nd
    for k in range(nd):
        index = here_ref[1] ^ k
        rows = pl.ds(pl.multiple_of(index * count, count), count)
        value = dot(q_turned[rows, :], upper_ref[range_ref[index]]).astype(BF)
        if k:
            grad_refs[2 * k - 1][...] = value[: count // 2]
            grad_refs[2 * k][...] = value[count // 2 :]
        else:
            grad_refs[0][...] = value


def products_kernel(where, plan, lanes, tok, ns, nd, here_ref, count_ref, q_ref, *refs):
    count = 3 + 2 * LEVELS
    held_ref, pieces, outs = refs[0], refs[1 : 1 + count], refs[1 + count :]
    prod_refs, inner_ref, w_ref, sums = outs[:ns], outs[ns], outs[ns + 1], outs[ns + 2]
    step = pl.program_id(0)
    rows_of = w_ref.shape[0] // nd
    for k in range(nd):
        at = pl.multiple_of((here_ref[1] ^ k) * rows_of, rows_of)
        w_ref[pl.ds(at, rows_of), :] = held_ref[:, k].reshape(rows_of, w_ref.shape[1])

    @pl.when(step == 0)
    def _():
        sums[...] = jnp.zeros_like(sums)

    for k in range(ns):
        at = here_ref[0] ^ k
        rows = pl.ds(pl.multiple_of(at * tok, tok), tok)
        values = [dot(q_ref[rows, a:b], w_ref[a:b, :]) for a, b in lanes]
        for j, value in enumerate(values):
            prod_refs[k][j] = value.astype(BF)
        for w in range(LEVELS):
            total = None
            for j in range(len(lanes)):
                if w in plan[j]:
                    term = values[j] * count_ref[j, w]
                    total = term if total is None else total + term
            part = total * level_block(pieces, where[w][k])
            folded = part[:, :LANES]
            for c in range(LANES, part.shape[1], LANES):
                folded = folded + part[:, c : c + LANES]
            sums[w, rows, :] += folded

    @pl.when(step == pl.num_programs(0) - 1)
    def _():
        lane = lax.broadcasted_iota(jnp.int32, sums.shape[1:], 1)
        total = jnp.zeros(sums.shape[1:], F32)
        for w in range(LEVELS):
            total = jnp.where(lane == w, jnp.sum(sums[w], axis=1, keepdims=True), total)
        inner_ref[...] = total.T[:LEVELS]


def gate_kernel(
    starts, wide, count_ref, upper_ref, w_ref, y_ref, z_ref, gain_ref, ratio_ref, mean_ref, dy_ref, dz_ref, grad_ref, coefs
):
    step = pl.program_id(0)

    @pl.when(step == 0)
    def _():
        cubes = ratio_ref[...] * ratio_ref[...] * ratio_ref[...] * mean_ref[...]
        rows = []
        for j in range(len(starts)):
            total = cubes[0:1] * count_ref[j, 0]
            for w in range(1, LEVELS):
                total = total + cubes[w : w + 1] * count_ref[j, w]
            rows.append(total)
        columns = as_columns(jnp.concatenate(rows))
        for j in range(len(starts)):
            coefs[j] = jnp.broadcast_to(columns[:, j : j + 1], coefs.shape[1:])

    grad_all = dot(upper_ref[0], w_ref[...], ((1,), (1,)))
    coef = coefs[tile_range(starts, wide, step)]
    for c in range(0, wide, LANES):
        at = slice(c, c + LANES)
        grad_t = grad_all[:, at]
        z = z_ref[:, at].astype(F32)
        sig = jax.nn.sigmoid(z)
        act = z * sig
        y = y_ref[:, at]
        q = y * act
        dq = gain_ref[:, at] * grad_t - q * coef
        dy_ref[:, at] = (dq * act).astype(BF)
        dz_ref[:, at] = (dq * y * (sig * (1.0 + z * (1.0 - sig)))).astype(BF)
        grad_ref[0:1, at] = jnp.sum(q * grad_t, axis=0, keepdims=True)


def tile_range(starts, wide, step):
    index = 0
    for start in starts[1:]:
        index = index + jnp.where(step * wide >= start, 1, 0)
    return index


def mixed_kernel(plan, split, ns, tok, here_ref, count_ref, ratio_ref, x_ref, *refs):
    shares, out_ref = refs[:-1], refs[-1]
    at = pl.ds(pl.multiple_of(here_ref[0] * tok, tok), tok)
    ratios = as_columns(ratio_ref[:, at])
    x = x_ref[...].astype(F32)
    for w in range(LEVELS):
        total = None
        for k in range(ns):
            for j in plan[w]:
                at = (k, j) if k < 3 or j < split else (k + 1, j - split)
                term = shares[at[0]][at[1]].astype(F32) * count_ref[k, j * LEVELS + w]
                total = term if total is None else total + term
        out_ref[w] = (x + ratios[:, w : w + 1] * total).astype(BF)


def dp_terms(others):
    return [swapped(other, "dp", k + 1) for k, other in enumerate(others)]


def over_seq(value):
    dense = value.reshape(-1, LANES)
    total = dense
    for k in range(1, lax.axis_size("seq")):
        total = total + swapped(dense, "seq", k)
    return total.reshape(value.shape)


def fsdp_half(own, got):
    nf = lax.axis_size("fsdp")
    f = lax.axis_index("fsdp")

    def part(offset):
        total = picked(own, f ^ offset).astype(F32)
        for other in got:
            total = total + picked(other, f ^ offset).astype(F32)
        return total.astype(BF)

    kept = jnp.stack([part(e) for e in range(0, nf, 2)])
    sent = jnp.stack([part(e ^ 1) for e in range(0, nf, 2)])
    return kept, sent


def fsdp_rest(kept, got):
    k = 2
    while k < lax.axis_size("fsdp"):
        total = (kept.astype(F32) + got.astype(F32)).astype(BF)
        kept, sent = total[::2], total[1::2]
        got = swapped(sent, "fsdp", k)
        k *= 2
    return kept[0], got[0]


def shards(
    tokens,
    lengths,
    norm_gain,
    w_in,
    w_dt,
    conv_w,
    conv_b,
    dt_bias,
    a_log,
    skip,
    gate_gain,
    w_out,
    cotangent,
):
    nd, ns, nf = lax.axis_size("dp"), lax.axis_size("seq"), lax.axis_size("fsdp")
    d, s, f = lax.axis_index("dp"), lax.axis_index("seq"), lax.axis_index("fsdp")
    tok = tokens.shape[1]
    length = ns * tok
    blocks = length // SPAN
    heads = HEADS // ns
    run = heads // nd
    width = heads * HEADDIM
    own_bc = 2 * STATE // ns
    used = width + own_bc
    cols = -(-(used + heads) // LANES) * LANES
    rows_in = w_in.shape[0]
    reach = CONV - 1

    levels = np.array(
        [[level_of(dd * (HEADS // nd) + ss * run + i) for dd in range(nd) for i in range(run)] for ss in range(ns)]
    )
    cuts = [0] + [h for h in range(1, heads) if (levels[:, h] != levels[:, h - 1]).any()] + [heads]
    ranges = [(a, b) for a, b in zip(cuts, cuts[1:])]
    range_level = np.array([[levels[ss, a] for a, _ in ranges] for ss in range(ns)])
    counts = (range_level[:, :, None] <= np.arange(LEVELS)[None, None, :]).astype(np.float32)
    counted = picked(jnp.asarray(counts), s)
    theirs = picked(
        jnp.asarray(np.stack([[counts[i ^ k].reshape(-1) for k in range(ns)] for i in range(ns)])), s
    )
    lowest = [int(range_level[ss].min()) for ss in range(ns)]

    def by_head(vector):
        lead = vector.shape[:-1]
        per = vector.shape[-1] // HEADS
        cut = vector.reshape(lead + (nd, ns, run * per))
        mine = lax.dynamic_index_in_dim(cut, s, len(lead) + 1, keepdims=False)
        return mine.reshape(lead + (heads * per,))

    def for_groups(matrix):
        per = matrix.shape[1] // HEADS
        cut = matrix.reshape(matrix.shape[0], nd, ns, run * per)
        return jnp.transpose(cut, (2, 0, 1, 3)).reshape(ns, matrix.shape[0], heads * per)

    def from_groups(stack):
        per = stack.shape[2] // heads
        cut = stack.reshape(ns, stack.shape[1], nd, run * per)
        return jnp.transpose(cut, (1, 2, 0, 3)).reshape(stack.shape[1], HEADS * per)

    pad_cols = cols - used - heads
    half = width // 2
    first = half + cols - width
    group_x = for_groups(w_in[:, INNER : 2 * INNER])
    stack = jnp.concatenate(
        [
            group_x[:, :, :half],
            w_in[:, 2 * INNER :].reshape(rows_in, ns, own_bc).transpose(1, 0, 2),
            for_groups(w_dt),
            jnp.zeros((ns, rows_in, pad_cols), BF),
            group_x[:, :, half:],
            for_groups(w_in[:, :INNER]),
        ],
        axis=2,
    )
    own_x = tokens[0].astype(F32)
    scale = lax.rsqrt(jnp.mean(own_x * own_x, axis=-1, keepdims=True) + EPS)
    xn_own = (own_x * scale * norm_gain).astype(BF)
    xn_across = swapped(xn_own, "seq", 2)
    xn_pieces = [xn_own, swapped(xn_own, "seq", 1), xn_across, swapped(xn_across, "seq", 1)]
    arrived = [picked(stack, s)] + [swapped(picked(stack, s ^ k), "seq", k) for k in range(1, ns)]
    mine = filled((ns, rows_in, stack.shape[2]), [(p, None, (s ^ k, None, None)) for k, p in enumerate(arrived)])
    mine_z = mine[:, :, cols:]

    def needed(at, level):
        return min(lowest[at], lowest[at ^ 1]) <= level

    halves = [cotangent[w : w + 2, 0] for w in range(0, LEVELS, 2)]
    singles = [cotangent[w, 0] for w in range(LEVELS)]

    def beside(level, *others):
        block = after(halves[level // 2], *others)
        return swapped(block, "seq", 1, lambda i, j: needed(j, level + 1))

    def across(level, *others):
        block = after(singles[level], *others)
        return swapped(block, "seq", 2, lambda i, j: needed(j, level))

    def far(level, block):
        return swapped(block, "seq", 1, lambda i, j: needed(j, level))

    positions = jnp.arange(length, dtype=jnp.int32)
    ends = jnp.cumsum(lengths[0])[:-1]
    seg = jnp.sum((positions[:, None] >= ends[None, :]).astype(jnp.int32), axis=1)
    seg_before = jnp.concatenate([jnp.full((1,), -1, jnp.int32), seg[SPAN - 1 : length - 1 : SPAN]])
    seg_pad = jnp.concatenate([jnp.full((reach,), -1, jnp.int32), seg])
    masks = [(seg_pad[k : k + length] == seg) for k in range(reach)]
    mask_cols = [m.astype(F32) for m in masks]
    mask_cols += [jnp.pad(m, (0, reach - k))[reach - k :] for k, m in enumerate(mask_cols)]
    mask_cols = jnp.pad(jnp.stack(mask_cols, axis=1), ((0, 0), (0, LANES - 2 * reach)))

    def conv_params(s_part, bc_part):
        return by_head(s_part), bc_part

    weight_s = jnp.concatenate(
        [by_head(conv_w[:, :INNER]), by_head(conv_b[None, :INNER]), jnp.zeros((3, width), F32)]
    )
    weight_r = jnp.pad(
        lax.dynamic_slice_in_dim(conv_w, INNER + s * own_bc, own_bc, 1), ((0, 0), (0, cols - used))
    )
    bias_r = jnp.pad(
        lax.dynamic_slice_in_dim(conv_b, INNER + s * own_bc, own_bc, 0), (0, cols - used)
    )
    bias = by_head(dt_bias)
    rate = -jnp.exp(by_head(a_log))
    skip_own = by_head(skip)
    gain = by_head(gate_gain)

    def over_fsdp(chunk):
        return lax.all_gather(chunk, "fsdp", axis=0, tiled=False)

    def over_dp(held):
        return [held] + [swapped(held, "dp", j) for j in range(1, nd)]

    def whole(pieces, columns):
        moves = [
            (piece, i, (d ^ j, None, i, None, None)) for j, piece in enumerate(pieces) for i in range(nf)
        ]
        return filled((nd, ns, nf, rows_in, columns), moves).reshape(D, columns)

    held_a = over_fsdp(mine[:, :, :first])
    held_b = over_fsdp(mine[:, :, first:cols])
    other_out = [swapped(w_out, "dp", j) for j in range(1, nd)]
    held_a, other_out = together(held_a, other_out)
    small_ones = (seg, seg_before, mask_cols, weight_s, weight_r, bias_r, bias, rate, skip_own, gain, theirs)
    held_a, small_ones, halves, singles = together(held_a, small_ones, halves, singles)
    seg, seg_before, mask_cols, weight_s, weight_r, bias_r, bias, rate, skip_own, gain, theirs = small_ones
    near_high, near_low = beside(2, held_a), beside(0, held_a)
    chip3 = across(3, held_a)
    pieces_a = over_dp(held_a)
    held_b, pieces_a, chip3, near_high, xn_pieces = together(
        held_b, pieces_a, chip3, near_high, xn_pieces
    )
    xn = filled((ns, tok, D), [(p, None, (s ^ k, None, None)) for k, p in enumerate(xn_pieces)])
    xn = xn.reshape(length, D)

    far3 = far(3, chip3)
    pieces_b = over_dp(held_b)
    held_z = over_fsdp(after(mine_z, held_a))
    held_out = over_fsdp(after(jnp.stack([w_out] + other_out), held_z))

    xn_turned = xn.T
    here = jnp.stack([s, d]).astype(jnp.int32)
    full_a = whole(pieces_a, first)
    proj_a = dot(xn, full_a).astype(BF)

    proj_r = proj_a[:, half:]
    mixer = jnp.concatenate([jnp.zeros((reach, cols - width), BF), proj_r], axis=0)

    def taken(k):
        rows = mixer[k : k + length].astype(F32)
        return rows * mask_cols[:, k : k + 1] if k < reach else rows

    pre_r = bias_r
    for k in range(CONV):
        pre_r = pre_r + taken(k) * weight_r[k]
    bc_own = jax.nn.silu(pre_r).astype(BF)[:, :own_bc]
    bc_across = swapped(bc_own, "seq", 2)
    bc = [bc_own, swapped(bc_own, "seq", 1), bc_across, swapped(bc_across, "seq", 1)]
    chip2, chip1 = across(2, bc[2]), across(1, bc[2])
    full_b = whole(pieces_b, half)
    proj_b = dot(xn, after(full_b, proj_a, xn_turned, bc[2])).astype(BF)
    proj_b, far3, near_low, held_z = together(proj_b, far3, near_low, held_z)
    pieces_z = over_dp(held_z)
    bc = reordered_by_xor(bc, s)
    b_in = jnp.concatenate(bc[: ns // 2], axis=1)
    c_out = jnp.concatenate(bc[ns // 2 :], axis=1)

    def padded(rows):
        return jnp.pad(rows, ((0, 0), (0, LANES - rows.shape[1])))

    pre_dt = proj_r[:, own_bc : own_bc + heads].astype(F32) + bias
    steps = jax.nn.softplus(pre_dt)
    tails = [
        p.reshape(blocks, SPAN, p.shape[1])[: blocks - 1, SPAN - HALO :, :half] for p in (proj_a, proj_b)
    ]
    operands = (
        seg_before,
        seg[:, None],
        seg[None, :],
        mask_cols,
        proj_a,
        proj_b,
        jnp.concatenate([jnp.zeros((1, HALO, width), BF), jnp.concatenate(tails, axis=2)]),
        weight_s,
        b_in,
        c_out,
        padded(steps),
        padded(rate[None, :]),
        jnp.repeat(skip_own, HEADDIM)[None, :],
    )
    y, priors = scan_forward(heads, blocks, operands)
    y, chip2 = together(y, chip2)
    far2, chip0 = far(2, chip2), across(0, y)
    parts = pieces_z if rows_in % 16 == 0 else [whole(pieces_z, width)]
    lanes = [(a * HEADDIM, b * HEADDIM) for a, b in ranges]
    starts = [a for a, _ in lanes]
    wide = min(min(b - a for a, b in lanes), TILE)
    proj_z, full_z, q_gain, q_turned, squares = gated_projection(
        here, xn, parts, nd, width, y, gain[None], starts, wide
    )
    squares, chip1 = together(squares[: len(lanes)], chip1)
    far1 = far(1, chip1)
    widths = np.array([[(HEADS >> 3 - w) * HEADDIM] for w in range(LEVELS)], np.float32)
    per_level = jnp.sum(counted[:, :, None] * squares[:, None, :], axis=0)
    ratio, chip0 = together(lax.rsqrt(over_seq(per_level) / widths + EPS), chip0)
    far0 = far(0, chip0)

    plan = [[w for w in range(LEVELS) if range_level[:, j].min() <= w] for j in range(len(lanes))]
    out_rows = width // nd
    range_of = [next(j for j, (a, b) in enumerate(lanes) if a <= i * out_rows < b) for i in range(nd)]
    smem = pl.BlockSpec(memory_space=pltpu.SMEM)
    cot_pieces = [cotangent, near_low, near_high, chip0, chip1, chip2, chip3, far0, far1, far2, far3]
    cot_specs = [pl.BlockSpec((LEVELS, 1, tok, WIDE), lambda i: (0, 0, 0, i))]
    cot_specs += [pl.BlockSpec((2, tok, WIDE), lambda i: (0, 0, i))] * 2
    cot_specs += [pl.BlockSpec((tok, WIDE), lambda i: (0, i))] * (2 * LEVELS)
    where = [[(0, (w, 0)), (1 + w // 2, (w % 2,)), (3 + w, ()), (3 + LEVELS + w, ())] for w in range(LEVELS)]
    upper, *grad_out = call(
        functools.partial(upper_kernel, where, plan, nd, tok, ns),
        grid=(D // WIDE,),
        in_specs=[
            smem,
            smem,
            smem,
            pl.BlockSpec((LEVELS, length), lambda i: (0, 0)),
            pl.BlockSpec((width, length), lambda i: (0, 0)),
        ]
        + cot_specs,
        out_specs=[pl.BlockSpec((len(lanes), length, WIDE), lambda i: (0, 0, i))]
        + [pl.BlockSpec((out_rows, WIDE), lambda i: (0, i))]
        + [pl.BlockSpec((out_rows // 2, WIDE), lambda i: (0, i))] * (2 * nd - 2),
        out_shape=[jax.ShapeDtypeStruct((len(lanes), length, D), BF)]
        + [jax.ShapeDtypeStruct((out_rows, D), BF)]
        + [jax.ShapeDtypeStruct((out_rows // 2, D), BF)] * (2 * nd - 2),
        scratch_shapes=[pltpu.VMEM((length, LANES), F32)],
        name="upper",
    )(here, jnp.asarray(range_of, jnp.int32), counted, ratio, q_turned, *cot_pieces)
    out_first, out_second = dp_terms(grad_out[1::2]), dp_terms(grad_out[2::2])

    held_out, upper = together(held_out, upper)
    *shares, inner, full_out = call(
        functools.partial(products_kernel, where, plan, lanes, tok, ns, nd),
        grid=(D // WIDE,),
        in_specs=[
            smem,
            smem,
            pl.BlockSpec((length, width), lambda i: (0, 0)),
        ]
        + [pl.BlockSpec((nf, nd, w_out.shape[0], WIDE), lambda i: (0, 0, 0, i))]
        + cot_specs,
        out_specs=[pl.BlockSpec((len(lanes), tok, WIDE), lambda i: (0, 0, i))] * ns
        + [pl.BlockSpec((LEVELS, length), lambda i: (0, 0))]
        + [pl.BlockSpec((width, WIDE), lambda i: (0, i))],
        out_shape=[jax.ShapeDtypeStruct((len(lanes), tok, D), BF)] * ns
        + [jax.ShapeDtypeStruct((LEVELS, length), F32)]
        + [jax.ShapeDtypeStruct((width, D), BF)],
        scratch_shapes=[pltpu.VMEM((LEVELS, length, LANES), F32)],
        name="products",
    )(here, counted, q_gain, held_out, *cot_pieces)
    means, out_first = together(over_seq(inner) / widths, out_first)
    shares[1:3] = [swapped(after(shares[k], means), "seq", k) for k in (1, 2)]
    split = (len(lanes) + 1) // 2
    third = [swapped(after(shares[3][:split], shares[1]), "seq", 3), shares[3][split:]]

    cols_of = pl.BlockSpec((length, wide), lambda i: (0, i))
    scalars = pl.BlockSpec((LEVELS, length), lambda i: (0, 0))
    dy, dz, grad_gate = call(
        functools.partial(gate_kernel, starts, wide),
        grid=(width // wide,),
        in_specs=[
            smem,
            pl.BlockSpec((1, length, D), lambda i: (tile_range(starts, wide, i), 0, 0)),
            pl.BlockSpec((wide, D), lambda i: (i, 0)),
            cols_of,
            cols_of,
            pl.BlockSpec((1, wide), lambda i: (0, i)),
            scalars,
            scalars,
        ],
        out_specs=[cols_of, cols_of, pl.BlockSpec((8, wide), lambda i: (0, i))],
        out_shape=[
            jax.ShapeDtypeStruct((length, width), BF),
            jax.ShapeDtypeStruct((length, width), BF),
            jax.ShapeDtypeStruct((8, width), F32),
        ],
        scratch_shapes=[pltpu.VMEM((len(lanes), length, LANES), F32)],
        name="gate_backward",
    )(counted, upper, full_out, y, proj_z, gain[None], ratio, means)
    grad_gate = grad_gate[0]

    def in_terms(dproj, at, first=0, columns=None):
        columns = columns or dproj.shape[1]
        out = row_terms(xn_turned, dproj, at, nd, ns, nf, first, columns)
        return out.reshape(nf, ns * rows_in, columns)

    z_other = [in_terms(dz, d ^ k) for k in range(1, nd)]
    z_got = dp_terms(z_other)
    dy, out_second, shares[1] = together(after(dy, *z_other), out_second, shares[1])
    chunk = (nf, out_rows // nf, D)
    out_got = [jnp.concatenate([u, v]).reshape(chunk) for u, v in zip(out_first, out_second)]
    out_kept, out_sent = fsdp_half(grad_out[0].reshape(chunk), out_got)
    dy = after(dy, out_sent)
    out_half = swapped(out_sent, "fsdp", 1)

    dproj_s, dbc, ddt, drate, dsum = scan_backward(heads, blocks, operands, y, priors, dy)
    dproj_s, dbc, out_half, shares[2], third = together(dproj_s, dbc, out_half, shares[2], third)
    out_pair = fsdp_rest(out_kept, out_half)

    dbc = dbc.astype(BF)
    slices = reordered_by_xor([dbc[:, j * own_bc : (j + 1) * own_bc] for j in range(ns)], s)
    beside_bc = swapped(jnp.concatenate([slices[1], slices[3]], axis=1), "seq", 1)
    sum_bc = jnp.concatenate([slices[0], slices[2]], axis=1).astype(F32) + beside_bc.astype(F32)
    across_bc = swapped(sum_bc[:, own_bc:].astype(BF), "seq", 2)

    z_own = in_terms(after(dz, dproj_s), d)
    z_own, z_got = together(z_own, z_got)
    z_kept, z_sent = fsdp_half(z_own, z_got)
    z_half = swapped(z_sent, "fsdp", 1)
    late_s = after(dproj_s, z_sent)
    left_other = [in_terms(late_s, d ^ k, 0, half) for k in range(1, nd)]
    left_got = dp_terms(left_other)
    third[1] = swapped(after(third[1], across_bc), "seq", 3)
    dbc_own = sum_bc[:, :own_bc] + across_bc.astype(F32)
    dproj_r, small_sums = small_back(
        own_bc,
        pre_r,
        padded(after(dbc_own, *left_other)),
        proj_r,
        mask_cols,
        weight_r,
        ddt,
        padded(pre_dt),
    )

    dxn = input_grad(dz, dproj_s, dproj_r, full_z, full_a, full_b, ns, tok)
    pair = swapped(jnp.stack([picked(dxn, s ^ 1), picked(dxn, s ^ 3)]), "seq", 1)

    late_s, late_r = together(dproj_s, after(dproj_r, dxn))
    right_other = [
        jnp.concatenate([in_terms(late_s, d ^ k, half, half), in_terms(late_r, d ^ k)], axis=2)
        for k in range(1, nd)
    ]
    right_other, z_half, left_got, out_pair = together(right_other, z_half, left_got, out_pair)
    right_got = dp_terms(right_other)
    z_pair = fsdp_rest(z_kept, z_half)
    own_s = in_terms(after(dproj_s, *right_other), d)
    left_kept, left_sent = fsdp_half(own_s[:, :, :half], left_got)
    left_half = swapped(left_sent, "fsdp", 1)
    own_r = in_terms(after(dproj_r, left_sent), d)
    flat = flattened(
        [
            jnp.concatenate([dsum[:CONV], small_sums[:CONV, :own_bc]], axis=1).reshape(-1),
            dsum[CONV],
            small_sums[CONV, :own_bc],
            grad_gate,
            small_sums[CONV + 1, :heads],
            drate[0, :heads] * rate,
            jnp.sum(dsum[CONV + 1].reshape(heads, HEADDIM), axis=1),
        ]
    )
    near = picked(dxn, s).astype(F32) + pair[0].astype(F32)
    far_sum = (picked(dxn, s ^ 2).astype(F32) + pair[1].astype(F32)).astype(BF)
    dxn_across = swapped(far_sum, "seq", 2)
    right_got, far_sum, left_half = together(right_got, far_sum, left_half)
    left_pair = fsdp_rest(left_kept, left_half)
    own_right = jnp.concatenate([own_s[:, :, half:], own_r], axis=2)
    right_kept, right_sent = fsdp_half(own_right, right_got)
    right_half = swapped(right_sent, "fsdp", 1)

    mixed = call(
        functools.partial(
            mixed_kernel,
            [[j for j in range(len(lanes)) if range_level[:, j].min() <= w] for w in range(LEVELS)],
            split,
            ns,
            tok,
        ),
        grid=(D // WIDE,),
        in_specs=[
            smem,
            smem,
            pl.BlockSpec((LEVELS, length), lambda i: (0, 0)),
            pl.BlockSpec((tok, WIDE), lambda i: (0, i)),
        ]
        + [pl.BlockSpec((p.shape[0], tok, WIDE), lambda i: (0, 0, i)) for p in shares[:3] + third],
        out_specs=pl.BlockSpec((LEVELS, tok, WIDE), lambda i: (0, 0, i)),
        out_shape=jax.ShapeDtypeStruct((LEVELS, tok, D), BF),
        name="mixed",
    )(here, theirs, ratio, tokens[0], *after(shares[:3] + third, right_sent))[:, None]
    right_half, mixed, dxn_across = together(right_half, mixed, dxn_across)
    right_kept = after(right_kept, mixed)
    right_pair = fsdp_rest(right_kept, right_half)
    dxn_own = near + dxn_across.astype(F32)
    grad_norm = jnp.sum(dxn_own * own_x * scale, axis=0)
    scaled = norm_gain * dxn_own
    dx = scale * scaled - own_x * scale**3 * jnp.mean(own_x * scaled, axis=-1, keepdims=True)
    dx = (dx + jnp.sum(after(cotangent, mixed)[:, 0].astype(F32), axis=0)).astype(BF)
    flat = jnp.concatenate([flat, grad_norm.reshape(-1, LANES)])
    flat = butterfly(flat, "dp")

    def whole_sum(pair):
        total = (pair[0].astype(F32) + pair[1].astype(F32)).astype(BF)
        return total.reshape(ns, rows_in, total.shape[1])

    z_pair, left_pair = together(z_pair, left_pair)
    early = jnp.concatenate([whole_sum(z_pair), whole_sum(left_pair)], axis=2)
    early_got = [picked(early, s)] + [swapped(picked(early, s ^ k), "seq", k) for k in range(1, ns)]
    early_got, right_pair, flat = together(early_got, right_pair, flat)
    flat = butterfly(flat, "fsdp")
    late = whole_sum(right_pair)
    late_got = [picked(late, s)] + [swapped(picked(late, s ^ k), "seq", k) for k in range(1, ns)]
    early = jnp.stack(reordered_by_xor(early_got, s))
    late = jnp.stack(reordered_by_xor(late_got, s))
    got_z = early[:, :, :width]
    got_x = jnp.concatenate([early[:, :, width:], late], axis=2)
    sum_out = out_pair[0].astype(F32) + out_pair[1].astype(F32)


    sum_in = jnp.concatenate(
        [
            from_groups(got_z),
            from_groups(got_x[:, :, :width]),
            jnp.transpose(got_x[:, :, width:used], (1, 0, 2)).reshape(rows_in, 2 * STATE),
        ],
        axis=1,
    ).astype(F32)
    sum_dt = from_groups(got_x[:, :, used : used + heads]).astype(F32)

    sizes = [CONV * used, used, width, heads, heads, heads]
    filling = -sum(sizes) % 1024
    sizes += [filling, D]
    every = seq_gather(flat, s).reshape(ns, -1)
    starts = np.cumsum([0] + sizes)
    pieces = [every[:, a : a + n] for a, n in zip(starts, sizes)]

    def heads_back(rows):
        lead = rows.shape[1:-1]
        cut = rows.reshape((ns,) + lead + (nd, rows.shape[-1] // nd))
        order = tuple(range(1, 1 + len(lead))) + (1 + len(lead), 0, 2 + len(lead))
        return jnp.transpose(cut, order).reshape(lead + (-1,))

    conv_rows = pieces[0].reshape(ns, CONV, used)
    conv_all = jnp.concatenate(
        [
            heads_back(conv_rows[:, :, :width]),
            jnp.transpose(conv_rows[:, :, width:], (1, 0, 2)).reshape(CONV, 2 * STATE),
        ],
        axis=1,
    )
    bias_all = jnp.concatenate([heads_back(pieces[1][:, :width]), pieces[1][:, width:].reshape(-1)])
    return (
        mixed,
        dx[None],
        jnp.sum(pieces[7], axis=0),
        sum_in,
        sum_dt,
        conv_all,
        bias_all,
        heads_back(pieces[3]),
        heads_back(pieces[4]),
        heads_back(pieces[5]),
        heads_back(pieces[2]),
        sum_out,
    )


def solution(mesh):
    rows = P(("dp", "seq", "fsdp"), None)
    held = P(("dp", "fsdp"), "seq", None)
    levels = P(None, ("dp", "fsdp"), "seq", None)
    placed = (held, P(("dp", "fsdp"), None), P(), rows, rows, P(), P(), P(), P(), P(), P(), rows, levels)
    return jax.shard_map(
        shards,
        mesh=mesh,
        in_specs=placed,
        out_specs=(levels, held, P(), rows, rows, P(), P(), P(), P(), P(), P(), rows),
        check_vma=False,
    )
```

```python
import functools

import jax
import jax.numpy as jnp
import numpy as np
from jax import lax
from jax.experimental import pallas as pl
from jax.experimental.pallas import tpu as pltpu
from jax.sharding import PartitionSpec as P

D = 2048
HEADS = 64
HEADDIM = 64
STATE = 128
CONV = 4
SPAN = 128
INNER = 4096
EPS = 1e-05
LEVELS = 4
BF = jnp.bfloat16
F32 = jnp.float32
HIGH = lax.Precision.HIGHEST
LANES = 128
HALO = 16
TILE = 256
WIDE = 512
VMEM_LIMIT = 48 * 1024 * 1024


def dot(a, b, dims=((1,), (0,)), precision=None):
    return lax.dot_general(a, b, (dims, ((), ())), preferred_element_type=F32, precision=precision)


def silu_slope(v):
    sig = jax.nn.sigmoid(v)
    return sig * (1.0 + v * (1.0 - sig))


def level_of(head):
    return 0 if head < 8 else 1 if head < 16 else 2 if head < 32 else 3


def swapped(value, axis, k, keep=None):
    pairs = [(i, i ^ k) for i in range(lax.axis_size(axis))]
    if keep is not None:
        pairs = [p for p in pairs if keep(*p)]
    return lax.ppermute(value, axis, pairs)


def after(value, *others):
    return lax.optimization_barrier((value,) + others)[0]


def together(*values):
    return lax.optimization_barrier(values)


def flattened(vectors):
    flat = jnp.concatenate(vectors)
    return jnp.pad(flat, (0, -flat.shape[0] % 1024)).reshape(-1, LANES)


def butterfly(value, axis):
    k = 1
    while k < lax.axis_size(axis):
        value = value + swapped(value, axis, k)
        k *= 2
    return value


def picked(array, index):
    return lax.dynamic_index_in_dim(array, index, 0, keepdims=False)


def seq_gather(block, here):
    return jnp.stack(reordered_by_xor([block] + [swapped(block, "seq", k) for k in range(1, 4)], here))


def reordered_by_xor(pieces, here):
    k = 1
    while k < len(pieces):
        flip = (here & k) > 0
        pieces = [jnp.where(flip, pieces[j ^ k], piece) for j, piece in enumerate(pieces)]
        k *= 2
    return pieces


def call(kernel, **kwargs):
    return pl.pallas_call(
        kernel,
        compiler_params=pltpu.CompilerParams(vmem_limit_bytes=VMEM_LIMIT),
        cost_estimate=pl.CostEstimate(flops=1, bytes_accessed=1, transcendentals=0),
        **kwargs,
    )


def filled(shape, moves):
    arrays, plan, rows = [], [], []
    block = tuple(size if index is None else 1 for size, index in zip(shape, moves[0][2]))
    for piece, lead, place in moves:
        at = next((i for i, a in enumerate(arrays) if a is piece), len(arrays))
        if at == len(arrays):
            arrays.append(piece)
        plan.append((at, lead))
        rows.append(jnp.stack([jnp.asarray(0 if n is None else n, jnp.int32) for n in place]))

    def kernel(index_ref, *refs):
        pieces, out = refs[:-1], refs[-1]
        for m, (at, lead) in enumerate(plan):

            @pl.when(pl.program_id(0) == m)
            def _():
                value = pieces[at][...] if lead is None else pieces[at][lead]
                out[...] = value.reshape(block)

    return call(
        kernel,
        grid_spec=pltpu.PrefetchScalarGridSpec(
            num_scalar_prefetch=1,
            grid=(len(plan),),
            in_specs=[
                pl.BlockSpec(a.shape, lambda i, t, n=a.ndim: (0,) * n) for a in arrays
            ],
            out_specs=pl.BlockSpec(
                block, lambda i, t: tuple(t[i, n] for n in range(len(shape)))
            ),
        ),
        out_shape=jax.ShapeDtypeStruct(shape, arrays[0].dtype),
        name="filled",
    )(jnp.stack(rows), *arrays)


def terms_kernel(ns, nf, at_ref, left_ref, right_ref, out_ref):
    value = dot(left_ref[...], right_ref[...]).astype(BF)
    rows = value.shape[0] // (ns * nf)
    for i in range(ns):
        for k in range(nf):
            out_ref[k, i] = value[(i * nf + k) * rows : (i * nf + k + 1) * rows]


def row_terms(turned, right, at, nd, ns, nf, first, columns):
    depth = turned.shape[1]
    rows = turned.shape[0] // nd
    wide = TILE if columns % TILE == 0 else LANES
    return call(
        functools.partial(terms_kernel, ns, nf),
        grid_spec=pltpu.PrefetchScalarGridSpec(
            num_scalar_prefetch=1,
            grid=(columns // wide,),
            in_specs=[
                pl.BlockSpec((rows, depth), lambda i, t: (t[0], 0)),
                pl.BlockSpec((depth, wide), lambda i, t: (0, i + first // wide)),
            ],
            out_specs=pl.BlockSpec((nf, ns, rows // (nf * ns), wide), lambda i, t: (0, 0, 0, i)),
        ),
        out_shape=jax.ShapeDtypeStruct((nf, ns, rows // (nf * ns), columns), BF),
        name="row_terms",
    )(at.astype(jnp.int32)[None], turned, right)


def small_back_kernel(
    width, pre_ref, dbc_ref, in_ref, mask_ref, weight_ref, ddt_ref, pre_dt_ref, out_ref, sum_ref, ext, dext
):
    rows = pre_ref.shape[0]
    ext[0:HALO] = jnp.zeros((HALO, LANES), F32)
    ext[HALO:] = in_ref[...].astype(F32)
    pre = pre_ref[...]
    sig = jax.nn.sigmoid(pre)
    dpre = dbc_ref[...] * (sig * (1.0 + pre * (1.0 - sig)))
    dext[0:rows] = dpre
    dext[rows:] = jnp.zeros((HALO, LANES), F32)
    total = dpre * weight_ref[CONV - 1 : CONV, :]
    for k in range(CONV):
        term = ext[pl.ds(HALO - CONV + 1 + k, rows), :]
        if k < CONV - 1:
            term = term * mask_ref[:, k : k + 1]
            later = dext[pl.ds(CONV - 1 - k, rows), :] * mask_ref[:, CONV - 1 + k : CONV + k]
            total = total + later * weight_ref[k : k + 1, :]
        sum_ref[k : k + 1, :] = jnp.sum(dpre * term, axis=0, keepdims=True)
    sum_ref[CONV : CONV + 1, :] = jnp.sum(dpre, axis=0, keepdims=True)
    draw = ddt_ref[...] * jax.nn.sigmoid(pre_dt_ref[...])
    sum_ref[CONV + 1 : CONV + 2, :] = jnp.sum(draw, axis=0, keepdims=True)
    out_ref[...] = (total + pltpu.roll(draw, width, axis=1)).astype(BF)


def small_back(width, pre, dbc, proj, masks, weight, ddt, pre_dt):
    rows = pre.shape[0]
    return call(
        functools.partial(small_back_kernel, width),
        out_shape=[
            jax.ShapeDtypeStruct((rows, LANES), BF),
            jax.ShapeDtypeStruct((8, LANES), F32),
        ],
        scratch_shapes=[pltpu.VMEM((HALO + rows, LANES), F32), pltpu.VMEM((rows + HALO, LANES), F32)],
        name="small_back",
    )(pre, dbc, proj, masks, weight, ddt, pre_dt)


def input_grad_kernel(blocks, dz_ref, ds_ref, dr_ref, wz_ref, wa_ref, wb_ref, out_ref):
    half = wb_ref.shape[1]
    columns = ((1,), (1,))
    total = dot(dz_ref[...], wz_ref[...], columns)
    total = total + dot(ds_ref[:, :half], wa_ref[:, :half], columns)
    total = total + dot(ds_ref[:, half:], wb_ref[...], columns)
    total = total + dot(dr_ref[...], wa_ref[:, half:], columns)
    total = total.astype(BF)
    tok = total.shape[0] // blocks
    for i in range(blocks):
        out_ref[i] = total[i * tok : (i + 1) * tok]


def input_grad(dz, ds, dr, wz, wa, wb, blocks, tok):
    def whole(a):
        return pl.BlockSpec(a.shape, lambda i: (0, 0))

    def rows(a):
        return pl.BlockSpec((TILE, a.shape[1]), lambda i: (i, 0))

    return call(
        functools.partial(input_grad_kernel, blocks),
        grid=(wz.shape[0] // TILE,),
        in_specs=[whole(dz), whole(ds), whole(dr), rows(wz), rows(wa), rows(wb)],
        out_specs=pl.BlockSpec((blocks, tok, TILE), lambda i: (0, 0, i)),
        out_shape=jax.ShapeDtypeStruct((blocks, tok, wz.shape[0]), BF),
        name="input_grad",
    )(dz, ds, dr, wz, wa, wb)


def assembled(here_ref, pieces, nd, full_ref):
    halves = len(pieces) // nd
    nf, ns, rows = pieces[0].shape[:3]
    for n, piece in enumerate(pieces):
        h, j = divmod(n, nd)
        for k in range(nf):
            for i in range(ns):
                block = ((here_ref[1] ^ j) * ns + i) * nf + k
                at = pl.multiple_of((block * halves + h) * rows, rows)
                full_ref[pl.ds(at, rows), :] = piece[k, i]


def gated_kernel(nd, count, starts, wide, here_ref, xn_ref, y_ref, gain_ref, *refs):
    pieces, (out_ref, full_ref, gated_ref, turned_ref, squares_ref, sums) = refs[:count], refs[count:]
    step = pl.program_id(0)

    @pl.when(step == 0)
    def _():
        sums[...] = jnp.zeros_like(sums)

    if nd:
        assembled(here_ref, pieces, nd, full_ref)
    else:
        full_ref[...] = pieces[0][...]
    value = dot(xn_ref[...], full_ref[...]).astype(BF)
    out_ref[...] = value
    where = tile_range(starts, wide, step)
    for c in range(0, wide, LANES):
        at = slice(c, c + LANES)
        z = value[:, at].astype(F32)
        q = y_ref[:, at] * (z * jax.nn.sigmoid(z))
        gated = (q * gain_ref[:, at]).astype(BF)
        gated_ref[:, at] = gated
        turned_ref[at, :] = gated.T
        sums[where] += q * q

    @pl.when(step == pl.num_programs(0) - 1)
    def _():
        lane = lax.broadcasted_iota(jnp.int32, sums.shape[1:], 1)
        total = jnp.zeros(sums.shape[1:], F32)
        for j in range(len(starts)):
            total = jnp.where(lane == j, jnp.sum(sums[j], axis=1, keepdims=True), total)
        squares_ref[...] = total.T[: squares_ref.shape[0]]


def gated_projection(here, xn, pieces, nd, columns, y, gain, starts, wide):
    if pieces[0].ndim == 2:
        nd = 0
    tokens, depth = xn.shape
    tile = pl.BlockSpec((tokens, wide), lambda i: (0, i))
    ins = [
        pl.BlockSpec(memory_space=pltpu.SMEM),
        pl.BlockSpec((tokens, depth), lambda i: (0, 0)),
        tile,
        pl.BlockSpec((1, wide), lambda i: (0, i)),
    ]
    for piece in pieces:
        lead = piece.shape[:-1]
        ins.append(pl.BlockSpec(lead + (wide,), lambda i, n=len(lead): (0,) * n + (i,)))
    return call(
        functools.partial(gated_kernel, nd, len(pieces), starts, wide),
        grid=(columns // wide,),
        in_specs=ins,
        out_specs=[
            tile,
            pl.BlockSpec((depth, wide), lambda i: (0, i)),
            tile,
            pl.BlockSpec((wide, tokens), lambda i: (i, 0)),
            pl.BlockSpec((8, tokens), lambda i: (0, 0)),
        ],
        out_shape=[
            jax.ShapeDtypeStruct((tokens, columns), BF),
            jax.ShapeDtypeStruct((depth, columns), BF),
            jax.ShapeDtypeStruct((tokens, columns), BF),
            jax.ShapeDtypeStruct((columns, tokens), BF),
            jax.ShapeDtypeStruct((8, tokens), F32),
        ],
        scratch_shapes=[pltpu.VMEM((len(starts), tokens, LANES), F32)],
        name="gated",
    )(here, xn, y, gain, *pieces)


def tri(rows_first):
    a = lax.broadcasted_iota(jnp.int32, (SPAN, SPAN), 0)
    b = lax.broadcasted_iota(jnp.int32, (SPAN, SPAN), 1)
    return (a >= b) if rows_first else (a <= b)


def decays(segc, segr, segp, dt, rate):
    cum = dot(tri(True).astype(F32), dt * rate, precision=HIGH)
    last = cum[SPAN - 1 : SPAN, :]
    keep = jnp.where(segc == segp, jnp.exp(cum), 0.0)
    to_end = jnp.where(segc == segr[:, SPAN - 1 : SPAN], jnp.exp(last - cum), 0.0)
    return cum, cum.T, keep, to_end


def expanded(columns, ones):
    high = columns.astype(BF)
    low = (columns - high.astype(F32)).astype(BF)
    return dot(high, ones) + dot(low, ones)


def head_of_channel(width):
    return (
        lax.broadcasted_iota(jnp.int32, (LANES, width), 1) // HEADDIM
        == lax.broadcasted_iota(jnp.int32, (LANES, width), 0)
    ).astype(BF)


def spread_columns(ref, first, count):
    return [jnp.broadcast_to(ref[:, first + k : first + k + 1], (SPAN, LANES)) for k in range(count)]


def taps(ext, masks, at):
    terms = [ext[pl.ds(HALO - CONV + 1 + k, SPAN), at] for k in range(CONV)]
    return [t * m for t, m in zip(terms, masks)] + terms[CONV - 1 :]


def convolved(terms, weight_ref, at):
    total = weight_ref[CONV : CONV + 1, at] + terms[0] * weight_ref[0:1, at]
    for k in range(1, CONV):
        total = total + terms[k] * weight_ref[k : k + 1, at]
    return total


def forward_kernel(
    heads,
    segp_ref,
    segc_ref,
    segr_ref,
    mask_ref,
    in_a_ref,
    in_b_ref,
    halo_ref,
    weight_ref,
    b_ref,
    c_ref,
    dt_ref,
    rate_ref,
    skip_ref,
    y_ref,
    prior_ref,
    carry,
    to_end_u,
    ext,
    wide_dt,
    wide_keep,
    wide_end,
):
    block = pl.program_id(0)
    width = heads * HEADDIM

    @pl.when(block == 0)
    def _():
        carry[...] = jnp.zeros_like(carry)

    prior_ref[0] = carry[...]
    ext[0:HALO] = halo_ref[0].astype(F32)
    half = in_b_ref.shape[1]
    ext[HALO:, :half] = in_a_ref[:, :half].astype(F32)
    ext[HALO:, half:] = in_b_ref[...].astype(F32)
    segc, segr = segc_ref[...], segr_ref[...]
    dt = dt_ref[...]
    cum, cumr, keep, to_end = decays(segc, segr, segp_ref[block], dt, rate_ref[...])
    bm, cm = b_ref[...], c_ref[...]
    mixing = dot(cm, bm, ((1,), (1,)))
    mixing = jnp.where(tri(True) & (segc == segr), mixing, 0.0)
    heads_ones = head_of_channel(width)
    wide_dt[...] = expanded(dt, heads_ones)
    wide_keep[...] = expanded(keep, heads_ones)
    wide_end[...] = expanded(to_end, heads_ones)
    masks = spread_columns(mask_ref, 0, CONV - 1)
    lo = lax.broadcasted_iota(jnp.int32, (SPAN, LANES), 1) < HEADDIM
    for p in range(heads // 2):
        at = slice(p * LANES, (p + 1) * LANES)
        pre = convolved(taps(ext, masks, at), weight_ref, at)
        x2 = pre * jax.nn.sigmoid(pre)
        u2 = x2 * wide_dt[:, at]
        ub = u2.astype(BF)
        total = dot(cm, carry[:, at].astype(BF)) * wide_keep[:, at] + skip_ref[:, at] * x2
        inner = []
        for h in (2 * p, 2 * p + 1):
            decay = jnp.exp(jnp.minimum(cum[:, h : h + 1] - cumr[h : h + 1, :], 0.0))
            inner.append(dot((decay * mixing).astype(BF), ub))
        y_ref[:, at] = total + jnp.where(lo, inner[0], inner[1])
        to_end_u[:, at] = (u2 * wide_end[:, at]).astype(BF)
    fresh = dot(bm, to_end_u[...], ((0,), (0,)))
    carry[...] = wide_keep[SPAN - 1 : SPAN, :] * carry[...] + fresh


def split_dot(value, ones):
    high = value.astype(BF)
    low = (value - high.astype(F32)).astype(BF)
    return dot(high, ones) + dot(low, ones)


def backward_kernel(
    heads,
    segp_ref,
    segc_ref,
    segr_ref,
    mask_ref,
    in_a_ref,
    in_b_ref,
    halo_ref,
    weight_ref,
    b_ref,
    c_ref,
    dt_ref,
    rate_ref,
    skip_ref,
    y_ref,
    prior_ref,
    dy_ref,
    din_ref,
    dbc_ref,
    ddt_ref,
    drate_ref,
    dsum_ref,
    dcarry,
    after_state,
    keep_dy,
    to_end_u,
    slopes,
    along,
    ext,
    dext,
    wide_dt,
    wide_keep,
    wide_end,
):
    step = pl.program_id(0)
    block = pl.num_programs(0) - 1 - step

    @pl.when(step == 0)
    def _():
        dcarry[...] = jnp.zeros_like(dcarry)
        after_state[...] = jnp.zeros_like(after_state)
        drate_ref[...] = jnp.zeros_like(drate_ref)
        dsum_ref[...] = jnp.zeros_like(dsum_ref)
        dext[SPAN:] = jnp.zeros((HALO, dext.shape[1]), F32)

    ext[0:HALO] = halo_ref[0].astype(F32)
    half = in_b_ref.shape[1]
    ext[HALO:, :half] = in_a_ref[:, :half].astype(F32)
    ext[HALO:, half:] = in_b_ref[...].astype(F32)
    segc, segr = segc_ref[...], segr_ref[...]
    dt = dt_ref[...]
    cum, cumr, keep, to_end = decays(segc, segr, segp_ref[block], dt, rate_ref[...])
    bm, cm = b_ref[...], c_ref[...]
    allowed = tri(False) & (segc == segr)
    mixing = jnp.where(allowed, dot(bm, cm, ((1,), (1,))), 0.0)
    heads_ones = head_of_channel(heads * HEADDIM)
    wide_dt[...] = expanded(dt, heads_ones)
    wide_keep[...] = expanded(keep, heads_ones)
    wide_end[...] = expanded(to_end, heads_ones)
    masks = spread_columns(mask_ref, 0, CONV - 1)
    moved = spread_columns(mask_ref, CONV - 1, CONV - 1)
    lo = lax.broadcasted_iota(jnp.int32, (SPAN, LANES), 1) < HEADDIM
    dmixing = jnp.zeros((SPAN, SPAN), F32)
    for p in range(heads // 2):
        at = slice(p * LANES, (p + 1) * LANES)
        terms = taps(ext, masks, at)
        pre = convolved(terms, weight_ref, at)
        sig = jax.nn.sigmoid(pre)
        x2 = pre * sig
        dt2 = wide_dt[:, at]
        u2 = x2 * dt2
        dyb = dy_ref[:, at]
        dy2 = dyb.astype(F32)
        skip = skip_ref[:, at]
        te2 = wide_end[:, at]
        u_sides = (jnp.where(lo, u2, 0.0).astype(BF), jnp.where(lo, 0.0, u2).astype(BF))
        du = te2 * dot(bm, dcarry[:, at].astype(BF))
        inner = []
        for k in range(2):
            h = 2 * p + k
            decay = jnp.exp(jnp.minimum(cumr[h : h + 1, :] - cum[:, h : h + 1], 0.0))
            inner.append(dot((decay * mixing).astype(BF), dyb))
            dmixing = dmixing + decay * dot(u_sides[k], dyb, ((1,), (1,)))
        du = du + jnp.where(lo, inner[0], inner[1])
        keep_dy[:, at] = (wide_keep[:, at] * dy2).astype(BF)
        to_end_u[:, at] = (te2 * u2).astype(BF)
        slopes[:, at] = dy2 * (y_ref[:, at] - skip * x2) - u2.astype(BF).astype(F32) * du
        along[:, at] = x2 * du
        dpre = (dt2 * du + skip * dy2) * (sig * (1.0 + pre * (1.0 - sig)))
        dext[0:SPAN, at] = dpre
        for k in range(CONV):
            dsum_ref[k : k + 1, at] += jnp.sum(dpre * terms[k], axis=0, keepdims=True)
        dsum_ref[CONV : CONV + 1, at] += jnp.sum(dpre, axis=0, keepdims=True)
        dsum_ref[CONV + 1 : CONV + 2, at] += jnp.sum(dy2 * x2, axis=0, keepdims=True)
        din = dpre * weight_ref[CONV - 1 : CONV, at]
        for k in range(CONV - 1):
            later = dext[pl.ds(CONV - 1 - k, SPAN), at]
            din = din + later * moved[k] * weight_ref[k : k + 1, at]
        din_ref[:, at] = din.astype(BF)
    dext[SPAN:] = dext[0:HALO]
    dmixing = jnp.where(allowed, dmixing, 0.0).astype(BF)
    dstate = dcarry[...].astype(BF)
    prior = prior_ref[0]
    dbc_ref[:, :STATE] = dot(dmixing, cm) + dot(to_end_u[...], dstate, ((1,), (1,)))
    dbc_ref[:, STATE:] = dot(dmixing, bm, ((0,), (0,))) + dot(
        keep_dy[...], prior.astype(BF), ((1,), (1,))
    )
    width = heads * HEADDIM
    ones = (
        lax.broadcasted_iota(jnp.int32, (width, LANES), 0) // HEADDIM
        == lax.broadcasted_iota(jnp.int32, (width, LANES), 1)
    ).astype(BF)
    at_end = jnp.sum(dcarry[...] * after_state[...], axis=0, keepdims=True)
    at_end = split_dot(jnp.broadcast_to(at_end, (16, width)), ones)[:1]
    dcum = split_dot(slopes[...], ones)
    da = dot(tri(False).astype(F32), dcum, precision=HIGH) + at_end
    ddt_ref[...] = rate_ref[...] * da + split_dot(along[...], ones)
    drate_ref[...] += jnp.sum(dt * da, axis=0, keepdims=True)
    fresh = dot(cm, keep_dy[...], ((0,), (0,)))
    dcarry[...] = wide_keep[SPAN - 1 : SPAN, :] * dcarry[...] + fresh
    after_state[...] = prior


def scan_specs(heads, at, in_widths):
    width = heads * HEADDIM

    def rows(n):
        return pl.BlockSpec((SPAN, n), lambda i: (at(i), 0))

    def whole(*shape):
        return pl.BlockSpec(shape, lambda i: (0,) * len(shape))

    ins = [
        pl.BlockSpec(memory_space=pltpu.SMEM),
        rows(1),
        pl.BlockSpec((1, SPAN), lambda i: (0, at(i))),
        rows(LANES),
        rows(in_widths[0]),
        rows(in_widths[1]),
        pl.BlockSpec((1, HALO, width), lambda i: (at(i), 0, 0)),
        whole(8, width),
        rows(STATE),
        rows(STATE),
        rows(LANES),
        whole(1, LANES),
        whole(1, width),
    ]
    prior = pl.BlockSpec((1, STATE, width), lambda i: (at(i), 0, 0))
    return rows, whole, ins, prior


def scan_forward(heads, blocks, operands):
    rows, whole, ins, prior = scan_specs(heads, lambda i: i, [operands[n].shape[1] for n in (4, 5)])
    width = heads * HEADDIM
    return call(
        functools.partial(forward_kernel, heads),
        grid=(blocks,),
        in_specs=ins,
        out_specs=[rows(width), prior],
        out_shape=[
            jax.ShapeDtypeStruct((blocks * SPAN, width), F32),
            jax.ShapeDtypeStruct((blocks, STATE, width), F32),
        ],
        scratch_shapes=[
            pltpu.VMEM((STATE, width), F32),
            pltpu.VMEM((SPAN, width), BF),
            pltpu.VMEM((HALO + SPAN, width), F32),
            pltpu.VMEM((SPAN, width), F32),
            pltpu.VMEM((SPAN, width), F32),
            pltpu.VMEM((SPAN, width), F32),
        ],
        name="scan_forward",
    )(*operands)


def scan_backward(heads, blocks, operands, y, priors, dy):
    rows, whole, ins, prior = scan_specs(
        heads, lambda i: blocks - 1 - i, [operands[n].shape[1] for n in (4, 5)]
    )
    width = heads * HEADDIM
    return call(
        functools.partial(backward_kernel, heads),
        grid=(blocks,),
        in_specs=ins + [rows(width), prior, rows(width)],
        out_specs=[rows(width), rows(2 * STATE), rows(LANES), whole(1, LANES), whole(8, width)],
        out_shape=[
            jax.ShapeDtypeStruct((blocks * SPAN, width), BF),
            jax.ShapeDtypeStruct((blocks * SPAN, 2 * STATE), F32),
            jax.ShapeDtypeStruct((blocks * SPAN, LANES), F32),
            jax.ShapeDtypeStruct((1, LANES), F32),
            jax.ShapeDtypeStruct((8, width), F32),
        ],
        scratch_shapes=[
            pltpu.VMEM((STATE, width), F32),
            pltpu.VMEM((STATE, width), F32),
            pltpu.VMEM((SPAN, width), BF),
            pltpu.VMEM((SPAN, width), BF),
            pltpu.VMEM((SPAN, width), F32),
            pltpu.VMEM((SPAN, width), F32),
            pltpu.VMEM((HALO + SPAN, width), F32),
            pltpu.VMEM((SPAN + HALO, width), F32),
            pltpu.VMEM((SPAN, width), F32),
            pltpu.VMEM((SPAN, width), F32),
            pltpu.VMEM((SPAN, width), F32),
        ],
        name="scan_backward",
    )(*operands, y, priors, dy)


def as_columns(rows):
    few, tokens = rows.shape
    return jnp.concatenate([rows, jnp.zeros((LANES - few, tokens), F32)]).T


def level_block(pieces, spot):
    piece, lead = spot
    return pieces[piece][lead + (slice(None), slice(None))].astype(F32)


def upper_kernel(where, plan, nd, tok, ns, here_ref, range_ref, count_ref, ratio_ref, q_turned, *refs):
    count = 3 + 2 * LEVELS
    pieces, outs = refs[:count], refs[count:]
    upper_ref, grad_refs, coefs = outs[0], outs[1 : 2 * nd], outs[2 * nd]

    @pl.when(pl.program_id(0) == 0)
    def _():
        rows = [count_ref[j, w] * ratio_ref[w : w + 1, :] for j in range(len(plan)) for w in range(LEVELS)]
        coefs[...] = as_columns(jnp.concatenate(rows))

    for k in range(ns):
        at = here_ref[0] ^ k
        rows = pl.ds(pl.multiple_of(at * tok, tok), tok)
        levels = [level_block(pieces, where[w][k]) for w in range(LEVELS)]
        for j in range(len(plan)):
            total = None
            for w in plan[j]:
                n = j * LEVELS + w
                term = coefs[rows, n : n + 1] * levels[w]
                total = term if total is None else total + term
            upper_ref[j, rows, :] = total.astype(BF)
    count = q_turned.shape[0] // nd
    for k in range(nd):
        index = here_ref[1] ^ k
        rows = pl.ds(pl.multiple_of(index * count, count), count)
        value = dot(q_turned[rows, :], upper_ref[range_ref[index]]).astype(BF)
        if k:
            grad_refs[2 * k - 1][...] = value[: count // 2]
            grad_refs[2 * k][...] = value[count // 2 :]
        else:
            grad_refs[0][...] = value


def products_kernel(where, plan, lanes, tok, ns, nd, here_ref, count_ref, q_ref, *refs):
    count = 3 + 2 * LEVELS
    held_ref, pieces, outs = refs[0], refs[1 : 1 + count], refs[1 + count :]
    prod_refs, inner_ref, w_ref, sums = outs[:ns], outs[ns], outs[ns + 1], outs[ns + 2]
    step = pl.program_id(0)
    rows_of = w_ref.shape[0] // nd
    for k in range(nd):
        at = pl.multiple_of((here_ref[1] ^ k) * rows_of, rows_of)
        w_ref[pl.ds(at, rows_of), :] = held_ref[:, k].reshape(rows_of, w_ref.shape[1])

    @pl.when(step == 0)
    def _():
        sums[...] = jnp.zeros_like(sums)

    for k in range(ns):
        at = here_ref[0] ^ k
        rows = pl.ds(pl.multiple_of(at * tok, tok), tok)
        values = [dot(q_ref[rows, a:b], w_ref[a:b, :]) for a, b in lanes]
        for j, value in enumerate(values):
            prod_refs[k][j] = value.astype(BF)
        for w in range(LEVELS):
            total = None
            for j in range(len(lanes)):
                if w in plan[j]:
                    term = values[j] * count_ref[j, w]
                    total = term if total is None else total + term
            part = total * level_block(pieces, where[w][k])
            folded = part[:, :LANES]
            for c in range(LANES, part.shape[1], LANES):
                folded = folded + part[:, c : c + LANES]
            sums[w, rows, :] += folded

    @pl.when(step == pl.num_programs(0) - 1)
    def _():
        lane = lax.broadcasted_iota(jnp.int32, sums.shape[1:], 1)
        total = jnp.zeros(sums.shape[1:], F32)
        for w in range(LEVELS):
            total = jnp.where(lane == w, jnp.sum(sums[w], axis=1, keepdims=True), total)
        inner_ref[...] = total.T[:LEVELS]


def gate_kernel(
    starts, wide, count_ref, upper_ref, w_ref, y_ref, z_ref, gain_ref, ratio_ref, mean_ref, dy_ref, dz_ref, grad_ref, coefs
):
    step = pl.program_id(0)

    @pl.when(step == 0)
    def _():
        cubes = ratio_ref[...] * ratio_ref[...] * ratio_ref[...] * mean_ref[...]
        rows = []
        for j in range(len(starts)):
            total = cubes[0:1] * count_ref[j, 0]
            for w in range(1, LEVELS):
                total = total + cubes[w : w + 1] * count_ref[j, w]
            rows.append(total)
        columns = as_columns(jnp.concatenate(rows))
        for j in range(len(starts)):
            coefs[j] = jnp.broadcast_to(columns[:, j : j + 1], coefs.shape[1:])

    grad_all = dot(upper_ref[0], w_ref[...], ((1,), (1,)))
    coef = coefs[tile_range(starts, wide, step)]
    for c in range(0, wide, LANES):
        at = slice(c, c + LANES)
        grad_t = grad_all[:, at]
        z = z_ref[:, at].astype(F32)
        sig = jax.nn.sigmoid(z)
        act = z * sig
        y = y_ref[:, at]
        q = y * act
        dq = gain_ref[:, at] * grad_t - q * coef
        dy_ref[:, at] = (dq * act).astype(BF)
        dz_ref[:, at] = (dq * y * (sig * (1.0 + z * (1.0 - sig)))).astype(BF)
        grad_ref[0:1, at] = jnp.sum(q * grad_t, axis=0, keepdims=True)


def tile_range(starts, wide, step):
    index = 0
    for start in starts[1:]:
        index = index + jnp.where(step * wide >= start, 1, 0)
    return index


def mixed_kernel(plan, split, ns, tok, here_ref, count_ref, ratio_ref, x_ref, *refs):
    shares, out_ref = refs[:-1], refs[-1]
    at = pl.ds(pl.multiple_of(here_ref[0] * tok, tok), tok)
    ratios = as_columns(ratio_ref[:, at])
    x = x_ref[...].astype(F32)
    for w in range(LEVELS):
        total = None
        for k in range(ns):
            for j in plan[w]:
                at = (k, j) if k < 3 or j < split else (k + 1, j - split)
                term = shares[at[0]][at[1]].astype(F32) * count_ref[k, j * LEVELS + w]
                total = term if total is None else total + term
        out_ref[w] = (x + ratios[:, w : w + 1] * total).astype(BF)


def dp_terms(others):
    return [swapped(other, "dp", k + 1) for k, other in enumerate(others)]


def over_seq(value):
    dense = value.reshape(-1, LANES)
    total = dense
    for k in range(1, lax.axis_size("seq")):
        total = total + swapped(dense, "seq", k)
    return total.reshape(value.shape)


def fsdp_half(own, got):
    nf = lax.axis_size("fsdp")
    f = lax.axis_index("fsdp")

    def part(offset):
        total = picked(own, f ^ offset).astype(F32)
        for other in got:
            total = total + picked(other, f ^ offset).astype(F32)
        return total.astype(BF)

    kept = jnp.stack([part(e) for e in range(0, nf, 2)])
    sent = jnp.stack([part(e ^ 1) for e in range(0, nf, 2)])
    return kept, sent


def fsdp_rest(kept, got):
    k = 2
    while k < lax.axis_size("fsdp"):
        total = (kept.astype(F32) + got.astype(F32)).astype(BF)
        kept, sent = total[::2], total[1::2]
        got = swapped(sent, "fsdp", k)
        k *= 2
    return kept[0], got[0]


def shards(
    tokens,
    lengths,
    norm_gain,
    w_in,
    w_dt,
    conv_w,
    conv_b,
    dt_bias,
    a_log,
    skip,
    gate_gain,
    w_out,
    cotangent,
):
    nd, ns, nf = lax.axis_size("dp"), lax.axis_size("seq"), lax.axis_size("fsdp")
    d, s, f = lax.axis_index("dp"), lax.axis_index("seq"), lax.axis_index("fsdp")
    tok = tokens.shape[1]
    length = ns * tok
    blocks = length // SPAN
    heads = HEADS // ns
    run = heads // nd
    width = heads * HEADDIM
    own_bc = 2 * STATE // ns
    used = width + own_bc
    cols = -(-(used + heads) // LANES) * LANES
    rows_in = w_in.shape[0]
    reach = CONV - 1

    levels = np.array(
        [[level_of(dd * (HEADS // nd) + ss * run + i) for dd in range(nd) for i in range(run)] for ss in range(ns)]
    )
    cuts = [0] + [h for h in range(1, heads) if (levels[:, h] != levels[:, h - 1]).any()] + [heads]
    ranges = [(a, b) for a, b in zip(cuts, cuts[1:])]
    range_level = np.array([[levels[ss, a] for a, _ in ranges] for ss in range(ns)])
    counts = (range_level[:, :, None] <= np.arange(LEVELS)[None, None, :]).astype(np.float32)
    counted = picked(jnp.asarray(counts), s)
    theirs = picked(
        jnp.asarray(np.stack([[counts[i ^ k].reshape(-1) for k in range(ns)] for i in range(ns)])), s
    )
    lowest = [int(range_level[ss].min()) for ss in range(ns)]

    def by_head(vector):
        lead = vector.shape[:-1]
        per = vector.shape[-1] // HEADS
        cut = vector.reshape(lead + (nd, ns, run * per))
        mine = lax.dynamic_index_in_dim(cut, s, len(lead) + 1, keepdims=False)
        return mine.reshape(lead + (heads * per,))

    def for_groups(matrix):
        per = matrix.shape[1] // HEADS
        cut = matrix.reshape(matrix.shape[0], nd, ns, run * per)
        return jnp.transpose(cut, (2, 0, 1, 3)).reshape(ns, matrix.shape[0], heads * per)

    def from_groups(stack):
        per = stack.shape[2] // heads
        cut = stack.reshape(ns, stack.shape[1], nd, run * per)
        return jnp.transpose(cut, (1, 2, 0, 3)).reshape(stack.shape[1], HEADS * per)

    pad_cols = cols - used - heads
    half = width // 2
    first = half + cols - width
    group_x = for_groups(w_in[:, INNER : 2 * INNER])
    stack = jnp.concatenate(
        [
            group_x[:, :, :half],
            w_in[:, 2 * INNER :].reshape(rows_in, ns, own_bc).transpose(1, 0, 2),
            for_groups(w_dt),
            jnp.zeros((ns, rows_in, pad_cols), BF),
            group_x[:, :, half:],
            for_groups(w_in[:, :INNER]),
        ],
        axis=2,
    )
    own_x = tokens[0].astype(F32)
    scale = lax.rsqrt(jnp.mean(own_x * own_x, axis=-1, keepdims=True) + EPS)
    xn_own = (own_x * scale * norm_gain).astype(BF)
    xn_across = swapped(xn_own, "seq", 2)
    xn_pieces = [xn_own, swapped(xn_own, "seq", 1), xn_across, swapped(xn_across, "seq", 1)]
    arrived = [picked(stack, s)] + [swapped(picked(stack, s ^ k), "seq", k) for k in range(1, ns)]
    mine = filled((ns, rows_in, stack.shape[2]), [(p, None, (s ^ k, None, None)) for k, p in enumerate(arrived)])
    mine_z = mine[:, :, cols:]

    def needed(at, level):
        return min(lowest[at], lowest[at ^ 1]) <= level

    halves = [cotangent[w : w + 2, 0] for w in range(0, LEVELS, 2)]
    singles = [cotangent[w, 0] for w in range(LEVELS)]

    def beside(level, *others):
        block = after(halves[level // 2], *others)
        return swapped(block, "seq", 1, lambda i, j: needed(j, level + 1))

    def across(level, *others):
        block = after(singles[level], *others)
        return swapped(block, "seq", 2, lambda i, j: needed(j, level))

    def far(level, block):
        return swapped(block, "seq", 1, lambda i, j: needed(j, level))

    positions = jnp.arange(length, dtype=jnp.int32)
    ends = jnp.cumsum(lengths[0])[:-1]
    seg = jnp.sum((positions[:, None] >= ends[None, :]).astype(jnp.int32), axis=1)
    seg_before = jnp.concatenate([jnp.full((1,), -1, jnp.int32), seg[SPAN - 1 : length - 1 : SPAN]])
    seg_pad = jnp.concatenate([jnp.full((reach,), -1, jnp.int32), seg])
    masks = [(seg_pad[k : k + length] == seg) for k in range(reach)]
    mask_cols = [m.astype(F32) for m in masks]
    mask_cols += [jnp.pad(m, (0, reach - k))[reach - k :] for k, m in enumerate(mask_cols)]
    mask_cols = jnp.pad(jnp.stack(mask_cols, axis=1), ((0, 0), (0, LANES - 2 * reach)))

    def conv_params(s_part, bc_part):
        return by_head(s_part), bc_part

    weight_s = jnp.concatenate(
        [by_head(conv_w[:, :INNER]), by_head(conv_b[None, :INNER]), jnp.zeros((3, width), F32)]
    )
    weight_r = jnp.pad(
        lax.dynamic_slice_in_dim(conv_w, INNER + s * own_bc, own_bc, 1), ((0, 0), (0, cols - used))
    )
    bias_r = jnp.pad(
        lax.dynamic_slice_in_dim(conv_b, INNER + s * own_bc, own_bc, 0), (0, cols - used)
    )
    bias = by_head(dt_bias)
    rate = -jnp.exp(by_head(a_log))
    skip_own = by_head(skip)
    gain = by_head(gate_gain)

    def over_fsdp(chunk):
        return lax.all_gather(chunk, "fsdp", axis=0, tiled=False)

    def over_dp(held):
        return [held] + [swapped(held, "dp", j) for j in range(1, nd)]

    def whole(pieces, columns):
        moves = [
            (piece, i, (d ^ j, None, i, None, None)) for j, piece in enumerate(pieces) for i in range(nf)
        ]
        return filled((nd, ns, nf, rows_in, columns), moves).reshape(D, columns)

    held_a = over_fsdp(mine[:, :, :first])
    held_b = over_fsdp(mine[:, :, first:cols])
    other_out = [swapped(w_out, "dp", j) for j in range(1, nd)]
    held_a, other_out, xn_pieces[2] = together(held_a, other_out, xn_pieces[2])
    small_ones = (seg, seg_before, mask_cols, weight_s, weight_r, bias_r, bias, rate, skip_own, gain, theirs)
    held_a, small_ones, halves, singles = together(held_a, small_ones, halves, singles)
    seg, seg_before, mask_cols, weight_s, weight_r, bias_r, bias, rate, skip_own, gain, theirs = small_ones
    near_high, near_low = beside(2, held_a), beside(0, held_a)
    chip3 = across(3, held_a)
    pieces_a = over_dp(held_a)
    held_b, pieces_a, chip3, near_high, xn_pieces = together(
        held_b, pieces_a, chip3, near_high, xn_pieces
    )
    xn = filled((ns, tok, D), [(p, None, (s ^ k, None, None)) for k, p in enumerate(xn_pieces)])
    xn = xn.reshape(length, D)

    far3 = far(3, chip3)
    pieces_b = over_dp(held_b)
    held_z = over_fsdp(after(mine_z, held_a))
    pair_out = jnp.stack([w_out] + other_out)

    xn_turned = xn.T
    here = jnp.stack([s, d]).astype(jnp.int32)
    full_a = whole(pieces_a, first)
    proj_a = dot(xn, full_a).astype(BF)

    proj_r = proj_a[:, half:]
    mixer = jnp.concatenate([jnp.zeros((reach, cols - width), BF), proj_r], axis=0)

    def taken(k):
        rows = mixer[k : k + length].astype(F32)
        return rows * mask_cols[:, k : k + 1] if k < reach else rows

    pre_r = bias_r
    for k in range(CONV):
        pre_r = pre_r + taken(k) * weight_r[k]
    bc_own = jax.nn.silu(pre_r).astype(BF)[:, :own_bc]
    bc_across = swapped(bc_own, "seq", 2)
    bc = [bc_own, swapped(bc_own, "seq", 1), bc_across, swapped(bc_across, "seq", 1)]
    chip2, chip1 = across(2, bc[2]), across(1, bc[2])
    full_b = whole(pieces_b, half)
    proj_b = dot(xn, after(full_b, proj_a, xn_turned, bc[2])).astype(BF)
    proj_b, far3, near_low, held_z = together(proj_b, far3, near_low, held_z)
    pieces_z = over_dp(held_z)
    held_out = over_fsdp(after(pair_out, proj_b))
    bc = reordered_by_xor(bc, s)
    b_in = jnp.concatenate(bc[: ns // 2], axis=1)
    c_out = jnp.concatenate(bc[ns // 2 :], axis=1)

    def padded(rows):
        return jnp.pad(rows, ((0, 0), (0, LANES - rows.shape[1])))

    pre_dt = proj_r[:, own_bc : own_bc + heads].astype(F32) + bias
    steps = jax.nn.softplus(pre_dt)
    tails = [
        p.reshape(blocks, SPAN, p.shape[1])[: blocks - 1, SPAN - HALO :, :half] for p in (proj_a, proj_b)
    ]
    operands = (
        seg_before,
        seg[:, None],
        seg[None, :],
        mask_cols,
        proj_a,
        proj_b,
        jnp.concatenate([jnp.zeros((1, HALO, width), BF), jnp.concatenate(tails, axis=2)]),
        weight_s,
        b_in,
        c_out,
        padded(steps),
        padded(rate[None, :]),
        jnp.repeat(skip_own, HEADDIM)[None, :],
    )
    y, priors = scan_forward(heads, blocks, operands)
    y, chip2 = together(y, chip2)
    far2, chip0 = far(2, chip2), across(0, y)
    parts = pieces_z if rows_in % 16 == 0 else [whole(pieces_z, width)]
    lanes = [(a * HEADDIM, b * HEADDIM) for a, b in ranges]
    starts = [a for a, _ in lanes]
    wide = min(min(b - a for a, b in lanes), TILE)
    proj_z, full_z, q_gain, q_turned, squares = gated_projection(
        here, xn, parts, nd, width, y, gain[None], starts, wide
    )
    squares, chip1 = together(squares[: len(lanes)], chip1)
    far1 = far(1, chip1)
    widths = np.array([[(HEADS >> 3 - w) * HEADDIM] for w in range(LEVELS)], np.float32)
    per_level = jnp.sum(counted[:, :, None] * squares[:, None, :], axis=0)
    ratio, chip0 = together(lax.rsqrt(over_seq(per_level) / widths + EPS), chip0)
    far0 = far(0, chip0)

    plan = [[w for w in range(LEVELS) if range_level[:, j].min() <= w] for j in range(len(lanes))]
    out_rows = width // nd
    range_of = [next(j for j, (a, b) in enumerate(lanes) if a <= i * out_rows < b) for i in range(nd)]
    smem = pl.BlockSpec(memory_space=pltpu.SMEM)
    cot_pieces = [cotangent, near_low, near_high, chip0, chip1, chip2, chip3, far0, far1, far2, far3]
    cot_specs = [pl.BlockSpec((LEVELS, 1, tok, WIDE), lambda i: (0, 0, 0, i))]
    cot_specs += [pl.BlockSpec((2, tok, WIDE), lambda i: (0, 0, i))] * 2
    cot_specs += [pl.BlockSpec((tok, WIDE), lambda i: (0, i))] * (2 * LEVELS)
    where = [[(0, (w, 0)), (1 + w // 2, (w % 2,)), (3 + w, ()), (3 + LEVELS + w, ())] for w in range(LEVELS)]
    upper, *grad_out = call(
        functools.partial(upper_kernel, where, plan, nd, tok, ns),
        grid=(D // WIDE,),
        in_specs=[
            smem,
            smem,
            smem,
            pl.BlockSpec((LEVELS, length), lambda i: (0, 0)),
            pl.BlockSpec((width, length), lambda i: (0, 0)),
        ]
        + cot_specs,
        out_specs=[pl.BlockSpec((len(lanes), length, WIDE), lambda i: (0, 0, i))]
        + [pl.BlockSpec((out_rows, WIDE), lambda i: (0, i))]
        + [pl.BlockSpec((out_rows // 2, WIDE), lambda i: (0, i))] * (2 * nd - 2),
        out_shape=[jax.ShapeDtypeStruct((len(lanes), length, D), BF)]
        + [jax.ShapeDtypeStruct((out_rows, D), BF)]
        + [jax.ShapeDtypeStruct((out_rows // 2, D), BF)] * (2 * nd - 2),
        scratch_shapes=[pltpu.VMEM((length, LANES), F32)],
        name="upper",
    )(here, jnp.asarray(range_of, jnp.int32), counted, ratio, q_turned, *cot_pieces)
    out_first, out_second = dp_terms(grad_out[1::2]), dp_terms(grad_out[2::2])

    held_out, upper = together(held_out, upper)
    *shares, inner, full_out = call(
        functools.partial(products_kernel, where, plan, lanes, tok, ns, nd),
        grid=(D // WIDE,),
        in_specs=[
            smem,
            smem,
            pl.BlockSpec((length, width), lambda i: (0, 0)),
        ]
        + [pl.BlockSpec((nf, nd, w_out.shape[0], WIDE), lambda i: (0, 0, 0, i))]
        + cot_specs,
        out_specs=[pl.BlockSpec((len(lanes), tok, WIDE), lambda i: (0, 0, i))] * ns
        + [pl.BlockSpec((LEVELS, length), lambda i: (0, 0))]
        + [pl.BlockSpec((width, WIDE), lambda i: (0, i))],
        out_shape=[jax.ShapeDtypeStruct((len(lanes), tok, D), BF)] * ns
        + [jax.ShapeDtypeStruct((LEVELS, length), F32)]
        + [jax.ShapeDtypeStruct((width, D), BF)],
        scratch_shapes=[pltpu.VMEM((LEVELS, length, LANES), F32)],
        name="products",
    )(here, counted, q_gain, held_out, *cot_pieces)
    means, out_first = together(over_seq(inner) / widths, out_first)
    shares[1:3] = [swapped(after(shares[k], means), "seq", k) for k in (1, 2)]
    split = (len(lanes) + 1) // 2
    third = [swapped(after(shares[3][:split], shares[1]), "seq", 3), shares[3][split:]]

    cols_of = pl.BlockSpec((length, wide), lambda i: (0, i))
    scalars = pl.BlockSpec((LEVELS, length), lambda i: (0, 0))
    dy, dz, grad_gate = call(
        functools.partial(gate_kernel, starts, wide),
        grid=(width // wide,),
        in_specs=[
            smem,
            pl.BlockSpec((1, length, D), lambda i: (tile_range(starts, wide, i), 0, 0)),
            pl.BlockSpec((wide, D), lambda i: (i, 0)),
            cols_of,
            cols_of,
            pl.BlockSpec((1, wide), lambda i: (0, i)),
            scalars,
            scalars,
        ],
        out_specs=[cols_of, cols_of, pl.BlockSpec((8, wide), lambda i: (0, i))],
        out_shape=[
            jax.ShapeDtypeStruct((length, width), BF),
            jax.ShapeDtypeStruct((length, width), BF),
            jax.ShapeDtypeStruct((8, width), F32),
        ],
        scratch_shapes=[pltpu.VMEM((len(lanes), length, LANES), F32)],
        name="gate_backward",
    )(counted, upper, full_out, y, proj_z, gain[None], ratio, means)
    grad_gate = grad_gate[0]

    def in_terms(dproj, at, first=0, columns=None):
        columns = columns or dproj.shape[1]
        out = row_terms(xn_turned, dproj, at, nd, ns, nf, first, columns)
        return out.reshape(nf, ns * rows_in, columns)

    z_other = [in_terms(dz, d ^ k) for k in range(1, nd)]
    z_got = dp_terms(z_other)
    dy, out_second, shares[1] = together(after(dy, *z_other), out_second, shares[1])
    chunk = (nf, out_rows // nf, D)
    out_got = [jnp.concatenate([u, v]).reshape(chunk) for u, v in zip(out_first, out_second)]
    out_kept, out_sent = fsdp_half(grad_out[0].reshape(chunk), out_got)
    dy = after(dy, out_sent)
    out_half = swapped(out_sent, "fsdp", 1)

    dproj_s, dbc, ddt, drate, dsum = scan_backward(heads, blocks, operands, y, priors, dy)
    dproj_s, dbc, out_half, shares[2], third = together(dproj_s, dbc, out_half, shares[2], third)
    out_pair = fsdp_rest(out_kept, out_half)

    dbc = dbc.astype(BF)
    slices = reordered_by_xor([dbc[:, j * own_bc : (j + 1) * own_bc] for j in range(ns)], s)
    beside_bc = swapped(jnp.concatenate([slices[1], slices[3]], axis=1), "seq", 1)
    sum_bc = jnp.concatenate([slices[0], slices[2]], axis=1).astype(F32) + beside_bc.astype(F32)
    across_bc = swapped(sum_bc[:, own_bc:].astype(BF), "seq", 2)

    z_own = in_terms(after(dz, dproj_s), d)
    z_own, z_got = together(z_own, z_got)
    z_kept, z_sent = fsdp_half(z_own, z_got)
    z_half = swapped(z_sent, "fsdp", 1)
    late_s = after(dproj_s, z_sent)
    left_other = [in_terms(late_s, d ^ k, 0, half) for k in range(1, nd)]
    left_got = dp_terms(left_other)
    third[1] = swapped(after(third[1], across_bc), "seq", 3)
    dbc_own = sum_bc[:, :own_bc] + across_bc.astype(F32)
    dproj_r, small_sums = small_back(
        own_bc,
        pre_r,
        padded(after(dbc_own, *left_other)),
        proj_r,
        mask_cols,
        weight_r,
        ddt,
        padded(pre_dt),
    )

    late_s, late_r = after(dproj_s, *left_other), dproj_r
    right_other = [
        jnp.concatenate([in_terms(late_s, d ^ k, half, half), in_terms(late_r, d ^ k)], axis=2)
        for k in range(1, nd)
    ]
    right_got = dp_terms(right_other)

    dxn = input_grad(dz, dproj_s, after(dproj_r, *right_other), full_z, full_a, full_b, ns, tok)
    pair = swapped(jnp.stack([picked(dxn, s ^ 1), picked(dxn, s ^ 3)]), "seq", 1)

    dxn, z_half, left_got, out_pair = together(dxn, z_half, left_got, out_pair)
    z_pair = fsdp_rest(z_kept, z_half)
    own_s = in_terms(after(dproj_s, dxn), d)
    left_kept, left_sent = fsdp_half(own_s[:, :, :half], left_got)
    left_half = swapped(left_sent, "fsdp", 1)
    own_r = in_terms(after(dproj_r, left_sent), d)
    flat = flattened(
        [
            jnp.concatenate([dsum[:CONV], small_sums[:CONV, :own_bc]], axis=1).reshape(-1),
            dsum[CONV],
            small_sums[CONV, :own_bc],
            grad_gate,
            small_sums[CONV + 1, :heads],
            drate[0, :heads] * rate,
            jnp.sum(dsum[CONV + 1].reshape(heads, HEADDIM), axis=1),
        ]
    )
    near = picked(dxn, s).astype(F32) + pair[0].astype(F32)
    far_sum = (picked(dxn, s ^ 2).astype(F32) + pair[1].astype(F32)).astype(BF)
    dxn_across = swapped(far_sum, "seq", 2)
    right_got, far_sum, left_half = together(right_got, far_sum, left_half)
    left_pair = fsdp_rest(left_kept, left_half)
    own_right = jnp.concatenate([own_s[:, :, half:], own_r], axis=2)
    right_kept, right_sent = fsdp_half(own_right, right_got)
    right_half = swapped(right_sent, "fsdp", 1)

    mixed = call(
        functools.partial(
            mixed_kernel,
            [[j for j in range(len(lanes)) if range_level[:, j].min() <= w] for w in range(LEVELS)],
            split,
            ns,
            tok,
        ),
        grid=(D // WIDE,),
        in_specs=[
            smem,
            smem,
            pl.BlockSpec((LEVELS, length), lambda i: (0, 0)),
            pl.BlockSpec((tok, WIDE), lambda i: (0, i)),
        ]
        + [pl.BlockSpec((p.shape[0], tok, WIDE), lambda i: (0, 0, i)) for p in shares[:3] + third],
        out_specs=pl.BlockSpec((LEVELS, tok, WIDE), lambda i: (0, 0, i)),
        out_shape=jax.ShapeDtypeStruct((LEVELS, tok, D), BF),
        name="mixed",
    )(here, theirs, ratio, tokens[0], *after(shares[:3] + third, right_sent))[:, None]
    right_half, mixed, dxn_across = together(right_half, mixed, dxn_across)
    right_kept = after(right_kept, mixed)
    right_pair = fsdp_rest(right_kept, right_half)
    dxn_own = near + dxn_across.astype(F32)
    grad_norm = jnp.sum(dxn_own * own_x * scale, axis=0)
    scaled = norm_gain * dxn_own
    dx = scale * scaled - own_x * scale**3 * jnp.mean(own_x * scaled, axis=-1, keepdims=True)
    dx = (dx + jnp.sum(after(cotangent, mixed)[:, 0].astype(F32), axis=0)).astype(BF)
    flat = jnp.concatenate([flat, grad_norm.reshape(-1, LANES)])
    flat = butterfly(flat, "dp")

    def whole_sum(pair):
        total = (pair[0].astype(F32) + pair[1].astype(F32)).astype(BF)
        return total.reshape(ns, rows_in, total.shape[1])

    z_pair, left_pair = together(z_pair, left_pair)
    early = jnp.concatenate([whole_sum(z_pair), whole_sum(left_pair)], axis=2)
    early_got = [picked(early, s)] + [swapped(picked(early, s ^ k), "seq", k) for k in range(1, ns)]
    early_got, right_pair, flat = together(early_got, right_pair, flat)
    flat = butterfly(flat, "fsdp")
    late = whole_sum(right_pair)
    late_got = [picked(late, s)] + [swapped(picked(late, s ^ k), "seq", k) for k in range(1, ns)]
    early = jnp.stack(reordered_by_xor(early_got, s))
    late = jnp.stack(reordered_by_xor(late_got, s))
    got_z = early[:, :, :width]
    got_x = jnp.concatenate([early[:, :, width:], late], axis=2)
    sum_out = out_pair[0].astype(F32) + out_pair[1].astype(F32)


    sum_in = jnp.concatenate(
        [
            from_groups(got_z),
            from_groups(got_x[:, :, :width]),
            jnp.transpose(got_x[:, :, width:used], (1, 0, 2)).reshape(rows_in, 2 * STATE),
        ],
        axis=1,
    ).astype(F32)
    sum_dt = from_groups(got_x[:, :, used : used + heads]).astype(F32)

    sizes = [CONV * used, used, width, heads, heads, heads]
    filling = -sum(sizes) % 1024
    sizes += [filling, D]
    every = seq_gather(flat, s).reshape(ns, -1)
    starts = np.cumsum([0] + sizes)
    pieces = [every[:, a : a + n] for a, n in zip(starts, sizes)]

    def heads_back(rows):
        lead = rows.shape[1:-1]
        cut = rows.reshape((ns,) + lead + (nd, rows.shape[-1] // nd))
        order = tuple(range(1, 1 + len(lead))) + (1 + len(lead), 0, 2 + len(lead))
        return jnp.transpose(cut, order).reshape(lead + (-1,))

    conv_rows = pieces[0].reshape(ns, CONV, used)
    conv_all = jnp.concatenate(
        [
            heads_back(conv_rows[:, :, :width]),
            jnp.transpose(conv_rows[:, :, width:], (1, 0, 2)).reshape(CONV, 2 * STATE),
        ],
        axis=1,
    )
    bias_all = jnp.concatenate([heads_back(pieces[1][:, :width]), pieces[1][:, width:].reshape(-1)])
    return (
        mixed,
        dx[None],
        jnp.sum(pieces[7], axis=0),
        sum_in,
        sum_dt,
        conv_all,
        bias_all,
        heads_back(pieces[3]),
        heads_back(pieces[4]),
        heads_back(pieces[5]),
        heads_back(pieces[2]),
        sum_out,
    )


def solution(mesh):
    rows = P(("dp", "seq", "fsdp"), None)
    held = P(("dp", "fsdp"), "seq", None)
    levels = P(None, ("dp", "fsdp"), "seq", None)
    placed = (held, P(("dp", "fsdp"), None), P(), rows, rows, P(), P(), P(), P(), P(), P(), rows, levels)
    return jax.shard_map(
        shards,
        mesh=mesh,
        in_specs=placed,
        out_specs=(levels, held, P(), rows, rows, P(), P(), P(), P(), P(), P(), rows),
        check_vma=False,
    )
```

```python
import functools

import jax
import jax.numpy as jnp
import numpy as np
from jax import lax
from jax.experimental import pallas as pl
from jax.experimental.pallas import tpu as pltpu
from jax.sharding import PartitionSpec as P

D = 2048
HEADS = 64
HEADDIM = 64
STATE = 128
CONV = 4
SPAN = 128
INNER = 4096
EPS = 1e-05
LEVELS = 4
BF = jnp.bfloat16
F32 = jnp.float32
HIGH = lax.Precision.HIGHEST
LANES = 128
HALO = 16
TILE = 256
WIDE = 512
VMEM_LIMIT = 48 * 1024 * 1024


def dot(a, b, dims=((1,), (0,)), precision=None):
    return lax.dot_general(a, b, (dims, ((), ())), preferred_element_type=F32, precision=precision)


def silu_slope(v):
    sig = jax.nn.sigmoid(v)
    return sig * (1.0 + v * (1.0 - sig))


def level_of(head):
    return 0 if head < 8 else 1 if head < 16 else 2 if head < 32 else 3


def swapped(value, axis, k, keep=None):
    pairs = [(i, i ^ k) for i in range(lax.axis_size(axis))]
    if keep is not None:
        pairs = [p for p in pairs if keep(*p)]
    return lax.ppermute(value, axis, pairs)


def after(value, *others):
    return lax.optimization_barrier((value,) + others)[0]


def together(*values):
    return lax.optimization_barrier(values)


def flattened(vectors):
    flat = jnp.concatenate(vectors)
    return jnp.pad(flat, (0, -flat.shape[0] % 1024)).reshape(-1, LANES)


def butterfly(value, axis):
    k = 1
    while k < lax.axis_size(axis):
        value = value + swapped(value, axis, k)
        k *= 2
    return value


def picked(array, index):
    return lax.dynamic_index_in_dim(array, index, 0, keepdims=False)


def seq_gather(block, here):
    return jnp.stack(reordered_by_xor([block] + [swapped(block, "seq", k) for k in range(1, 4)], here))


def reordered_by_xor(pieces, here):
    k = 1
    while k < len(pieces):
        flip = (here & k) > 0
        pieces = [jnp.where(flip, pieces[j ^ k], piece) for j, piece in enumerate(pieces)]
        k *= 2
    return pieces


def call(kernel, **kwargs):
    return pl.pallas_call(
        kernel,
        compiler_params=pltpu.CompilerParams(vmem_limit_bytes=VMEM_LIMIT),
        cost_estimate=pl.CostEstimate(flops=1, bytes_accessed=1, transcendentals=0),
        **kwargs,
    )


def filled(shape, moves):
    arrays, plan, rows = [], [], []
    block = tuple(size if index is None else 1 for size, index in zip(shape, moves[0][2]))
    for piece, lead, place in moves:
        at = next((i for i, a in enumerate(arrays) if a is piece), len(arrays))
        if at == len(arrays):
            arrays.append(piece)
        plan.append((at, lead))
        rows.append(jnp.stack([jnp.asarray(0 if n is None else n, jnp.int32) for n in place]))

    def kernel(index_ref, *refs):
        pieces, out = refs[:-1], refs[-1]
        for m, (at, lead) in enumerate(plan):

            @pl.when(pl.program_id(0) == m)
            def _():
                value = pieces[at][...] if lead is None else pieces[at][lead]
                out[...] = value.reshape(block)

    return call(
        kernel,
        grid_spec=pltpu.PrefetchScalarGridSpec(
            num_scalar_prefetch=1,
            grid=(len(plan),),
            in_specs=[
                pl.BlockSpec(a.shape, lambda i, t, n=a.ndim: (0,) * n) for a in arrays
            ],
            out_specs=pl.BlockSpec(
                block, lambda i, t: tuple(t[i, n] for n in range(len(shape)))
            ),
        ),
        out_shape=jax.ShapeDtypeStruct(shape, arrays[0].dtype),
        name="filled",
    )(jnp.stack(rows), *arrays)


def terms_kernel(ns, nf, at_ref, left_ref, right_ref, out_ref):
    value = dot(left_ref[...], right_ref[...]).astype(BF)
    rows = value.shape[0] // (ns * nf)
    for i in range(ns):
        for k in range(nf):
            out_ref[k, i] = value[(i * nf + k) * rows : (i * nf + k + 1) * rows]


def row_terms(turned, right, at, nd, ns, nf, first, columns):
    depth = turned.shape[1]
    rows = turned.shape[0] // nd
    wide = TILE if columns % TILE == 0 else LANES
    return call(
        functools.partial(terms_kernel, ns, nf),
        grid_spec=pltpu.PrefetchScalarGridSpec(
            num_scalar_prefetch=1,
            grid=(columns // wide,),
            in_specs=[
                pl.BlockSpec((rows, depth), lambda i, t: (t[0], 0)),
                pl.BlockSpec((depth, wide), lambda i, t: (0, i + first // wide)),
            ],
            out_specs=pl.BlockSpec((nf, ns, rows // (nf * ns), wide), lambda i, t: (0, 0, 0, i)),
        ),
        out_shape=jax.ShapeDtypeStruct((nf, ns, rows // (nf * ns), columns), BF),
        name="row_terms",
    )(at.astype(jnp.int32)[None], turned, right)


def small_back_kernel(
    width, pre_ref, dbc_ref, in_ref, mask_ref, weight_ref, ddt_ref, pre_dt_ref, out_ref, sum_ref, ext, dext
):
    rows = pre_ref.shape[0]
    ext[0:HALO] = jnp.zeros((HALO, LANES), F32)
    ext[HALO:] = in_ref[...].astype(F32)
    pre = pre_ref[...]
    sig = jax.nn.sigmoid(pre)
    dpre = dbc_ref[...] * (sig * (1.0 + pre * (1.0 - sig)))
    dext[0:rows] = dpre
    dext[rows:] = jnp.zeros((HALO, LANES), F32)
    total = dpre * weight_ref[CONV - 1 : CONV, :]
    for k in range(CONV):
        term = ext[pl.ds(HALO - CONV + 1 + k, rows), :]
        if k < CONV - 1:
            term = term * mask_ref[:, k : k + 1]
            later = dext[pl.ds(CONV - 1 - k, rows), :] * mask_ref[:, CONV - 1 + k : CONV + k]
            total = total + later * weight_ref[k : k + 1, :]
        sum_ref[k : k + 1, :] = jnp.sum(dpre * term, axis=0, keepdims=True)
    sum_ref[CONV : CONV + 1, :] = jnp.sum(dpre, axis=0, keepdims=True)
    draw = ddt_ref[...] * jax.nn.sigmoid(pre_dt_ref[...])
    sum_ref[CONV + 1 : CONV + 2, :] = jnp.sum(draw, axis=0, keepdims=True)
    out_ref[...] = (total + pltpu.roll(draw, width, axis=1)).astype(BF)


def small_back(width, pre, dbc, proj, masks, weight, ddt, pre_dt):
    rows = pre.shape[0]
    return call(
        functools.partial(small_back_kernel, width),
        out_shape=[
            jax.ShapeDtypeStruct((rows, LANES), BF),
            jax.ShapeDtypeStruct((8, LANES), F32),
        ],
        scratch_shapes=[pltpu.VMEM((HALO + rows, LANES), F32), pltpu.VMEM((rows + HALO, LANES), F32)],
        name="small_back",
    )(pre, dbc, proj, masks, weight, ddt, pre_dt)


def input_grad_kernel(blocks, dz_ref, ds_ref, dr_ref, wz_ref, wa_ref, wb_ref, out_ref):
    half = wb_ref.shape[1]
    columns = ((1,), (1,))
    total = dot(dz_ref[...], wz_ref[...], columns)
    total = total + dot(ds_ref[:, :half], wa_ref[:, :half], columns)
    total = total + dot(ds_ref[:, half:], wb_ref[...], columns)
    total = total + dot(dr_ref[...], wa_ref[:, half:], columns)
    total = total.astype(BF)
    tok = total.shape[0] // blocks
    for i in range(blocks):
        out_ref[i] = total[i * tok : (i + 1) * tok]


def input_grad(dz, ds, dr, wz, wa, wb, blocks, tok):
    def whole(a):
        return pl.BlockSpec(a.shape, lambda i: (0, 0))

    def rows(a):
        return pl.BlockSpec((TILE, a.shape[1]), lambda i: (i, 0))

    return call(
        functools.partial(input_grad_kernel, blocks),
        grid=(wz.shape[0] // TILE,),
        in_specs=[whole(dz), whole(ds), whole(dr), rows(wz), rows(wa), rows(wb)],
        out_specs=pl.BlockSpec((blocks, tok, TILE), lambda i: (0, 0, i)),
        out_shape=jax.ShapeDtypeStruct((blocks, tok, wz.shape[0]), BF),
        name="input_grad",
    )(dz, ds, dr, wz, wa, wb)


def assembled(here_ref, pieces, nd, full_ref):
    halves = len(pieces) // nd
    nf, ns, rows = pieces[0].shape[:3]
    for n, piece in enumerate(pieces):
        h, j = divmod(n, nd)
        for k in range(nf):
            for i in range(ns):
                block = ((here_ref[1] ^ j) * ns + i) * nf + k
                at = pl.multiple_of((block * halves + h) * rows, rows)
                full_ref[pl.ds(at, rows), :] = piece[k, i]


def gated_kernel(nd, count, starts, wide, here_ref, xn_ref, y_ref, gain_ref, *refs):
    pieces, (out_ref, full_ref, gated_ref, turned_ref, squares_ref, sums) = refs[:count], refs[count:]
    step = pl.program_id(0)

    @pl.when(step == 0)
    def _():
        sums[...] = jnp.zeros_like(sums)

    if nd:
        assembled(here_ref, pieces, nd, full_ref)
    else:
        full_ref[...] = pieces[0][...]
    value = dot(xn_ref[...], full_ref[...]).astype(BF)
    out_ref[...] = value
    where = tile_range(starts, wide, step)
    for c in range(0, wide, LANES):
        at = slice(c, c + LANES)
        z = value[:, at].astype(F32)
        q = y_ref[:, at] * (z * jax.nn.sigmoid(z))
        gated = (q * gain_ref[:, at]).astype(BF)
        gated_ref[:, at] = gated
        turned_ref[at, :] = gated.T
        sums[where] += q * q

    @pl.when(step == pl.num_programs(0) - 1)
    def _():
        lane = lax.broadcasted_iota(jnp.int32, sums.shape[1:], 1)
        total = jnp.zeros(sums.shape[1:], F32)
        for j in range(len(starts)):
            total = jnp.where(lane == j, jnp.sum(sums[j], axis=1, keepdims=True), total)
        squares_ref[...] = total.T[: squares_ref.shape[0]]


def gated_projection(here, xn, pieces, nd, columns, y, gain, starts, wide):
    if pieces[0].ndim == 2:
        nd = 0
    tokens, depth = xn.shape
    tile = pl.BlockSpec((tokens, wide), lambda i: (0, i))
    ins = [
        pl.BlockSpec(memory_space=pltpu.SMEM),
        pl.BlockSpec((tokens, depth), lambda i: (0, 0)),
        tile,
        pl.BlockSpec((1, wide), lambda i: (0, i)),
    ]
    for piece in pieces:
        lead = piece.shape[:-1]
        ins.append(pl.BlockSpec(lead + (wide,), lambda i, n=len(lead): (0,) * n + (i,)))
    return call(
        functools.partial(gated_kernel, nd, len(pieces), starts, wide),
        grid=(columns // wide,),
        in_specs=ins,
        out_specs=[
            tile,
            pl.BlockSpec((depth, wide), lambda i: (0, i)),
            tile,
            pl.BlockSpec((wide, tokens), lambda i: (i, 0)),
            pl.BlockSpec((8, tokens), lambda i: (0, 0)),
        ],
        out_shape=[
            jax.ShapeDtypeStruct((tokens, columns), BF),
            jax.ShapeDtypeStruct((depth, columns), BF),
            jax.ShapeDtypeStruct((tokens, columns), BF),
            jax.ShapeDtypeStruct((columns, tokens), BF),
            jax.ShapeDtypeStruct((8, tokens), F32),
        ],
        scratch_shapes=[pltpu.VMEM((len(starts), tokens, LANES), F32)],
        name="gated",
    )(here, xn, y, gain, *pieces)


def tri(rows_first):
    a = lax.broadcasted_iota(jnp.int32, (SPAN, SPAN), 0)
    b = lax.broadcasted_iota(jnp.int32, (SPAN, SPAN), 1)
    return (a >= b) if rows_first else (a <= b)


def decays(segc, segr, segp, dt, rate):
    cum = dot(tri(True).astype(F32), dt * rate, precision=HIGH)
    last = cum[SPAN - 1 : SPAN, :]
    keep = jnp.where(segc == segp, jnp.exp(cum), 0.0)
    to_end = jnp.where(segc == segr[:, SPAN - 1 : SPAN], jnp.exp(last - cum), 0.0)
    return cum, cum.T, keep, to_end


def expanded(columns, ones):
    high = columns.astype(BF)
    low = (columns - high.astype(F32)).astype(BF)
    return dot(high, ones) + dot(low, ones)


def head_of_channel(width):
    return (
        lax.broadcasted_iota(jnp.int32, (LANES, width), 1) // HEADDIM
        == lax.broadcasted_iota(jnp.int32, (LANES, width), 0)
    ).astype(BF)


def spread_columns(ref, first, count):
    return [jnp.broadcast_to(ref[:, first + k : first + k + 1], (SPAN, LANES)) for k in range(count)]


def taps(ext, masks, at):
    terms = [ext[pl.ds(HALO - CONV + 1 + k, SPAN), at] for k in range(CONV)]
    return [t * m for t, m in zip(terms, masks)] + terms[CONV - 1 :]


def convolved(terms, weight_ref, at):
    total = weight_ref[CONV : CONV + 1, at] + terms[0] * weight_ref[0:1, at]
    for k in range(1, CONV):
        total = total + terms[k] * weight_ref[k : k + 1, at]
    return total


def forward_kernel(
    heads,
    segp_ref,
    segc_ref,
    segr_ref,
    mask_ref,
    in_a_ref,
    in_b_ref,
    halo_ref,
    weight_ref,
    b_ref,
    c_ref,
    dt_ref,
    rate_ref,
    skip_ref,
    y_ref,
    prior_ref,
    carry,
    to_end_u,
    ext,
    wide_dt,
    wide_keep,
    wide_end,
):
    block = pl.program_id(0)
    width = heads * HEADDIM

    @pl.when(block == 0)
    def _():
        carry[...] = jnp.zeros_like(carry)

    prior_ref[0] = carry[...]
    ext[0:HALO] = halo_ref[0].astype(F32)
    half = in_b_ref.shape[1]
    ext[HALO:, :half] = in_a_ref[:, :half].astype(F32)
    ext[HALO:, half:] = in_b_ref[...].astype(F32)
    segc, segr = segc_ref[...], segr_ref[...]
    dt = dt_ref[...]
    cum, cumr, keep, to_end = decays(segc, segr, segp_ref[block], dt, rate_ref[...])
    bm, cm = b_ref[...], c_ref[...]
    mixing = dot(cm, bm, ((1,), (1,)))
    mixing = jnp.where(tri(True) & (segc == segr), mixing, 0.0)
    heads_ones = head_of_channel(width)
    wide_dt[...] = expanded(dt, heads_ones)
    wide_keep[...] = expanded(keep, heads_ones)
    wide_end[...] = expanded(to_end, heads_ones)
    masks = spread_columns(mask_ref, 0, CONV - 1)
    lo = lax.broadcasted_iota(jnp.int32, (SPAN, LANES), 1) < HEADDIM
    for p in range(heads // 2):
        at = slice(p * LANES, (p + 1) * LANES)
        pre = convolved(taps(ext, masks, at), weight_ref, at)
        x2 = pre * jax.nn.sigmoid(pre)
        u2 = x2 * wide_dt[:, at]
        ub = u2.astype(BF)
        total = dot(cm, carry[:, at].astype(BF)) * wide_keep[:, at] + skip_ref[:, at] * x2
        inner = []
        for h in (2 * p, 2 * p + 1):
            decay = jnp.exp(jnp.minimum(cum[:, h : h + 1] - cumr[h : h + 1, :], 0.0))
            inner.append(dot((decay * mixing).astype(BF), ub))
        y_ref[:, at] = total + jnp.where(lo, inner[0], inner[1])
        to_end_u[:, at] = (u2 * wide_end[:, at]).astype(BF)
    fresh = dot(bm, to_end_u[...], ((0,), (0,)))
    carry[...] = wide_keep[SPAN - 1 : SPAN, :] * carry[...] + fresh


def split_dot(value, ones):
    high = value.astype(BF)
    low = (value - high.astype(F32)).astype(BF)
    return dot(high, ones) + dot(low, ones)


def backward_kernel(
    heads,
    segp_ref,
    segc_ref,
    segr_ref,
    mask_ref,
    in_a_ref,
    in_b_ref,
    halo_ref,
    weight_ref,
    b_ref,
    c_ref,
    dt_ref,
    rate_ref,
    skip_ref,
    y_ref,
    prior_ref,
    dy_ref,
    din_ref,
    dbc_ref,
    ddt_ref,
    drate_ref,
    dsum_ref,
    dcarry,
    after_state,
    keep_dy,
    to_end_u,
    slopes,
    along,
    ext,
    dext,
    wide_dt,
    wide_keep,
    wide_end,
):
    step = pl.program_id(0)
    block = pl.num_programs(0) - 1 - step

    @pl.when(step == 0)
    def _():
        dcarry[...] = jnp.zeros_like(dcarry)
        after_state[...] = jnp.zeros_like(after_state)
        drate_ref[...] = jnp.zeros_like(drate_ref)
        dsum_ref[...] = jnp.zeros_like(dsum_ref)
        dext[SPAN:] = jnp.zeros((HALO, dext.shape[1]), F32)

    ext[0:HALO] = halo_ref[0].astype(F32)
    half = in_b_ref.shape[1]
    ext[HALO:, :half] = in_a_ref[:, :half].astype(F32)
    ext[HALO:, half:] = in_b_ref[...].astype(F32)
    segc, segr = segc_ref[...], segr_ref[...]
    dt = dt_ref[...]
    cum, cumr, keep, to_end = decays(segc, segr, segp_ref[block], dt, rate_ref[...])
    bm, cm = b_ref[...], c_ref[...]
    allowed = tri(False) & (segc == segr)
    mixing = jnp.where(allowed, dot(bm, cm, ((1,), (1,))), 0.0)
    heads_ones = head_of_channel(heads * HEADDIM)
    wide_dt[...] = expanded(dt, heads_ones)
    wide_keep[...] = expanded(keep, heads_ones)
    wide_end[...] = expanded(to_end, heads_ones)
    masks = spread_columns(mask_ref, 0, CONV - 1)
    moved = spread_columns(mask_ref, CONV - 1, CONV - 1)
    lo = lax.broadcasted_iota(jnp.int32, (SPAN, LANES), 1) < HEADDIM
    dmixing = jnp.zeros((SPAN, SPAN), F32)
    for p in range(heads // 2):
        at = slice(p * LANES, (p + 1) * LANES)
        terms = taps(ext, masks, at)
        pre = convolved(terms, weight_ref, at)
        sig = jax.nn.sigmoid(pre)
        x2 = pre * sig
        dt2 = wide_dt[:, at]
        u2 = x2 * dt2
        dyb = dy_ref[:, at]
        dy2 = dyb.astype(F32)
        skip = skip_ref[:, at]
        te2 = wide_end[:, at]
        u_sides = (jnp.where(lo, u2, 0.0).astype(BF), jnp.where(lo, 0.0, u2).astype(BF))
        du = te2 * dot(bm, dcarry[:, at].astype(BF))
        inner = []
        for k in range(2):
            h = 2 * p + k
            decay = jnp.exp(jnp.minimum(cumr[h : h + 1, :] - cum[:, h : h + 1], 0.0))
            inner.append(dot((decay * mixing).astype(BF), dyb))
            dmixing = dmixing + decay * dot(u_sides[k], dyb, ((1,), (1,)))
        du = du + jnp.where(lo, inner[0], inner[1])
        keep_dy[:, at] = (wide_keep[:, at] * dy2).astype(BF)
        to_end_u[:, at] = (te2 * u2).astype(BF)
        slopes[:, at] = dy2 * (y_ref[:, at] - skip * x2) - u2.astype(BF).astype(F32) * du
        along[:, at] = x2 * du
        dpre = (dt2 * du + skip * dy2) * (sig * (1.0 + pre * (1.0 - sig)))
        dext[0:SPAN, at] = dpre
        for k in range(CONV):
            dsum_ref[k : k + 1, at] += jnp.sum(dpre * terms[k], axis=0, keepdims=True)
        dsum_ref[CONV : CONV + 1, at] += jnp.sum(dpre, axis=0, keepdims=True)
        dsum_ref[CONV + 1 : CONV + 2, at] += jnp.sum(dy2 * x2, axis=0, keepdims=True)
        din = dpre * weight_ref[CONV - 1 : CONV, at]
        for k in range(CONV - 1):
            later = dext[pl.ds(CONV - 1 - k, SPAN), at]
            din = din + later * moved[k] * weight_ref[k : k + 1, at]
        din_ref[:, at] = din.astype(BF)
    dext[SPAN:] = dext[0:HALO]
    dmixing = jnp.where(allowed, dmixing, 0.0).astype(BF)
    dstate = dcarry[...].astype(BF)
    prior = prior_ref[0]
    dbc_ref[:, :STATE] = dot(dmixing, cm) + dot(to_end_u[...], dstate, ((1,), (1,)))
    dbc_ref[:, STATE:] = dot(dmixing, bm, ((0,), (0,))) + dot(
        keep_dy[...], prior.astype(BF), ((1,), (1,))
    )
    width = heads * HEADDIM
    ones = (
        lax.broadcasted_iota(jnp.int32, (width, LANES), 0) // HEADDIM
        == lax.broadcasted_iota(jnp.int32, (width, LANES), 1)
    ).astype(BF)
    at_end = jnp.sum(dcarry[...] * after_state[...], axis=0, keepdims=True)
    at_end = split_dot(jnp.broadcast_to(at_end, (16, width)), ones)[:1]
    dcum = split_dot(slopes[...], ones)
    da = dot(tri(False).astype(F32), dcum, precision=HIGH) + at_end
    ddt_ref[...] = rate_ref[...] * da + split_dot(along[...], ones)
    drate_ref[...] += jnp.sum(dt * da, axis=0, keepdims=True)
    fresh = dot(cm, keep_dy[...], ((0,), (0,)))
    dcarry[...] = wide_keep[SPAN - 1 : SPAN, :] * dcarry[...] + fresh
    after_state[...] = prior


def scan_specs(heads, at, in_widths):
    width = heads * HEADDIM

    def rows(n):
        return pl.BlockSpec((SPAN, n), lambda i: (at(i), 0))

    def whole(*shape):
        return pl.BlockSpec(shape, lambda i: (0,) * len(shape))

    ins = [
        pl.BlockSpec(memory_space=pltpu.SMEM),
        rows(1),
        pl.BlockSpec((1, SPAN), lambda i: (0, at(i))),
        rows(LANES),
        rows(in_widths[0]),
        rows(in_widths[1]),
        pl.BlockSpec((1, HALO, width), lambda i: (at(i), 0, 0)),
        whole(8, width),
        rows(STATE),
        rows(STATE),
        rows(LANES),
        whole(1, LANES),
        whole(1, width),
    ]
    prior = pl.BlockSpec((1, STATE, width), lambda i: (at(i), 0, 0))
    return rows, whole, ins, prior


def scan_forward(heads, blocks, operands):
    rows, whole, ins, prior = scan_specs(heads, lambda i: i, [operands[n].shape[1] for n in (4, 5)])
    width = heads * HEADDIM
    return call(
        functools.partial(forward_kernel, heads),
        grid=(blocks,),
        in_specs=ins,
        out_specs=[rows(width), prior],
        out_shape=[
            jax.ShapeDtypeStruct((blocks * SPAN, width), F32),
            jax.ShapeDtypeStruct((blocks, STATE, width), F32),
        ],
        scratch_shapes=[
            pltpu.VMEM((STATE, width), F32),
            pltpu.VMEM((SPAN, width), BF),
            pltpu.VMEM((HALO + SPAN, width), F32),
            pltpu.VMEM((SPAN, width), F32),
            pltpu.VMEM((SPAN, width), F32),
            pltpu.VMEM((SPAN, width), F32),
        ],
        name="scan_forward",
    )(*operands)


def scan_backward(heads, blocks, operands, y, priors, dy):
    rows, whole, ins, prior = scan_specs(
        heads, lambda i: blocks - 1 - i, [operands[n].shape[1] for n in (4, 5)]
    )
    width = heads * HEADDIM
    return call(
        functools.partial(backward_kernel, heads),
        grid=(blocks,),
        in_specs=ins + [rows(width), prior, rows(width)],
        out_specs=[rows(width), rows(2 * STATE), rows(LANES), whole(1, LANES), whole(8, width)],
        out_shape=[
            jax.ShapeDtypeStruct((blocks * SPAN, width), BF),
            jax.ShapeDtypeStruct((blocks * SPAN, 2 * STATE), F32),
            jax.ShapeDtypeStruct((blocks * SPAN, LANES), F32),
            jax.ShapeDtypeStruct((1, LANES), F32),
            jax.ShapeDtypeStruct((8, width), F32),
        ],
        scratch_shapes=[
            pltpu.VMEM((STATE, width), F32),
            pltpu.VMEM((STATE, width), F32),
            pltpu.VMEM((SPAN, width), BF),
            pltpu.VMEM((SPAN, width), BF),
            pltpu.VMEM((SPAN, width), F32),
            pltpu.VMEM((SPAN, width), F32),
            pltpu.VMEM((HALO + SPAN, width), F32),
            pltpu.VMEM((SPAN + HALO, width), F32),
            pltpu.VMEM((SPAN, width), F32),
            pltpu.VMEM((SPAN, width), F32),
            pltpu.VMEM((SPAN, width), F32),
        ],
        name="scan_backward",
    )(*operands, y, priors, dy)


def as_columns(rows):
    few, tokens = rows.shape
    return jnp.concatenate([rows, jnp.zeros((LANES - few, tokens), F32)]).T


def level_block(pieces, spot):
    piece, lead = spot
    return pieces[piece][lead + (slice(None), slice(None))].astype(F32)


def upper_kernel(where, plan, nd, tok, ns, here_ref, range_ref, count_ref, ratio_ref, q_turned, *refs):
    count = 3 + 2 * LEVELS
    pieces, outs = refs[:count], refs[count:]
    upper_ref, grad_refs, coefs = outs[0], outs[1 : 2 * nd], outs[2 * nd]

    @pl.when(pl.program_id(0) == 0)
    def _():
        rows = [count_ref[j, w] * ratio_ref[w : w + 1, :] for j in range(len(plan)) for w in range(LEVELS)]
        coefs[...] = as_columns(jnp.concatenate(rows))

    for k in range(ns):
        at = here_ref[0] ^ k
        rows = pl.ds(pl.multiple_of(at * tok, tok), tok)
        levels = [level_block(pieces, where[w][k]) for w in range(LEVELS)]
        for j in range(len(plan)):
            total = None
            for w in plan[j]:
                n = j * LEVELS + w
                term = coefs[rows, n : n + 1] * levels[w]
                total = term if total is None else total + term
            upper_ref[j, rows, :] = total.astype(BF)
    count = q_turned.shape[0] // nd
    for k in range(nd):
        index = here_ref[1] ^ k
        rows = pl.ds(pl.multiple_of(index * count, count), count)
        value = dot(q_turned[rows, :], upper_ref[range_ref[index]]).astype(BF)
        if k:
            grad_refs[2 * k - 1][...] = value[: count // 2]
            grad_refs[2 * k][...] = value[count // 2 :]
        else:
            grad_refs[0][...] = value


def products_kernel(where, plan, lanes, tok, ns, nd, here_ref, count_ref, q_ref, *refs):
    count = 3 + 2 * LEVELS
    held_ref, pieces, outs = refs[0], refs[1 : 1 + count], refs[1 + count :]
    prod_refs, inner_ref, w_ref, sums = outs[:ns], outs[ns], outs[ns + 1], outs[ns + 2]
    step = pl.program_id(0)
    rows_of = w_ref.shape[0] // nd
    for k in range(nd):
        at = pl.multiple_of((here_ref[1] ^ k) * rows_of, rows_of)
        w_ref[pl.ds(at, rows_of), :] = held_ref[:, k].reshape(rows_of, w_ref.shape[1])

    @pl.when(step == 0)
    def _():
        sums[...] = jnp.zeros_like(sums)

    for k in range(ns):
        at = here_ref[0] ^ k
        rows = pl.ds(pl.multiple_of(at * tok, tok), tok)
        values = [dot(q_ref[rows, a:b], w_ref[a:b, :]) for a, b in lanes]
        for j, value in enumerate(values):
            prod_refs[k][j] = value.astype(BF)
        for w in range(LEVELS):
            total = None
            for j in range(len(lanes)):
                if w in plan[j]:
                    term = values[j] * count_ref[j, w]
                    total = term if total is None else total + term
            part = total * level_block(pieces, where[w][k])
            folded = part[:, :LANES]
            for c in range(LANES, part.shape[1], LANES):
                folded = folded + part[:, c : c + LANES]
            sums[w, rows, :] += folded

    @pl.when(step == pl.num_programs(0) - 1)
    def _():
        lane = lax.broadcasted_iota(jnp.int32, sums.shape[1:], 1)
        total = jnp.zeros(sums.shape[1:], F32)
        for w in range(LEVELS):
            total = jnp.where(lane == w, jnp.sum(sums[w], axis=1, keepdims=True), total)
        inner_ref[...] = total.T[:LEVELS]


def gate_kernel(
    starts, wide, count_ref, upper_ref, w_ref, y_ref, z_ref, gain_ref, ratio_ref, mean_ref, dy_ref, dz_ref, grad_ref, coefs
):
    step = pl.program_id(0)

    @pl.when(step == 0)
    def _():
        cubes = ratio_ref[...] * ratio_ref[...] * ratio_ref[...] * mean_ref[...]
        rows = []
        for j in range(len(starts)):
            total = cubes[0:1] * count_ref[j, 0]
            for w in range(1, LEVELS):
                total = total + cubes[w : w + 1] * count_ref[j, w]
            rows.append(total)
        columns = as_columns(jnp.concatenate(rows))
        for j in range(len(starts)):
            coefs[j] = jnp.broadcast_to(columns[:, j : j + 1], coefs.shape[1:])

    grad_all = dot(upper_ref[0], w_ref[...], ((1,), (1,)))
    coef = coefs[tile_range(starts, wide, step)]
    for c in range(0, wide, LANES):
        at = slice(c, c + LANES)
        grad_t = grad_all[:, at]
        z = z_ref[:, at].astype(F32)
        sig = jax.nn.sigmoid(z)
        act = z * sig
        y = y_ref[:, at]
        q = y * act
        dq = gain_ref[:, at] * grad_t - q * coef
        dy_ref[:, at] = (dq * act).astype(BF)
        dz_ref[:, at] = (dq * y * (sig * (1.0 + z * (1.0 - sig)))).astype(BF)
        grad_ref[0:1, at] = jnp.sum(q * grad_t, axis=0, keepdims=True)


def tile_range(starts, wide, step):
    index = 0
    for start in starts[1:]:
        index = index + jnp.where(step * wide >= start, 1, 0)
    return index


def mixed_kernel(plan, split, ns, tok, here_ref, count_ref, ratio_ref, x_ref, *refs):
    shares, out_ref = refs[:-1], refs[-1]
    at = pl.ds(pl.multiple_of(here_ref[0] * tok, tok), tok)
    ratios = as_columns(ratio_ref[:, at])
    x = x_ref[...].astype(F32)
    for w in range(LEVELS):
        total = None
        for k in range(ns):
            for j in plan[w]:
                at = (k, j) if k < 3 or j < split else (k + 1, j - split)
                term = shares[at[0]][at[1]].astype(F32) * count_ref[k, j * LEVELS + w]
                total = term if total is None else total + term
        out_ref[w] = (x + ratios[:, w : w + 1] * total).astype(BF)


def dp_terms(others):
    return [swapped(other, "dp", k + 1) for k, other in enumerate(others)]


def over_seq(value):
    dense = value.reshape(-1, LANES)
    total = dense
    for k in range(1, lax.axis_size("seq")):
        total = total + swapped(dense, "seq", k)
    return total.reshape(value.shape)


def fsdp_half(own, got):
    nf = lax.axis_size("fsdp")
    f = lax.axis_index("fsdp")

    def part(offset):
        total = picked(own, f ^ offset).astype(F32)
        for other in got:
            total = total + picked(other, f ^ offset).astype(F32)
        return total.astype(BF)

    kept = jnp.stack([part(e) for e in range(0, nf, 2)])
    sent = jnp.stack([part(e ^ 1) for e in range(0, nf, 2)])
    return kept, sent


def fsdp_rest(kept, got):
    k = 2
    while k < lax.axis_size("fsdp"):
        total = (kept.astype(F32) + got.astype(F32)).astype(BF)
        kept, sent = total[::2], total[1::2]
        got = swapped(sent, "fsdp", k)
        k *= 2
    return kept[0], got[0]


def shards(
    tokens,
    lengths,
    norm_gain,
    w_in,
    w_dt,
    conv_w,
    conv_b,
    dt_bias,
    a_log,
    skip,
    gate_gain,
    w_out,
    cotangent,
):
    nd, ns, nf = lax.axis_size("dp"), lax.axis_size("seq"), lax.axis_size("fsdp")
    d, s, f = lax.axis_index("dp"), lax.axis_index("seq"), lax.axis_index("fsdp")
    tok = tokens.shape[1]
    length = ns * tok
    blocks = length // SPAN
    heads = HEADS // ns
    run = heads // nd
    width = heads * HEADDIM
    own_bc = 2 * STATE // ns
    used = width + own_bc
    cols = -(-(used + heads) // LANES) * LANES
    rows_in = w_in.shape[0]
    reach = CONV - 1

    levels = np.array(
        [[level_of(dd * (HEADS // nd) + ss * run + i) for dd in range(nd) for i in range(run)] for ss in range(ns)]
    )
    cuts = [0] + [h for h in range(1, heads) if (levels[:, h] != levels[:, h - 1]).any()] + [heads]
    ranges = [(a, b) for a, b in zip(cuts, cuts[1:])]
    range_level = np.array([[levels[ss, a] for a, _ in ranges] for ss in range(ns)])
    counts = (range_level[:, :, None] <= np.arange(LEVELS)[None, None, :]).astype(np.float32)
    counted = picked(jnp.asarray(counts), s)
    theirs = picked(
        jnp.asarray(np.stack([[counts[i ^ k].reshape(-1) for k in range(ns)] for i in range(ns)])), s
    )
    lowest = [int(range_level[ss].min()) for ss in range(ns)]

    def by_head(vector):
        lead = vector.shape[:-1]
        per = vector.shape[-1] // HEADS
        cut = vector.reshape(lead + (nd, ns, run * per))
        mine = lax.dynamic_index_in_dim(cut, s, len(lead) + 1, keepdims=False)
        return mine.reshape(lead + (heads * per,))

    def for_groups(matrix):
        per = matrix.shape[1] // HEADS
        cut = matrix.reshape(matrix.shape[0], nd, ns, run * per)
        return jnp.transpose(cut, (2, 0, 1, 3)).reshape(ns, matrix.shape[0], heads * per)

    def from_groups(stack):
        per = stack.shape[2] // heads
        cut = stack.reshape(ns, stack.shape[1], nd, run * per)
        return jnp.transpose(cut, (1, 2, 0, 3)).reshape(stack.shape[1], HEADS * per)

    pad_cols = cols - used - heads
    half = width // 2
    first = half + cols - width
    group_x = for_groups(w_in[:, INNER : 2 * INNER])
    stack = jnp.concatenate(
        [
            group_x[:, :, :half],
            w_in[:, 2 * INNER :].reshape(rows_in, ns, own_bc).transpose(1, 0, 2),
            for_groups(w_dt),
            jnp.zeros((ns, rows_in, pad_cols), BF),
            group_x[:, :, half:],
            for_groups(w_in[:, :INNER]),
        ],
        axis=2,
    )
    own_x = tokens[0].astype(F32)
    scale = lax.rsqrt(jnp.mean(own_x * own_x, axis=-1, keepdims=True) + EPS)
    xn_own = (own_x * scale * norm_gain).astype(BF)
    xn_across = swapped(xn_own, "seq", 2)
    xn_pieces = [xn_own, swapped(xn_own, "seq", 1), xn_across, swapped(xn_across, "seq", 1)]
    arrived = [picked(stack, s)] + [swapped(picked(stack, s ^ k), "seq", k) for k in range(1, ns)]
    mine = filled((ns, rows_in, stack.shape[2]), [(p, None, (s ^ k, None, None)) for k, p in enumerate(arrived)])
    mine_z = mine[:, :, cols:]

    def needed(at, level):
        return min(lowest[at], lowest[at ^ 1]) <= level

    halves = [cotangent[w : w + 2, 0] for w in range(0, LEVELS, 2)]
    singles = [cotangent[w, 0] for w in range(LEVELS)]

    def beside(level, *others):
        block = after(halves[level // 2], *others)
        return swapped(block, "seq", 1, lambda i, j: needed(j, level + 1))

    def across(level, *others):
        block = after(singles[level], *others)
        return swapped(block, "seq", 2, lambda i, j: needed(j, level))

    def far(level, block):
        return swapped(block, "seq", 1, lambda i, j: needed(j, level))

    positions = jnp.arange(length, dtype=jnp.int32)
    ends = jnp.cumsum(lengths[0])[:-1]
    seg = jnp.sum((positions[:, None] >= ends[None, :]).astype(jnp.int32), axis=1)
    seg_before = jnp.concatenate([jnp.full((1,), -1, jnp.int32), seg[SPAN - 1 : length - 1 : SPAN]])
    seg_pad = jnp.concatenate([jnp.full((reach,), -1, jnp.int32), seg])
    masks = [(seg_pad[k : k + length] == seg) for k in range(reach)]
    mask_cols = [m.astype(F32) for m in masks]
    mask_cols += [jnp.pad(m, (0, reach - k))[reach - k :] for k, m in enumerate(mask_cols)]
    mask_cols = jnp.pad(jnp.stack(mask_cols, axis=1), ((0, 0), (0, LANES - 2 * reach)))

    def conv_params(s_part, bc_part):
        return by_head(s_part), bc_part

    weight_s = jnp.concatenate(
        [by_head(conv_w[:, :INNER]), by_head(conv_b[None, :INNER]), jnp.zeros((3, width), F32)]
    )
    weight_r = jnp.pad(
        lax.dynamic_slice_in_dim(conv_w, INNER + s * own_bc, own_bc, 1), ((0, 0), (0, cols - used))
    )
    bias_r = jnp.pad(
        lax.dynamic_slice_in_dim(conv_b, INNER + s * own_bc, own_bc, 0), (0, cols - used)
    )
    bias = by_head(dt_bias)
    rate = -jnp.exp(by_head(a_log))
    skip_own = by_head(skip)
    gain = by_head(gate_gain)

    def over_fsdp(chunk):
        return lax.all_gather(chunk, "fsdp", axis=0, tiled=False)

    def over_dp(held):
        return [held] + [swapped(held, "dp", j) for j in range(1, nd)]

    def whole(pieces, columns):
        moves = [
            (piece, i, (d ^ j, None, i, None, None)) for j, piece in enumerate(pieces) for i in range(nf)
        ]
        return filled((nd, ns, nf, rows_in, columns), moves).reshape(D, columns)

    held_a = over_fsdp(mine[:, :, :first])
    held_b = over_fsdp(mine[:, :, first:cols])
    other_out = [swapped(w_out, "dp", j) for j in range(1, nd)]
    held_a, other_out, xn_pieces[2] = together(held_a, other_out, xn_pieces[2])
    small_ones = (seg, seg_before, mask_cols, weight_s, weight_r, bias_r, bias, rate, skip_own, gain, theirs)
    held_a, small_ones, halves, singles = together(held_a, small_ones, halves, singles)
    seg, seg_before, mask_cols, weight_s, weight_r, bias_r, bias, rate, skip_own, gain, theirs = small_ones
    near_high, near_low = beside(2, held_a), beside(0, held_a)
    chip3 = across(3, held_a)
    pieces_a = over_dp(held_a)
    held_b, pieces_a, chip3, near_high, xn_pieces = together(
        held_b, pieces_a, chip3, near_high, xn_pieces
    )
    xn = filled((ns, tok, D), [(p, None, (s ^ k, None, None)) for k, p in enumerate(xn_pieces)])
    xn = xn.reshape(length, D)

    far3 = far(3, chip3)
    pieces_b = over_dp(held_b)
    held_z = over_fsdp(after(mine_z, held_a))
    pair_out = jnp.stack([w_out] + other_out)

    xn_turned = xn.T
    here = jnp.stack([s, d]).astype(jnp.int32)
    full_a = whole(pieces_a, first)
    proj_a = dot(xn, full_a).astype(BF)

    proj_r = proj_a[:, half:]
    mixer = jnp.concatenate([jnp.zeros((reach, cols - width), BF), proj_r], axis=0)

    def taken(k):
        rows = mixer[k : k + length].astype(F32)
        return rows * mask_cols[:, k : k + 1] if k < reach else rows

    pre_r = bias_r
    for k in range(CONV):
        pre_r = pre_r + taken(k) * weight_r[k]
    bc_own = jax.nn.silu(pre_r).astype(BF)[:, :own_bc]
    bc_across = swapped(bc_own, "seq", 2)
    bc = [bc_own, swapped(bc_own, "seq", 1), bc_across, swapped(bc_across, "seq", 1)]
    chip2, chip1 = across(2, bc[2]), across(1, bc[2])
    full_b = whole(pieces_b, half)
    proj_b = dot(xn, after(full_b, proj_a, xn_turned, bc[2])).astype(BF)
    proj_b, far3, near_low, held_z = together(proj_b, far3, near_low, held_z)
    pieces_z = over_dp(held_z)
    held_out = over_fsdp(after(pair_out, proj_b))
    bc = reordered_by_xor(bc, s)
    b_in = jnp.concatenate(bc[: ns // 2], axis=1)
    c_out = jnp.concatenate(bc[ns // 2 :], axis=1)

    def padded(rows):
        return jnp.pad(rows, ((0, 0), (0, LANES - rows.shape[1])))

    pre_dt = proj_r[:, own_bc : own_bc + heads].astype(F32) + bias
    steps = jax.nn.softplus(pre_dt)
    tails = [
        p.reshape(blocks, SPAN, p.shape[1])[: blocks - 1, SPAN - HALO :, :half] for p in (proj_a, proj_b)
    ]
    operands = (
        seg_before,
        seg[:, None],
        seg[None, :],
        mask_cols,
        proj_a,
        proj_b,
        jnp.concatenate([jnp.zeros((1, HALO, width), BF), jnp.concatenate(tails, axis=2)]),
        weight_s,
        b_in,
        c_out,
        padded(steps),
        padded(rate[None, :]),
        jnp.repeat(skip_own, HEADDIM)[None, :],
    )
    y, priors = scan_forward(heads, blocks, operands)
    y, chip2 = together(y, chip2)
    far2, chip0 = far(2, chip2), across(0, y)
    parts = pieces_z if rows_in % 16 == 0 else [whole(pieces_z, width)]
    lanes = [(a * HEADDIM, b * HEADDIM) for a, b in ranges]
    starts = [a for a, _ in lanes]
    wide = min(min(b - a for a, b in lanes), TILE)
    proj_z, full_z, q_gain, q_turned, squares = gated_projection(
        here, xn, parts, nd, width, y, gain[None], starts, wide
    )
    squares, chip1 = together(squares[: len(lanes)], chip1)
    far1 = far(1, chip1)
    widths = np.array([[(HEADS >> 3 - w) * HEADDIM] for w in range(LEVELS)], np.float32)
    per_level = jnp.sum(counted[:, :, None] * squares[:, None, :], axis=0)
    ratio, chip0 = together(lax.rsqrt(over_seq(per_level) / widths + EPS), chip0)
    far0 = far(0, chip0)

    plan = [[w for w in range(LEVELS) if range_level[:, j].min() <= w] for j in range(len(lanes))]
    out_rows = width // nd
    range_of = [next(j for j, (a, b) in enumerate(lanes) if a <= i * out_rows < b) for i in range(nd)]
    smem = pl.BlockSpec(memory_space=pltpu.SMEM)
    cot_pieces = [cotangent, near_low, near_high, chip0, chip1, chip2, chip3, far0, far1, far2, far3]
    cot_specs = [pl.BlockSpec((LEVELS, 1, tok, WIDE), lambda i: (0, 0, 0, i))]
    cot_specs += [pl.BlockSpec((2, tok, WIDE), lambda i: (0, 0, i))] * 2
    cot_specs += [pl.BlockSpec((tok, WIDE), lambda i: (0, i))] * (2 * LEVELS)
    where = [[(0, (w, 0)), (1 + w // 2, (w % 2,)), (3 + w, ()), (3 + LEVELS + w, ())] for w in range(LEVELS)]
    upper, *grad_out = call(
        functools.partial(upper_kernel, where, plan, nd, tok, ns),
        grid=(D // WIDE,),
        in_specs=[
            smem,
            smem,
            smem,
            pl.BlockSpec((LEVELS, length), lambda i: (0, 0)),
            pl.BlockSpec((width, length), lambda i: (0, 0)),
        ]
        + cot_specs,
        out_specs=[pl.BlockSpec((len(lanes), length, WIDE), lambda i: (0, 0, i))]
        + [pl.BlockSpec((out_rows, WIDE), lambda i: (0, i))]
        + [pl.BlockSpec((out_rows // 2, WIDE), lambda i: (0, i))] * (2 * nd - 2),
        out_shape=[jax.ShapeDtypeStruct((len(lanes), length, D), BF)]
        + [jax.ShapeDtypeStruct((out_rows, D), BF)]
        + [jax.ShapeDtypeStruct((out_rows // 2, D), BF)] * (2 * nd - 2),
        scratch_shapes=[pltpu.VMEM((length, LANES), F32)],
        name="upper",
    )(here, jnp.asarray(range_of, jnp.int32), counted, ratio, q_turned, *cot_pieces)
    out_first, out_second = dp_terms(grad_out[1::2]), dp_terms(grad_out[2::2])

    held_out, upper = together(held_out, upper)
    *shares, inner, full_out = call(
        functools.partial(products_kernel, where, plan, lanes, tok, ns, nd),
        grid=(D // WIDE,),
        in_specs=[
            smem,
            smem,
            pl.BlockSpec((length, width), lambda i: (0, 0)),
        ]
        + [pl.BlockSpec((nf, nd, w_out.shape[0], WIDE), lambda i: (0, 0, 0, i))]
        + cot_specs,
        out_specs=[pl.BlockSpec((len(lanes), tok, WIDE), lambda i: (0, 0, i))] * ns
        + [pl.BlockSpec((LEVELS, length), lambda i: (0, 0))]
        + [pl.BlockSpec((width, WIDE), lambda i: (0, i))],
        out_shape=[jax.ShapeDtypeStruct((len(lanes), tok, D), BF)] * ns
        + [jax.ShapeDtypeStruct((LEVELS, length), F32)]
        + [jax.ShapeDtypeStruct((width, D), BF)],
        scratch_shapes=[pltpu.VMEM((LEVELS, length, LANES), F32)],
        name="products",
    )(here, counted, q_gain, held_out, *cot_pieces)
    means, out_first = together(over_seq(inner) / widths, out_first)
    shares[1:3] = [swapped(after(shares[k], means), "seq", k) for k in (1, 2)]
    split = (len(lanes) + 1) // 2
    third = [swapped(after(shares[3][:split], shares[1]), "seq", 3), shares[3][split:]]

    cols_of = pl.BlockSpec((length, wide), lambda i: (0, i))
    scalars = pl.BlockSpec((LEVELS, length), lambda i: (0, 0))
    dy, dz, grad_gate = call(
        functools.partial(gate_kernel, starts, wide),
        grid=(width // wide,),
        in_specs=[
            smem,
            pl.BlockSpec((1, length, D), lambda i: (tile_range(starts, wide, i), 0, 0)),
            pl.BlockSpec((wide, D), lambda i: (i, 0)),
            cols_of,
            cols_of,
            pl.BlockSpec((1, wide), lambda i: (0, i)),
            scalars,
            scalars,
        ],
        out_specs=[cols_of, cols_of, pl.BlockSpec((8, wide), lambda i: (0, i))],
        out_shape=[
            jax.ShapeDtypeStruct((length, width), BF),
            jax.ShapeDtypeStruct((length, width), BF),
            jax.ShapeDtypeStruct((8, width), F32),
        ],
        scratch_shapes=[pltpu.VMEM((len(lanes), length, LANES), F32)],
        name="gate_backward",
    )(counted, upper, full_out, y, proj_z, gain[None], ratio, means)
    grad_gate = grad_gate[0]

    def in_terms(dproj, at, first=0, columns=None):
        columns = columns or dproj.shape[1]
        out = row_terms(xn_turned, dproj, at, nd, ns, nf, first, columns)
        return out.reshape(nf, ns * rows_in, columns)

    z_other = [in_terms(dz, d ^ k) for k in range(1, nd)]
    z_got = dp_terms(z_other)
    dy, out_second, shares[1] = together(after(dy, *z_other), out_second, shares[1])
    chunk = (nf, out_rows // nf, D)
    out_got = [jnp.concatenate([u, v]).reshape(chunk) for u, v in zip(out_first, out_second)]
    out_kept, out_sent = fsdp_half(grad_out[0].reshape(chunk), out_got)
    dy = after(dy, out_sent)
    out_half = swapped(out_sent, "fsdp", 1)

    dproj_s, dbc, ddt, drate, dsum = scan_backward(heads, blocks, operands, y, priors, dy)
    dproj_s, dbc, out_half, shares[2], third = together(dproj_s, dbc, out_half, shares[2], third)
    out_pair = fsdp_rest(out_kept, out_half)

    dbc = dbc.astype(BF)
    slices = reordered_by_xor([dbc[:, j * own_bc : (j + 1) * own_bc] for j in range(ns)], s)
    beside_bc = swapped(jnp.concatenate([slices[1], slices[3]], axis=1), "seq", 1)
    sum_bc = jnp.concatenate([slices[0], slices[2]], axis=1).astype(F32) + beside_bc.astype(F32)
    across_bc = swapped(sum_bc[:, own_bc:].astype(BF), "seq", 2)

    z_own = in_terms(after(dz, dproj_s), d)
    z_own, z_got = together(z_own, z_got)
    z_kept, z_sent = fsdp_half(z_own, z_got)
    z_half = swapped(z_sent, "fsdp", 1)
    late_s = after(dproj_s, z_sent)
    left_other = [in_terms(late_s, d ^ k, 0, half) for k in range(1, nd)]
    left_got = dp_terms(left_other)
    third[1] = swapped(after(third[1], across_bc), "seq", 3)
    dbc_own = sum_bc[:, :own_bc] + across_bc.astype(F32)
    dproj_r, small_sums = small_back(
        own_bc,
        pre_r,
        padded(after(dbc_own, *left_other)),
        proj_r,
        mask_cols,
        weight_r,
        ddt,
        padded(pre_dt),
    )

    late_s, late_r = after(dproj_s, *left_other), dproj_r
    right_other = [
        jnp.concatenate([in_terms(late_s, d ^ k, half, half), in_terms(late_r, d ^ k)], axis=2)
        for k in range(1, nd)
    ]
    right_got = dp_terms(right_other)

    dxn = input_grad(dz, dproj_s, after(dproj_r, *right_other), full_z, full_a, full_b, ns, tok)
    pair = swapped(jnp.stack([picked(dxn, s ^ 1), picked(dxn, s ^ 3)]), "seq", 1)

    dxn, z_half, left_got, out_pair = together(dxn, z_half, left_got, out_pair)
    z_pair = fsdp_rest(z_kept, z_half)
    own_s = in_terms(after(dproj_s, dxn), d)
    left_kept, left_sent = fsdp_half(own_s[:, :, :half], left_got)
    left_half = swapped(left_sent, "fsdp", 1)
    own_r = in_terms(after(dproj_r, left_sent), d)
    flat = flattened(
        [
            jnp.concatenate([dsum[:CONV], small_sums[:CONV, :own_bc]], axis=1).reshape(-1),
            dsum[CONV],
            small_sums[CONV, :own_bc],
            grad_gate,
            small_sums[CONV + 1, :heads],
            drate[0, :heads] * rate,
            jnp.sum(dsum[CONV + 1].reshape(heads, HEADDIM), axis=1),
        ]
    )
    near = picked(dxn, s).astype(F32) + pair[0].astype(F32)
    far_sum = (picked(dxn, s ^ 2).astype(F32) + pair[1].astype(F32)).astype(BF)
    dxn_across = swapped(far_sum, "seq", 2)
    right_got, far_sum, left_half = together(right_got, far_sum, left_half)
    left_pair = fsdp_rest(left_kept, left_half)
    own_right = jnp.concatenate([own_s[:, :, half:], own_r], axis=2)
    right_kept, right_sent = fsdp_half(own_right, right_got)
    right_half = swapped(right_sent, "fsdp", 1)

    mixed = call(
        functools.partial(
            mixed_kernel,
            [[j for j in range(len(lanes)) if range_level[:, j].min() <= w] for w in range(LEVELS)],
            split,
            ns,
            tok,
        ),
        grid=(D // WIDE,),
        in_specs=[
            smem,
            smem,
            pl.BlockSpec((LEVELS, length), lambda i: (0, 0)),
            pl.BlockSpec((tok, WIDE), lambda i: (0, i)),
        ]
        + [pl.BlockSpec((p.shape[0], tok, WIDE), lambda i: (0, 0, i)) for p in shares[:3] + third],
        out_specs=pl.BlockSpec((LEVELS, tok, WIDE), lambda i: (0, 0, i)),
        out_shape=jax.ShapeDtypeStruct((LEVELS, tok, D), BF),
        name="mixed",
    )(here, theirs, ratio, tokens[0], *after(shares[:3] + third, right_sent))[:, None]
    mixed, dxn_across = together(mixed, dxn_across)
    dxn_own = near + dxn_across.astype(F32)
    grad_norm = jnp.sum(dxn_own * own_x * scale, axis=0)
    scaled = norm_gain * dxn_own
    dx = scale * scaled - own_x * scale**3 * jnp.mean(own_x * scaled, axis=-1, keepdims=True)
    dx = (dx + jnp.sum(after(cotangent, mixed)[:, 0].astype(F32), axis=0)).astype(BF)
    flat = jnp.concatenate([flat, grad_norm.reshape(-1, LANES)])
    flat = butterfly(flat, "dp")
    right_half, flat, dx = together(right_half, flat, dx)
    right_pair = fsdp_rest(right_kept, right_half)

    def whole_sum(pair):
        total = (pair[0].astype(F32) + pair[1].astype(F32)).astype(BF)
        return total.reshape(ns, rows_in, total.shape[1])

    z_pair, left_pair = together(z_pair, left_pair)
    early = jnp.concatenate([whole_sum(z_pair), whole_sum(left_pair)], axis=2)
    early_got = [picked(early, s)] + [swapped(picked(early, s ^ k), "seq", k) for k in range(1, ns)]
    flat = butterfly(flat, "fsdp")
    early_got, right_pair, flat = together(early_got, right_pair, flat)
    late = whole_sum(right_pair)
    late_got = [picked(late, s)] + [swapped(picked(late, s ^ k), "seq", k) for k in range(1, ns)]
    early = jnp.stack(reordered_by_xor(early_got, s))
    late = jnp.stack(reordered_by_xor(late_got, s))
    got_z = early[:, :, :width]
    got_x = jnp.concatenate([early[:, :, width:], late], axis=2)
    sum_out = out_pair[0].astype(F32) + out_pair[1].astype(F32)


    sum_in = jnp.concatenate(
        [
            from_groups(got_z),
            from_groups(got_x[:, :, :width]),
            jnp.transpose(got_x[:, :, width:used], (1, 0, 2)).reshape(rows_in, 2 * STATE),
        ],
        axis=1,
    ).astype(F32)
    sum_dt = from_groups(got_x[:, :, used : used + heads]).astype(F32)

    sizes = [CONV * used, used, width, heads, heads, heads]
    filling = -sum(sizes) % 1024
    sizes += [filling, D]
    every = seq_gather(flat, s).reshape(ns, -1)
    starts = np.cumsum([0] + sizes)
    pieces = [every[:, a : a + n] for a, n in zip(starts, sizes)]

    def heads_back(rows):
        lead = rows.shape[1:-1]
        cut = rows.reshape((ns,) + lead + (nd, rows.shape[-1] // nd))
        order = tuple(range(1, 1 + len(lead))) + (1 + len(lead), 0, 2 + len(lead))
        return jnp.transpose(cut, order).reshape(lead + (-1,))

    conv_rows = pieces[0].reshape(ns, CONV, used)
    conv_all = jnp.concatenate(
        [
            heads_back(conv_rows[:, :, :width]),
            jnp.transpose(conv_rows[:, :, width:], (1, 0, 2)).reshape(CONV, 2 * STATE),
        ],
        axis=1,
    )
    bias_all = jnp.concatenate([heads_back(pieces[1][:, :width]), pieces[1][:, width:].reshape(-1)])
    return (
        mixed,
        dx[None],
        jnp.sum(pieces[7], axis=0),
        sum_in,
        sum_dt,
        conv_all,
        bias_all,
        heads_back(pieces[3]),
        heads_back(pieces[4]),
        heads_back(pieces[5]),
        heads_back(pieces[2]),
        sum_out,
    )


def solution(mesh):
    rows = P(("dp", "seq", "fsdp"), None)
    held = P(("dp", "fsdp"), "seq", None)
    levels = P(None, ("dp", "fsdp"), "seq", None)
    placed = (held, P(("dp", "fsdp"), None), P(), rows, rows, P(), P(), P(), P(), P(), P(), rows, levels)
    return jax.shard_map(
        shards,
        mesh=mesh,
        in_specs=placed,
        out_specs=(levels, held, P(), rows, rows, P(), P(), P(), P(), P(), P(), rows),
        check_vma=False,
    )
```

```python
import functools

import jax
import jax.numpy as jnp
import numpy as np
from jax import lax
from jax.experimental import pallas as pl
from jax.experimental.pallas import tpu as pltpu
from jax.sharding import PartitionSpec as P

D = 2048
HEADS = 64
HEADDIM = 64
STATE = 128
CONV = 4
SPAN = 128
INNER = 4096
EPS = 1e-05
LEVELS = 4
BF = jnp.bfloat16
F32 = jnp.float32
HIGH = lax.Precision.HIGHEST
LANES = 128
HALO = 16
TILE = 256
WIDE = 512
VMEM_LIMIT = 48 * 1024 * 1024


def dot(a, b, dims=((1,), (0,)), precision=None):
    return lax.dot_general(a, b, (dims, ((), ())), preferred_element_type=F32, precision=precision)


def silu_slope(v):
    sig = jax.nn.sigmoid(v)
    return sig * (1.0 + v * (1.0 - sig))


def level_of(head):
    return 0 if head < 8 else 1 if head < 16 else 2 if head < 32 else 3


def swapped(value, axis, k, keep=None):
    pairs = [(i, i ^ k) for i in range(lax.axis_size(axis))]
    if keep is not None:
        pairs = [p for p in pairs if keep(*p)]
    return lax.ppermute(value, axis, pairs)


def after(value, *others):
    return lax.optimization_barrier((value,) + others)[0]


def together(*values):
    return lax.optimization_barrier(values)


def flattened(vectors):
    flat = jnp.concatenate(vectors)
    return jnp.pad(flat, (0, -flat.shape[0] % 1024)).reshape(-1, LANES)


def butterfly(value, axis):
    k = 1
    while k < lax.axis_size(axis):
        value = value + swapped(value, axis, k)
        k *= 2
    return value


def picked(array, index):
    return lax.dynamic_index_in_dim(array, index, 0, keepdims=False)


def seq_gather(block, here):
    return jnp.stack(reordered_by_xor([block] + [swapped(block, "seq", k) for k in range(1, 4)], here))


def reordered_by_xor(pieces, here):
    k = 1
    while k < len(pieces):
        flip = (here & k) > 0
        pieces = [jnp.where(flip, pieces[j ^ k], piece) for j, piece in enumerate(pieces)]
        k *= 2
    return pieces


def call(kernel, **kwargs):
    return pl.pallas_call(
        kernel,
        compiler_params=pltpu.CompilerParams(vmem_limit_bytes=VMEM_LIMIT),
        cost_estimate=pl.CostEstimate(flops=1, bytes_accessed=1, transcendentals=0),
        **kwargs,
    )


def filled(shape, moves):
    arrays, plan, rows = [], [], []
    block = tuple(size if index is None else 1 for size, index in zip(shape, moves[0][2]))
    for piece, lead, place in moves:
        at = next((i for i, a in enumerate(arrays) if a is piece), len(arrays))
        if at == len(arrays):
            arrays.append(piece)
        plan.append((at, lead))
        rows.append(jnp.stack([jnp.asarray(0 if n is None else n, jnp.int32) for n in place]))

    def kernel(index_ref, *refs):
        pieces, out = refs[:-1], refs[-1]
        for m, (at, lead) in enumerate(plan):

            @pl.when(pl.program_id(0) == m)
            def _():
                value = pieces[at][...] if lead is None else pieces[at][lead]
                out[...] = value.reshape(block)

    return call(
        kernel,
        grid_spec=pltpu.PrefetchScalarGridSpec(
            num_scalar_prefetch=1,
            grid=(len(plan),),
            in_specs=[
                pl.BlockSpec(a.shape, lambda i, t, n=a.ndim: (0,) * n) for a in arrays
            ],
            out_specs=pl.BlockSpec(
                block, lambda i, t: tuple(t[i, n] for n in range(len(shape)))
            ),
        ),
        out_shape=jax.ShapeDtypeStruct(shape, arrays[0].dtype),
        name="filled",
    )(jnp.stack(rows), *arrays)


def terms_kernel(ns, nf, at_ref, left_ref, right_ref, out_ref):
    value = dot(left_ref[...], right_ref[...]).astype(BF)
    rows = value.shape[0] // (ns * nf)
    for i in range(ns):
        for k in range(nf):
            out_ref[k, i] = value[(i * nf + k) * rows : (i * nf + k + 1) * rows]


def row_terms(turned, right, at, nd, ns, nf, first, columns):
    depth = turned.shape[1]
    rows = turned.shape[0] // nd
    wide = TILE if columns % TILE == 0 else LANES
    return call(
        functools.partial(terms_kernel, ns, nf),
        grid_spec=pltpu.PrefetchScalarGridSpec(
            num_scalar_prefetch=1,
            grid=(columns // wide,),
            in_specs=[
                pl.BlockSpec((rows, depth), lambda i, t: (t[0], 0)),
                pl.BlockSpec((depth, wide), lambda i, t: (0, i + first // wide)),
            ],
            out_specs=pl.BlockSpec((nf, ns, rows // (nf * ns), wide), lambda i, t: (0, 0, 0, i)),
        ),
        out_shape=jax.ShapeDtypeStruct((nf, ns, rows // (nf * ns), columns), BF),
        name="row_terms",
    )(at.astype(jnp.int32)[None], turned, right)


def small_back_kernel(
    width, pre_ref, dbc_ref, in_ref, mask_ref, weight_ref, ddt_ref, pre_dt_ref, out_ref, sum_ref, ext, dext
):
    rows = pre_ref.shape[0]
    ext[0:HALO] = jnp.zeros((HALO, LANES), F32)
    ext[HALO:] = in_ref[...].astype(F32)
    pre = pre_ref[...]
    sig = jax.nn.sigmoid(pre)
    dpre = dbc_ref[...] * (sig * (1.0 + pre * (1.0 - sig)))
    dext[0:rows] = dpre
    dext[rows:] = jnp.zeros((HALO, LANES), F32)
    total = dpre * weight_ref[CONV - 1 : CONV, :]
    for k in range(CONV):
        term = ext[pl.ds(HALO - CONV + 1 + k, rows), :]
        if k < CONV - 1:
            term = term * mask_ref[:, k : k + 1]
            later = dext[pl.ds(CONV - 1 - k, rows), :] * mask_ref[:, CONV - 1 + k : CONV + k]
            total = total + later * weight_ref[k : k + 1, :]
        sum_ref[k : k + 1, :] = jnp.sum(dpre * term, axis=0, keepdims=True)
    sum_ref[CONV : CONV + 1, :] = jnp.sum(dpre, axis=0, keepdims=True)
    draw = ddt_ref[...] * jax.nn.sigmoid(pre_dt_ref[...])
    sum_ref[CONV + 1 : CONV + 2, :] = jnp.sum(draw, axis=0, keepdims=True)
    out_ref[...] = (total + pltpu.roll(draw, width, axis=1)).astype(BF)


def small_back(width, pre, dbc, proj, masks, weight, ddt, pre_dt):
    rows = pre.shape[0]
    return call(
        functools.partial(small_back_kernel, width),
        out_shape=[
            jax.ShapeDtypeStruct((rows, LANES), BF),
            jax.ShapeDtypeStruct((8, LANES), F32),
        ],
        scratch_shapes=[pltpu.VMEM((HALO + rows, LANES), F32), pltpu.VMEM((rows + HALO, LANES), F32)],
        name="small_back",
    )(pre, dbc, proj, masks, weight, ddt, pre_dt)


def input_grad_kernel(blocks, dz_ref, ds_ref, dr_ref, wz_ref, wa_ref, wb_ref, out_ref):
    half = wb_ref.shape[1]
    columns = ((1,), (1,))
    total = dot(dz_ref[...], wz_ref[...], columns)
    total = total + dot(ds_ref[:, :half], wa_ref[:, :half], columns)
    total = total + dot(ds_ref[:, half:], wb_ref[...], columns)
    total = total + dot(dr_ref[...], wa_ref[:, half:], columns)
    total = total.astype(BF)
    tok = total.shape[0] // blocks
    for i in range(blocks):
        out_ref[i] = total[i * tok : (i + 1) * tok]


def input_grad(dz, ds, dr, wz, wa, wb, blocks, tok):
    def whole(a):
        return pl.BlockSpec(a.shape, lambda i: (0, 0))

    def rows(a):
        return pl.BlockSpec((TILE, a.shape[1]), lambda i: (i, 0))

    return call(
        functools.partial(input_grad_kernel, blocks),
        grid=(wz.shape[0] // TILE,),
        in_specs=[whole(dz), whole(ds), whole(dr), rows(wz), rows(wa), rows(wb)],
        out_specs=pl.BlockSpec((blocks, tok, TILE), lambda i: (0, 0, i)),
        out_shape=jax.ShapeDtypeStruct((blocks, tok, wz.shape[0]), BF),
        name="input_grad",
    )(dz, ds, dr, wz, wa, wb)


def assembled(here_ref, pieces, nd, full_ref):
    halves = len(pieces) // nd
    nf, ns, rows = pieces[0].shape[:3]
    for n, piece in enumerate(pieces):
        h, j = divmod(n, nd)
        for k in range(nf):
            for i in range(ns):
                block = ((here_ref[1] ^ j) * ns + i) * nf + k
                at = pl.multiple_of((block * halves + h) * rows, rows)
                full_ref[pl.ds(at, rows), :] = piece[k, i]


def gated_kernel(nd, count, starts, wide, here_ref, xn_ref, y_ref, gain_ref, *refs):
    pieces, (out_ref, full_ref, gated_ref, turned_ref, squares_ref, sums) = refs[:count], refs[count:]
    step = pl.program_id(0)

    @pl.when(step == 0)
    def _():
        sums[...] = jnp.zeros_like(sums)

    if nd:
        assembled(here_ref, pieces, nd, full_ref)
    else:
        full_ref[...] = pieces[0][...]
    value = dot(xn_ref[...], full_ref[...]).astype(BF)
    out_ref[...] = value
    where = tile_range(starts, wide, step)
    for c in range(0, wide, LANES):
        at = slice(c, c + LANES)
        z = value[:, at].astype(F32)
        q = y_ref[:, at] * (z * jax.nn.sigmoid(z))
        gated = (q * gain_ref[:, at]).astype(BF)
        gated_ref[:, at] = gated
        turned_ref[at, :] = gated.T
        sums[where] += q * q

    @pl.when(step == pl.num_programs(0) - 1)
    def _():
        lane = lax.broadcasted_iota(jnp.int32, sums.shape[1:], 1)
        total = jnp.zeros(sums.shape[1:], F32)
        for j in range(len(starts)):
            total = jnp.where(lane == j, jnp.sum(sums[j], axis=1, keepdims=True), total)
        squares_ref[...] = total.T[: squares_ref.shape[0]]


def gated_projection(here, xn, pieces, nd, columns, y, gain, starts, wide):
    if pieces[0].ndim == 2:
        nd = 0
    tokens, depth = xn.shape
    tile = pl.BlockSpec((tokens, wide), lambda i: (0, i))
    ins = [
        pl.BlockSpec(memory_space=pltpu.SMEM),
        pl.BlockSpec((tokens, depth), lambda i: (0, 0)),
        tile,
        pl.BlockSpec((1, wide), lambda i: (0, i)),
    ]
    for piece in pieces:
        lead = piece.shape[:-1]
        ins.append(pl.BlockSpec(lead + (wide,), lambda i, n=len(lead): (0,) * n + (i,)))
    return call(
        functools.partial(gated_kernel, nd, len(pieces), starts, wide),
        grid=(columns // wide,),
        in_specs=ins,
        out_specs=[
            tile,
            pl.BlockSpec((depth, wide), lambda i: (0, i)),
            tile,
            pl.BlockSpec((wide, tokens), lambda i: (i, 0)),
            pl.BlockSpec((8, tokens), lambda i: (0, 0)),
        ],
        out_shape=[
            jax.ShapeDtypeStruct((tokens, columns), BF),
            jax.ShapeDtypeStruct((depth, columns), BF),
            jax.ShapeDtypeStruct((tokens, columns), BF),
            jax.ShapeDtypeStruct((columns, tokens), BF),
            jax.ShapeDtypeStruct((8, tokens), F32),
        ],
        scratch_shapes=[pltpu.VMEM((len(starts), tokens, LANES), F32)],
        name="gated",
    )(here, xn, y, gain, *pieces)


def tri(rows_first):
    a = lax.broadcasted_iota(jnp.int32, (SPAN, SPAN), 0)
    b = lax.broadcasted_iota(jnp.int32, (SPAN, SPAN), 1)
    return (a >= b) if rows_first else (a <= b)


def decays(segc, segr, segp, dt, rate):
    cum = dot(tri(True).astype(F32), dt * rate, precision=HIGH)
    last = cum[SPAN - 1 : SPAN, :]
    keep = jnp.where(segc == segp, jnp.exp(cum), 0.0)
    to_end = jnp.where(segc == segr[:, SPAN - 1 : SPAN], jnp.exp(last - cum), 0.0)
    return cum, cum.T, keep, to_end


def expanded(columns, ones):
    high = columns.astype(BF)
    low = (columns - high.astype(F32)).astype(BF)
    return dot(high, ones) + dot(low, ones)


def head_of_channel(width):
    return (
        lax.broadcasted_iota(jnp.int32, (LANES, width), 1) // HEADDIM
        == lax.broadcasted_iota(jnp.int32, (LANES, width), 0)
    ).astype(BF)


def spread_columns(ref, first, count):
    return [jnp.broadcast_to(ref[:, first + k : first + k + 1], (SPAN, LANES)) for k in range(count)]


def taps(ext, masks, at):
    terms = [ext[pl.ds(HALO - CONV + 1 + k, SPAN), at] for k in range(CONV)]
    return [t * m for t, m in zip(terms, masks)] + terms[CONV - 1 :]


def convolved(terms, weight_ref, at):
    total = weight_ref[CONV : CONV + 1, at] + terms[0] * weight_ref[0:1, at]
    for k in range(1, CONV):
        total = total + terms[k] * weight_ref[k : k + 1, at]
    return total


def forward_kernel(
    heads,
    segp_ref,
    segc_ref,
    segr_ref,
    mask_ref,
    in_a_ref,
    in_b_ref,
    halo_ref,
    weight_ref,
    b_ref,
    c_ref,
    dt_ref,
    rate_ref,
    skip_ref,
    y_ref,
    prior_ref,
    carry,
    to_end_u,
    ext,
    wide_dt,
    wide_keep,
    wide_end,
):
    block = pl.program_id(0)
    width = heads * HEADDIM

    @pl.when(block == 0)
    def _():
        carry[...] = jnp.zeros_like(carry)

    prior_ref[0] = carry[...]
    ext[0:HALO] = halo_ref[0].astype(F32)
    half = in_b_ref.shape[1]
    ext[HALO:, :half] = in_a_ref[:, :half].astype(F32)
    ext[HALO:, half:] = in_b_ref[...].astype(F32)
    segc, segr = segc_ref[...], segr_ref[...]
    dt = dt_ref[...]
    cum, cumr, keep, to_end = decays(segc, segr, segp_ref[block], dt, rate_ref[...])
    bm, cm = b_ref[...], c_ref[...]
    mixing = dot(cm, bm, ((1,), (1,)))
    mixing = jnp.where(tri(True) & (segc == segr), mixing, 0.0)
    heads_ones = head_of_channel(width)
    wide_dt[...] = expanded(dt, heads_ones)
    wide_keep[...] = expanded(keep, heads_ones)
    wide_end[...] = expanded(to_end, heads_ones)
    masks = spread_columns(mask_ref, 0, CONV - 1)
    lo = lax.broadcasted_iota(jnp.int32, (SPAN, LANES), 1) < HEADDIM
    for p in range(heads // 2):
        at = slice(p * LANES, (p + 1) * LANES)
        pre = convolved(taps(ext, masks, at), weight_ref, at)
        x2 = pre * jax.nn.sigmoid(pre)
        u2 = x2 * wide_dt[:, at]
        ub = u2.astype(BF)
        total = dot(cm, carry[:, at].astype(BF)) * wide_keep[:, at] + skip_ref[:, at] * x2
        inner = []
        for h in (2 * p, 2 * p + 1):
            decay = jnp.exp(jnp.minimum(cum[:, h : h + 1] - cumr[h : h + 1, :], 0.0))
            inner.append(dot((decay * mixing).astype(BF), ub))
        y_ref[:, at] = total + jnp.where(lo, inner[0], inner[1])
        to_end_u[:, at] = (u2 * wide_end[:, at]).astype(BF)
    fresh = dot(bm, to_end_u[...], ((0,), (0,)))
    carry[...] = wide_keep[SPAN - 1 : SPAN, :] * carry[...] + fresh


def split_dot(value, ones):
    high = value.astype(BF)
    low = (value - high.astype(F32)).astype(BF)
    return dot(high, ones) + dot(low, ones)


def backward_kernel(heads, last, begins, *refs):
    (
        segp_ref,
        segc_ref,
        segr_ref,
        mask_ref,
        in_a_ref,
        in_b_ref,
        halo_ref,
        weight_ref,
        b_ref,
        c_ref,
        dt_ref,
        rate_ref,
        skip_ref,
        y_ref,
        prior_ref,
        dy_ref,
    ) = refs[:16]
    rest = refs[16:] if begins else refs[24:]
    din_ref, dbc_ref, ddt_ref, drate_ref, dsum_ref, carry_ref, tail_ref = rest[:7]
    (
        dcarry,
        after_state,
        keep_dy,
        to_end_u,
        slopes,
        along,
        ext,
        dext,
        wide_dt,
        wide_keep,
        wide_end,
    ) = rest[7:]
    step = pl.program_id(0)
    block = last - step

    @pl.when(step == 0)
    def _():
        if begins:
            dcarry[...] = jnp.zeros_like(dcarry)
            after_state[...] = jnp.zeros_like(after_state)
            drate_ref[...] = jnp.zeros_like(drate_ref)
            dsum_ref[...] = jnp.zeros_like(dsum_ref)
            dext[SPAN:] = jnp.zeros((HALO, dext.shape[1]), F32)
        else:
            drate_in, dsum_in, carry_in, tail_in, after_in = refs[16:21]
            dcarry[...] = carry_in[...]
            after_state[...] = after_in[0]
            drate_ref[...] = drate_in[...]
            dsum_ref[...] = dsum_in[...]
            dext[SPAN:] = tail_in[...]

    ext[0:HALO] = halo_ref[0].astype(F32)
    half = in_b_ref.shape[1]
    ext[HALO:, :half] = in_a_ref[:, :half].astype(F32)
    ext[HALO:, half:] = in_b_ref[...].astype(F32)
    segc, segr = segc_ref[...], segr_ref[...]
    dt = dt_ref[...]
    cum, cumr, keep, to_end = decays(segc, segr, segp_ref[block], dt, rate_ref[...])
    bm, cm = b_ref[...], c_ref[...]
    allowed = tri(False) & (segc == segr)
    mixing = jnp.where(allowed, dot(bm, cm, ((1,), (1,))), 0.0)
    heads_ones = head_of_channel(heads * HEADDIM)
    wide_dt[...] = expanded(dt, heads_ones)
    wide_keep[...] = expanded(keep, heads_ones)
    wide_end[...] = expanded(to_end, heads_ones)
    masks = spread_columns(mask_ref, 0, CONV - 1)
    moved = spread_columns(mask_ref, CONV - 1, CONV - 1)
    lo = lax.broadcasted_iota(jnp.int32, (SPAN, LANES), 1) < HEADDIM
    dmixing = jnp.zeros((SPAN, SPAN), F32)
    for p in range(heads // 2):
        at = slice(p * LANES, (p + 1) * LANES)
        terms = taps(ext, masks, at)
        pre = convolved(terms, weight_ref, at)
        sig = jax.nn.sigmoid(pre)
        x2 = pre * sig
        dt2 = wide_dt[:, at]
        u2 = x2 * dt2
        dyb = dy_ref[:, at]
        dy2 = dyb.astype(F32)
        skip = skip_ref[:, at]
        te2 = wide_end[:, at]
        u_sides = (jnp.where(lo, u2, 0.0).astype(BF), jnp.where(lo, 0.0, u2).astype(BF))
        du = te2 * dot(bm, dcarry[:, at].astype(BF))
        inner = []
        for k in range(2):
            h = 2 * p + k
            decay = jnp.exp(jnp.minimum(cumr[h : h + 1, :] - cum[:, h : h + 1], 0.0))
            inner.append(dot((decay * mixing).astype(BF), dyb))
            dmixing = dmixing + decay * dot(u_sides[k], dyb, ((1,), (1,)))
        du = du + jnp.where(lo, inner[0], inner[1])
        keep_dy[:, at] = (wide_keep[:, at] * dy2).astype(BF)
        to_end_u[:, at] = (te2 * u2).astype(BF)
        slopes[:, at] = dy2 * (y_ref[:, at] - skip * x2) - u2.astype(BF).astype(F32) * du
        along[:, at] = x2 * du
        dpre = (dt2 * du + skip * dy2) * (sig * (1.0 + pre * (1.0 - sig)))
        dext[0:SPAN, at] = dpre
        for k in range(CONV):
            dsum_ref[k : k + 1, at] += jnp.sum(dpre * terms[k], axis=0, keepdims=True)
        dsum_ref[CONV : CONV + 1, at] += jnp.sum(dpre, axis=0, keepdims=True)
        dsum_ref[CONV + 1 : CONV + 2, at] += jnp.sum(dy2 * x2, axis=0, keepdims=True)
        din = dpre * weight_ref[CONV - 1 : CONV, at]
        for k in range(CONV - 1):
            later = dext[pl.ds(CONV - 1 - k, SPAN), at]
            din = din + later * moved[k] * weight_ref[k : k + 1, at]
        din_ref[:, at] = din.astype(BF)
    dext[SPAN:] = dext[0:HALO]
    dmixing = jnp.where(allowed, dmixing, 0.0).astype(BF)
    dstate = dcarry[...].astype(BF)
    prior = prior_ref[0]
    dbc_ref[:, :STATE] = dot(dmixing, cm) + dot(to_end_u[...], dstate, ((1,), (1,)))
    dbc_ref[:, STATE:] = dot(dmixing, bm, ((0,), (0,))) + dot(
        keep_dy[...], prior.astype(BF), ((1,), (1,))
    )
    width = heads * HEADDIM
    ones = (
        lax.broadcasted_iota(jnp.int32, (width, LANES), 0) // HEADDIM
        == lax.broadcasted_iota(jnp.int32, (width, LANES), 1)
    ).astype(BF)
    at_end = jnp.sum(dcarry[...] * after_state[...], axis=0, keepdims=True)
    at_end = split_dot(jnp.broadcast_to(at_end, (16, width)), ones)[:1]
    dcum = split_dot(slopes[...], ones)
    da = dot(tri(False).astype(F32), dcum, precision=HIGH) + at_end
    ddt_ref[...] = rate_ref[...] * da + split_dot(along[...], ones)
    drate_ref[...] += jnp.sum(dt * da, axis=0, keepdims=True)
    fresh = dot(cm, keep_dy[...], ((0,), (0,)))
    dcarry[...] = wide_keep[SPAN - 1 : SPAN, :] * dcarry[...] + fresh
    after_state[...] = prior

    @pl.when(step == pl.num_programs(0) - 1)
    def _():
        carry_ref[...] = dcarry[...]
        tail_ref[...] = dext[SPAN:]


def scan_specs(heads, at, in_widths):
    width = heads * HEADDIM

    def rows(n):
        return pl.BlockSpec((SPAN, n), lambda i: (at(i), 0))

    def whole(*shape):
        return pl.BlockSpec(shape, lambda i: (0,) * len(shape))

    ins = [
        pl.BlockSpec(memory_space=pltpu.SMEM),
        rows(1),
        pl.BlockSpec((1, SPAN), lambda i: (0, at(i))),
        rows(LANES),
        rows(in_widths[0]),
        rows(in_widths[1]),
        pl.BlockSpec((1, HALO, width), lambda i: (at(i), 0, 0)),
        whole(8, width),
        rows(STATE),
        rows(STATE),
        rows(LANES),
        whole(1, LANES),
        whole(1, width),
    ]
    prior = pl.BlockSpec((1, STATE, width), lambda i: (at(i), 0, 0))
    return rows, whole, ins, prior


def scan_forward(heads, blocks, operands):
    rows, whole, ins, prior = scan_specs(heads, lambda i: i, [operands[n].shape[1] for n in (4, 5)])
    width = heads * HEADDIM
    return call(
        functools.partial(forward_kernel, heads),
        grid=(blocks,),
        in_specs=ins,
        out_specs=[rows(width), prior],
        out_shape=[
            jax.ShapeDtypeStruct((blocks * SPAN, width), F32),
            jax.ShapeDtypeStruct((blocks, STATE, width), F32),
        ],
        scratch_shapes=[
            pltpu.VMEM((STATE, width), F32),
            pltpu.VMEM((SPAN, width), BF),
            pltpu.VMEM((HALO + SPAN, width), F32),
            pltpu.VMEM((SPAN, width), F32),
            pltpu.VMEM((SPAN, width), F32),
            pltpu.VMEM((SPAN, width), F32),
        ],
        name="scan_forward",
    )(*operands)


def scan_backward(heads, blocks, lowest, last, operands, y, priors, dy, before=None):
    rows, whole, ins, prior = scan_specs(
        heads, lambda i: last - i, [operands[n].shape[1] for n in (4, 5)]
    )
    width = heads * HEADDIM
    more, more_specs, aliases = [], [], {}
    if before is not None:
        more = list(before[3:]) + [priors] + list(before[:3])
        more_specs = [
            whole(1, LANES),
            whole(8, width),
            whole(STATE, width),
            whole(HALO, width),
            pl.BlockSpec((1, STATE, width), lambda i: (last + 1, 0, 0)),
        ] + [pl.BlockSpec(memory_space=pl.ANY)] * 3
        aliases = {len(ins) + 8 + n: n for n in range(3)}
    return call(
        functools.partial(backward_kernel, heads, last, before is None),
        grid=(last - lowest + 1,),
        in_specs=ins + [rows(width), prior, rows(width)] + more_specs,
        out_specs=[
            rows(width),
            rows(2 * STATE),
            rows(LANES),
            whole(1, LANES),
            whole(8, width),
            whole(STATE, width),
            whole(HALO, width),
        ],
        out_shape=[
            jax.ShapeDtypeStruct((blocks * SPAN, width), BF),
            jax.ShapeDtypeStruct((blocks * SPAN, 2 * STATE), F32),
            jax.ShapeDtypeStruct((blocks * SPAN, LANES), F32),
            jax.ShapeDtypeStruct((1, LANES), F32),
            jax.ShapeDtypeStruct((8, width), F32),
            jax.ShapeDtypeStruct((STATE, width), F32),
            jax.ShapeDtypeStruct((HALO, width), F32),
        ],
        scratch_shapes=[
            pltpu.VMEM((STATE, width), F32),
            pltpu.VMEM((STATE, width), F32),
            pltpu.VMEM((SPAN, width), BF),
            pltpu.VMEM((SPAN, width), BF),
            pltpu.VMEM((SPAN, width), F32),
            pltpu.VMEM((SPAN, width), F32),
            pltpu.VMEM((HALO + SPAN, width), F32),
            pltpu.VMEM((SPAN + HALO, width), F32),
            pltpu.VMEM((SPAN, width), F32),
            pltpu.VMEM((SPAN, width), F32),
            pltpu.VMEM((SPAN, width), F32),
        ],
        input_output_aliases=aliases,
        name="scan_backward",
    )(*operands, y, priors, dy, *more)


def as_columns(rows):
    few, tokens = rows.shape
    return jnp.concatenate([rows, jnp.zeros((LANES - few, tokens), F32)]).T


def level_block(pieces, spot):
    piece, lead = spot
    return pieces[piece][lead + (slice(None), slice(None))].astype(F32)


def upper_kernel(where, plan, nd, tok, ns, here_ref, range_ref, count_ref, ratio_ref, q_turned, *refs):
    count = 3 + 2 * LEVELS
    pieces, outs = refs[:count], refs[count:]
    upper_ref, grad_refs, coefs = outs[0], outs[1 : 2 * nd], outs[2 * nd]

    @pl.when(pl.program_id(0) == 0)
    def _():
        rows = [count_ref[j, w] * ratio_ref[w : w + 1, :] for j in range(len(plan)) for w in range(LEVELS)]
        coefs[...] = as_columns(jnp.concatenate(rows))

    for k in range(ns):
        at = here_ref[0] ^ k
        rows = pl.ds(pl.multiple_of(at * tok, tok), tok)
        levels = [level_block(pieces, where[w][k]) for w in range(LEVELS)]
        for j in range(len(plan)):
            total = None
            for w in plan[j]:
                n = j * LEVELS + w
                term = coefs[rows, n : n + 1] * levels[w]
                total = term if total is None else total + term
            upper_ref[j, rows, :] = total.astype(BF)
    count = q_turned.shape[0] // nd
    for k in range(nd):
        index = here_ref[1] ^ k
        rows = pl.ds(pl.multiple_of(index * count, count), count)
        value = dot(q_turned[rows, :], upper_ref[range_ref[index]]).astype(BF)
        if k:
            grad_refs[2 * k - 1][...] = value[: count // 2]
            grad_refs[2 * k][...] = value[count // 2 :]
        else:
            grad_refs[0][...] = value


def products_kernel(where, plan, lanes, tok, ns, nd, here_ref, count_ref, q_ref, *refs):
    count = 3 + 2 * LEVELS
    held_ref, pieces, outs = refs[0], refs[1 : 1 + count], refs[1 + count :]
    prod_refs, inner_ref, w_ref, sums = outs[:ns], outs[ns], outs[ns + 1], outs[ns + 2]
    step = pl.program_id(0)
    rows_of = w_ref.shape[0] // nd
    for k in range(nd):
        at = pl.multiple_of((here_ref[1] ^ k) * rows_of, rows_of)
        w_ref[pl.ds(at, rows_of), :] = held_ref[:, k].reshape(rows_of, w_ref.shape[1])

    @pl.when(step == 0)
    def _():
        sums[...] = jnp.zeros_like(sums)

    for k in range(ns):
        at = here_ref[0] ^ k
        rows = pl.ds(pl.multiple_of(at * tok, tok), tok)
        values = [dot(q_ref[rows, a:b], w_ref[a:b, :]) for a, b in lanes]
        for j, value in enumerate(values):
            prod_refs[k][j] = value.astype(BF)
        for w in range(LEVELS):
            total = None
            for j in range(len(lanes)):
                if w in plan[j]:
                    term = values[j] * count_ref[j, w]
                    total = term if total is None else total + term
            part = total * level_block(pieces, where[w][k])
            folded = part[:, :LANES]
            for c in range(LANES, part.shape[1], LANES):
                folded = folded + part[:, c : c + LANES]
            sums[w, rows, :] += folded

    @pl.when(step == pl.num_programs(0) - 1)
    def _():
        lane = lax.broadcasted_iota(jnp.int32, sums.shape[1:], 1)
        total = jnp.zeros(sums.shape[1:], F32)
        for w in range(LEVELS):
            total = jnp.where(lane == w, jnp.sum(sums[w], axis=1, keepdims=True), total)
        inner_ref[...] = total.T[:LEVELS]


def gate_kernel(
    starts, wide, count_ref, upper_ref, w_ref, y_ref, z_ref, gain_ref, ratio_ref, mean_ref, dy_ref, dz_ref, grad_ref, coefs
):
    step = pl.program_id(0)

    @pl.when(step == 0)
    def _():
        cubes = ratio_ref[...] * ratio_ref[...] * ratio_ref[...] * mean_ref[...]
        rows = []
        for j in range(len(starts)):
            total = cubes[0:1] * count_ref[j, 0]
            for w in range(1, LEVELS):
                total = total + cubes[w : w + 1] * count_ref[j, w]
            rows.append(total)
        columns = as_columns(jnp.concatenate(rows))
        for j in range(len(starts)):
            coefs[j] = jnp.broadcast_to(columns[:, j : j + 1], coefs.shape[1:])

    grad_all = dot(upper_ref[0], w_ref[...], ((1,), (1,)))
    coef = coefs[tile_range(starts, wide, step)]
    for c in range(0, wide, LANES):
        at = slice(c, c + LANES)
        grad_t = grad_all[:, at]
        z = z_ref[:, at].astype(F32)
        sig = jax.nn.sigmoid(z)
        act = z * sig
        y = y_ref[:, at]
        q = y * act
        dq = gain_ref[:, at] * grad_t - q * coef
        dy_ref[:, at] = (dq * act).astype(BF)
        dz_ref[:, at] = (dq * y * (sig * (1.0 + z * (1.0 - sig)))).astype(BF)
        grad_ref[0:1, at] = jnp.sum(q * grad_t, axis=0, keepdims=True)


def tile_range(starts, wide, step):
    index = 0
    for start in starts[1:]:
        index = index + jnp.where(step * wide >= start, 1, 0)
    return index


def mixed_kernel(plan, split, ns, tok, here_ref, count_ref, ratio_ref, x_ref, *refs):
    shares, out_ref = refs[:-1], refs[-1]
    at = pl.ds(pl.multiple_of(here_ref[0] * tok, tok), tok)
    ratios = as_columns(ratio_ref[:, at])
    x = x_ref[...].astype(F32)
    for w in range(LEVELS):
        total = None
        for k in range(ns):
            for j in plan[w]:
                at = (k, j) if k < 3 or j < split else (k + 1, j - split)
                term = shares[at[0]][at[1]].astype(F32) * count_ref[k, j * LEVELS + w]
                total = term if total is None else total + term
        out_ref[w] = (x + ratios[:, w : w + 1] * total).astype(BF)


def dp_terms(others):
    return [swapped(other, "dp", k + 1) for k, other in enumerate(others)]


def over_seq(value):
    dense = value.reshape(-1, LANES)
    total = dense
    for k in range(1, lax.axis_size("seq")):
        total = total + swapped(dense, "seq", k)
    return total.reshape(value.shape)


def fsdp_half(own, got):
    nf = lax.axis_size("fsdp")
    f = lax.axis_index("fsdp")

    def part(offset):
        total = picked(own, f ^ offset).astype(F32)
        for other in got:
            total = total + picked(other, f ^ offset).astype(F32)
        return total.astype(BF)

    kept = jnp.stack([part(e) for e in range(0, nf, 2)])
    sent = jnp.stack([part(e ^ 1) for e in range(0, nf, 2)])
    return kept, sent


def fsdp_rest(kept, got):
    k = 2
    while k < lax.axis_size("fsdp"):
        total = (kept.astype(F32) + got.astype(F32)).astype(BF)
        kept, sent = total[::2], total[1::2]
        got = swapped(sent, "fsdp", k)
        k *= 2
    return kept[0], got[0]


def shards(
    tokens,
    lengths,
    norm_gain,
    w_in,
    w_dt,
    conv_w,
    conv_b,
    dt_bias,
    a_log,
    skip,
    gate_gain,
    w_out,
    cotangent,
):
    nd, ns, nf = lax.axis_size("dp"), lax.axis_size("seq"), lax.axis_size("fsdp")
    d, s, f = lax.axis_index("dp"), lax.axis_index("seq"), lax.axis_index("fsdp")
    tok = tokens.shape[1]
    length = ns * tok
    blocks = length // SPAN
    heads = HEADS // ns
    run = heads // nd
    width = heads * HEADDIM
    own_bc = 2 * STATE // ns
    used = width + own_bc
    cols = -(-(used + heads) // LANES) * LANES
    rows_in = w_in.shape[0]
    reach = CONV - 1

    levels = np.array(
        [[level_of(dd * (HEADS // nd) + ss * run + i) for dd in range(nd) for i in range(run)] for ss in range(ns)]
    )
    cuts = [0] + [h for h in range(1, heads) if (levels[:, h] != levels[:, h - 1]).any()] + [heads]
    ranges = [(a, b) for a, b in zip(cuts, cuts[1:])]
    range_level = np.array([[levels[ss, a] for a, _ in ranges] for ss in range(ns)])
    counts = (range_level[:, :, None] <= np.arange(LEVELS)[None, None, :]).astype(np.float32)
    counted = picked(jnp.asarray(counts), s)
    theirs = picked(
        jnp.asarray(np.stack([[counts[i ^ k].reshape(-1) for k in range(ns)] for i in range(ns)])), s
    )
    lowest = [int(range_level[ss].min()) for ss in range(ns)]

    def by_head(vector):
        lead = vector.shape[:-1]
        per = vector.shape[-1] // HEADS
        cut = vector.reshape(lead + (nd, ns, run * per))
        mine = lax.dynamic_index_in_dim(cut, s, len(lead) + 1, keepdims=False)
        return mine.reshape(lead + (heads * per,))

    def for_groups(matrix):
        per = matrix.shape[1] // HEADS
        cut = matrix.reshape(matrix.shape[0], nd, ns, run * per)
        return jnp.transpose(cut, (2, 0, 1, 3)).reshape(ns, matrix.shape[0], heads * per)

    def from_groups(stack):
        per = stack.shape[2] // heads
        cut = stack.reshape(ns, stack.shape[1], nd, run * per)
        return jnp.transpose(cut, (1, 2, 0, 3)).reshape(stack.shape[1], HEADS * per)

    pad_cols = cols - used - heads
    half = width // 2
    first = half + cols - width
    group_x = for_groups(w_in[:, INNER : 2 * INNER])
    stack = jnp.concatenate(
        [
            group_x[:, :, :half],
            w_in[:, 2 * INNER :].reshape(rows_in, ns, own_bc).transpose(1, 0, 2),
            for_groups(w_dt),
            jnp.zeros((ns, rows_in, pad_cols), BF),
            group_x[:, :, half:],
            for_groups(w_in[:, :INNER]),
        ],
        axis=2,
    )
    own_x = tokens[0].astype(F32)
    scale = lax.rsqrt(jnp.mean(own_x * own_x, axis=-1, keepdims=True) + EPS)
    xn_own = (own_x * scale * norm_gain).astype(BF)
    xn_across = swapped(xn_own, "seq", 2)
    xn_pieces = [xn_own, swapped(xn_own, "seq", 1), xn_across, swapped(xn_across, "seq", 1)]
    arrived = [picked(stack, s)] + [swapped(picked(stack, s ^ k), "seq", k) for k in range(1, ns)]
    mine = filled((ns, rows_in, stack.shape[2]), [(p, None, (s ^ k, None, None)) for k, p in enumerate(arrived)])
    mine_z = mine[:, :, cols:]

    def needed(at, level):
        return min(lowest[at], lowest[at ^ 1]) <= level

    halves = [cotangent[w : w + 2, 0] for w in range(0, LEVELS, 2)]
    singles = [cotangent[w, 0] for w in range(LEVELS)]

    def beside(level, *others):
        block = after(halves[level // 2], *others)
        return swapped(block, "seq", 1, lambda i, j: needed(j, level + 1))

    def across(level, *others):
        block = after(singles[level], *others)
        return swapped(block, "seq", 2, lambda i, j: needed(j, level))

    def far(level, block):
        return swapped(block, "seq", 1, lambda i, j: needed(j, level))

    positions = jnp.arange(length, dtype=jnp.int32)
    ends = jnp.cumsum(lengths[0])[:-1]
    seg = jnp.sum((positions[:, None] >= ends[None, :]).astype(jnp.int32), axis=1)
    seg_before = jnp.concatenate([jnp.full((1,), -1, jnp.int32), seg[SPAN - 1 : length - 1 : SPAN]])
    seg_pad = jnp.concatenate([jnp.full((reach,), -1, jnp.int32), seg])
    masks = [(seg_pad[k : k + length] == seg) for k in range(reach)]
    mask_cols = [m.astype(F32) for m in masks]
    mask_cols += [jnp.pad(m, (0, reach - k))[reach - k :] for k, m in enumerate(mask_cols)]
    mask_cols = jnp.pad(jnp.stack(mask_cols, axis=1), ((0, 0), (0, LANES - 2 * reach)))

    def conv_params(s_part, bc_part):
        return by_head(s_part), bc_part

    weight_s = jnp.concatenate(
        [by_head(conv_w[:, :INNER]), by_head(conv_b[None, :INNER]), jnp.zeros((3, width), F32)]
    )
    weight_r = jnp.pad(
        lax.dynamic_slice_in_dim(conv_w, INNER + s * own_bc, own_bc, 1), ((0, 0), (0, cols - used))
    )
    bias_r = jnp.pad(
        lax.dynamic_slice_in_dim(conv_b, INNER + s * own_bc, own_bc, 0), (0, cols - used)
    )
    bias = by_head(dt_bias)
    rate = -jnp.exp(by_head(a_log))
    skip_own = by_head(skip)
    gain = by_head(gate_gain)

    def over_fsdp(chunk):
        return lax.all_gather(chunk, "fsdp", axis=0, tiled=False)

    def over_dp(held):
        return [held] + [swapped(held, "dp", j) for j in range(1, nd)]

    def whole(pieces, columns):
        moves = [
            (piece, i, (d ^ j, None, i, None, None)) for j, piece in enumerate(pieces) for i in range(nf)
        ]
        return filled((nd, ns, nf, rows_in, columns), moves).reshape(D, columns)

    held_a = over_fsdp(mine[:, :, :first])
    held_b = over_fsdp(mine[:, :, first:cols])
    other_out = [swapped(w_out, "dp", j) for j in range(1, nd)]
    held_a, other_out, xn_pieces[2] = together(held_a, other_out, xn_pieces[2])
    small_ones = (seg, seg_before, mask_cols, weight_s, weight_r, bias_r, bias, rate, skip_own, gain, theirs)
    held_a, small_ones, halves, singles = together(held_a, small_ones, halves, singles)
    seg, seg_before, mask_cols, weight_s, weight_r, bias_r, bias, rate, skip_own, gain, theirs = small_ones
    near_high, near_low = beside(2, held_a), beside(0, held_a)
    chip3 = across(3, held_a)
    pieces_a = over_dp(held_a)
    held_b, pieces_a, chip3, near_high, xn_pieces = together(
        held_b, pieces_a, chip3, near_high, xn_pieces
    )
    xn = filled((ns, tok, D), [(p, None, (s ^ k, None, None)) for k, p in enumerate(xn_pieces)])
    xn = xn.reshape(length, D)

    far3 = far(3, chip3)
    pieces_b = over_dp(held_b)
    held_z = over_fsdp(after(mine_z, held_a))
    pair_out = jnp.stack([w_out] + other_out)

    xn_turned = xn.T
    here = jnp.stack([s, d]).astype(jnp.int32)
    full_a = whole(pieces_a, first)
    proj_a = dot(xn, full_a).astype(BF)

    proj_r = proj_a[:, half:]
    mixer = jnp.concatenate([jnp.zeros((reach, cols - width), BF), proj_r], axis=0)

    def taken(k):
        rows = mixer[k : k + length].astype(F32)
        return rows * mask_cols[:, k : k + 1] if k < reach else rows

    pre_r = bias_r
    for k in range(CONV):
        pre_r = pre_r + taken(k) * weight_r[k]
    bc_own = jax.nn.silu(pre_r).astype(BF)[:, :own_bc]
    bc_across = swapped(bc_own, "seq", 2)
    bc = [bc_own, swapped(bc_own, "seq", 1), bc_across, swapped(bc_across, "seq", 1)]
    chip2, chip1 = across(2, bc[2]), across(1, bc[2])
    full_b = whole(pieces_b, half)
    proj_b = dot(xn, after(full_b, proj_a, xn_turned, bc[2])).astype(BF)
    proj_b, far3, near_low, held_z = together(proj_b, far3, near_low, held_z)
    pieces_z = over_dp(held_z)
    held_out = over_fsdp(after(pair_out, proj_b))
    bc = reordered_by_xor(bc, s)
    b_in = jnp.concatenate(bc[: ns // 2], axis=1)
    c_out = jnp.concatenate(bc[ns // 2 :], axis=1)

    def padded(rows):
        return jnp.pad(rows, ((0, 0), (0, LANES - rows.shape[1])))

    pre_dt = proj_r[:, own_bc : own_bc + heads].astype(F32) + bias
    steps = jax.nn.softplus(pre_dt)
    tails = [
        p.reshape(blocks, SPAN, p.shape[1])[: blocks - 1, SPAN - HALO :, :half] for p in (proj_a, proj_b)
    ]
    operands = (
        seg_before,
        seg[:, None],
        seg[None, :],
        mask_cols,
        proj_a,
        proj_b,
        jnp.concatenate([jnp.zeros((1, HALO, width), BF), jnp.concatenate(tails, axis=2)]),
        weight_s,
        b_in,
        c_out,
        padded(steps),
        padded(rate[None, :]),
        jnp.repeat(skip_own, HEADDIM)[None, :],
    )
    y, priors = scan_forward(heads, blocks, operands)
    y, chip2 = together(y, chip2)
    far2, chip0 = far(2, chip2), across(0, y)
    parts = pieces_z if rows_in % 16 == 0 else [whole(pieces_z, width)]
    lanes = [(a * HEADDIM, b * HEADDIM) for a, b in ranges]
    starts = [a for a, _ in lanes]
    wide = min(min(b - a for a, b in lanes), TILE)
    proj_z, full_z, q_gain, q_turned, squares = gated_projection(
        here, xn, parts, nd, width, y, gain[None], starts, wide
    )
    squares, chip1 = together(squares[: len(lanes)], chip1)
    far1 = far(1, chip1)
    widths = np.array([[(HEADS >> 3 - w) * HEADDIM] for w in range(LEVELS)], np.float32)
    per_level = jnp.sum(counted[:, :, None] * squares[:, None, :], axis=0)
    ratio, chip0 = together(lax.rsqrt(over_seq(per_level) / widths + EPS), chip0)
    far0 = far(0, chip0)

    plan = [[w for w in range(LEVELS) if range_level[:, j].min() <= w] for j in range(len(lanes))]
    out_rows = width // nd
    range_of = [next(j for j, (a, b) in enumerate(lanes) if a <= i * out_rows < b) for i in range(nd)]
    smem = pl.BlockSpec(memory_space=pltpu.SMEM)
    cot_pieces = [cotangent, near_low, near_high, chip0, chip1, chip2, chip3, far0, far1, far2, far3]
    cot_specs = [pl.BlockSpec((LEVELS, 1, tok, WIDE), lambda i: (0, 0, 0, i))]
    cot_specs += [pl.BlockSpec((2, tok, WIDE), lambda i: (0, 0, i))] * 2
    cot_specs += [pl.BlockSpec((tok, WIDE), lambda i: (0, i))] * (2 * LEVELS)
    where = [[(0, (w, 0)), (1 + w // 2, (w % 2,)), (3 + w, ()), (3 + LEVELS + w, ())] for w in range(LEVELS)]
    upper, *grad_out = call(
        functools.partial(upper_kernel, where, plan, nd, tok, ns),
        grid=(D // WIDE,),
        in_specs=[
            smem,
            smem,
            smem,
            pl.BlockSpec((LEVELS, length), lambda i: (0, 0)),
            pl.BlockSpec((width, length), lambda i: (0, 0)),
        ]
        + cot_specs,
        out_specs=[pl.BlockSpec((len(lanes), length, WIDE), lambda i: (0, 0, i))]
        + [pl.BlockSpec((out_rows, WIDE), lambda i: (0, i))]
        + [pl.BlockSpec((out_rows // 2, WIDE), lambda i: (0, i))] * (2 * nd - 2),
        out_shape=[jax.ShapeDtypeStruct((len(lanes), length, D), BF)]
        + [jax.ShapeDtypeStruct((out_rows, D), BF)]
        + [jax.ShapeDtypeStruct((out_rows // 2, D), BF)] * (2 * nd - 2),
        scratch_shapes=[pltpu.VMEM((length, LANES), F32)],
        name="upper",
    )(here, jnp.asarray(range_of, jnp.int32), counted, ratio, q_turned, *cot_pieces)
    out_first, out_second = dp_terms(grad_out[1::2]), dp_terms(grad_out[2::2])

    held_out, upper = together(held_out, upper)
    *shares, inner, full_out = call(
        functools.partial(products_kernel, where, plan, lanes, tok, ns, nd),
        grid=(D // WIDE,),
        in_specs=[
            smem,
            smem,
            pl.BlockSpec((length, width), lambda i: (0, 0)),
        ]
        + [pl.BlockSpec((nf, nd, w_out.shape[0], WIDE), lambda i: (0, 0, 0, i))]
        + cot_specs,
        out_specs=[pl.BlockSpec((len(lanes), tok, WIDE), lambda i: (0, 0, i))] * ns
        + [pl.BlockSpec((LEVELS, length), lambda i: (0, 0))]
        + [pl.BlockSpec((width, WIDE), lambda i: (0, i))],
        out_shape=[jax.ShapeDtypeStruct((len(lanes), tok, D), BF)] * ns
        + [jax.ShapeDtypeStruct((LEVELS, length), F32)]
        + [jax.ShapeDtypeStruct((width, D), BF)],
        scratch_shapes=[pltpu.VMEM((LEVELS, length, LANES), F32)],
        name="products",
    )(here, counted, q_gain, held_out, *cot_pieces)
    means, out_first = together(over_seq(inner) / widths, out_first)
    shares[1:3] = [swapped(after(shares[k], means), "seq", k) for k in (1, 2)]
    split = (len(lanes) + 1) // 2
    third = [swapped(after(shares[3][:split], shares[1]), "seq", 3), shares[3][split:]]

    cols_of = pl.BlockSpec((length, wide), lambda i: (0, i))
    scalars = pl.BlockSpec((LEVELS, length), lambda i: (0, 0))
    dy, dz, grad_gate = call(
        functools.partial(gate_kernel, starts, wide),
        grid=(width // wide,),
        in_specs=[
            smem,
            pl.BlockSpec((1, length, D), lambda i: (tile_range(starts, wide, i), 0, 0)),
            pl.BlockSpec((wide, D), lambda i: (i, 0)),
            cols_of,
            cols_of,
            pl.BlockSpec((1, wide), lambda i: (0, i)),
            scalars,
            scalars,
        ],
        out_specs=[cols_of, cols_of, pl.BlockSpec((8, wide), lambda i: (0, i))],
        out_shape=[
            jax.ShapeDtypeStruct((length, width), BF),
            jax.ShapeDtypeStruct((length, width), BF),
            jax.ShapeDtypeStruct((8, width), F32),
        ],
        scratch_shapes=[pltpu.VMEM((len(lanes), length, LANES), F32)],
        name="gate_backward",
    )(counted, upper, full_out, y, proj_z, gain[None], ratio, means)
    grad_gate = grad_gate[0]

    def in_terms(dproj, at, first=0, columns=None):
        columns = columns or dproj.shape[1]
        out = row_terms(xn_turned, dproj, at, nd, ns, nf, first, columns)
        return out.reshape(nf, ns * rows_in, columns)

    z_other = [in_terms(dz, d ^ k) for k in range(1, nd)]
    z_got = dp_terms(z_other)
    dy, out_second, shares[1] = together(after(dy, *z_other), out_second, shares[1])
    chunk = (nf, out_rows // nf, D)
    out_got = [jnp.concatenate([u, v]).reshape(chunk) for u, v in zip(out_first, out_second)]
    out_kept, out_sent = fsdp_half(grad_out[0].reshape(chunk), out_got)
    dy = after(dy, out_sent)
    out_half = swapped(out_sent, "fsdp", 1)

    middle = blocks * 3 // 8
    later = list(scan_backward(heads, blocks, middle, blocks - 1, operands, y, priors, dy))
    carry, out_half = together(later[5], out_half)
    out_pair = fsdp_rest(out_kept, out_half)
    later = later[:5] + [carry] + later[6:]
    dproj_s, dbc, ddt, drate, dsum, _, _ = scan_backward(
        heads, blocks, 0, middle - 1, operands, y, priors, dy, later
    )
    dproj_s, dbc, out_pair, shares[2], third = together(dproj_s, dbc, out_pair, shares[2], third)

    dbc = dbc.astype(BF)
    slices = reordered_by_xor([dbc[:, j * own_bc : (j + 1) * own_bc] for j in range(ns)], s)
    beside_bc = swapped(jnp.concatenate([slices[1], slices[3]], axis=1), "seq", 1)
    sum_bc = jnp.concatenate([slices[0], slices[2]], axis=1).astype(F32) + beside_bc.astype(F32)
    across_bc = swapped(sum_bc[:, own_bc:].astype(BF), "seq", 2)

    z_own = in_terms(after(dz, dproj_s), d)
    z_own, z_got = together(z_own, z_got)
    z_kept, z_sent = fsdp_half(z_own, z_got)
    z_half = swapped(z_sent, "fsdp", 1)
    late_s = after(dproj_s, z_sent)
    left_other = [in_terms(late_s, d ^ k, 0, half) for k in range(1, nd)]
    left_got = dp_terms(left_other)
    third[1] = swapped(after(third[1], across_bc), "seq", 3)
    dbc_own = sum_bc[:, :own_bc] + across_bc.astype(F32)
    dproj_r, small_sums = small_back(
        own_bc,
        pre_r,
        padded(after(dbc_own, *left_other)),
        proj_r,
        mask_cols,
        weight_r,
        ddt,
        padded(pre_dt),
    )

    late_s, late_r = after(dproj_s, *left_other), dproj_r
    right_other = [
        jnp.concatenate([in_terms(late_s, d ^ k, half, half), in_terms(late_r, d ^ k)], axis=2)
        for k in range(1, nd)
    ]
    right_got = dp_terms(right_other)

    dxn = input_grad(dz, dproj_s, after(dproj_r, *right_other), full_z, full_a, full_b, ns, tok)
    pair = swapped(jnp.stack([picked(dxn, s ^ 1), picked(dxn, s ^ 3)]), "seq", 1)

    dxn, z_half, left_got = together(dxn, z_half, left_got)
    z_pair = fsdp_rest(z_kept, z_half)
    own_s = in_terms(after(dproj_s, dxn), d)
    left_kept, left_sent = fsdp_half(own_s[:, :, :half], left_got)
    left_half = swapped(left_sent, "fsdp", 1)
    own_r = in_terms(after(dproj_r, left_sent), d)
    flat = flattened(
        [
            jnp.concatenate([dsum[:CONV], small_sums[:CONV, :own_bc]], axis=1).reshape(-1),
            dsum[CONV],
            small_sums[CONV, :own_bc],
            grad_gate,
            small_sums[CONV + 1, :heads],
            drate[0, :heads] * rate,
            jnp.sum(dsum[CONV + 1].reshape(heads, HEADDIM), axis=1),
        ]
    )
    near = picked(dxn, s).astype(F32) + pair[0].astype(F32)
    far_sum = (picked(dxn, s ^ 2).astype(F32) + pair[1].astype(F32)).astype(BF)
    dxn_across = swapped(far_sum, "seq", 2)
    right_got, far_sum, left_half = together(right_got, far_sum, left_half)
    left_pair = fsdp_rest(left_kept, left_half)
    own_right = jnp.concatenate([own_s[:, :, half:], own_r], axis=2)
    right_kept, right_sent = fsdp_half(own_right, right_got)
    right_half = swapped(right_sent, "fsdp", 1)

    mixed = call(
        functools.partial(
            mixed_kernel,
            [[j for j in range(len(lanes)) if range_level[:, j].min() <= w] for w in range(LEVELS)],
            split,
            ns,
            tok,
        ),
        grid=(D // WIDE,),
        in_specs=[
            smem,
            smem,
            pl.BlockSpec((LEVELS, length), lambda i: (0, 0)),
            pl.BlockSpec((tok, WIDE), lambda i: (0, i)),
        ]
        + [pl.BlockSpec((p.shape[0], tok, WIDE), lambda i: (0, 0, i)) for p in shares[:3] + third],
        out_specs=pl.BlockSpec((LEVELS, tok, WIDE), lambda i: (0, 0, i)),
        out_shape=jax.ShapeDtypeStruct((LEVELS, tok, D), BF),
        name="mixed",
    )(here, theirs, ratio, tokens[0], *after(shares[:3] + third, right_sent))[:, None]
    right_half, mixed, dxn_across = together(right_half, mixed, dxn_across)
    right_kept = after(right_kept, mixed)
    right_pair = fsdp_rest(right_kept, right_half)
    dxn_own = near + dxn_across.astype(F32)
    grad_norm = jnp.sum(dxn_own * own_x * scale, axis=0)
    scaled = norm_gain * dxn_own
    dx = scale * scaled - own_x * scale**3 * jnp.mean(own_x * scaled, axis=-1, keepdims=True)
    dx = (dx + jnp.sum(after(cotangent, mixed)[:, 0].astype(F32), axis=0)).astype(BF)
    flat = jnp.concatenate([flat, grad_norm.reshape(-1, LANES)])
    flat = butterfly(flat, "dp")

    def whole_sum(pair):
        total = (pair[0].astype(F32) + pair[1].astype(F32)).astype(BF)
        return total.reshape(ns, rows_in, total.shape[1])

    z_pair, left_pair = together(z_pair, left_pair)
    early = jnp.concatenate([whole_sum(z_pair), whole_sum(left_pair)], axis=2)
    early_got = [picked(early, s)] + [swapped(picked(early, s ^ k), "seq", k) for k in range(1, ns)]
    early_got, right_pair, flat = together(early_got, right_pair, flat)
    flat = butterfly(flat, "fsdp")
    late = whole_sum(right_pair)
    late_got = [picked(late, s)] + [swapped(picked(late, s ^ k), "seq", k) for k in range(1, ns)]
    early = jnp.stack(reordered_by_xor(early_got, s))
    late = jnp.stack(reordered_by_xor(late_got, s))
    got_z = early[:, :, :width]
    got_x = jnp.concatenate([early[:, :, width:], late], axis=2)
    sum_out = out_pair[0].astype(F32) + out_pair[1].astype(F32)


    sum_in = jnp.concatenate(
        [
            from_groups(got_z),
            from_groups(got_x[:, :, :width]),
            jnp.transpose(got_x[:, :, width:used], (1, 0, 2)).reshape(rows_in, 2 * STATE),
        ],
        axis=1,
    ).astype(F32)
    sum_dt = from_groups(got_x[:, :, used : used + heads]).astype(F32)

    sizes = [CONV * used, used, width, heads, heads, heads]
    filling = -sum(sizes) % 1024
    sizes += [filling, D]
    every = seq_gather(flat, s).reshape(ns, -1)
    starts = np.cumsum([0] + sizes)
    pieces = [every[:, a : a + n] for a, n in zip(starts, sizes)]

    def heads_back(rows):
        lead = rows.shape[1:-1]
        cut = rows.reshape((ns,) + lead + (nd, rows.shape[-1] // nd))
        order = tuple(range(1, 1 + len(lead))) + (1 + len(lead), 0, 2 + len(lead))
        return jnp.transpose(cut, order).reshape(lead + (-1,))

    conv_rows = pieces[0].reshape(ns, CONV, used)
    conv_all = jnp.concatenate(
        [
            heads_back(conv_rows[:, :, :width]),
            jnp.transpose(conv_rows[:, :, width:], (1, 0, 2)).reshape(CONV, 2 * STATE),
        ],
        axis=1,
    )
    bias_all = jnp.concatenate([heads_back(pieces[1][:, :width]), pieces[1][:, width:].reshape(-1)])
    return (
        mixed,
        dx[None],
        jnp.sum(pieces[7], axis=0),
        sum_in,
        sum_dt,
        conv_all,
        bias_all,
        heads_back(pieces[3]),
        heads_back(pieces[4]),
        heads_back(pieces[5]),
        heads_back(pieces[2]),
        sum_out,
    )


def solution(mesh):
    rows = P(("dp", "seq", "fsdp"), None)
    held = P(("dp", "fsdp"), "seq", None)
    levels = P(None, ("dp", "fsdp"), "seq", None)
    placed = (held, P(("dp", "fsdp"), None), P(), rows, rows, P(), P(), P(), P(), P(), P(), rows, levels)
    return jax.shard_map(
        shards,
        mesh=mesh,
        in_specs=placed,
        out_specs=(levels, held, P(), rows, rows, P(), P(), P(), P(), P(), P(), rows),
        check_vma=False,
    )
```

```python
import functools

import jax
import jax.numpy as jnp
import numpy as np
from jax import lax
from jax.experimental import pallas as pl
from jax.experimental.pallas import tpu as pltpu
from jax.sharding import PartitionSpec as P

D = 2048
HEADS = 64
HEADDIM = 64
STATE = 128
CONV = 4
SPAN = 128
INNER = 4096
EPS = 1e-05
LEVELS = 4
BF = jnp.bfloat16
F32 = jnp.float32
HIGH = lax.Precision.HIGHEST
LANES = 128
HALO = 16
TILE = 256
WIDE = 512
VMEM_LIMIT = 48 * 1024 * 1024


def dot(a, b, dims=((1,), (0,)), precision=None):
    return lax.dot_general(a, b, (dims, ((), ())), preferred_element_type=F32, precision=precision)


def silu_slope(v):
    sig = jax.nn.sigmoid(v)
    return sig * (1.0 + v * (1.0 - sig))


def level_of(head):
    return 0 if head < 8 else 1 if head < 16 else 2 if head < 32 else 3


def swapped(value, axis, k, keep=None):
    pairs = [(i, i ^ k) for i in range(lax.axis_size(axis))]
    if keep is not None:
        pairs = [p for p in pairs if keep(*p)]
    return lax.ppermute(value, axis, pairs)


def after(value, *others):
    return lax.optimization_barrier((value,) + others)[0]


def together(*values):
    return lax.optimization_barrier(values)


def flattened(vectors):
    flat = jnp.concatenate(vectors)
    return jnp.pad(flat, (0, -flat.shape[0] % 1024)).reshape(-1, LANES)


def butterfly(value, axis):
    k = 1
    while k < lax.axis_size(axis):
        value = value + swapped(value, axis, k)
        k *= 2
    return value


def picked(array, index):
    return lax.dynamic_index_in_dim(array, index, 0, keepdims=False)


def seq_gather(block, here):
    return jnp.stack(reordered_by_xor([block] + [swapped(block, "seq", k) for k in range(1, 4)], here))


def reordered_by_xor(pieces, here):
    k = 1
    while k < len(pieces):
        flip = (here & k) > 0
        pieces = [jnp.where(flip, pieces[j ^ k], piece) for j, piece in enumerate(pieces)]
        k *= 2
    return pieces


def call(kernel, **kwargs):
    return pl.pallas_call(
        kernel,
        compiler_params=pltpu.CompilerParams(vmem_limit_bytes=VMEM_LIMIT),
        cost_estimate=pl.CostEstimate(flops=1, bytes_accessed=1, transcendentals=0),
        **kwargs,
    )


def filled(shape, moves):
    arrays, plan, rows = [], [], []
    block = tuple(size if index is None else 1 for size, index in zip(shape, moves[0][2]))
    for piece, lead, place in moves:
        at = next((i for i, a in enumerate(arrays) if a is piece), len(arrays))
        if at == len(arrays):
            arrays.append(piece)
        plan.append((at, lead))
        rows.append(jnp.stack([jnp.asarray(0 if n is None else n, jnp.int32) for n in place]))

    def kernel(index_ref, *refs):
        pieces, out = refs[:-1], refs[-1]
        for m, (at, lead) in enumerate(plan):

            @pl.when(pl.program_id(0) == m)
            def _():
                value = pieces[at][...] if lead is None else pieces[at][lead]
                out[...] = value.reshape(block)

    return call(
        kernel,
        grid_spec=pltpu.PrefetchScalarGridSpec(
            num_scalar_prefetch=1,
            grid=(len(plan),),
            in_specs=[
                pl.BlockSpec(a.shape, lambda i, t, n=a.ndim: (0,) * n) for a in arrays
            ],
            out_specs=pl.BlockSpec(
                block, lambda i, t: tuple(t[i, n] for n in range(len(shape)))
            ),
        ),
        out_shape=jax.ShapeDtypeStruct(shape, arrays[0].dtype),
        name="filled",
    )(jnp.stack(rows), *arrays)


def terms_kernel(ns, nf, at_ref, left_ref, right_ref, out_ref):
    value = dot(left_ref[...], right_ref[...]).astype(BF)
    rows = value.shape[0] // (ns * nf)
    for i in range(ns):
        for k in range(nf):
            out_ref[k, i] = value[(i * nf + k) * rows : (i * nf + k + 1) * rows]


def row_terms(turned, right, at, nd, ns, nf, first, columns):
    depth = turned.shape[1]
    rows = turned.shape[0] // nd
    wide = TILE if columns % TILE == 0 else LANES
    return call(
        functools.partial(terms_kernel, ns, nf),
        grid_spec=pltpu.PrefetchScalarGridSpec(
            num_scalar_prefetch=1,
            grid=(columns // wide,),
            in_specs=[
                pl.BlockSpec((rows, depth), lambda i, t: (t[0], 0)),
                pl.BlockSpec((depth, wide), lambda i, t: (0, i + first // wide)),
            ],
            out_specs=pl.BlockSpec((nf, ns, rows // (nf * ns), wide), lambda i, t: (0, 0, 0, i)),
        ),
        out_shape=jax.ShapeDtypeStruct((nf, ns, rows // (nf * ns), columns), BF),
        name="row_terms",
    )(at.astype(jnp.int32)[None], turned, right)


def small_back_kernel(
    width, pre_ref, dbc_ref, in_ref, mask_ref, weight_ref, ddt_ref, pre_dt_ref, out_ref, sum_ref, ext, dext
):
    rows = pre_ref.shape[0]
    ext[0:HALO] = jnp.zeros((HALO, LANES), F32)
    ext[HALO:] = in_ref[...].astype(F32)
    pre = pre_ref[...]
    sig = jax.nn.sigmoid(pre)
    dpre = dbc_ref[...] * (sig * (1.0 + pre * (1.0 - sig)))
    dext[0:rows] = dpre
    dext[rows:] = jnp.zeros((HALO, LANES), F32)
    total = dpre * weight_ref[CONV - 1 : CONV, :]
    for k in range(CONV):
        term = ext[pl.ds(HALO - CONV + 1 + k, rows), :]
        if k < CONV - 1:
            term = term * mask_ref[:, k : k + 1]
            later = dext[pl.ds(CONV - 1 - k, rows), :] * mask_ref[:, CONV - 1 + k : CONV + k]
            total = total + later * weight_ref[k : k + 1, :]
        sum_ref[k : k + 1, :] = jnp.sum(dpre * term, axis=0, keepdims=True)
    sum_ref[CONV : CONV + 1, :] = jnp.sum(dpre, axis=0, keepdims=True)
    draw = ddt_ref[...] * jax.nn.sigmoid(pre_dt_ref[...])
    sum_ref[CONV + 1 : CONV + 2, :] = jnp.sum(draw, axis=0, keepdims=True)
    out_ref[...] = (total + pltpu.roll(draw, width, axis=1)).astype(BF)


def small_back(width, pre, dbc, proj, masks, weight, ddt, pre_dt):
    rows = pre.shape[0]
    return call(
        functools.partial(small_back_kernel, width),
        out_shape=[
            jax.ShapeDtypeStruct((rows, LANES), BF),
            jax.ShapeDtypeStruct((8, LANES), F32),
        ],
        scratch_shapes=[pltpu.VMEM((HALO + rows, LANES), F32), pltpu.VMEM((rows + HALO, LANES), F32)],
        name="small_back",
    )(pre, dbc, proj, masks, weight, ddt, pre_dt)


def input_grad_kernel(blocks, dz_ref, ds_ref, dr_ref, wz_ref, wa_ref, wb_ref, out_ref):
    half = wb_ref.shape[1]
    columns = ((1,), (1,))
    total = dot(dz_ref[...], wz_ref[...], columns)
    total = total + dot(ds_ref[:, :half], wa_ref[:, :half], columns)
    total = total + dot(ds_ref[:, half:], wb_ref[...], columns)
    total = total + dot(dr_ref[...], wa_ref[:, half:], columns)
    total = total.astype(BF)
    tok = total.shape[0] // blocks
    for i in range(blocks):
        out_ref[i] = total[i * tok : (i + 1) * tok]


def input_grad(dz, ds, dr, wz, wa, wb, blocks, tok):
    def whole(a):
        return pl.BlockSpec(a.shape, lambda i: (0, 0))

    def rows(a):
        return pl.BlockSpec((TILE, a.shape[1]), lambda i: (i, 0))

    return call(
        functools.partial(input_grad_kernel, blocks),
        grid=(wz.shape[0] // TILE,),
        in_specs=[whole(dz), whole(ds), whole(dr), rows(wz), rows(wa), rows(wb)],
        out_specs=pl.BlockSpec((blocks, tok, TILE), lambda i: (0, 0, i)),
        out_shape=jax.ShapeDtypeStruct((blocks, tok, wz.shape[0]), BF),
        name="input_grad",
    )(dz, ds, dr, wz, wa, wb)


def assembled(here_ref, pieces, nd, full_ref):
    halves = len(pieces) // nd
    nf, ns, rows = pieces[0].shape[:3]
    for n, piece in enumerate(pieces):
        h, j = divmod(n, nd)
        for k in range(nf):
            for i in range(ns):
                block = ((here_ref[1] ^ j) * ns + i) * nf + k
                at = pl.multiple_of((block * halves + h) * rows, rows)
                full_ref[pl.ds(at, rows), :] = piece[k, i]


def gated_kernel(nd, count, starts, wide, here_ref, xn_ref, y_ref, gain_ref, *refs):
    pieces, (out_ref, full_ref, gated_ref, turned_ref, squares_ref, sums) = refs[:count], refs[count:]
    step = pl.program_id(0)

    @pl.when(step == 0)
    def _():
        sums[...] = jnp.zeros_like(sums)

    if nd:
        assembled(here_ref, pieces, nd, full_ref)
    else:
        full_ref[...] = pieces[0][...]
    value = dot(xn_ref[...], full_ref[...]).astype(BF)
    out_ref[...] = value
    where = tile_range(starts, wide, step)
    for c in range(0, wide, LANES):
        at = slice(c, c + LANES)
        z = value[:, at].astype(F32)
        q = y_ref[:, at] * (z * jax.nn.sigmoid(z))
        gated = (q * gain_ref[:, at]).astype(BF)
        gated_ref[:, at] = gated
        turned_ref[at, :] = gated.T
        sums[where] += q * q

    @pl.when(step == pl.num_programs(0) - 1)
    def _():
        lane = lax.broadcasted_iota(jnp.int32, sums.shape[1:], 1)
        total = jnp.zeros(sums.shape[1:], F32)
        for j in range(len(starts)):
            total = jnp.where(lane == j, jnp.sum(sums[j], axis=1, keepdims=True), total)
        squares_ref[...] = total.T[: squares_ref.shape[0]]


def gated_projection(here, xn, pieces, nd, columns, y, gain, starts, wide):
    if pieces[0].ndim == 2:
        nd = 0
    tokens, depth = xn.shape
    tile = pl.BlockSpec((tokens, wide), lambda i: (0, i))
    ins = [
        pl.BlockSpec(memory_space=pltpu.SMEM),
        pl.BlockSpec((tokens, depth), lambda i: (0, 0)),
        tile,
        pl.BlockSpec((1, wide), lambda i: (0, i)),
    ]
    for piece in pieces:
        lead = piece.shape[:-1]
        ins.append(pl.BlockSpec(lead + (wide,), lambda i, n=len(lead): (0,) * n + (i,)))
    return call(
        functools.partial(gated_kernel, nd, len(pieces), starts, wide),
        grid=(columns // wide,),
        in_specs=ins,
        out_specs=[
            tile,
            pl.BlockSpec((depth, wide), lambda i: (0, i)),
            tile,
            pl.BlockSpec((wide, tokens), lambda i: (i, 0)),
            pl.BlockSpec((8, tokens), lambda i: (0, 0)),
        ],
        out_shape=[
            jax.ShapeDtypeStruct((tokens, columns), BF),
            jax.ShapeDtypeStruct((depth, columns), BF),
            jax.ShapeDtypeStruct((tokens, columns), BF),
            jax.ShapeDtypeStruct((columns, tokens), BF),
            jax.ShapeDtypeStruct((8, tokens), F32),
        ],
        scratch_shapes=[pltpu.VMEM((len(starts), tokens, LANES), F32)],
        name="gated",
    )(here, xn, y, gain, *pieces)


def tri(rows_first):
    a = lax.broadcasted_iota(jnp.int32, (SPAN, SPAN), 0)
    b = lax.broadcasted_iota(jnp.int32, (SPAN, SPAN), 1)
    return (a >= b) if rows_first else (a <= b)


def decays(segc, segr, segp, dt, rate):
    cum = dot(tri(True).astype(F32), dt * rate, precision=HIGH)
    last = cum[SPAN - 1 : SPAN, :]
    keep = jnp.where(segc == segp, jnp.exp(cum), 0.0)
    to_end = jnp.where(segc == segr[:, SPAN - 1 : SPAN], jnp.exp(last - cum), 0.0)
    return cum, cum.T, keep, to_end


def expanded(columns, ones):
    high = columns.astype(BF)
    low = (columns - high.astype(F32)).astype(BF)
    return dot(high, ones) + dot(low, ones)


def head_of_channel(width):
    return (
        lax.broadcasted_iota(jnp.int32, (LANES, width), 1) // HEADDIM
        == lax.broadcasted_iota(jnp.int32, (LANES, width), 0)
    ).astype(BF)


def spread_columns(ref, first, count):
    return [jnp.broadcast_to(ref[:, first + k : first + k + 1], (SPAN, LANES)) for k in range(count)]


def taps(ext, masks, at):
    terms = [ext[pl.ds(HALO - CONV + 1 + k, SPAN), at] for k in range(CONV)]
    return [t * m for t, m in zip(terms, masks)] + terms[CONV - 1 :]


def convolved(terms, weight_ref, at):
    total = weight_ref[CONV : CONV + 1, at] + terms[0] * weight_ref[0:1, at]
    for k in range(1, CONV):
        total = total + terms[k] * weight_ref[k : k + 1, at]
    return total


def forward_kernel(
    heads,
    segp_ref,
    segc_ref,
    segr_ref,
    mask_ref,
    in_a_ref,
    in_b_ref,
    halo_ref,
    weight_ref,
    b_ref,
    c_ref,
    dt_ref,
    rate_ref,
    skip_ref,
    y_ref,
    prior_ref,
    carry,
    to_end_u,
    ext,
    wide_dt,
    wide_keep,
    wide_end,
):
    block = pl.program_id(0)
    width = heads * HEADDIM

    @pl.when(block == 0)
    def _():
        carry[...] = jnp.zeros_like(carry)

    prior_ref[0] = carry[...]
    ext[0:HALO] = halo_ref[0].astype(F32)
    half = in_b_ref.shape[1]
    ext[HALO:, :half] = in_a_ref[:, :half].astype(F32)
    ext[HALO:, half:] = in_b_ref[...].astype(F32)
    segc, segr = segc_ref[...], segr_ref[...]
    dt = dt_ref[...]
    cum, cumr, keep, to_end = decays(segc, segr, segp_ref[block], dt, rate_ref[...])
    bm, cm = b_ref[...], c_ref[...]
    mixing = dot(cm, bm, ((1,), (1,)))
    mixing = jnp.where(tri(True) & (segc == segr), mixing, 0.0)
    heads_ones = head_of_channel(width)
    wide_dt[...] = expanded(dt, heads_ones)
    wide_keep[...] = expanded(keep, heads_ones)
    wide_end[...] = expanded(to_end, heads_ones)
    masks = spread_columns(mask_ref, 0, CONV - 1)
    lo = lax.broadcasted_iota(jnp.int32, (SPAN, LANES), 1) < HEADDIM
    for p in range(heads // 2):
        at = slice(p * LANES, (p + 1) * LANES)
        pre = convolved(taps(ext, masks, at), weight_ref, at)
        x2 = pre * jax.nn.sigmoid(pre)
        u2 = x2 * wide_dt[:, at]
        ub = u2.astype(BF)
        total = dot(cm, carry[:, at].astype(BF)) * wide_keep[:, at] + skip_ref[:, at] * x2
        inner = []
        for h in (2 * p, 2 * p + 1):
            decay = jnp.exp(jnp.minimum(cum[:, h : h + 1] - cumr[h : h + 1, :], 0.0))
            inner.append(dot((decay * mixing).astype(BF), ub))
        y_ref[:, at] = total + jnp.where(lo, inner[0], inner[1])
        to_end_u[:, at] = (u2 * wide_end[:, at]).astype(BF)
    fresh = dot(bm, to_end_u[...], ((0,), (0,)))
    carry[...] = wide_keep[SPAN - 1 : SPAN, :] * carry[...] + fresh


def split_dot(value, ones):
    high = value.astype(BF)
    low = (value - high.astype(F32)).astype(BF)
    return dot(high, ones) + dot(low, ones)


def backward_kernel(heads, last, begins, *refs):
    (
        segp_ref,
        segc_ref,
        segr_ref,
        mask_ref,
        in_a_ref,
        in_b_ref,
        halo_ref,
        weight_ref,
        b_ref,
        c_ref,
        dt_ref,
        rate_ref,
        skip_ref,
        y_ref,
        prior_ref,
        dy_ref,
    ) = refs[:16]
    rest = refs[16:] if begins else refs[24:]
    din_ref, dbc_ref, ddt_ref, drate_ref, dsum_ref, carry_ref, tail_ref = rest[:7]
    (
        dcarry,
        after_state,
        keep_dy,
        to_end_u,
        slopes,
        along,
        ext,
        dext,
        wide_dt,
        wide_keep,
        wide_end,
    ) = rest[7:]
    step = pl.program_id(0)
    block = last - step

    @pl.when(step == 0)
    def _():
        if begins:
            dcarry[...] = jnp.zeros_like(dcarry)
            after_state[...] = jnp.zeros_like(after_state)
            drate_ref[...] = jnp.zeros_like(drate_ref)
            dsum_ref[...] = jnp.zeros_like(dsum_ref)
            dext[SPAN:] = jnp.zeros((HALO, dext.shape[1]), F32)
        else:
            drate_in, dsum_in, carry_in, tail_in, after_in = refs[16:21]
            dcarry[...] = carry_in[...]
            after_state[...] = after_in[0]
            drate_ref[...] = drate_in[...]
            dsum_ref[...] = dsum_in[...]
            dext[SPAN:] = tail_in[...]

    ext[0:HALO] = halo_ref[0].astype(F32)
    half = in_b_ref.shape[1]
    ext[HALO:, :half] = in_a_ref[:, :half].astype(F32)
    ext[HALO:, half:] = in_b_ref[...].astype(F32)
    segc, segr = segc_ref[...], segr_ref[...]
    dt = dt_ref[...]
    cum, cumr, keep, to_end = decays(segc, segr, segp_ref[block], dt, rate_ref[...])
    bm, cm = b_ref[...], c_ref[...]
    allowed = tri(False) & (segc == segr)
    mixing = jnp.where(allowed, dot(bm, cm, ((1,), (1,))), 0.0)
    heads_ones = head_of_channel(heads * HEADDIM)
    wide_dt[...] = expanded(dt, heads_ones)
    wide_keep[...] = expanded(keep, heads_ones)
    wide_end[...] = expanded(to_end, heads_ones)
    masks = spread_columns(mask_ref, 0, CONV - 1)
    moved = spread_columns(mask_ref, CONV - 1, CONV - 1)
    lo = lax.broadcasted_iota(jnp.int32, (SPAN, LANES), 1) < HEADDIM
    dmixing = jnp.zeros((SPAN, SPAN), F32)
    for p in range(heads // 2):
        at = slice(p * LANES, (p + 1) * LANES)
        terms = taps(ext, masks, at)
        pre = convolved(terms, weight_ref, at)
        sig = jax.nn.sigmoid(pre)
        x2 = pre * sig
        dt2 = wide_dt[:, at]
        u2 = x2 * dt2
        dyb = dy_ref[:, at]
        dy2 = dyb.astype(F32)
        skip = skip_ref[:, at]
        te2 = wide_end[:, at]
        u_sides = (jnp.where(lo, u2, 0.0).astype(BF), jnp.where(lo, 0.0, u2).astype(BF))
        du = te2 * dot(bm, dcarry[:, at].astype(BF))
        inner = []
        for k in range(2):
            h = 2 * p + k
            decay = jnp.exp(jnp.minimum(cumr[h : h + 1, :] - cum[:, h : h + 1], 0.0))
            inner.append(dot((decay * mixing).astype(BF), dyb))
            dmixing = dmixing + decay * dot(u_sides[k], dyb, ((1,), (1,)))
        du = du + jnp.where(lo, inner[0], inner[1])
        keep_dy[:, at] = (wide_keep[:, at] * dy2).astype(BF)
        to_end_u[:, at] = (te2 * u2).astype(BF)
        slopes[:, at] = dy2 * (y_ref[:, at] - skip * x2) - u2.astype(BF).astype(F32) * du
        along[:, at] = x2 * du
        dpre = (dt2 * du + skip * dy2) * (sig * (1.0 + pre * (1.0 - sig)))
        dext[0:SPAN, at] = dpre
        for k in range(CONV):
            dsum_ref[k : k + 1, at] += jnp.sum(dpre * terms[k], axis=0, keepdims=True)
        dsum_ref[CONV : CONV + 1, at] += jnp.sum(dpre, axis=0, keepdims=True)
        dsum_ref[CONV + 1 : CONV + 2, at] += jnp.sum(dy2 * x2, axis=0, keepdims=True)
        din = dpre * weight_ref[CONV - 1 : CONV, at]
        for k in range(CONV - 1):
            later = dext[pl.ds(CONV - 1 - k, SPAN), at]
            din = din + later * moved[k] * weight_ref[k : k + 1, at]
        din_ref[:, at] = din.astype(BF)
    dext[SPAN:] = dext[0:HALO]
    dmixing = jnp.where(allowed, dmixing, 0.0).astype(BF)
    dstate = dcarry[...].astype(BF)
    prior = prior_ref[0]
    dbc_ref[:, :STATE] = dot(dmixing, cm) + dot(to_end_u[...], dstate, ((1,), (1,)))
    dbc_ref[:, STATE:] = dot(dmixing, bm, ((0,), (0,))) + dot(
        keep_dy[...], prior.astype(BF), ((1,), (1,))
    )
    width = heads * HEADDIM
    ones = (
        lax.broadcasted_iota(jnp.int32, (width, LANES), 0) // HEADDIM
        == lax.broadcasted_iota(jnp.int32, (width, LANES), 1)
    ).astype(BF)
    at_end = jnp.sum(dcarry[...] * after_state[...], axis=0, keepdims=True)
    at_end = split_dot(jnp.broadcast_to(at_end, (16, width)), ones)[:1]
    dcum = split_dot(slopes[...], ones)
    da = dot(tri(False).astype(F32), dcum, precision=HIGH) + at_end
    ddt_ref[...] = rate_ref[...] * da + split_dot(along[...], ones)
    drate_ref[...] += jnp.sum(dt * da, axis=0, keepdims=True)
    fresh = dot(cm, keep_dy[...], ((0,), (0,)))
    dcarry[...] = wide_keep[SPAN - 1 : SPAN, :] * dcarry[...] + fresh
    after_state[...] = prior

    @pl.when(step == pl.num_programs(0) - 1)
    def _():
        carry_ref[...] = dcarry[...]
        tail_ref[...] = dext[SPAN:]


def scan_specs(heads, at, in_widths):
    width = heads * HEADDIM

    def rows(n):
        return pl.BlockSpec((SPAN, n), lambda i: (at(i), 0))

    def whole(*shape):
        return pl.BlockSpec(shape, lambda i: (0,) * len(shape))

    ins = [
        pl.BlockSpec(memory_space=pltpu.SMEM),
        rows(1),
        pl.BlockSpec((1, SPAN), lambda i: (0, at(i))),
        rows(LANES),
        rows(in_widths[0]),
        rows(in_widths[1]),
        pl.BlockSpec((1, HALO, width), lambda i: (at(i), 0, 0)),
        whole(8, width),
        rows(STATE),
        rows(STATE),
        rows(LANES),
        whole(1, LANES),
        whole(1, width),
    ]
    prior = pl.BlockSpec((1, STATE, width), lambda i: (at(i), 0, 0))
    return rows, whole, ins, prior


def scan_forward(heads, blocks, operands):
    rows, whole, ins, prior = scan_specs(heads, lambda i: i, [operands[n].shape[1] for n in (4, 5)])
    width = heads * HEADDIM
    return call(
        functools.partial(forward_kernel, heads),
        grid=(blocks,),
        in_specs=ins,
        out_specs=[rows(width), prior],
        out_shape=[
            jax.ShapeDtypeStruct((blocks * SPAN, width), F32),
            jax.ShapeDtypeStruct((blocks, STATE, width), F32),
        ],
        scratch_shapes=[
            pltpu.VMEM((STATE, width), F32),
            pltpu.VMEM((SPAN, width), BF),
            pltpu.VMEM((HALO + SPAN, width), F32),
            pltpu.VMEM((SPAN, width), F32),
            pltpu.VMEM((SPAN, width), F32),
            pltpu.VMEM((SPAN, width), F32),
        ],
        name="scan_forward",
    )(*operands)


def scan_backward(heads, blocks, lowest, last, operands, y, priors, dy, before=None):
    rows, whole, ins, prior = scan_specs(
        heads, lambda i: last - i, [operands[n].shape[1] for n in (4, 5)]
    )
    width = heads * HEADDIM
    more, more_specs, aliases = [], [], {}
    if before is not None:
        more = list(before[3:]) + [priors] + list(before[:3])
        more_specs = [
            whole(1, LANES),
            whole(8, width),
            whole(STATE, width),
            whole(HALO, width),
            pl.BlockSpec((1, STATE, width), lambda i: (last + 1, 0, 0)),
        ] + [pl.BlockSpec(memory_space=pl.ANY)] * 3
        aliases = {len(ins) + 8 + n: n for n in range(3)}
    return call(
        functools.partial(backward_kernel, heads, last, before is None),
        grid=(last - lowest + 1,),
        in_specs=ins + [rows(width), prior, rows(width)] + more_specs,
        out_specs=[
            rows(width),
            rows(2 * STATE),
            rows(LANES),
            whole(1, LANES),
            whole(8, width),
            whole(STATE, width),
            whole(HALO, width),
        ],
        out_shape=[
            jax.ShapeDtypeStruct((blocks * SPAN, width), BF),
            jax.ShapeDtypeStruct((blocks * SPAN, 2 * STATE), F32),
            jax.ShapeDtypeStruct((blocks * SPAN, LANES), F32),
            jax.ShapeDtypeStruct((1, LANES), F32),
            jax.ShapeDtypeStruct((8, width), F32),
            jax.ShapeDtypeStruct((STATE, width), F32),
            jax.ShapeDtypeStruct((HALO, width), F32),
        ],
        scratch_shapes=[
            pltpu.VMEM((STATE, width), F32),
            pltpu.VMEM((STATE, width), F32),
            pltpu.VMEM((SPAN, width), BF),
            pltpu.VMEM((SPAN, width), BF),
            pltpu.VMEM((SPAN, width), F32),
            pltpu.VMEM((SPAN, width), F32),
            pltpu.VMEM((HALO + SPAN, width), F32),
            pltpu.VMEM((SPAN + HALO, width), F32),
            pltpu.VMEM((SPAN, width), F32),
            pltpu.VMEM((SPAN, width), F32),
            pltpu.VMEM((SPAN, width), F32),
        ],
        input_output_aliases=aliases,
        name="scan_backward",
    )(*operands, y, priors, dy, *more)


def as_columns(rows):
    few, tokens = rows.shape
    return jnp.concatenate([rows, jnp.zeros((LANES - few, tokens), F32)]).T


def level_block(pieces, spot):
    piece, lead = spot
    return pieces[piece][lead + (slice(None), slice(None))].astype(F32)


def upper_kernel(where, plan, nd, tok, ns, here_ref, range_ref, count_ref, ratio_ref, q_turned, *refs):
    count = 3 + 2 * LEVELS
    pieces, outs = refs[:count], refs[count:]
    upper_ref, grad_refs, coefs = outs[0], outs[1 : 2 * nd], outs[2 * nd]

    @pl.when(pl.program_id(0) == 0)
    def _():
        rows = [count_ref[j, w] * ratio_ref[w : w + 1, :] for j in range(len(plan)) for w in range(LEVELS)]
        coefs[...] = as_columns(jnp.concatenate(rows))

    for k in range(ns):
        at = here_ref[0] ^ k
        rows = pl.ds(pl.multiple_of(at * tok, tok), tok)
        levels = [level_block(pieces, where[w][k]) for w in range(LEVELS)]
        for j in range(len(plan)):
            total = None
            for w in plan[j]:
                n = j * LEVELS + w
                term = coefs[rows, n : n + 1] * levels[w]
                total = term if total is None else total + term
            upper_ref[j, rows, :] = total.astype(BF)
    count = q_turned.shape[0] // nd
    for k in range(nd):
        index = here_ref[1] ^ k
        rows = pl.ds(pl.multiple_of(index * count, count), count)
        value = dot(q_turned[rows, :], upper_ref[range_ref[index]]).astype(BF)
        if k:
            grad_refs[2 * k - 1][...] = value[: count // 2]
            grad_refs[2 * k][...] = value[count // 2 :]
        else:
            grad_refs[0][...] = value


def products_kernel(where, plan, lanes, tok, ns, nd, here_ref, count_ref, q_ref, *refs):
    count = 3 + 2 * LEVELS
    held_ref, pieces, outs = refs[0], refs[1 : 1 + count], refs[1 + count :]
    prod_refs, inner_ref, w_ref, sums = outs[:ns], outs[ns], outs[ns + 1], outs[ns + 2]
    step = pl.program_id(0)
    rows_of = w_ref.shape[0] // nd
    for k in range(nd):
        at = pl.multiple_of((here_ref[1] ^ k) * rows_of, rows_of)
        w_ref[pl.ds(at, rows_of), :] = held_ref[:, k].reshape(rows_of, w_ref.shape[1])

    @pl.when(step == 0)
    def _():
        sums[...] = jnp.zeros_like(sums)

    for k in range(ns):
        at = here_ref[0] ^ k
        rows = pl.ds(pl.multiple_of(at * tok, tok), tok)
        values = [dot(q_ref[rows, a:b], w_ref[a:b, :]) for a, b in lanes]
        for j, value in enumerate(values):
            prod_refs[k][j] = value.astype(BF)
        for w in range(LEVELS):
            total = None
            for j in range(len(lanes)):
                if w in plan[j]:
                    term = values[j] * count_ref[j, w]
                    total = term if total is None else total + term
            part = total * level_block(pieces, where[w][k])
            folded = part[:, :LANES]
            for c in range(LANES, part.shape[1], LANES):
                folded = folded + part[:, c : c + LANES]
            sums[w, rows, :] += folded

    @pl.when(step == pl.num_programs(0) - 1)
    def _():
        lane = lax.broadcasted_iota(jnp.int32, sums.shape[1:], 1)
        total = jnp.zeros(sums.shape[1:], F32)
        for w in range(LEVELS):
            total = jnp.where(lane == w, jnp.sum(sums[w], axis=1, keepdims=True), total)
        inner_ref[...] = total.T[:LEVELS]


def gate_kernel(
    starts, wide, count_ref, upper_ref, w_ref, y_ref, z_ref, gain_ref, ratio_ref, mean_ref, dy_ref, dz_ref, grad_ref, coefs
):
    step = pl.program_id(0)

    @pl.when(step == 0)
    def _():
        cubes = ratio_ref[...] * ratio_ref[...] * ratio_ref[...] * mean_ref[...]
        rows = []
        for j in range(len(starts)):
            total = cubes[0:1] * count_ref[j, 0]
            for w in range(1, LEVELS):
                total = total + cubes[w : w + 1] * count_ref[j, w]
            rows.append(total)
        columns = as_columns(jnp.concatenate(rows))
        for j in range(len(starts)):
            coefs[j] = jnp.broadcast_to(columns[:, j : j + 1], coefs.shape[1:])

    grad_all = dot(upper_ref[0], w_ref[...], ((1,), (1,)))
    coef = coefs[tile_range(starts, wide, step)]
    for c in range(0, wide, LANES):
        at = slice(c, c + LANES)
        grad_t = grad_all[:, at]
        z = z_ref[:, at].astype(F32)
        sig = jax.nn.sigmoid(z)
        act = z * sig
        y = y_ref[:, at]
        q = y * act
        dq = gain_ref[:, at] * grad_t - q * coef
        dy_ref[:, at] = (dq * act).astype(BF)
        dz_ref[:, at] = (dq * y * (sig * (1.0 + z * (1.0 - sig)))).astype(BF)
        grad_ref[0:1, at] = jnp.sum(q * grad_t, axis=0, keepdims=True)


def tile_range(starts, wide, step):
    index = 0
    for start in starts[1:]:
        index = index + jnp.where(step * wide >= start, 1, 0)
    return index


def mixed_kernel(plan, split, ns, tok, here_ref, count_ref, ratio_ref, x_ref, *refs):
    shares, out_ref = refs[:-1], refs[-1]
    at = pl.ds(pl.multiple_of(here_ref[0] * tok, tok), tok)
    ratios = as_columns(ratio_ref[:, at])
    x = x_ref[...].astype(F32)
    for w in range(LEVELS):
        total = None
        for k in range(ns):
            for j in plan[w]:
                at = (k, j) if k < 3 or j < split else (k + 1, j - split)
                term = shares[at[0]][at[1]].astype(F32) * count_ref[k, j * LEVELS + w]
                total = term if total is None else total + term
        out_ref[w] = (x + ratios[:, w : w + 1] * total).astype(BF)


def dp_terms(others):
    return [swapped(other, "dp", k + 1) for k, other in enumerate(others)]


def over_seq(value):
    dense = value.reshape(-1, LANES)
    total = dense
    for k in range(1, lax.axis_size("seq")):
        total = total + swapped(dense, "seq", k)
    return total.reshape(value.shape)


def fsdp_half(own, got):
    nf = lax.axis_size("fsdp")
    f = lax.axis_index("fsdp")

    def part(offset):
        total = picked(own, f ^ offset).astype(F32)
        for other in got:
            total = total + picked(other, f ^ offset).astype(F32)
        return total.astype(BF)

    kept = jnp.stack([part(e) for e in range(0, nf, 2)])
    sent = jnp.stack([part(e ^ 1) for e in range(0, nf, 2)])
    return kept, sent


def fsdp_rest(kept, got):
    k = 2
    while k < lax.axis_size("fsdp"):
        total = (kept.astype(F32) + got.astype(F32)).astype(BF)
        kept, sent = total[::2], total[1::2]
        got = swapped(sent, "fsdp", k)
        k *= 2
    return kept[0], got[0]


def shards(
    tokens,
    lengths,
    norm_gain,
    w_in,
    w_dt,
    conv_w,
    conv_b,
    dt_bias,
    a_log,
    skip,
    gate_gain,
    w_out,
    cotangent,
):
    nd, ns, nf = lax.axis_size("dp"), lax.axis_size("seq"), lax.axis_size("fsdp")
    d, s, f = lax.axis_index("dp"), lax.axis_index("seq"), lax.axis_index("fsdp")
    tok = tokens.shape[1]
    length = ns * tok
    blocks = length // SPAN
    heads = HEADS // ns
    run = heads // nd
    width = heads * HEADDIM
    own_bc = 2 * STATE // ns
    used = width + own_bc
    cols = -(-(used + heads) // LANES) * LANES
    rows_in = w_in.shape[0]
    reach = CONV - 1

    levels = np.array(
        [[level_of(dd * (HEADS // nd) + ss * run + i) for dd in range(nd) for i in range(run)] for ss in range(ns)]
    )
    cuts = [0] + [h for h in range(1, heads) if (levels[:, h] != levels[:, h - 1]).any()] + [heads]
    ranges = [(a, b) for a, b in zip(cuts, cuts[1:])]
    range_level = np.array([[levels[ss, a] for a, _ in ranges] for ss in range(ns)])
    counts = (range_level[:, :, None] <= np.arange(LEVELS)[None, None, :]).astype(np.float32)
    counted = picked(jnp.asarray(counts), s)
    theirs = picked(
        jnp.asarray(np.stack([[counts[i ^ k].reshape(-1) for k in range(ns)] for i in range(ns)])), s
    )
    lowest = [int(range_level[ss].min()) for ss in range(ns)]

    def by_head(vector):
        lead = vector.shape[:-1]
        per = vector.shape[-1] // HEADS
        cut = vector.reshape(lead + (nd, ns, run * per))
        mine = lax.dynamic_index_in_dim(cut, s, len(lead) + 1, keepdims=False)
        return mine.reshape(lead + (heads * per,))

    def for_groups(matrix):
        per = matrix.shape[1] // HEADS
        cut = matrix.reshape(matrix.shape[0], nd, ns, run * per)
        return jnp.transpose(cut, (2, 0, 1, 3)).reshape(ns, matrix.shape[0], heads * per)

    def from_groups(stack):
        per = stack.shape[2] // heads
        cut = stack.reshape(ns, stack.shape[1], nd, run * per)
        return jnp.transpose(cut, (1, 2, 0, 3)).reshape(stack.shape[1], HEADS * per)

    pad_cols = cols - used - heads
    half = width // 2
    first = half + cols - width
    group_x = for_groups(w_in[:, INNER : 2 * INNER])
    stack = jnp.concatenate(
        [
            group_x[:, :, :half],
            w_in[:, 2 * INNER :].reshape(rows_in, ns, own_bc).transpose(1, 0, 2),
            for_groups(w_dt),
            jnp.zeros((ns, rows_in, pad_cols), BF),
            group_x[:, :, half:],
            for_groups(w_in[:, :INNER]),
        ],
        axis=2,
    )
    own_x = tokens[0].astype(F32)
    scale = lax.rsqrt(jnp.mean(own_x * own_x, axis=-1, keepdims=True) + EPS)
    xn_own = (own_x * scale * norm_gain).astype(BF)
    xn_across = swapped(xn_own, "seq", 2)
    xn_pieces = [xn_own, swapped(xn_own, "seq", 1), xn_across, swapped(xn_across, "seq", 1)]
    arrived = [picked(stack, s)] + [swapped(picked(stack, s ^ k), "seq", k) for k in range(1, ns)]
    mine = filled((ns, rows_in, stack.shape[2]), [(p, None, (s ^ k, None, None)) for k, p in enumerate(arrived)])
    mine_z = mine[:, :, cols:]

    def needed(at, level):
        return min(lowest[at], lowest[at ^ 1]) <= level

    halves = [cotangent[w : w + 2, 0] for w in range(0, LEVELS, 2)]
    singles = [cotangent[w, 0] for w in range(LEVELS)]

    def beside(level, *others):
        block = after(halves[level // 2], *others)
        return swapped(block, "seq", 1, lambda i, j: needed(j, level + 1))

    def across(level, *others):
        block = after(singles[level], *others)
        return swapped(block, "seq", 2, lambda i, j: needed(j, level))

    def far(level, block):
        return swapped(block, "seq", 1, lambda i, j: needed(j, level))

    positions = jnp.arange(length, dtype=jnp.int32)
    ends = jnp.cumsum(lengths[0])[:-1]
    seg = jnp.sum((positions[:, None] >= ends[None, :]).astype(jnp.int32), axis=1)
    seg_before = jnp.concatenate([jnp.full((1,), -1, jnp.int32), seg[SPAN - 1 : length - 1 : SPAN]])
    seg_pad = jnp.concatenate([jnp.full((reach,), -1, jnp.int32), seg])
    masks = [(seg_pad[k : k + length] == seg) for k in range(reach)]
    mask_cols = [m.astype(F32) for m in masks]
    mask_cols += [jnp.pad(m, (0, reach - k))[reach - k :] for k, m in enumerate(mask_cols)]
    mask_cols = jnp.pad(jnp.stack(mask_cols, axis=1), ((0, 0), (0, LANES - 2 * reach)))

    def conv_params(s_part, bc_part):
        return by_head(s_part), bc_part

    weight_s = jnp.concatenate(
        [by_head(conv_w[:, :INNER]), by_head(conv_b[None, :INNER]), jnp.zeros((3, width), F32)]
    )
    weight_r = jnp.pad(
        lax.dynamic_slice_in_dim(conv_w, INNER + s * own_bc, own_bc, 1), ((0, 0), (0, cols - used))
    )
    bias_r = jnp.pad(
        lax.dynamic_slice_in_dim(conv_b, INNER + s * own_bc, own_bc, 0), (0, cols - used)
    )
    bias = by_head(dt_bias)
    rate = -jnp.exp(by_head(a_log))
    skip_own = by_head(skip)
    gain = by_head(gate_gain)

    def over_fsdp(chunk):
        return lax.all_gather(chunk, "fsdp", axis=0, tiled=False)

    def over_dp(held):
        return [held] + [swapped(held, "dp", j) for j in range(1, nd)]

    def whole(pieces, columns):
        moves = [
            (piece, i, (d ^ j, None, i, None, None)) for j, piece in enumerate(pieces) for i in range(nf)
        ]
        return filled((nd, ns, nf, rows_in, columns), moves).reshape(D, columns)

    held_a = over_fsdp(mine[:, :, :first])
    held_b = over_fsdp(mine[:, :, first:cols])
    other_out = [swapped(w_out, "dp", j) for j in range(1, nd)]
    held_a, other_out, xn_pieces[2] = together(held_a, other_out, xn_pieces[2])
    small_ones = (seg, seg_before, mask_cols, weight_s, weight_r, bias_r, bias, rate, skip_own, gain, theirs)
    held_a, small_ones, halves, singles = together(held_a, small_ones, halves, singles)
    seg, seg_before, mask_cols, weight_s, weight_r, bias_r, bias, rate, skip_own, gain, theirs = small_ones
    near_high, near_low = beside(2, held_a), beside(0, held_a)
    chip3 = across(3, held_a)
    pieces_a = over_dp(held_a)
    held_b, pieces_a, chip3, near_high, xn_pieces = together(
        held_b, pieces_a, chip3, near_high, xn_pieces
    )
    xn = filled((ns, tok, D), [(p, None, (s ^ k, None, None)) for k, p in enumerate(xn_pieces)])
    xn = xn.reshape(length, D)

    far3 = far(3, chip3)
    pieces_b = over_dp(held_b)
    held_z = over_fsdp(after(mine_z, held_a))
    pair_out = jnp.stack([w_out] + other_out)

    xn_turned = xn.T
    here = jnp.stack([s, d]).astype(jnp.int32)
    full_a = whole(pieces_a, first)
    proj_a = dot(xn, full_a).astype(BF)

    proj_r = proj_a[:, half:]
    mixer = jnp.concatenate([jnp.zeros((reach, cols - width), BF), proj_r], axis=0)

    def taken(k):
        rows = mixer[k : k + length].astype(F32)
        return rows * mask_cols[:, k : k + 1] if k < reach else rows

    pre_r = bias_r
    for k in range(CONV):
        pre_r = pre_r + taken(k) * weight_r[k]
    bc_own = jax.nn.silu(pre_r).astype(BF)[:, :own_bc]
    bc_across = swapped(bc_own, "seq", 2)
    bc = [bc_own, swapped(bc_own, "seq", 1), bc_across, swapped(bc_across, "seq", 1)]
    chip2, chip1 = across(2, bc[2]), across(1, bc[2])
    full_b = whole(pieces_b, half)
    proj_b = dot(xn, after(full_b, proj_a, xn_turned, bc[2])).astype(BF)
    proj_b, far3, near_low, held_z = together(proj_b, far3, near_low, held_z)
    pieces_z = over_dp(held_z)
    held_out = over_fsdp(after(pair_out, proj_b))
    bc = reordered_by_xor(bc, s)
    b_in = jnp.concatenate(bc[: ns // 2], axis=1)
    c_out = jnp.concatenate(bc[ns // 2 :], axis=1)

    def padded(rows):
        return jnp.pad(rows, ((0, 0), (0, LANES - rows.shape[1])))

    pre_dt = proj_r[:, own_bc : own_bc + heads].astype(F32) + bias
    steps = jax.nn.softplus(pre_dt)
    tails = [
        p.reshape(blocks, SPAN, p.shape[1])[: blocks - 1, SPAN - HALO :, :half] for p in (proj_a, proj_b)
    ]
    operands = (
        seg_before,
        seg[:, None],
        seg[None, :],
        mask_cols,
        proj_a,
        proj_b,
        jnp.concatenate([jnp.zeros((1, HALO, width), BF), jnp.concatenate(tails, axis=2)]),
        weight_s,
        b_in,
        c_out,
        padded(steps),
        padded(rate[None, :]),
        jnp.repeat(skip_own, HEADDIM)[None, :],
    )
    y, priors = scan_forward(heads, blocks, operands)
    y, chip2 = together(y, chip2)
    far2, chip0 = far(2, chip2), across(0, y)
    parts = pieces_z if rows_in % 16 == 0 else [whole(pieces_z, width)]
    lanes = [(a * HEADDIM, b * HEADDIM) for a, b in ranges]
    starts = [a for a, _ in lanes]
    wide = min(min(b - a for a, b in lanes), TILE)
    proj_z, full_z, q_gain, q_turned, squares = gated_projection(
        here, xn, parts, nd, width, y, gain[None], starts, wide
    )
    squares, chip1 = together(squares[: len(lanes)], chip1)
    far1 = far(1, chip1)
    widths = np.array([[(HEADS >> 3 - w) * HEADDIM] for w in range(LEVELS)], np.float32)
    per_level = jnp.sum(counted[:, :, None] * squares[:, None, :], axis=0)
    ratio, chip0 = together(lax.rsqrt(over_seq(per_level) / widths + EPS), chip0)
    far0 = far(0, chip0)

    plan = [[w for w in range(LEVELS) if range_level[:, j].min() <= w] for j in range(len(lanes))]
    out_rows = width // nd
    range_of = [next(j for j, (a, b) in enumerate(lanes) if a <= i * out_rows < b) for i in range(nd)]
    smem = pl.BlockSpec(memory_space=pltpu.SMEM)
    cot_pieces = [cotangent, near_low, near_high, chip0, chip1, chip2, chip3, far0, far1, far2, far3]
    cot_specs = [pl.BlockSpec((LEVELS, 1, tok, WIDE), lambda i: (0, 0, 0, i))]
    cot_specs += [pl.BlockSpec((2, tok, WIDE), lambda i: (0, 0, i))] * 2
    cot_specs += [pl.BlockSpec((tok, WIDE), lambda i: (0, i))] * (2 * LEVELS)
    where = [[(0, (w, 0)), (1 + w // 2, (w % 2,)), (3 + w, ()), (3 + LEVELS + w, ())] for w in range(LEVELS)]
    upper, *grad_out = call(
        functools.partial(upper_kernel, where, plan, nd, tok, ns),
        grid=(D // WIDE,),
        in_specs=[
            smem,
            smem,
            smem,
            pl.BlockSpec((LEVELS, length), lambda i: (0, 0)),
            pl.BlockSpec((width, length), lambda i: (0, 0)),
        ]
        + cot_specs,
        out_specs=[pl.BlockSpec((len(lanes), length, WIDE), lambda i: (0, 0, i))]
        + [pl.BlockSpec((out_rows, WIDE), lambda i: (0, i))]
        + [pl.BlockSpec((out_rows // 2, WIDE), lambda i: (0, i))] * (2 * nd - 2),
        out_shape=[jax.ShapeDtypeStruct((len(lanes), length, D), BF)]
        + [jax.ShapeDtypeStruct((out_rows, D), BF)]
        + [jax.ShapeDtypeStruct((out_rows // 2, D), BF)] * (2 * nd - 2),
        scratch_shapes=[pltpu.VMEM((length, LANES), F32)],
        name="upper",
    )(here, jnp.asarray(range_of, jnp.int32), counted, ratio, q_turned, *cot_pieces)
    out_first, out_second = dp_terms(grad_out[1::2]), dp_terms(grad_out[2::2])

    held_out, upper = together(held_out, upper)
    *shares, inner, full_out = call(
        functools.partial(products_kernel, where, plan, lanes, tok, ns, nd),
        grid=(D // WIDE,),
        in_specs=[
            smem,
            smem,
            pl.BlockSpec((length, width), lambda i: (0, 0)),
        ]
        + [pl.BlockSpec((nf, nd, w_out.shape[0], WIDE), lambda i: (0, 0, 0, i))]
        + cot_specs,
        out_specs=[pl.BlockSpec((len(lanes), tok, WIDE), lambda i: (0, 0, i))] * ns
        + [pl.BlockSpec((LEVELS, length), lambda i: (0, 0))]
        + [pl.BlockSpec((width, WIDE), lambda i: (0, i))],
        out_shape=[jax.ShapeDtypeStruct((len(lanes), tok, D), BF)] * ns
        + [jax.ShapeDtypeStruct((LEVELS, length), F32)]
        + [jax.ShapeDtypeStruct((width, D), BF)],
        scratch_shapes=[pltpu.VMEM((LEVELS, length, LANES), F32)],
        name="products",
    )(here, counted, q_gain, held_out, *cot_pieces)
    means, out_first = together(over_seq(inner) / widths, out_first)
    shares[1:3] = [swapped(after(shares[k], means), "seq", k) for k in (1, 2)]
    split = (len(lanes) + 1) // 2
    third = [swapped(after(shares[3][:split], shares[1]), "seq", 3), shares[3][split:]]

    cols_of = pl.BlockSpec((length, wide), lambda i: (0, i))
    scalars = pl.BlockSpec((LEVELS, length), lambda i: (0, 0))
    dy, dz, grad_gate = call(
        functools.partial(gate_kernel, starts, wide),
        grid=(width // wide,),
        in_specs=[
            smem,
            pl.BlockSpec((1, length, D), lambda i: (tile_range(starts, wide, i), 0, 0)),
            pl.BlockSpec((wide, D), lambda i: (i, 0)),
            cols_of,
            cols_of,
            pl.BlockSpec((1, wide), lambda i: (0, i)),
            scalars,
            scalars,
        ],
        out_specs=[cols_of, cols_of, pl.BlockSpec((8, wide), lambda i: (0, i))],
        out_shape=[
            jax.ShapeDtypeStruct((length, width), BF),
            jax.ShapeDtypeStruct((length, width), BF),
            jax.ShapeDtypeStruct((8, width), F32),
        ],
        scratch_shapes=[pltpu.VMEM((len(lanes), length, LANES), F32)],
        name="gate_backward",
    )(counted, upper, full_out, y, proj_z, gain[None], ratio, means)
    grad_gate = grad_gate[0]

    def in_terms(dproj, at, first=0, columns=None):
        columns = columns or dproj.shape[1]
        out = row_terms(xn_turned, dproj, at, nd, ns, nf, first, columns)
        return out.reshape(nf, ns * rows_in, columns)

    z_other = [in_terms(dz, d ^ k) for k in range(1, nd)]
    z_got = dp_terms(z_other)
    dy, out_second, shares[1] = together(after(dy, *z_other), out_second, shares[1])
    chunk = (nf, out_rows // nf, D)
    out_got = [jnp.concatenate([u, v]).reshape(chunk) for u, v in zip(out_first, out_second)]
    out_kept, out_sent = fsdp_half(grad_out[0].reshape(chunk), out_got)
    dy = after(dy, out_sent)
    out_half = swapped(out_sent, "fsdp", 1)

    middle = blocks * 3 // 8
    later = list(scan_backward(heads, blocks, middle, blocks - 1, operands, y, priors, dy))
    carry, out_half, shares[2] = together(later[5], out_half, shares[2])
    out_pair = fsdp_rest(out_kept, out_half)
    later = later[:5] + [carry] + later[6:]
    dproj_s, dbc, ddt, drate, dsum, _, _ = scan_backward(
        heads, blocks, 0, middle - 1, operands, y, priors, dy, later
    )
    dproj_s, dbc, out_pair = together(dproj_s, dbc, out_pair)

    dbc = dbc.astype(BF)
    slices = reordered_by_xor([dbc[:, j * own_bc : (j + 1) * own_bc] for j in range(ns)], s)
    beside_bc = swapped(jnp.concatenate([slices[1], slices[3]], axis=1), "seq", 1)
    sum_bc = jnp.concatenate([slices[0], slices[2]], axis=1).astype(F32) + beside_bc.astype(F32)
    across_bc = swapped(sum_bc[:, own_bc:].astype(BF), "seq", 2)

    z_own = in_terms(after(dz, dproj_s), d)
    z_own, z_got = together(z_own, z_got)
    z_kept, z_sent = fsdp_half(z_own, z_got)
    z_half = swapped(z_sent, "fsdp", 1)
    late_s = after(dproj_s, z_sent)
    left_other = [in_terms(late_s, d ^ k, 0, half) for k in range(1, nd)]
    left_got = dp_terms(left_other)
    third[1] = swapped(after(third[1], across_bc), "seq", 3)
    dbc_own = sum_bc[:, :own_bc] + across_bc.astype(F32)
    dproj_r, small_sums = small_back(
        own_bc,
        pre_r,
        padded(after(dbc_own, *left_other)),
        proj_r,
        mask_cols,
        weight_r,
        ddt,
        padded(pre_dt),
    )

    late_s, late_r = after(dproj_s, *left_other), dproj_r
    right_other = [
        jnp.concatenate([in_terms(late_s, d ^ k, half, half), in_terms(late_r, d ^ k)], axis=2)
        for k in range(1, nd)
    ]
    right_got = dp_terms(right_other)

    dxn = input_grad(dz, dproj_s, after(dproj_r, *right_other), full_z, full_a, full_b, ns, tok)
    pair = swapped(jnp.stack([picked(dxn, s ^ 1), picked(dxn, s ^ 3)]), "seq", 1)

    dxn, z_half, left_got, third[0] = together(dxn, z_half, left_got, third[0])
    z_pair = fsdp_rest(z_kept, z_half)
    own_s = in_terms(after(dproj_s, dxn), d)
    left_kept, left_sent = fsdp_half(own_s[:, :, :half], left_got)
    left_half = swapped(left_sent, "fsdp", 1)
    own_r = in_terms(after(dproj_r, left_sent), d)
    flat = flattened(
        [
            jnp.concatenate([dsum[:CONV], small_sums[:CONV, :own_bc]], axis=1).reshape(-1),
            dsum[CONV],
            small_sums[CONV, :own_bc],
            grad_gate,
            small_sums[CONV + 1, :heads],
            drate[0, :heads] * rate,
            jnp.sum(dsum[CONV + 1].reshape(heads, HEADDIM), axis=1),
        ]
    )
    near = picked(dxn, s).astype(F32) + pair[0].astype(F32)
    far_sum = (picked(dxn, s ^ 2).astype(F32) + pair[1].astype(F32)).astype(BF)
    dxn_across = swapped(far_sum, "seq", 2)
    right_got, far_sum, left_half = together(right_got, far_sum, left_half)
    left_pair = fsdp_rest(left_kept, left_half)
    own_right = jnp.concatenate([own_s[:, :, half:], own_r], axis=2)
    right_kept, right_sent = fsdp_half(own_right, right_got)
    right_half = swapped(right_sent, "fsdp", 1)

    mixed = call(
        functools.partial(
            mixed_kernel,
            [[j for j in range(len(lanes)) if range_level[:, j].min() <= w] for w in range(LEVELS)],
            split,
            ns,
            tok,
        ),
        grid=(D // WIDE,),
        in_specs=[
            smem,
            smem,
            pl.BlockSpec((LEVELS, length), lambda i: (0, 0)),
            pl.BlockSpec((tok, WIDE), lambda i: (0, i)),
        ]
        + [pl.BlockSpec((p.shape[0], tok, WIDE), lambda i: (0, 0, i)) for p in shares[:3] + third],
        out_specs=pl.BlockSpec((LEVELS, tok, WIDE), lambda i: (0, 0, i)),
        out_shape=jax.ShapeDtypeStruct((LEVELS, tok, D), BF),
        name="mixed",
    )(here, theirs, ratio, tokens[0], *after(shares[:3] + third, right_sent))[:, None]
    right_half, mixed, dxn_across = together(right_half, mixed, dxn_across)
    right_kept = after(right_kept, mixed)
    right_pair = fsdp_rest(right_kept, right_half)
    dxn_own = near + dxn_across.astype(F32)
    grad_norm = jnp.sum(dxn_own * own_x * scale, axis=0)
    scaled = norm_gain * dxn_own
    dx = scale * scaled - own_x * scale**3 * jnp.mean(own_x * scaled, axis=-1, keepdims=True)
    dx = (dx + jnp.sum(after(cotangent, mixed)[:, 0].astype(F32), axis=0)).astype(BF)
    flat = jnp.concatenate([flat, grad_norm.reshape(-1, LANES)])
    flat = butterfly(flat, "dp")

    def whole_sum(pair):
        total = (pair[0].astype(F32) + pair[1].astype(F32)).astype(BF)
        return total.reshape(ns, rows_in, total.shape[1])

    z_pair, left_pair = together(z_pair, left_pair)
    early = jnp.concatenate([whole_sum(z_pair), whole_sum(left_pair)], axis=2)
    early_got = [picked(early, s)] + [swapped(picked(early, s ^ k), "seq", k) for k in range(1, ns)]
    early_got, right_pair, flat = together(early_got, right_pair, flat)
    flat = butterfly(flat, "fsdp")
    late = whole_sum(right_pair)
    late_got = [picked(late, s)] + [swapped(picked(late, s ^ k), "seq", k) for k in range(1, ns)]
    early = jnp.stack(reordered_by_xor(early_got, s))
    late = jnp.stack(reordered_by_xor(late_got, s))
    got_z = early[:, :, :width]
    got_x = jnp.concatenate([early[:, :, width:], late], axis=2)
    sum_out = out_pair[0].astype(F32) + out_pair[1].astype(F32)


    sum_in = jnp.concatenate(
        [
            from_groups(got_z),
            from_groups(got_x[:, :, :width]),
            jnp.transpose(got_x[:, :, width:used], (1, 0, 2)).reshape(rows_in, 2 * STATE),
        ],
        axis=1,
    ).astype(F32)
    sum_dt = from_groups(got_x[:, :, used : used + heads]).astype(F32)

    sizes = [CONV * used, used, width, heads, heads, heads]
    filling = -sum(sizes) % 1024
    sizes += [filling, D]
    every = seq_gather(flat, s).reshape(ns, -1)
    starts = np.cumsum([0] + sizes)
    pieces = [every[:, a : a + n] for a, n in zip(starts, sizes)]

    def heads_back(rows):
        lead = rows.shape[1:-1]
        cut = rows.reshape((ns,) + lead + (nd, rows.shape[-1] // nd))
        order = tuple(range(1, 1 + len(lead))) + (1 + len(lead), 0, 2 + len(lead))
        return jnp.transpose(cut, order).reshape(lead + (-1,))

    conv_rows = pieces[0].reshape(ns, CONV, used)
    conv_all = jnp.concatenate(
        [
            heads_back(conv_rows[:, :, :width]),
            jnp.transpose(conv_rows[:, :, width:], (1, 0, 2)).reshape(CONV, 2 * STATE),
        ],
        axis=1,
    )
    bias_all = jnp.concatenate([heads_back(pieces[1][:, :width]), pieces[1][:, width:].reshape(-1)])
    return (
        mixed,
        dx[None],
        jnp.sum(pieces[7], axis=0),
        sum_in,
        sum_dt,
        conv_all,
        bias_all,
        heads_back(pieces[3]),
        heads_back(pieces[4]),
        heads_back(pieces[5]),
        heads_back(pieces[2]),
        sum_out,
    )


def solution(mesh):
    rows = P(("dp", "seq", "fsdp"), None)
    held = P(("dp", "fsdp"), "seq", None)
    levels = P(None, ("dp", "fsdp"), "seq", None)
    placed = (held, P(("dp", "fsdp"), None), P(), rows, rows, P(), P(), P(), P(), P(), P(), rows, levels)
    return jax.shard_map(
        shards,
        mesh=mesh,
        in_specs=placed,
        out_specs=(levels, held, P(), rows, rows, P(), P(), P(), P(), P(), P(), rows),
        check_vma=False,
    )
```
